32 devices in a mesh: section: 2 (over x), tensor: 4 (over y, core), dp: 4 (over z).
Axes of the slice: x: 2, y: 2, z: 4, core: 2. Of those that a mesh axis runs over, the one named last changes fastest.
Arguments:
- inputs: float32 [16, 32, 512], P('dp'), may hold values from -6 to 6
- lengths: int32 [16], P('dp'), may hold values from 1 to 32, 384 in all
- cotangent: float32 [16, 32, 512], P('dp'), may hold values from -6 to 6
- norm_gain: float32 [2, 5, 512], P('section'), may hold values from 0.5 to 1.5
- norm_bias: float32 [2, 5, 512], P('section'), may hold values from -2 to 2
- ffn_in: bfloat16 [2, 2, 512, 2048], P('section', None, None, 'tensor'), may hold values from -0.25 to 0.25
- ffn_out: bfloat16 [2, 2, 2048, 512], P('section', None, 'tensor'), may hold values from -0.125 to 0.125
- attn_in: bfloat16 [2, 4, 512, 512], P('section', None, None, 'tensor'), may hold values from -0.25 to 0.25
- pos_bias: float32 [2, 2, 512], P('section', None, 'tensor'), may hold values from -3 to 3
- attn_out: bfloat16 [2, 512, 512], P('section', 'tensor'), may hold values from -0.375 to 0.375
- conv_in: bfloat16 [2, 512, 2, 512], P('section', None, None, 'tensor'), may hold values from -0.25 to 0.25
- depthwise: float32 [2, 31, 512], P('section', None, 'tensor'), may hold values from -1 to 1
- bn_gain: float32 [2, 512], P('section', 'tensor'), may hold values from 0.5 to 1.5
- bn_shift: float32 [2, 512], P('section', 'tensor'), may hold values from -3 to 3
- conv_out: bfloat16 [2, 512, 512], P('section', 'tensor'), may hold values from -0.25 to 0.25
Outputs:
- layer_out: float32 [2, 16, 32, 512], P('section', 'dp')
- input_grads: float32 [2, 16, 32, 512], P('section', 'dp')
- grad_norm_gain: float32 [2, 5, 512], P('section')
- grad_norm_bias: float32 [2, 5, 512], P('section')
- grad_ffn_in: float32 [2, 2, 512, 2048], P('section', None, None, 'tensor')
- grad_ffn_out: float32 [2, 2, 2048, 512], P('section', None, 'tensor')
- grad_attn_in: float32 [2, 4, 512, 512], P('section', None, None, 'tensor')
- grad_pos_bias: float32 [2, 2, 512], P('section', None, 'tensor')
- grad_attn_out: float32 [2, 512, 512], P('section', 'tensor')
- grad_conv_in: float32 [2, 512, 2, 512], P('section', None, None, 'tensor')
- grad_depthwise: float32 [2, 31, 512], P('section', None, 'tensor')
- grad_bn_gain: float32 [2, 512], P('section', 'tensor')
- grad_bn_shift: float32 [2, 512], P('section', 'tensor')
- grad_conv_out: float32 [2, 512, 512], P('section', 'tensor')
The draws below stay inside these ranges and needn't reach their ends.
Inputs may be any that keep to these rules, and one draw needn't show every extreme that they name: `lengths`: frames of each utterance; they sum to 384 and the longest has exactly 32.
All inputs are finite; a program needn't handle non-finite values. No bound on the sum of `lengths` on one device may be relied on, other than what follows from the above.
Results may differ from the reference program's by a relative error of at most 0.035.
Values may be sent and summed in bfloat16 or wider, within the bound.
A program may use at most 128 MiB of HBM per device.

```python
import math
import jax
import jax.numpy as jnp
import numpy as np
from jax import lax

WIDTH = 512
HIDDEN_SIZE = 2048
HEAD = 64
KERNEL = 31
MICRO = 4
FRAMES = 32
UTTS = 16


def steps_of(stream_key, dims, pieces, least, top_value):
    def one(position, blocks):
        heights = jax.random.uniform(jax.random.fold_in(jax.random.fold_in(stream_key, 6), position), (blocks,), jnp.float32, least / len(pieces), top_value / len(pieces))
        return jnp.repeat(jnp.exp(heights), dims[position] // blocks).reshape((-1,) + (1,) * (len(dims) - position - 1))

    factor_of = one(*pieces[0])
    for cut in pieces[1:]:
        factor_of = factor_of * one(*cut)
    return factor_of


def length_profile(number_of, total, limit, slope):
    portions = [(1 << 20) // math.isqrt(grade ** slope) + 1 for grade in range(2, number_of + 1)]
    surplus, counts = total - limit - (number_of - 1), [1] * (number_of - 1)
    while surplus > 0:
        candidates = [i for i in range(number_of - 1) if counts[i] < limit]
        whole, remaining = sum([portions[i] for i in candidates]), surplus
        for i in candidates:
            more = min(limit - counts[i], max(1, remaining * portions[i] // whole), surplus)
            counts[i] = counts[i] + more
            surplus = surplus - more
    return np.array([limit] + counts)


def ragged_sizes(key, amount, total, most, lean):
    if amount == 2:
        one = jax.random.randint(key, (), max(1, total - most), min(most, total - 1) + 1)
        return jnp.stack([one, total - one])
    tallies = jnp.asarray(length_profile(amount, total, most, lean), jnp.int32)
    pairs = (amount - 1) // 2
    source_of, sink = tallies[1:1 + 2 * pairs:2], tallies[2:2 + 2 * pairs:2]
    room = jnp.minimum(source_of - 1, most - sink)
    shifted = jax.random.randint(jax.random.fold_in(key, 1), (pairs,), 0, 1 << 20) % (room + 1)
    tallies = tallies.at[1:1 + 2 * pairs:2].set(source_of - shifted).at[2:2 + 2 * pairs:2].set(sink + shifted)
    return tallies[jax.random.permutation(jax.random.fold_in(key, 2), amount)]


def normal_values(rng, dims, scale, limit, cuts=(), held_as=jnp.bfloat16):
    factor_of = steps_of(rng, dims, cuts, -0.22, 0.18) if cuts else 1.0
    drawn = jax.random.normal(rng, dims, jnp.float32) * scale * factor_of
    return jnp.minimum(jnp.maximum(drawn, -limit), limit).astype(held_as)


def setup_inputs(seed: int = 0) -> dict:
    key_of = jax.random.split(jax.random.key(seed), 16)
    return {
        "inputs": normal_values(key_of[0], (UTTS, FRAMES, WIDTH), 1.0, 6.0, ((0, 4),), jnp.float32),
        "lengths": ragged_sizes(key_of[1], UTTS, 3 * UTTS * FRAMES // 4, FRAMES, 2).astype(jnp.int32),
        "cotangent": normal_values(key_of[2], (UTTS, FRAMES, WIDTH), 1.0, 6.0, ((0, 4),), jnp.float32),
        "norm_gain": jnp.clip(1.0 + 0.1 * jax.random.normal(key_of[3], (2, 5, WIDTH), jnp.float32), 0.5, 1.5),
        "norm_bias": normal_values(key_of[4], (2, 5, WIDTH), 0.3, 2.0, ((0, 2),), jnp.float32),
        "ffn_in": normal_values(key_of[5], (2, 2, WIDTH, HIDDEN_SIZE), WIDTH ** -0.5, 0.25, ((0, 2), (3, 4))),
        "ffn_out": normal_values(key_of[6], (2, 2, HIDDEN_SIZE, WIDTH), HIDDEN_SIZE ** -0.5, 0.125, ((0, 2), (2, 4))),
        "attn_in": normal_values(key_of[7], (2, 4, WIDTH, WIDTH), WIDTH ** -0.5, 0.25, ((0, 2), (3, 4))),
        "pos_bias": normal_values(key_of[8], (2, 2, WIDTH), 0.5, 3.0, ((0, 2), (2, 4)), jnp.float32),
        "attn_out": normal_values(key_of[9], (2, WIDTH, WIDTH), (max(16 * WIDTH // FRAMES, 1)) ** -0.5, 0.375, ((0, 2), (1, 4))),
        "conv_in": normal_values(key_of[10], (2, WIDTH, 2, WIDTH), WIDTH ** -0.5, 0.25, ((0, 2), (3, 4))),
        "depthwise": normal_values(key_of[11], (2, KERNEL, WIDTH), KERNEL ** -0.5, 1.0, ((0, 2), (2, 4)), jnp.float32),
        "bn_gain": jnp.clip(1.0 + 0.1 * jax.random.normal(key_of[12], (2, WIDTH), jnp.float32), 0.5, 1.5),
        "bn_shift": normal_values(key_of[13], (2, WIDTH), 0.5, 3.0, ((0, 2), (1, 4)), jnp.float32),
        "conv_out": normal_values(key_of[14], (2, WIDTH, WIDTH), WIDTH ** -0.5, 0.25, ((0, 2), (1, 4))),
    }


@jax.custom_vjp
def low(v):
    return lax.optimization_barrier(v.astype(jnp.bfloat16)).astype(jnp.float32)

@jax.custom_vjp
def low_back(v):
    return v

def low_keep(v):
    return (low(v), None)

def low_pass(kept, grad):
    return (grad,)

def back_keep(v):
    return (v, None)

def back_low(kept, grad):
    return (low(grad),)
low.defvjp(low_keep, low_pass)
low_back.defvjp(back_keep, back_low)
highest_precision = lax.Precision.HIGHEST
epsilon = 1e-05

def layer_norm(states, norm_gain, norm_bias):
    centre = states - lax.optimization_barrier(jnp.mean(states, -1, keepdims=True))
    spread = lax.optimization_barrier(jnp.mean(centre * centre, -1, keepdims=True))
    return centre * lax.rsqrt(spread + epsilon) * norm_gain + norm_bias

def positions(frames, model_width):
    offset = jnp.arange(2 * frames - 1, dtype=jnp.float32) - (frames - 1)
    freq_rates = jnp.exp(jnp.arange(model_width // 2, dtype=jnp.float32) * (-2.0 * math.log(10000.0) / model_width))
    angles = offset[:, None] * freq_rates[None, :]
    return jnp.stack([jnp.sin(angles), jnp.cos(angles)], -1).reshape(2 * frames - 1, model_width)

def offsets(frames):
    row_index = jnp.arange(frames, dtype=jnp.int32)
    return (row_index[:, None] - row_index[None, :] + (frames - 1)).astype(jnp.int32)

def depth_conv(signal, kernel):
    tap_count = kernel.shape[0]
    return lax.conv_general_dilated(signal, kernel[:, None, :], (1,), [(tap_count // 2, tap_count // 2)], dimension_numbers=('NWC', 'WIO', 'NWC'), feature_group_count=signal.shape[-1], precision=highest_precision)

def feed(states, norm_gain, norm_bias, weight_in, weight_out):
    normed = low(layer_norm(states, norm_gain, norm_bias))
    hidden = low_back(jnp.einsum('gtd,df->gtf', normed, weight_in, precision=highest_precision))
    active = low(jax.nn.silu(hidden))
    branch = low_back(jnp.einsum('gtf,fd->gtd', active, weight_out, precision=highest_precision))
    return states + 0.5 * branch

def attend(query_u, query_position_bias, key_rows, values, relative_key_rows, frame_mask):
    frames = query_u.shape[0]
    content = jnp.einsum('ihd,jhd->hij', query_u, key_rows, precision=highest_precision)
    complete_relative = jnp.einsum('rnv,cnv->nrc', query_position_bias, relative_key_rows, precision=highest_precision)
    placed = jnp.take_along_axis(complete_relative, jnp.broadcast_to(offsets(frames)[None], content.shape), 2)
    scores = low_back((content + placed) * HEAD ** (-0.5))
    scores = jnp.where(frame_mask[None, None, :] > 0, scores, -1e+30)
    attn_probs = low(jax.nn.softmax(scores, -1))
    return jnp.einsum('hij,jhd->ihd', attn_probs, values, precision=highest_precision)

def attention(states, frame_mask, norm_gain, norm_bias, weight_in, pos_bias, weight_out):
    groups, frames, model_width = states.shape
    normed = low(layer_norm(states, norm_gain, norm_bias))

    def project(matrix):
        return jnp.einsum('gtd,de->gte', normed, matrix, precision=highest_precision)
    queries = low_back(project(weight_in[0]))
    key_rows = low(low_back(project(weight_in[1])))
    values = low(low_back(project(weight_in[2])))
    relative_key_rows = low(low_back(jnp.dot(low(positions(frames, model_width)), weight_in[3], precision=highest_precision)))
    query_u = low(queries + pos_bias[0])
    query_position_bias = low(queries + pos_bias[1])
    head_count = model_width // HEAD

    def split_heads(member):
        return member.reshape(member.shape[:-1] + (head_count, HEAD))
    rel_heads = split_heads(relative_key_rows)

    def attend_item(item_list):
        return attend(item_list[0], item_list[1], item_list[2], item_list[3], rel_heads, item_list[4])
    mixed_out = lax.map(jax.checkpoint(attend_item), (split_heads(query_u), split_heads(query_position_bias), split_heads(key_rows), split_heads(values), frame_mask))
    mixed_out = low(low_back(mixed_out.reshape(groups, frames, model_width)))
    branch = low_back(jnp.einsum('gte,ed->gtd', mixed_out, weight_out, precision=highest_precision))
    return states + branch

def convolve(states, frame_mask, norm_gain, norm_bias, weight_in, kernel, bn_gain, bn_shift, weight_out):
    normed = low(layer_norm(states, norm_gain, norm_bias))
    gate_rows = low_back(jnp.einsum('gtd,dkc->gtkc', normed, weight_in, precision=highest_precision))
    mask_col = frame_mask[..., None]
    signal = gate_rows[:, :, 0] * jax.nn.sigmoid(gate_rows[:, :, 1]) * mask_col
    mixed_out = depth_conv(signal, kernel)
    frame_count = jnp.sum(frame_mask)
    batch_mean = lax.optimization_barrier(jnp.sum(mixed_out * mask_col, (0, 1))) / frame_count
    square_sum = lax.optimization_barrier(jnp.sum(mixed_out * mixed_out * mask_col, (0, 1))) / frame_count
    scaled = (mixed_out - batch_mean) * lax.rsqrt(square_sum - batch_mean * batch_mean + epsilon) * bn_gain + bn_shift
    branch = low_back(jnp.einsum('gtc,cd->gtd', low(jax.nn.silu(scaled)), weight_out, precision=highest_precision))
    return states + branch

def layer(states, frame_mask, params):
    norm_gain, norm_bias, ffn_in, ffn_out, attn_in, pos_bias, attn_out, conv_in, kernel, bn_gain, bn_shift, conv_out = params
    states = feed(states, norm_gain[0], norm_bias[0], ffn_in[0], ffn_out[0])
    states = attention(states, frame_mask, norm_gain[1], norm_bias[1], attn_in, pos_bias, attn_out)
    states = convolve(states, frame_mask, norm_gain[2], norm_bias[2], conv_in, kernel, bn_gain, bn_shift, conv_out)
    states = feed(states, norm_gain[3], norm_bias[3], ffn_in[1], ffn_out[1])
    return layer_norm(states, norm_gain[4], norm_bias[4]) * frame_mask[..., None]

def reference(inputs, lengths, cotangent, norm_gain, norm_bias, ffn_in, ffn_out, attn_in, pos_bias, attn_out, conv_in, depthwise, bn_gain, bn_shift, conv_out):
    params = tuple((member.astype(jnp.float32) for member in (norm_gain, norm_bias, ffn_in, ffn_out, attn_in, pos_bias, attn_out, conv_in, depthwise, bn_gain, bn_shift, conv_out)))
    utterances, frames, model_width = inputs.shape
    groups = utterances // MICRO
    frame_mask = (jnp.arange(frames, dtype=jnp.int32)[None, :] < lengths[:, None]).astype(jnp.float32)
    frame_mask = frame_mask.reshape(groups, MICRO, frames)

    def forward(states, weights, offset):
        grouped = states.reshape(groups, MICRO, frames, model_width)
        first_params = tuple((member[0] for member in weights))
        second_params = tuple((member[1] for member in weights))
        first_out = jnp.stack([layer(grouped[:, micro_index], frame_mask[:, micro_index], first_params) for micro_index in range(MICRO)], 1)
        middle = low(low_back(first_out)) + offset
        second = jnp.stack([layer(middle[:, micro_index], frame_mask[:, micro_index], second_params) for micro_index in range(MICRO)], 1)
        return (middle, second)
    offset = jnp.zeros((groups, MICRO, frames, model_width), jnp.float32)
    (middle, second), pull_back = jax.vjp(forward, inputs.astype(jnp.float32), params, offset)
    input_grad, weight_grads, middle_grad = pull_back((jnp.zeros_like(middle), cotangent.astype(jnp.float32).reshape(second.shape)))
    layer_out = jnp.stack([middle.reshape(inputs.shape), second.reshape(inputs.shape)])
    input_grads = jnp.stack([input_grad, middle_grad.reshape(inputs.shape)])
    return (layer_out, input_grads, weight_grads[0], weight_grads[1], weight_grads[2], weight_grads[3], weight_grads[4], weight_grads[5], weight_grads[6], weight_grads[7], weight_grads[8], weight_grads[9], weight_grads[10], weight_grads[11])
```

```python
import math

import jax
import jax.numpy as jnp
import numpy as np
from jax import lax
from jax.experimental import pallas as pl
from jax.experimental.pallas import tpu as pltpu
from jax.sharding import PartitionSpec as P

HEAD = 64
EPSILON = 1e-05
MESH = pl.DeviceIdType.MESH
PLACE = (0, 2, 1, 3)
SMALL_ROWS = 40
bf16, f32 = jnp.bfloat16, jnp.float32


def dot(left, right, left_dim=1, right_dim=0):
    return lax.dot_general(
        left, right, (((left_dim,), (right_dim,)), ((), ())), preferred_element_type=f32
    )


def position_rows(frames, width):
    offset = np.arange(2 * frames - 1, dtype=np.float32) - np.float32(frames - 1)
    rates = np.exp(
        np.arange(width // 2, dtype=np.float32) * np.float32(-2.0 * math.log(10000.0) / width)
    )
    angles = (offset[:, None] * rates[None, :]).astype(np.float32)
    table = np.stack([np.sin(angles), np.cos(angles)], -1).reshape(2 * frames - 1, width)
    blank = np.zeros((1, width), np.float32)
    return jnp.asarray(np.concatenate([table[::-1], blank, table, blank]), bf16)


def layer_kernel(dims, *refs):
    frames, width, dp, groups = dims
    T = frames
    C = width // 4
    (lengths, inputs, cot, ng, nb, fin, fout, ain, aout, cin, cout, pos, bng, bns, dw, e2) = refs[:16]
    (Nall, Ball, Sf, Sb, LO, IG, PA, PB) = refs[16:24]
    (Win, Wout, Wqkv, Wr, Wo, Wci, Wco, R2, SM) = refs[24:33]
    (H, XH, RS, X, ARR, HOP, QKV, PRB, GVG, CT, UP, DP, SfSt, SbSt, PAst, PAin, PBin, STF, STB) = refs[33:52]
    ss, rs, ls = refs[52:55]

    s, t, d = lax.axis_index("section"), lax.axis_index("tensor"), lax.axis_index("dp")
    taps = dw.shape[0]
    peers = [(s, t ^ k, d) for k in range(4)]
    sib, yp = peers[1], peers[2]
    ahead = [lax.rem(d + r, dp) for r in range(dp)]
    behind = [lax.rem(d - r + dp, dp) for r in range(dp)]
    zpeers = [(s, t, ahead[r]) for r in range(dp)]
    zpair = (s, t, d ^ 1)
    partner = (1 - s, t, d)
    half = lax.rem(d, 2)
    other = 1 - half
    R4 = 4 * T
    base = pl.multiple_of(d * R4, R4) if groups > 1 else 0
    zbase = [pl.multiple_of(behind[r] * R4, R4) for r in range(dp)]
    zhigh = [pl.multiple_of(z + 2 * T, 2 * T) for z in zbase]
    trow = pl.multiple_of(t * T, T)

    index, pending = {}, []

    def copy_of(key, src, dst, dev):
        i = index.setdefault(key, len(index))
        return pltpu.make_async_remote_copy(
            src_ref=src, dst_ref=dst, send_sem=ss.at[i], recv_sem=rs.at[i],
            device_id=dev, device_id_type=MESH,
        )

    def start(key, src, dst, dev, cond=None):
        if cond is None:
            c = copy_of(key, src, dst, dev)
            c.start()
            pending.append((None, lambda: c))
        else:
            again = lambda: copy_of(key, src(), dst(), dev)
            again().start()
            pending.append((cond, again))

    def arrived(key, dst):
        copy_of(key, dst, dst, partner).wait_recv()

    def rows_of(ref_rows, part):
        if part is None:
            return pl.ds(0, ref_rows)
        n = ref_rows // 2
        return pl.ds(pl.multiple_of(part * n, n), n)

    halves = {}
    for n in (width, C):
        m = n // 2
        halves[n] = {"own": pl.multiple_of(half * m, m), "other": pl.multiple_of(other * m, m)}
    slot_rows = {
        (k, w): pl.multiple_of(C * k + halves[C][w], C // 2) for k in range(4) for w in ("own", "other")
    }

    def lines(n, which):
        return pl.ds(0, n) if which is None else pl.ds(halves[n][which], n // 2)

    def slot_lines(k, which):
        return pl.ds(C * k, C) if which is None else pl.ds(slot_rows[k, which], C // 2)

    def cols(k):
        return pl.ds(C * k, C)

    chunks = [
        (lambda w: fin.at[0, lines(width, w)], lambda k, w: Win.at[0, k, lines(width, w)]),
        (lambda w: fout.at[0, lines(width, w)], lambda k, w: Wout.at[0, k, lines(width, w)]),
        (lambda w: ain.at[pl.ds(0, 3), lines(width, w)], lambda k, w: Wqkv.at[:, lines(width, w), cols(k)]),
        (lambda w: aout.at[lines(C, w)], lambda k, w: Wo.at[slot_lines(k, w)]),
        (lambda w: cin.at[:, lines(width, w)], lambda k, w: Wci.at[:, lines(width, w), cols(k)]),
        (lambda w: cout.at[lines(C, w)], lambda k, w: Wco.at[slot_lines(k, w)]),
        (lambda w: fin.at[1, lines(width, w)], lambda k, w: Win.at[1, k, lines(width, w)]),
        (lambda w: fout.at[1, lines(width, w)], lambda k, w: Wout.at[1, k, lines(width, w)]),
    ]
    local = [pltpu.make_async_copy(ain.at[3], Wr, ls.at[8])] + [
        pltpu.make_async_copy(src(None), dst(0, None), ls.at[i]) for i, (src, dst) in enumerate(chunks)
    ]
    for c in local:
        c.start()

    barrier = pltpu.get_barrier_semaphore()
    greet = peers[1:] + zpeers[1:] + [partner]
    for dev in greet:
        pl.semaphore_signal(barrier, inc=1, device_id=dev, device_id_type=MESH)
    pl.semaphore_wait(barrier, len(greet))

    def send_chunk(i):
        src, dst = chunks[i]
        start(("sib", i), src(None), dst(1, None), sib)
        start(("y", i), src("own"), dst(2, "own"), yp)

    def step_a(i, cond):
        dst = chunks[i][1]
        arrived(("y", i), dst(2, "own"))
        start(("z", i), lambda: dst(2, "own"), lambda: dst(2, "own"), zpair, cond)
        start(("sib2", i), lambda: dst(2, "own"), lambda: dst(3, "own"), sib, cond)

    def step_b(i, cond):
        dst = chunks[i][1]
        arrived(("z", i), dst(2, "other"))
        start(("sib3", i), lambda: dst(2, "other"), lambda: dst(3, "other"), sib, cond)

    def step_c(i):
        dst = chunks[i][1]
        arrived(("sib", i), dst(1, None))
        arrived(("sib2", i), dst(3, "own"))
        arrived(("sib3", i), dst(3, "other"))

    def gather(i, cond):
        if i == 0:
            step_a(0, cond)
        if i + 1 < len(chunks):
            step_a(i + 1, cond)
        step_b(i, cond)
        step_c(i)

    def first_only(i):
        @pl.when(s == 0)
        def _():
            gather(i, 0)

    send_chunk(0)
    send_chunk(1)
    SM[:, 0:C] = jnp.zeros((SMALL_ROWS, C), f32)
    SM[0:2, 0:C] = pos[...]
    SM[2:3, 0:C] = bng[...]
    SM[3:4, 0:C] = bns[...]
    SM[4 : 4 + taps, 0:C] = dw[...]
    for k in (1, 2, 3):
        start(("small", k), SM.at[:, cols(0)], SM.at[:, cols(k)], peers[k])
    local[0].wait()
    R2[:, 0:C] = dot(e2[...], Wr[...]).astype(bf16)
    for k in (1, 2, 3):
        start(("rel", k), R2.at[:, cols(0)], R2.at[:, cols(k)], peers[k])
    for i in range(2, len(chunks)):
        send_chunk(i)
    for c in local[1:]:
        c.wait()

    margin = 16
    UP[...] = jnp.zeros(UP.shape, f32)
    DP[...] = jnp.zeros(DP.shape, f32)
    PAst[...] = jnp.zeros(PAst.shape, f32)
    PBin[t] = jnp.zeros(PBin.shape[1:], f32)

    length = lengths[t]
    row_mask = (lax.broadcasted_iota(jnp.int32, (T, 1), 0) < length).astype(f32)
    key_mask = lax.broadcasted_iota(jnp.int32, (2 * T, T), 1) < length
    first_head = lax.broadcasted_iota(jnp.int32, (T, 2 * HEAD), 1) < HEAD
    flip = (
        lax.broadcasted_iota(jnp.int32, (T, 4 * T), 0) + lax.broadcasted_iota(jnp.int32, (T, 4 * T), 1)
        == T - 1
    ).astype(f32).astype(bf16)

    def norm(i, x):
        centre = x - jnp.mean(x, -1, keepdims=True)
        rate = lax.rsqrt(jnp.mean(centre * centre, -1, keepdims=True) + EPSILON)
        hat = centre * rate
        XH[i] = hat
        RS[i] = jnp.broadcast_to(rate, RS.shape[1:])
        return hat * ng[i : i + 1] + nb[i : i + 1]

    def norm_back(i, grad):
        hat = XH[i]
        PBin[t, i : i + 1] = jnp.sum(grad * hat, 0, keepdims=True)
        PBin[t, 8 + i : 9 + i] = jnp.sum(grad, 0, keepdims=True)
        g = grad * ng[i : i + 1]
        return RS[i][:, 0:1] * (
            g - jnp.mean(g, -1, keepdims=True) - hat * jnp.mean(g * hat, -1, keepdims=True)
        )

    def pair_rows(v):
        return jnp.concatenate([jnp.where(first_head, v, 0.0), jnp.where(first_head, 0.0, v)], 0)

    def unpair(v):
        return jnp.where(first_head, v[:T], v[T:])

    own = pl.ds(base, T)

    @pl.when(s == 1)
    def _():
        for i in range(len(chunks)):
            gather(i, 1)
        arrived("hop", ARR)
        X[0] = ARR[...].astype(f32)

    @pl.when(s == 0)
    def _():
        X[0] = inputs[t]

    def feed(j, i, before, after):
        x = X[before]
        a = norm(i, x).astype(bf16)
        Nall[own, i * width : (i + 1) * width] = a
        first_only(6 * j)
        active = []
        for k in range(4):
            h = dot(a, Win[j, k])
            H[j, k] = h
            active.append((h * jax.nn.sigmoid(h)).astype(bf16))
        first_only(6 * j + 1)
        total = dot(active[0], Wout[j, 0])
        for k in range(1, 4):
            total += dot(active[k], Wout[j, k])
        X[after] = x + 0.5 * total

    feed(0, 0, 0, 1)

    x = X[1]
    a = norm(1, x).astype(bf16)
    Nall[own, width : 2 * width] = a
    for k in (1, 2, 3):
        arrived(("small", k), SM.at[:, cols(k)])
        arrived(("rel", k), R2.at[:, cols(k)])
    first_only(2)
    q = dot(a, Wqkv[0])
    QKV[0] = q + SM[0:1]
    QKV[1] = q + SM[1:2]
    QKV[2] = dot(a, Wqkv[1])
    QKV[3] = dot(a, Wqkv[2])
    mixed = []
    for p in range(4):
        c = pl.ds(2 * HEAD * p, 2 * HEAD)
        qu = pair_rows(QKV[0, :, c]).astype(bf16)
        qv = pair_rows(QKV[1, :, c]).astype(bf16)
        content = dot(qu, QKV[2, :, c].astype(bf16), 1, 1)
        whole = dot(qv, R2[:, c], 1, 1)
        placed = jnp.concatenate(
            [
                pltpu.roll(whole[e * T : (e + 1) * T], 4 * T - (T - 1), 1, stride=1, stride_axis=0)[:, :T]
                for e in range(2)
            ],
            0,
        )
        scores = jnp.where(key_mask, (content + placed) * HEAD ** (-0.5), -1e30)
        e = jnp.exp(scores - jnp.max(scores, -1, keepdims=True))
        probs = e / jnp.sum(e, -1, keepdims=True)
        PRB[p] = probs
        mixed.append(unpair(dot(probs.astype(bf16), QKV[3, :, c].astype(bf16))).astype(bf16))
    for k in range(4):
        SfSt[k, :, 0:C] = mixed[k]
    first_only(3)
    total = dot(mixed[0], Wo[0:C])
    for k in range(1, 4):
        total += dot(mixed[k], Wo[C * k : C * (k + 1)])
    x = x + total
    X[2] = x

    a = norm(2, x).astype(bf16)
    Nall[own, 2 * width : 3 * width] = a
    first_only(4)
    GVG[0] = dot(a, Wci[0])
    GVG[1] = dot(a, Wci[1])
    UP[margin : margin + T] = GVG[0] * jax.nn.sigmoid(GVG[1]) * row_mask
    for p in range(4):
        c = pl.ds(C * p, C)
        acc = SM[4:5, c] * UP[margin - taps // 2 : margin - taps // 2 + T, c]
        for k in range(1, taps):
            o = margin - taps // 2 + k
            acc += SM[4 + k : 5 + k, c] * UP[o : o + T, c]
        CT[:, c] = acc
    conv = CT[...]
    masked = conv * row_mask
    STF[d] = jnp.concatenate(
        [
            jnp.sum(masked, 0, keepdims=True),
            jnp.sum(masked * conv, 0, keepdims=True),
            jnp.broadcast_to(jnp.sum(row_mask, 0, keepdims=True), (1, width)),
            jnp.zeros((5, width), f32),
        ],
        0,
    )
    for r in range(1, dp):
        start(("bnf", r), STF.at[d], STF.at[d], zpeers[r])
    first_only(5)
    for r in range(1, dp):
        arrived(("bnf", r), STF.at[behind[r]])
    sums = STF[0]
    for r in range(1, dp):
        sums += STF[r]
    count = sums[2:3]
    bn_mean = sums[0:1] / count
    inv_std = lax.rsqrt(sums[1:2] / count - bn_mean * bn_mean + EPSILON)
    hat = (conv - bn_mean) * inv_std
    CT[...] = hat
    y = hat * SM[2:3] + SM[3:4]
    active = (y * jax.nn.sigmoid(y)).astype(bf16)
    for k in range(4):
        SfSt[k, :, C : 2 * C] = active[:, C * k : C * (k + 1)]
    x = X[2] + dot(active, Wco[...])
    X[3] = x

    feed(1, 3, 3, 4)

    out = (norm(4, X[4]) * row_mask).astype(bf16)
    HOP[...] = out

    @pl.when(s == 0)
    def _():
        start("hop", lambda: HOP, lambda: ARR, partner, 0)

    LO[pl.ds(trow, T)] = out
    for k in (1, 2, 3):
        mine = pl.ds(trow, T)
        start(("out", k), LO.at[mine], LO.at[mine], peers[k])

    def place(k):
        return pl.ds(base + T * PLACE[k], T)

    def to_tensor(name, ref, c):
        for k in (1, 2, 3):
            start((name, k), ref.at[own, c], ref.at[place(k), c], peers[k])

    def from_tensor(name, ref, c, which=(1, 2, 3)):
        for k in which:
            arrived((name, k), ref.at[place(k), c])

    def to_dp(name, ref, n, c, cond=None):
        for r in range(1, groups):
            there = lambda: ref.at[pl.ds(base, n), c]
            if cond is None:
                start((name, "z", r), there(), there(), zpeers[r])
            else:
                start((name, "z", r), there, there, zpeers[r], cond)

    def from_dp(name, ref, n, c):
        for r in range(1, groups):
            arrived((name, "z", r), ref.at[pl.ds(zbase[r], n), c])

    def to_core(name, ref, c, cond=None):
        for r in range(1, groups):
            src = lambda r=r: ref.at[pl.ds(zbase[r], 2 * T), c]
            dst = lambda r=r: ref.at[pl.ds(zhigh[r], 2 * T), c]
            if cond is None:
                start((name, "c", r), src(), dst(), sib)
            else:
                start((name, "c", r), src, dst, sib, cond)

    def from_core(name, ref, c):
        for r in range(1, groups):
            arrived((name, "c", r), ref.at[pl.ds(zhigh[r], 2 * T), c])

    def block(i):
        return pl.ds(i * width, width)

    every = pl.ds(0, 4 * width)
    sf_cols, sb_cols = pl.ds(0, 2 * C), pl.ds(0, 5 * C)
    to_tensor("n", Nall, every)
    Sf[own] = SfSt[0]
    for k in (1, 2, 3):
        start(("sf", k), SfSt.at[k], Sf.at[place(k)], peers[k])

    def spread_forward(cond):
        from_tensor("n", Nall, every)
        to_dp("n", Nall, 2 * T, every, cond)
        from_tensor("sf", Sf, sf_cols)
        to_dp("sf", Sf, R4, sf_cols, cond)

    @pl.when(s == 0)
    def _():
        spread_forward(0)
        from_dp("n", Nall, 2 * T, every)
        to_core("n", Nall, every, 0)
        arrived("back", ARR)
        X[0] = ARR[...].astype(f32)

    @pl.when(s == 1)
    def _():
        X[0] = cot[t]

    def feed_back(j, i, g):
        b = (0.5 * g).astype(bf16)
        Ball[own, i * width : (i + 1) * width] = b
        to_tensor(("b", i), Ball, block(i))
        grad = None
        for k in range(4):
            h = H[j, k]
            sig = jax.nn.sigmoid(h)
            hg = (dot(b, Wout[j, k], 1, 1) * (sig * (1.0 + h * (1.0 - sig)))).astype(bf16)
            part = dot(hg, Win[j, k], 1, 1)
            grad = part if grad is None else grad + part
        return g + norm_back(i, grad)

    g = norm_back(4, X[0] * row_mask)
    g = feed_back(1, 3, g)

    @pl.when(s == 1)
    def _():
        spread_forward(1)

    b = g.astype(bf16)
    Ball[own, 2 * width : 3 * width] = b
    to_tensor(("b", 2), Ball, block(2))
    hat = CT[...]
    y = hat * SM[2:3] + SM[3:4]
    sig = jax.nn.sigmoid(y)
    dy = dot(b, Wco[...], 1, 1) * (sig * (1.0 + y * (1.0 - sig)))
    PAst[2:3] = jnp.sum(dy * hat, 0, keepdims=True)
    PAst[3:4] = jnp.sum(dy, 0, keepdims=True)
    dhat = dy * SM[2:3]
    masked = dhat * row_mask
    STB[d] = jnp.concatenate(
        [
            jnp.sum(masked, 0, keepdims=True),
            jnp.sum(masked * hat, 0, keepdims=True),
            jnp.zeros((6, width), f32),
        ],
        0,
    )
    for r in range(1, dp):
        start(("bnb", r), STB.at[d], STB.at[d], zpeers[r])
    for r in range(1, dp):
        arrived(("bnb", r), STB.at[behind[r]])
    sums = STB[0]
    for r in range(1, dp):
        sums += STB[r]
    dc = inv_std * (dhat - (sums[0:1] + hat * sums[1:2]) / count) * row_mask
    DP[margin : margin + T] = dc
    from_tensor(("b", 3), Ball, block(3))
    to_dp(("b", 3), Ball, 2 * T, block(3))
    for p in range(4):
        c = pl.ds(C * p, C)
        here = DP[margin : margin + T, c]
        acc = None
        for k in range(taps):
            o = margin + taps // 2 - k
            term = SM[4 + k : 5 + k, c] * DP[o : o + T, c]
            acc = term if acc is None else acc + term
            o = margin - taps // 2 + k
            PAst[4 + k : 5 + k, c] = jnp.sum(here * UP[o : o + T, c], 0, keepdims=True)
        CT[:, c] = acc
    du = CT[...] * row_mask
    sig = jax.nn.sigmoid(GVG[1])
    dvalue = (du * sig).astype(bf16)
    dgate = (du * GVG[0] * (sig * (1.0 - sig))).astype(bf16)
    for k in range(4):
        SbSt[k, :, 3 * C : 4 * C] = dvalue[:, C * k : C * (k + 1)]
        SbSt[k, :, 4 * C : 5 * C] = dgate[:, C * k : C * (k + 1)]
    g = g + norm_back(2, dot(dvalue, Wci[0], 1, 1) + dot(dgate, Wci[1], 1, 1))

    b = g.astype(bf16)
    Ball[own, width : 2 * width] = b
    to_tensor(("b", 1), Ball, block(1))
    dmix = dot(b, Wo[...], 1, 1).astype(bf16).astype(f32)
    scale = HEAD ** (-0.5)
    dq, dk, dv = [], [], []
    for p in range(4):
        c = pl.ds(2 * HEAD * p, 2 * HEAD)
        qu = pair_rows(QKV[0, :, c]).astype(bf16)
        qv = pair_rows(QKV[1, :, c]).astype(bf16)
        key = QKV[2, :, c].astype(bf16)
        val = QKV[3, :, c].astype(bf16)
        do = pair_rows(dmix[:, 2 * HEAD * p : 2 * HEAD * (p + 1)]).astype(bf16)
        probs = PRB[p]
        dprob = dot(do, val, 1, 1)
        ds = (probs * (dprob - jnp.sum(probs * dprob, -1, keepdims=True))).astype(bf16)
        du_rows = unpair(dot(ds, key)) * scale
        turned = dot(ds, flip)
        whole = jnp.concatenate(
            [
                pltpu.roll(turned[e * T : (e + 1) * T], 0, 1, stride=1, stride_axis=0)[:, : 2 * T]
                for e in range(2)
            ],
            0,
        ).astype(bf16)
        dv_rows = unpair(dot(whole, R2[2 * T : 4 * T, c])) * scale
        dk.append((dot(ds, qu, 0, 0) * scale).astype(bf16))
        dv.append(dot(probs.astype(bf16), do, 0, 0).astype(bf16))
        dq.append((du_rows + dv_rows).astype(bf16))
        PAst[0:1, c] = jnp.sum(du_rows, 0, keepdims=True)
        PAst[1:2, c] = jnp.sum(dv_rows, 0, keepdims=True)
        drel = dot(whole, qv, 0, 0) * scale
        PAst[SMALL_ROWS : SMALL_ROWS + 2 * T, c] = drel.astype(bf16).astype(f32)
    for k in range(4):
        SbSt[k, :, 0:C] = dq[k]
        SbSt[k, :, C : 2 * C] = dk[k]
        SbSt[k, :, 2 * C : 3 * C] = dv[k]
    Sb[own] = SbSt[0]
    grad = dot(jnp.concatenate(dq, 1), Wqkv[0], 1, 1)
    grad += dot(jnp.concatenate(dk, 1), Wqkv[1], 1, 1)
    grad += dot(jnp.concatenate(dv, 1), Wqkv[2], 1, 1)
    g = g + norm_back(1, grad)

    g = feed_back(0, 0, g)
    low = g.astype(bf16)
    back_rows = lambda: IG.at[pl.ds(trow, T)]
    IG[pl.ds(trow, T)] = low

    @pl.when(s == 1)
    def _():
        start("back", back_rows, lambda: ARR, partner, 1)

    for k in (1, 2, 3):
        start(("grad", k), back_rows(), back_rows(), peers[k])
    for k in (1, 2, 3):
        start(("sb", k), SbSt.at[k], Sb.at[place(k)], peers[k])
        start(("pa", k), PAst.at[:, cols(k)], PAin.at[k], peers[k])
        start(("pb", k), PBin.at[t], PBin.at[t], peers[k])

    for i in (2, 1, 0):
        from_tensor(("b", i), Ball, block(i))
        to_dp(("b", i), Ball, 2 * T, block(i))
    from_tensor("sb", Sb, sb_cols)
    to_dp("sb", Sb, R4, sb_cols)
    PAin[0] = PAst[:, 0:C]
    for k in (1, 2, 3):
        arrived(("pa", k), PAin.at[k])
    mine = d if groups > 1 else 0
    PA[mine] = PAin[0] + PAin[1] + PAin[2] + PAin[3]
    for r in range(1, groups):
        start(("pa", "z", r), PA.at[d], PA.at[d], zpeers[r])
    for k in (1, 2, 3):
        arrived(("pb", k), PBin.at[t ^ k])
    PB[mine] = PBin[0] + PBin[1] + PBin[2] + PBin[3]
    for r in range(1, groups):
        start(("pb", "z", r), PB.at[d], PB.at[d], zpeers[r])

    @pl.when(s == 1)
    def _():
        from_dp("n", Nall, 2 * T, every)
        to_core("n", Nall, every, 1)

    for i in (3, 2, 1, 0):
        from_dp(("b", i), Ball, 2 * T, block(i))
        to_core(("b", i), Ball, block(i))
    from_dp("sf", Sf, R4, sf_cols)
    from_dp("sb", Sb, R4, sb_cols)
    for r in range(1, groups):
        arrived(("pa", "z", r), PA.at[behind[r]])
        arrived(("pb", "z", r), PB.at[behind[r]])
    for k in (1, 2, 3):
        theirs = pl.ds(pl.multiple_of((t ^ k) * T, T), T)
        arrived(("out", k), LO.at[theirs])
        arrived(("grad", k), IG.at[theirs])
    from_core("n", Nall, every)
    for i in (3, 2, 1, 0):
        from_core(("b", i), Ball, block(i))

    for cond, c in pending:
        if cond is None:
            c().wait_send()
    for which in (0, 1):

        @pl.when(s == which)
        def _():
            for cond, c in pending:
                if cond == which:
                    c().wait_send()


def on_device(
    inputs, lengths, cotangent, norm_gain, norm_bias, ffn_in, ffn_out, attn_in, pos_bias, attn_out,
    conv_in, depthwise, bn_gain, bn_shift, conv_out,
):
    dp = lax.axis_size("dp")
    group, frames, width = inputs.shape
    C = width // 4
    taps = depthwise.shape[1]
    groups = dp if dp <= 4 else 1
    R = groups * group * frames
    table = position_rows(frames, width)
    vm = pl.BlockSpec(memory_space=pltpu.VMEM)
    hbm = pl.BlockSpec(memory_space=pl.ANY)
    sm = pl.BlockSpec(memory_space=pltpu.SMEM)
    sums_rows = SMALL_ROWS + 2 * frames

    def shape(dims, dtype=bf16):
        return jax.ShapeDtypeStruct(dims, dtype)

    n_copies = 150 + 6 * (groups - 1) + 2 * dp
    operands = (
        lengths, inputs, cotangent, norm_gain[0], norm_bias[0], ffn_in[0], ffn_out[0], attn_in[0],
        attn_out[0], conv_in[0].transpose(1, 0, 2), conv_out[0], pos_bias[0], bn_gain, bn_shift,
        depthwise[0], table,
    )
    nall, ball, sf, sb, lo, ig, pa, pb = pl.pallas_call(
        lambda *refs: layer_kernel((frames, width, dp, groups), *refs),
        out_shape=[
            shape((R, 4 * width)), shape((R, 4 * width)), shape((R, 2 * C)), shape((R, 5 * C)),
            shape((group * frames, width)), shape((group * frames, width)),
            shape((groups, sums_rows, C), f32), shape((groups, 16, width), f32),
        ],
        in_specs=[sm, vm, vm, vm, vm, hbm, hbm, hbm, hbm, hbm, hbm, vm, vm, vm, vm, vm],
        out_specs=[vm] * 8,
        scratch_shapes=[
            pltpu.VMEM((2, 4, width, width), bf16),
            pltpu.VMEM((2, 4, width, width), bf16),
            pltpu.VMEM((3, width, width), bf16),
            pltpu.VMEM((width, C), bf16),
            pltpu.VMEM((width, width), bf16),
            pltpu.VMEM((2, width, width), bf16),
            pltpu.VMEM((width, width), bf16),
            pltpu.VMEM((4 * frames, width), bf16),
            pltpu.VMEM((SMALL_ROWS, width), f32),
            pltpu.VMEM((2, 4, frames, width), f32),
            pltpu.VMEM((5, frames, width), f32),
            pltpu.VMEM((5, frames, 128), f32),
            pltpu.VMEM((5, frames, width), f32),
            pltpu.VMEM((frames, width), bf16),
            pltpu.VMEM((frames, width), bf16),
            pltpu.VMEM((4, frames, width), f32),
            pltpu.VMEM((4, 2 * frames, frames), f32),
            pltpu.VMEM((2, frames, width), f32),
            pltpu.VMEM((frames, width), f32),
            pltpu.VMEM((frames + 32, width), f32),
            pltpu.VMEM((frames + 32, width), f32),
            pltpu.VMEM((4, frames, 2 * C), bf16),
            pltpu.VMEM((4, frames, 5 * C), bf16),
            pltpu.VMEM((sums_rows, width), f32),
            pltpu.VMEM((4, sums_rows, C), f32),
            pltpu.VMEM((4, 16, width), f32),
            pltpu.VMEM((dp, 8, width), f32),
            pltpu.VMEM((dp, 8, width), f32),
            pltpu.SemaphoreType.DMA((n_copies,)),
            pltpu.SemaphoreType.DMA((n_copies,)),
            pltpu.SemaphoreType.DMA((9,)),
        ],
        compiler_params=pltpu.CompilerParams(
            collective_id=0, has_side_effects=True, vmem_limit_bytes=48 * 2**20
        ),
    )(*operands)

    def part(ref, i, n):
        return ref[:, i * n : (i + 1) * n]

    def feed_grads(j, i):
        n, b = part(nall, i, width), part(ball, i, width)
        h = dot(n, ffn_in[0, j])
        sig = jax.nn.sigmoid(h)
        active = (h * sig).astype(bf16)
        hg = (dot(b, ffn_out[0, j], 1, 1) * (sig * (1.0 + h * (1.0 - sig)))).astype(bf16)
        return dot(n, hg, 0, 0), dot(active, b, 0, 0)

    in0, out0 = feed_grads(0, 0)
    in1, out1 = feed_grads(1, 3)
    pa, pb = jnp.sum(pa, 0), jnp.sum(pb, 0)
    n1, n2 = part(nall, 1, width), part(nall, 2, width)
    qkv = [dot(n1, part(sb, i, C), 0, 0) for i in range(3)]
    rel = dot(table[2 * frames :], pa[SMALL_ROWS:].astype(bf16), 0, 0)
    gates = [dot(n2, part(sb, i, C), 0, 0) for i in (3, 4)]
    grads = [
        pb[0:5], pb[8:13], jnp.stack([in0, in1]), jnp.stack([out0, out1]), jnp.stack(qkv + [rel]),
        pa[0:2], dot(part(sf, 0, C), part(ball, 1, width), 0, 0), jnp.stack(gates, 1),
        pa[4 : 4 + taps], pa[2], pa[3], dot(part(sf, 1, C), part(ball, 2, width), 0, 0),
    ]
    if groups == 1:
        grads = [lax.psum(m.astype(bf16), "dp").astype(f32) for m in grads]
    rows = (group, frames, width)
    outs = [lo.reshape(rows).astype(f32), ig.reshape(rows).astype(f32)] + grads
    return tuple(m[None] for m in outs)


def solution(mesh):
    placed = (
        P("dp", None, None),
        P("dp"),
        P("dp", None, None),
        P("section", None, None),
        P("section", None, None),
        P("section", None, None, "tensor"),
        P("section", None, "tensor", None),
        P("section", None, None, "tensor"),
        P("section", None, "tensor"),
        P("section", "tensor", None),
        P("section", None, None, "tensor"),
        P("section", None, "tensor"),
        P("section", "tensor"),
        P("section", "tensor"),
        P("section", "tensor", None),
    )
    return jax.shard_map(
        on_device,
        mesh=mesh,
        in_specs=placed,
        out_specs=(
            P("section", "dp", None, None),
            P("section", "dp", None, None),
            P("section", None, None),
            P("section", None, None),
            P("section", None, None, "tensor"),
            P("section", None, "tensor", None),
            P("section", None, None, "tensor"),
            P("section", None, "tensor"),
            P("section", "tensor", None),
            P("section", None, None, "tensor"),
            P("section", None, "tensor"),
            P("section", "tensor"),
            P("section", "tensor"),
            P("section", "tensor", None),
        ),
        check_vma=False,
    )
```

```python
import math

import jax
import jax.numpy as jnp
import numpy as np
from jax import lax
from jax.experimental import pallas as pl
from jax.experimental.pallas import tpu as pltpu
from jax.sharding import PartitionSpec as P

HEAD = 64
EPSILON = 1e-05
MESH = pl.DeviceIdType.MESH
SECTION, TENSOR, DATA = "section", "tensor", "dp"
PLACE = (0, 2, 1, 3)
SMALL_ROWS = 48
bf16, f32 = jnp.bfloat16, jnp.float32


def dot(left, right, left_dim=1, right_dim=0):
    return lax.dot_general(
        left, right, (((left_dim,), (right_dim,)), ((), ())), preferred_element_type=f32
    )


def position_rows(frames, width):
    offset = np.arange(2 * frames - 1, dtype=np.float32) - np.float32(frames - 1)
    rates = np.exp(
        np.arange(width // 2, dtype=np.float32) * np.float32(-2.0 * math.log(10000.0) / width)
    )
    angles = (offset[:, None] * rates[None, :]).astype(np.float32)
    table = np.stack([np.sin(angles), np.cos(angles)], -1).reshape(2 * frames - 1, width)
    blank = np.zeros((1, width), np.float32)
    return jnp.asarray(np.concatenate([table[::-1], blank, table, blank]), bf16)


def layer_kernel(dims, *refs):
    T, width, dp, groups = dims
    C = width // 4
    (lengths, inputs, cot, ng_in, nb_in, fin, fout, ain, aout, cin, cout, pos_in, bng_in, bns_in, dw_in, e2_in) = refs[:16]
    (Nall, Ball, Sf, Sb, LO, IG, PA, PB) = refs[16:24]
    (Win, Wout, Wqkv, Wr, Wo, Wci, Wco, R2, SM) = refs[24:33]
    (H, XH, RS, X, G, ARR, HOP, QKV, PRB, GVG, CT, UP, DP) = refs[33:46]
    (SfSt, SbSt, PAst, PAb, PAin, PBst, PBin, STF, STB, RSst, RSin) = refs[46:57]
    (ng, nb, pos, bng, bns, dw, e2, lens, pairs, spread) = refs[57:67]
    ss, rs, ls = refs[67:70]

    s, t, d = lax.axis_index(SECTION), lax.axis_index(TENSOR), lax.axis_index(DATA)
    first, second = s == 0, s == 1
    taps = dw.shape[0]
    peers = [(s, t ^ k, d) for k in range(4)]
    sib, yp = peers[1], peers[2]
    around = {j: lax.rem(d + j + dp, dp) for j in range(1 - dp, dp)}
    zpeers = [(s, t, around[r]) for r in range(dp)]
    zpair = (s, t, d ^ 1)
    partner = (1 - s, t, d)
    half = lax.rem(d, 2)
    R4 = 4 * T
    reach = range(1 - groups, groups)
    base_of = {j: pl.multiple_of(around[j] * R4, R4) if groups > 1 else 0 for j in reach}
    second_of, high_of, last_of = (
        {j: pl.multiple_of(around[j] * R4 + n * T, T) if groups > 1 else n * T for j in reach} for n in (1, 2, 3)
    )
    there = {j: d + j >= 0 if j < 0 else d + j <= dp - 1 for j in reach}
    through = {
        (j, to): there[j] & there[to] for j in reach for to in (1, -1) if j * to < 0 and groups > 1
    }
    base = base_of[0]
    trow = pl.multiple_of(t * T, T)
    mine = d if groups > 1 else 0

    index, pending = {}, {}

    def copy_of(key, src, dst, dev):
        i = index.setdefault(key, len(index))
        return pltpu.make_async_remote_copy(
            src_ref=src, dst_ref=dst, send_sem=ss.at[i], recv_sem=rs.at[i],
            device_id=dev, device_id_type=MESH,
        )

    def start(key, src, dst, dev, cond=None):
        again = lambda: copy_of(key, src(), dst(), dev)
        again().start()
        pending[key] = (cond, again)

    def arrived(key, dst):
        copy_of(key, dst, dst, partner).wait_recv()

    locals_ = {}

    def fetch(name, src, dst):
        locals_[name] = lambda: pltpu.make_async_copy(src(), dst(), ls.at[list(locals_).index(name)])
        locals_[name]().start()

    def fetched(*names):
        for name in names:
            locals_[name]().wait()

    @pl.when(first)
    def _():
        pltpu.make_async_copy(inputs.at[t], X.at[0], ls.at[20]).start()

    @pl.when(second)
    def _():
        pltpu.make_async_copy(cot.at[t], G, ls.at[20]).start()

    fetch("ng", lambda: ng_in, lambda: ng)
    fetch("nb", lambda: nb_in, lambda: nb)
    fetch("in0", lambda: fin.at[0], lambda: Win.at[0, 0])
    fetch("out0", lambda: fout.at[0], lambda: Wout.at[0, 0])
    fetch("wr", lambda: ain.at[3], lambda: Wr)
    fetch("e2", lambda: e2_in, lambda: e2)
    fetch("pos", lambda: pos_in, lambda: pos)
    fetch("bng", lambda: bng_in, lambda: bng)
    fetch("bns", lambda: bns_in, lambda: bns)
    fetch("dw", lambda: dw_in, lambda: dw)
    fetch("len", lambda: lengths, lambda: lens)
    fetch("qkv", lambda: ain.at[pl.ds(0, 3)], lambda: Wqkv.at[:, :, pl.ds(0, C)])
    fetch("o", lambda: aout, lambda: Wo.at[pl.ds(0, C)])
    fetch("ci", lambda: cin, lambda: pairs)
    fetch("co", lambda: cout, lambda: Wco.at[pl.ds(0, C)])
    fetch("in1", lambda: fin.at[1], lambda: Win.at[1, 0])
    fetch("out1", lambda: fout.at[1], lambda: Wout.at[1, 0])

    barrier = pltpu.get_barrier_semaphore()
    greet = peers[1:] + zpeers[1:] + [partner]
    for dev in greet:
        pl.semaphore_signal(barrier, inc=1, device_id=dev, device_id_type=MESH)
    pl.semaphore_wait(barrier, len(greet))

    starts = {}

    def lines(first_row, n, which):
        if which is None:
            return pl.ds(first_row, n)
        at = (first_row, n, which)
        if at not in starts:
            starts[at] = pl.multiple_of(first_row + n // 2 * (half if which == "own" else 1 - half), n // 2)
        return pl.ds(starts[at], n // 2)

    def cols(k):
        return pl.ds(C * k, C)

    def feed_chunks(j):
        Q = width // 2
        return [
            (
                lambda w, src=src, q=q: src.at[j, lines(Q * q, Q, w)],
                lambda k, w, dst=dst, q=q: dst.at[j, k, lines(Q * q, Q, w)],
            )
            for src, dst in ((fin, Win), (fout, Wout))
            for q in range(2)
        ]

    def row_chunk(src, dst):
        return [(lambda w: src.at[lines(0, C, w)], lambda k, w: dst.at[lines(C * k, C, w)])]

    def column_chunks(src, dst, n):
        return [
            (lambda w, i=i: src(i, lines(0, width, w)), lambda k, w, i=i: dst.at[i, lines(0, width, w), cols(k)])
            for i in range(n)
        ]

    chunks = (
        feed_chunks(0)
        + column_chunks(lambda i, rows: ain.at[i, rows], Wqkv, 3)
        + row_chunk(aout, Wo)
        + column_chunks(lambda i, rows: Wci.at[i, rows, cols(0)], Wci, 2)
        + row_chunk(cout, Wco)
        + feed_chunks(1)
    )
    for n, at in ((width // 2, 0), (width // 2, width // 2), (width, 0)) + tuple((C, C * k) for k in range(4)):
        for w in ("own", "other"):
            lines(at, n, w)
    only = {i: second for i in range(4)}

    def send_chunks(names):
        for i in names:
            src, dst = chunks[i]
            start(("sib", i), lambda src=src: src(None), lambda dst=dst: dst(1, None), sib, only.get(i))
            start(("y", i), lambda src=src: src("own"), lambda dst=dst: dst(2, "own"), yp, only.get(i))

    def step_a(i):
        dst = chunks[i][1]
        arrived(("y", i), dst(2, "own"))
        start(("z", i), lambda: dst(2, "own"), lambda: dst(2, "own"), zpair, only.get(i))
        start(("sib2", i), lambda: dst(2, "own"), lambda: dst(3, "own"), sib, only.get(i))

    def step_b(i):
        dst = chunks[i][1]
        arrived(("z", i), dst(2, "other"))
        start(("sib3", i), lambda: dst(2, "other"), lambda: dst(3, "other"), sib, only.get(i))

    def step_c(i):
        dst = chunks[i][1]
        arrived(("sib", i), dst(1, None))
        arrived(("sib2", i), dst(3, "own"))
        arrived(("sib3", i), dst(3, "other"))

    def steps(cond, *plan):
        @pl.when(cond)
        def _():
            for step, i in plan:
                step(i)

    A, B, W = step_a, step_b, step_c

    def norm(i, x):
        centre = x - jnp.mean(x, -1, keepdims=True)
        rate = lax.rsqrt(jnp.mean(centre * centre, -1, keepdims=True) + EPSILON)
        hat = centre * rate
        XH[i] = hat
        RS[i] = jnp.broadcast_to(rate, RS.shape[1:])
        return hat * ng[i] + nb[i]

    def norm_back(i, grad):
        hat = XH[i]
        PBst[i : i + 1] = jnp.sum(grad * hat, 0, keepdims=True)
        PBst[8 + i : 9 + i] = jnp.sum(grad, 0, keepdims=True)
        g = grad * ng[i]
        return RS[i][:, 0:1] * (
            g - jnp.mean(g, -1, keepdims=True) - hat * jnp.mean(g * hat, -1, keepdims=True)
        )

    def silu(h):
        return h * jax.nn.sigmoid(h)

    def place(k):
        return pl.ds(base + T * PLACE[k], T)

    own, four = pl.ds(base, T), pl.ds(base, R4)

    def block(i, n=1):
        return pl.ds(i * width, n * width)

    def to_tensor(name, ref, c):
        for k in (1, 2, 3):
            start((name, k), lambda: ref.at[own, c], lambda k=k: ref.at[place(k), c], peers[k])

    def from_tensor(name, ref, c, which=(1, 2, 3)):
        for k in which:
            arrived((name, k), ref.at[place(k), c])

    def feed(j, i, before, after):
        x = X[before]
        a = norm(i, x).astype(bf16)
        Nall[own, i * width : (i + 1) * width] = a
        to_tensor(("n", i), Nall, block(i))
        active = []
        for k in range(4):
            h = dot(a, Win[j, k])
            H[j, k] = h
            active.append(silu(h).astype(bf16))
        total = dot(active[0], Wout[j, 0])
        for k in range(1, 4):
            total += dot(active[k], Wout[j, k])
        X[after] = x + 0.5 * total

    def sum_to_owner(name, slot, total):
        for k in (1, 2, 3):
            RSst[slot, k - 1] = total[T * PLACE[k] : T * (PLACE[k] + 1)].astype(bf16)
        for k in (1, 2, 3):
            start(
                (name, k), lambda k=k: RSst.at[slot, k - 1], lambda k=k: RSin.at[slot, k - 1], peers[k], first
            )
        return total[0:T]

    def summed_here(name, slot, total):
        for k in (1, 2, 3):
            arrived((name, k), RSin.at[slot, k - 1])
            total += RSin[slot, k - 1].astype(f32)
        return total

    def shared_feed(j, i):
        from_tensor(("n", i), Nall, block(i))
        active = silu(dot(Nall[four, i * width : (i + 1) * width], Win[j, 0])).astype(bf16)
        return sum_to_owner(("s", j), j, dot(active, Wout[j, 0]))

    fetched("ng", "nb")

    @pl.when(first)
    def _():
        send_chunks((4,))
        pltpu.make_async_copy(inputs.at[t], X.at[0], ls.at[20]).wait()
        Nall[own, 0:width] = norm(0, X[0]).astype(bf16)
        to_tensor(("n", 0), Nall, block(0))
        send_chunks((5,))

    @pl.when(second)
    def _():
        send_chunks(range(4))
        pltpu.make_async_copy(cot.at[t], G, ls.at[20]).wait()

    fetched("in0", "out0")

    @pl.when(first)
    def _():
        X[1] = shared_feed(0, 0)
        send_chunks((6,))
        step_a(4)

    fetched("pos", "bng", "bns", "dw", "wr", "e2", "len", "ci")
    spread[...] = pairs[...].astype(f32)
    for i in range(2):
        Wci[i, :, 0:C] = spread[pl.ds(i, width, stride=2), :].astype(bf16)
    SM[:, 0:C] = jnp.zeros((SMALL_ROWS, C), f32)
    SM[0:2, 0:C] = pos[...]
    SM[2:3, 0:C] = bng[...]
    SM[3:4, 0:C] = bns[...]
    for k in range(taps):
        SM[4 + k : 5 + k, 0:C] = dw[k]
    R2[:, 0:C] = dot(e2[...], Wr[...]).astype(bf16)
    for k in (1, 2, 3):
        start(("small", k), lambda: SM.at[:, cols(0)], lambda k=k: SM.at[:, cols(k)], peers[k])
        start(("rel", k), lambda: R2.at[:, cols(0)], lambda k=k: R2.at[:, cols(k)], peers[k])
    @pl.when(first)
    def _():
        send_chunks(range(7, 13))
        step_a(5)
        X[1] = X[0] + 0.5 * summed_here(("s", 0), 0, X[1])
        step_a(6)
        step_b(4)
        step_b(5)

    @pl.when(second)
    def _():
        send_chunks(range(4, 15))

    fetched("qkv", "o", "co", "in1", "out1")
    margin = 16
    UP[...] = jnp.zeros(UP.shape, f32)
    DP[...] = jnp.zeros(DP.shape, f32)
    PAst[...] = jnp.zeros(PAst.shape, f32)
    PBst[...] = jnp.zeros(PBst.shape, f32)

    length = lens[t]
    row_mask = (lax.broadcasted_iota(jnp.int32, (T, 1), 0) < length).astype(f32)
    key_mask = lax.broadcasted_iota(jnp.int32, (2 * T, T), 1) < length
    first_head = lax.broadcasted_iota(jnp.int32, (T, 2 * HEAD), 1) < HEAD
    flip = (
        lax.broadcasted_iota(jnp.int32, (T, 4 * T), 0) + lax.broadcasted_iota(jnp.int32, (T, 4 * T), 1)
        == T - 1
    ).astype(f32).astype(bf16)

    def pair_rows(v):
        return jnp.concatenate([jnp.where(first_head, v, 0.0), jnp.where(first_head, 0.0, v)], 0)

    def unpair(v):
        return jnp.where(first_head, v[:T], v[T:])

    @pl.when(second)
    def _():
        for i in range(14):
            step_a(i)
            if i > 1:
                step_b(i - 2)
        for i in range(7):
            step_c(i)
        arrived("hop", ARR)
        X[0] = ARR[...].astype(f32)
        feed(0, 0, 0, 1)

    def send_rows_second(i):
        @pl.when(second)
        def _():
            to_tensor(("n", i), Nall, block(i))

    x = X[1]
    a = norm(1, x).astype(bf16)
    Nall[own, width : 2 * width] = a
    send_rows_second(1)
    steps(first, (W, 4), (W, 5))
    for k in (1, 2, 3):
        arrived(("small", k), SM.at[:, cols(k)])
        arrived(("rel", k), R2.at[:, cols(k)])
    steps(first, (A, 7), (B, 6), (W, 6))
    q = dot(a, Wqkv[0])
    QKV[0] = q + SM[0:1]
    QKV[1] = q + SM[1:2]
    QKV[2] = dot(a, Wqkv[1])
    QKV[3] = dot(a, Wqkv[2])
    mixed = []
    for p in range(4):
        c = pl.ds(2 * HEAD * p, 2 * HEAD)
        qu = pair_rows(QKV[0, :, c]).astype(bf16)
        qv = pair_rows(QKV[1, :, c]).astype(bf16)
        content = dot(qu, QKV[2, :, c].astype(bf16), 1, 1)
        whole = dot(qv, R2[:, c], 1, 1)
        placed = jnp.concatenate(
            [
                pltpu.roll(whole[e * T : (e + 1) * T], 4 * T - (T - 1), 1, stride=1, stride_axis=0)[:, :T]
                for e in range(2)
            ],
            0,
        )
        scores = jnp.where(key_mask, (content + placed) * HEAD ** (-0.5), -1e30)
        e = jnp.exp(scores - jnp.max(scores, -1, keepdims=True))
        probs = e / jnp.sum(e, -1, keepdims=True)
        PRB[p] = probs
        mixed.append(unpair(dot(probs.astype(bf16), QKV[3, :, c].astype(bf16))).astype(bf16))
    for k in range(4):
        SfSt[k, :, 0:C] = mixed[k]
    steps(first, (A, 8), (B, 7), (A, 9))
    step_c(7)
    steps(second, (A, 14), (B, 12))
    total = dot(mixed[0], Wo[0:C])
    for k in range(1, 4):
        total += dot(mixed[k], Wo[C * k : C * (k + 1)])
    x = x + total
    X[2] = x

    a = norm(2, x).astype(bf16)
    Nall[own, 2 * width : 3 * width] = a
    send_rows_second(2)
    steps(first, (B, 8), (A, 10), (B, 9))
    step_c(8)
    step_c(9)
    GVG[0] = dot(a, Wci[0])
    GVG[1] = dot(a, Wci[1])
    UP[margin : margin + T] = GVG[0] * jax.nn.sigmoid(GVG[1]) * row_mask
    for p in range(4):
        c = pl.ds(C * p, C)
        acc = SM[4:5, c] * UP[margin - taps // 2 : margin - taps // 2 + T, c]
        for k in range(1, taps):
            o = margin - taps // 2 + k
            acc += SM[4 + k : 5 + k, c] * UP[o : o + T, c]
        CT[:, c] = acc
    conv = CT[...]

    def dp_sums(name, ref, rows):
        n = len(rows)
        ref[d] = jnp.concatenate(rows + [jnp.zeros((8 - n, width), f32)], 0)
        for r in range(1, dp):
            start((name, r), lambda: ref.at[d], lambda: ref.at[d], zpeers[r])

    def summed(name, ref):
        for r in range(1, dp):
            arrived((name, r), ref.at[around[-r]])
        total = ref[0]
        for r in range(1, dp):
            total += ref[r]
        return total

    def total_of(v):
        return jnp.sum(v, 0, keepdims=True)

    masked = conv * row_mask
    frames_row = jnp.broadcast_to(total_of(row_mask), (1, width))
    dp_sums("bnf", STF, [total_of(masked), total_of(masked * conv), frames_row])
    steps(first, (B, 10))
    step_c(10)
    sums = summed("bnf", STF)
    count = sums[2:3]
    bn_mean = sums[0:1] / count
    inv_std = lax.rsqrt(sums[1:2] / count - bn_mean * bn_mean + EPSILON)
    hat = (conv - bn_mean) * inv_std
    CT[...] = hat
    active = silu(hat * SM[2:3] + SM[3:4]).astype(bf16)
    for k in range(4):
        SfSt[k, :, C : 2 * C] = active[:, C * k : C * (k + 1)]
    X[3] = X[2] + dot(active, Wco[...])

    @pl.when(first)
    def _():
        Nall[own, 3 * width : 4 * width] = norm(3, X[3]).astype(bf16)
        to_tensor(("n", 3), Nall, block(3))
        total = shared_feed(1, 3)
        send_chunks((13, 14))
        step_a(11)
        step_a(12)
        X[4] = X[3] + 0.5 * summed_here(("s", 1), 1, total)

    @pl.when(second)
    def _():
        for i in (13, 14):
            step_b(i)
        for i in range(11, 15):
            step_c(i)
        feed(1, 3, 3, 4)
    out = (norm(4, X[4]) * row_mask).astype(bf16)
    HOP[...] = out

    @pl.when(first)
    def _():
        start("hop", lambda: HOP, lambda: ARR, partner, first)

    LO[pl.ds(trow, T)] = out
    out_rows = lambda: LO.at[pl.ds(trow, T)]
    for k in (1, 2, 3):
        start(("out", k), out_rows, out_rows, peers[k])

    def line_start(name, region):
        for way, to, back in (("up", 1, -1), ("down", -1, 1)):
            if groups > 1:

                @pl.when(there[to])
                def _():
                    start((name, way, 1), lambda: region(0), lambda: region(0), (s, t, around[to]), there[to])

    def line_hop(name, region, n, after=None):
        for way, to, back in (("up", 1, -1), ("down", -1, 1)):
            if n < groups:

                @pl.when(there[back * n])
                def _():
                    j = back * n
                    arrived((name, way, n), region(j))
                    if n + 1 < groups:

                        @pl.when(there[to])
                        def _():
                            start(
                                (name, way, n + 1), lambda: region(j), lambda: region(j),
                                (s, t, around[to]), through[j, to],
                            )

                    if after is not None:
                        after(name, j)

    def rows_region(ref, n, c):
        return lambda j: ref.at[pl.ds(base_of[j], n), c]

    def share(ref, c):
        def go(name, j):
            rows = lambda: ref.at[pl.ds(base_of[j], T), c]
            start((name, "y", j), rows, lambda: ref.at[pl.ds(second_of[j], T), c], yp, there[j])
            start((name, "core", j), rows, lambda: ref.at[pl.ds(high_of[j], T), c], sib, there[j])

        return go

    def share_on(name, ref, c, n):
        for j in (n, -n):
            if n < groups:

                @pl.when(there[j])
                def _():
                    rows = lambda: ref.at[pl.ds(second_of[j], T), c]
                    arrived((name, "y", j), rows())
                    start((name, "core2", j), rows, lambda: ref.at[pl.ds(last_of[j], T), c], sib, there[j])

    def shared(name, ref, c):
        for j in reach:
            if j:

                @pl.when(there[j])
                def _():
                    arrived((name, "core", j), ref.at[pl.ds(high_of[j], T), c])
                    arrived((name, "core2", j), ref.at[pl.ds(last_of[j], T), c])

    every = block(0, 4)
    sf_cols = pl.ds(0, 2 * C)
    qkv_cols, gate_cols = pl.ds(0, 3 * C), pl.ds(3 * C, 2 * C)
    lines_of = {
        "n": (rows_region(Nall, T, every), share(Nall, every)),
        "sf": (rows_region(Sf, R4, sf_cols), None),
        "gates": (rows_region(Sb, R4, gate_cols), None),
        "qkv": (rows_region(Sb, R4, qkv_cols), None),
        "pa": (lambda j: PA.at[around[j] if groups > 1 else 0], None),
        "pb": (lambda j: PB.at[around[j] if groups > 1 else 0], None),
    }
    for i in range(4):
        lines_of["b", i] = (rows_region(Ball, T, block(i)), share(Ball, block(i)))

    def set_off(*names):
        for name in names:
            line_start(name, lines_of[name][0])

    def hop(n, *names):
        for name in names:
            line_hop(name, lines_of[name][0], n, lines_of[name][1])

    def hand_on(n, *names):
        for name in names:
            ref, c = (Nall, every) if name == "n" else (Ball, block(name[1]))
            share_on(name, ref, c, n)

    Sf[own] = SfSt[0]
    for k in (1, 2, 3):
        start(("sf", k), lambda k=k: SfSt.at[k], lambda k=k: Sf.at[place(k)], peers[k])

    @pl.when(first)
    def _():
        set_off("n")
        for i in (1, 2):
            to_tensor(("n", i), Nall, block(i))
        step_b(11)
        step_b(12)
        from_tensor("sf", Sf, sf_cols)
        set_off("sf")
        step_a(13)
        hop(1, "n", "sf")
        step_a(14)
        step_b(13)
        hop(2, "n", "sf")
        step_b(14)
        for i in range(11, 15):
            step_c(i)
        for k in range(4):
            H[1, k] = dot(Nall[own, 3 * width : 4 * width], Win[1, k])
        hand_on(1, "n")
        hop(3, "n", "sf")
        for i in (1, 2):
            from_tensor(("n", i), Nall, block(i))
        hand_on(2, "n")
        hand_on(3, "n")

    @pl.when(first)
    def _():
        arrived("back", ARR)
        G[...] = ARR[...].astype(f32)

    back_rows = lambda: IG.at[pl.ds(trow, T)]

    def feed_back(j, i, g):
        b = (0.5 * g).astype(bf16)
        Ball[own, i * width : (i + 1) * width] = b
        to_tensor(("b", i), Ball, block(i))
        grad = None
        for k in range(4):
            h = H[j, k]
            sig = jax.nn.sigmoid(h)
            hg = (dot(b, Wout[j, k], 1, 1) * (sig * (1.0 + h * (1.0 - sig)))).astype(bf16)
            part = dot(hg, Win[j, k], 1, 1)
            grad = part if grad is None else grad + part
        return g + norm_back(i, grad)
    g = norm_back(4, G[...] * row_mask)
    g = feed_back(1, 3, g)
    b = g.astype(bf16)
    Ball[own, 2 * width : 3 * width] = b
    to_tensor(("b", 2), Ball, block(2))
    hat = CT[...]
    y = hat * SM[2:3] + SM[3:4]
    sig = jax.nn.sigmoid(y)
    dy = dot(b, Wco[...], 1, 1) * (sig * (1.0 + y * (1.0 - sig)))
    PAst[2:3] = total_of(dy * hat)
    PAst[3:4] = total_of(dy)
    dhat = dy * SM[2:3]
    masked = dhat * row_mask
    dp_sums("bnb", STB, [total_of(masked), total_of(masked * hat)])
    sums = summed("bnb", STB)

    @pl.when(second)
    def _():
        set_off("n")
        from_tensor("sf", Sf, sf_cols)
        set_off("sf")

    set_off(("b", 3), ("b", 2))
    dc = inv_std * (dhat - (sums[0:1] + hat * sums[1:2]) / count) * row_mask
    DP[margin : margin + T] = dc
    for p in range(4):
        c = pl.ds(C * p, C)
        here = DP[margin : margin + T, c]
        acc = None
        for k in range(taps):
            o = margin + taps // 2 - k
            term = SM[4 + k : 5 + k, c] * DP[o : o + T, c]
            acc = term if acc is None else acc + term
            o = margin - taps // 2 + k
            PAst[4 + k : 5 + k, c] = total_of(here * UP[o : o + T, c])
        CT[:, c] = acc
    du = CT[...] * row_mask
    sig = jax.nn.sigmoid(GVG[1])
    dvalue = (du * sig).astype(bf16)
    dgate = (du * GVG[0] * (sig * (1.0 - sig))).astype(bf16)
    for k in range(4):
        SbSt[k, :, 3 * C : 4 * C] = dvalue[:, C * k : C * (k + 1)]
        SbSt[k, :, 4 * C : 5 * C] = dgate[:, C * k : C * (k + 1)]
    Sb[own, 3 * C : 5 * C] = SbSt[0, :, 3 * C : 5 * C]

    def sb_to_tensor(name, c):
        for k in (1, 2, 3):
            start((name, k), lambda k=k: SbSt.at[k, :, c], lambda k=k: Sb.at[place(k), c], peers[k])

    sb_to_tensor("gates", gate_cols)
    g = g + norm_back(2, dot(dvalue, Wci[0], 1, 1) + dot(dgate, Wci[1], 1, 1))
    b = g.astype(bf16)
    Ball[own, width : 2 * width] = b
    to_tensor(("b", 1), Ball, block(1))
    dmix = dot(b, Wo[...], 1, 1).astype(bf16).astype(f32)
    scale = HEAD ** (-0.5)
    dq, dk, dv = [], [], []
    for p in range(4):
        c = pl.ds(2 * HEAD * p, 2 * HEAD)
        qu = pair_rows(QKV[0, :, c]).astype(bf16)
        qv = pair_rows(QKV[1, :, c]).astype(bf16)
        key = QKV[2, :, c].astype(bf16)
        val = QKV[3, :, c].astype(bf16)
        do = pair_rows(dmix[:, 2 * HEAD * p : 2 * HEAD * (p + 1)]).astype(bf16)
        probs = PRB[p]
        dprob = dot(do, val, 1, 1)
        ds = (probs * (dprob - jnp.sum(probs * dprob, -1, keepdims=True))).astype(bf16)
        du_rows = unpair(dot(ds, key)) * scale
        turned = dot(ds, flip)
        whole = jnp.concatenate(
            [
                pltpu.roll(turned[e * T : (e + 1) * T], 0, 1, stride=1, stride_axis=0)[:, : 2 * T]
                for e in range(2)
            ],
            0,
        ).astype(bf16)
        dv_rows = unpair(dot(whole, R2[2 * T : 4 * T, c])) * scale
        dk.append((dot(ds, qu, 0, 0) * scale).astype(bf16))
        dv.append(dot(probs.astype(bf16), do, 0, 0).astype(bf16))
        dq.append((du_rows + dv_rows).astype(bf16))
        PAst[0:1, c] = total_of(du_rows)
        PAst[1:2, c] = total_of(dv_rows)
        PAst[SMALL_ROWS : SMALL_ROWS + 2 * T, c] = dot(whole, qv, 0, 0) * scale
    for k in range(4):
        SbSt[k, :, 0:C] = dq[k]
        SbSt[k, :, C : 2 * C] = dk[k]
        SbSt[k, :, 2 * C : 3 * C] = dv[k]
    Sb[own, 0 : 3 * C] = SbSt[0, :, 0 : 3 * C]
    sb_to_tensor("qkv", qkv_cols)
    set_off(("b", 1))

    @pl.when(first)
    def _():
        from_tensor("gates", Sb, gate_cols)
        set_off("gates")
        hop(1, ("b", 3), ("b", 2))
    grad = dot(jnp.concatenate(dq, 1), Wqkv[0], 1, 1)
    grad += dot(jnp.concatenate(dk, 1), Wqkv[1], 1, 1)
    grad += dot(jnp.concatenate(dv, 1), Wqkv[2], 1, 1)
    g = g + norm_back(1, grad)

    @pl.when(second)
    def _():
        IG[pl.ds(trow, T)] = feed_back(0, 0, g).astype(bf16)
        start("back", back_rows, lambda: ARR, partner, second)

    @pl.when(first)
    def _():
        Ball[own, 0:width] = (0.5 * g).astype(bf16)
        to_tensor(("b", 0), Ball, block(0))
        G[...] = g

    set_off(("b", 0))
    PAb[...] = PAst[...].astype(bf16)
    for k in (1, 2, 3):
        start(("pa", k), lambda k=k: PAb.at[:, cols(k)], lambda k=k: PAin.at[k], peers[k])


    @pl.when(second)
    def _():
        from_tensor("gates", Sb, gate_cols)
        set_off("gates")

    from_tensor("qkv", Sb, qkv_cols)
    set_off("qkv")

    @pl.when(first)
    def _():
        from_tensor(("b", 0), Ball, block(0))
        h = dot(Nall[four, 0:width], Win[0, 0])
        sig = jax.nn.sigmoid(h)
        hg = dot(Ball[four, 0:width], Wout[0, 0], 1, 1) * (sig * (1.0 + h * (1.0 - sig)))
        total = sum_to_owner("s2", 2, dot(hg.astype(bf16), Win[0, 0], 1, 1))
        hop(2, ("b", 3), ("b", 2))
        hop(1, "gates", ("b", 1))
        hand_on(1, ("b", 3), ("b", 2))
        g = G[...] + norm_back(0, summed_here("s2", 2, total))
        IG[pl.ds(trow, T)] = g.astype(bf16)

    PBin[t] = PBst[...].astype(bf16)
    for k in (1, 2, 3):
        start(("pb", k), lambda: PBin.at[t], lambda: PBin.at[t], peers[k])
        start(("grad", k), back_rows, back_rows, peers[k])
    PAin[0] = PAb[:, 0:C]
    for k in (1, 2, 3):
        arrived(("pa", k), PAin.at[k])
    PA[mine] = sum(PAin[k].astype(f32) for k in range(4)).astype(bf16)
    set_off("pa")

    @pl.when(second)
    def _():
        for n in (1, 2):
            hop(n, "n", "sf", ("b", 3), ("b", 2))
        hand_on(1, "n", ("b", 3), ("b", 2))
        hop(1, "gates", ("b", 1))
    hop(1, ("b", 0), "qkv")
    hop(3, ("b", 3), ("b", 2))
    hop(2, "gates", ("b", 1))
    for k in (1, 2, 3):
        arrived(("pb", k), PBin.at[t ^ k])
    PB[mine] = sum(PBin[k].astype(f32) for k in range(4)).astype(bf16)
    set_off("pb")
    hop(1, "pa")
    hand_on(1, ("b", 1), ("b", 0))
    hand_on(2, ("b", 3), ("b", 2))

    @pl.when(second)
    def _():
        hop(3, "n", "sf")
        hand_on(2, "n")
    hop(2, ("b", 0), "qkv")
    hop(3, "gates", ("b", 1))
    hop(1, "pb")
    hop(2, "pa")
    hand_on(2, ("b", 1), ("b", 0))
    hand_on(3, ("b", 3), ("b", 2))

    @pl.when(second)
    def _():
        hand_on(3, "n")
    hop(3, ("b", 0), "qkv")
    hop(2, "pb")
    hop(3, "pa")
    hand_on(3, ("b", 1), ("b", 0))
    hop(3, "pb")
    for k in (1, 2, 3):
        theirs = pl.ds(pl.multiple_of((t ^ k) * T, T), T)
        arrived(("out", k), LO.at[theirs])
        arrived(("grad", k), IG.at[theirs])
    for i in (3, 2, 1):
        from_tensor(("b", i), Ball, block(i))

    @pl.when(second)
    def _():
        from_tensor(("b", 0), Ball, block(0))
        for i in range(4):
            from_tensor(("n", i), Nall, block(i))

    shared("n", Nall, every)
    for i in (3, 2, 1, 0):
        shared(("b", i), Ball, block(i))
    conds = {}
    for cond, copy in pending.values():
        conds.setdefault(id(cond), (cond, []))[1].append(copy)
    for cond, copies in conds.values():
        if cond is None:
            for copy in copies:
                copy().wait_send()
        else:

            @pl.when(cond)
            def _():
                for copy in copies:
                    copy().wait_send()


def gradient_kernel(*refs):
    given, outs, held, made = refs[:11], refs[11:25], refs[25:36], refs[36:50]
    active, hidden, in_sems, out_sems = refs[50:]
    nall, ball, sf, sb, lo, ig, pa, pb, fin, fout, table = held
    (LO, IG, ng, nb, w_in, w_out, w_ain, pos, w_aout, w_cin, w_dw, bng, bns, w_cout) = made
    R, width, C = nall.shape[0], fin.shape[1], sf.shape[1] // 2
    loads = [pltpu.make_async_copy(given[i], held[i], in_sems.at[i]) for i in range(len(given))]
    for i in (8, 9, 0, 1, 2, 3, 4, 5, 6, 7, 10):
        loads[i].start()
    stores = []

    def store(src, dst, sem):
        copy = pltpu.make_async_copy(src, dst, out_sems.at[sem])
        copy.start()
        stores.append(copy)

    def block(ref, i, n):
        return ref[:, i * n : (i + 1) * n]

    for i in (8, 9, 0, 1):
        loads[i].wait()
    step = min(128, R)
    for j, i in ((0, 0), (1, 3)):
        c = slice(i * width, (i + 1) * width)
        for r in range(0, R, step):
            rows = slice(r, r + step)
            h = dot(nall[rows, c], fin[j])
            sig = jax.nn.sigmoid(h)
            active[rows] = (h * sig).astype(bf16)
            grad = dot(ball[rows, c], fout[j], 1, 1)
            hidden[rows] = (grad * (sig * (1.0 + h * (1.0 - sig)))).astype(bf16)
        w_in[j] = dot(nall[:, c], hidden[...], 0, 0)
        store(w_in.at[j], outs[4].at[j], 4 if j == 0 else 14)
        w_out[j] = dot(active[...], ball[:, c], 0, 0)
        store(w_out.at[j], outs[5].at[j], 5 if j == 0 else 15)
    for i in (2, 3, 4, 5, 6, 7, 10):
        loads[i].wait()
    qkv = dot(block(nall, 1, width), sb[:, 0 : 3 * C], 0, 0)
    for i in range(3):
        w_ain[i] = qkv[:, C * i : C * (i + 1)]
    sums = pa[0].astype(f32)
    for g in range(1, pa.shape[0]):
        sums += pa[g].astype(f32)
    w_ain[3] = dot(table[...], sums[SMALL_ROWS:].astype(bf16), 0, 0)
    store(w_ain, outs[6], 6)
    gates = dot(block(nall, 2, width), sb[:, 3 * C : 5 * C], 0, 0)
    for i in range(2):
        w_cin[pl.ds(i, width, stride=2), :] = gates[:, C * i : C * (i + 1)]
    store(w_cin, outs[9], 9)
    w_aout[...] = dot(sf[:, 0:C], block(ball, 1, width), 0, 0)
    store(w_aout, outs[8], 8)
    w_cout[...] = dot(sf[:, C : 2 * C], block(ball, 2, width), 0, 0)
    store(w_cout, outs[13], 13)
    LO[...] = lo[...].astype(f32)
    IG[...] = ig[...].astype(f32)
    norms = pb[0].astype(f32)
    for g in range(1, pb.shape[0]):
        norms += pb[g].astype(f32)
    for i in range(5):
        ng[i] = norms[i : i + 1]
        nb[i] = norms[8 + i : 9 + i]
    pos[...] = sums[0:2]
    bng[...] = sums[2:3]
    bns[...] = sums[3:4]
    for k in range(w_dw.shape[0]):
        w_dw[k] = sums[4 + k : 5 + k]
    for i in (0, 1, 2, 3, 7, 10, 11, 12):
        store(made[i], outs[i], i)
    for copy in stores:
        copy.wait()


def on_device(
    inputs, lengths, cotangent, norm_gain, norm_bias, ffn_in, ffn_out, attn_in, pos_bias, attn_out,
    conv_in, depthwise, bn_gain, bn_shift, conv_out,
):
    dp = lax.axis_size(DATA)
    group, frames, width = inputs.shape
    C = width // 4
    taps = depthwise.shape[1]
    groups = dp if dp <= 4 else 1
    R = groups * group * frames
    table = position_rows(frames, width)
    vm = pl.BlockSpec(memory_space=pltpu.VMEM)
    hbm = pl.BlockSpec(memory_space=pltpu.HBM)
    sums_rows = SMALL_ROWS + 2 * frames

    def shape(dims, dtype=bf16):
        return jax.ShapeDtypeStruct(dims, dtype)

    n_copies = 200 + 50 * (groups - 1) + 2 * dp
    operands = (
        lengths, inputs, cotangent, norm_gain.transpose(1, 0, 2), norm_bias.transpose(1, 0, 2), ffn_in[0],
        ffn_out[0], attn_in[0], attn_out[0], conv_in.reshape(2 * width, C), conv_out[0], pos_bias[0], bn_gain,
        bn_shift, depthwise.transpose(1, 0, 2), table,
    )
    nall, ball, sf, sb, lo, ig, pa, pb = pl.pallas_call(
        lambda *refs: layer_kernel((frames, width, dp, groups), *refs),
        out_shape=[
            shape((R, 4 * width)), shape((R, 4 * width)), shape((R, 2 * C)), shape((R, 5 * C)),
            shape((group * frames, width)), shape((group * frames, width)),
            shape((groups, sums_rows, C)), shape((groups, 16, width)),
        ],
        in_specs=[hbm] * 16,
        out_specs=[vm] * 8,
        scratch_shapes=[
            pltpu.VMEM((2, 4, width, width), bf16),
            pltpu.VMEM((2, 4, width, width), bf16),
            pltpu.VMEM((3, width, width), bf16),
            pltpu.VMEM((width, C), bf16),
            pltpu.VMEM((width, width), bf16),
            pltpu.VMEM((2, width, width), bf16),
            pltpu.VMEM((width, width), bf16),
            pltpu.VMEM((4 * frames, width), bf16),
            pltpu.VMEM((SMALL_ROWS, width), f32),
            pltpu.VMEM((2, 4, frames, width), f32),
            pltpu.VMEM((5, frames, width), f32),
            pltpu.VMEM((5, frames, 128), f32),
            pltpu.VMEM((5, frames, width), f32),
            pltpu.VMEM((frames, width), f32),
            pltpu.VMEM((frames, width), bf16),
            pltpu.VMEM((frames, width), bf16),
            pltpu.VMEM((4, frames, width), f32),
            pltpu.VMEM((4, 2 * frames, frames), f32),
            pltpu.VMEM((2, frames, width), f32),
            pltpu.VMEM((frames, width), f32),
            pltpu.VMEM((frames + 32, width), f32),
            pltpu.VMEM((frames + 32, width), f32),
            pltpu.VMEM((4, frames, 2 * C), bf16),
            pltpu.VMEM((4, frames, 5 * C), bf16),
            pltpu.VMEM((sums_rows, width), f32),
            pltpu.VMEM((sums_rows, width), bf16),
            pltpu.VMEM((4, sums_rows, C), bf16),
            pltpu.VMEM((16, width), f32),
            pltpu.VMEM((4, 16, width), bf16),
            pltpu.VMEM((dp, 8, width), f32),
            pltpu.VMEM((dp, 8, width), f32),
            pltpu.VMEM((3, 3, frames, width), bf16),
            pltpu.VMEM((3, 3, frames, width), bf16),
            pltpu.VMEM((5, 1, width), f32),
            pltpu.VMEM((5, 1, width), f32),
            pltpu.VMEM((2, C), f32),
            pltpu.VMEM((1, C), f32),
            pltpu.VMEM((1, C), f32),
            pltpu.VMEM((taps, 1, C), f32),
            pltpu.VMEM((4 * frames, width), bf16),
            pltpu.SMEM((group,), jnp.int32),
            pltpu.VMEM((2 * width, C), bf16),
            pltpu.VMEM((2 * width, C), f32),
            pltpu.SemaphoreType.DMA((n_copies,)),
            pltpu.SemaphoreType.DMA((n_copies,)),
            pltpu.SemaphoreType.DMA((21,)),
        ],
        compiler_params=pltpu.CompilerParams(
            collective_id=0, has_side_effects=True, vmem_limit_bytes=62 * 2**20
        ),
    )(*operands)

    gradients = [
        shape((group * frames, width), f32), shape((group * frames, width), f32), shape((5, 1, width), f32),
        shape((5, 1, width), f32), shape((2, width, width), f32), shape((2, width, width), f32),
        shape((4, width, C), f32), shape((2, C), f32), shape((C, width), f32), shape((2 * width, C), f32),
        shape((taps, 1, C), f32), shape((1, C), f32), shape((1, C), f32), shape((C, width), f32),
    ]
    given = (nall, ball, sf, sb, lo, ig, pa, pb, ffn_in[0], ffn_out[0], table[2 * frames :])
    outs = pl.pallas_call(
        gradient_kernel,
        out_shape=gradients,
        in_specs=[hbm] * len(given),
        out_specs=[hbm] * len(gradients),
        scratch_shapes=[pltpu.VMEM(m.shape, m.dtype) for m in given]
        + [pltpu.VMEM(m.shape, m.dtype) for m in gradients]
        + [
            pltpu.VMEM((R, width), bf16),
            pltpu.VMEM((R, width), bf16),
            pltpu.SemaphoreType.DMA((len(given),)),
            pltpu.SemaphoreType.DMA((len(gradients) + 2,)),
        ],
        compiler_params=pltpu.CompilerParams(vmem_limit_bytes=62 * 2**20),
    )(*given)
    if groups == 1:
        outs = list(outs[:2]) + [lax.psum(m.astype(bf16), DATA).astype(f32) for m in outs[2:]]
    (lo, ig, ng, nb, w_in, w_out, w_ain, pos, w_aout, w_cin, w_dw, bng, bns, w_cout) = outs
    rows = (1, group, frames, width)
    return (
        lo.reshape(rows), ig.reshape(rows), ng.transpose(1, 0, 2), nb.transpose(1, 0, 2), w_in[None], w_out[None],
        w_ain[None], pos[None], w_aout[None], w_cin.reshape(conv_in.shape), w_dw.transpose(1, 0, 2), bng, bns,
        w_cout[None],
    )


def solution(mesh):
    placed = (
        P(DATA, None, None),
        P(DATA),
        P(DATA, None, None),
        P(SECTION, None, None),
        P(SECTION, None, None),
        P(SECTION, None, None, TENSOR),
        P(SECTION, None, TENSOR, None),
        P(SECTION, None, None, TENSOR),
        P(SECTION, None, TENSOR),
        P(SECTION, TENSOR, None),
        P(SECTION, None, None, TENSOR),
        P(SECTION, None, TENSOR),
        P(SECTION, TENSOR),
        P(SECTION, TENSOR),
        P(SECTION, TENSOR, None),
    )
    return jax.shard_map(
        on_device,
        mesh=mesh,
        in_specs=placed,
        out_specs=(
            P(SECTION, DATA, None, None),
            P(SECTION, DATA, None, None),
            P(SECTION, None, None),
            P(SECTION, None, None),
            P(SECTION, None, None, TENSOR),
            P(SECTION, None, TENSOR, None),
            P(SECTION, None, None, TENSOR),
            P(SECTION, None, TENSOR),
            P(SECTION, TENSOR, None),
            P(SECTION, None, None, TENSOR),
            P(SECTION, None, TENSOR),
            P(SECTION, TENSOR),
            P(SECTION, TENSOR),
            P(SECTION, TENSOR, None),
        ),
        check_vma=False,
    )
```

```python
import math

import jax
import jax.numpy as jnp
import numpy as np
from jax import lax
from jax.experimental import pallas as pl
from jax.experimental.pallas import tpu as pltpu
from jax.sharding import PartitionSpec as P

HEAD = 64
EPSILON = 1e-05
MESH = pl.DeviceIdType.MESH
SECTION, TENSOR, DATA = "section", "tensor", "dp"
PLACE = (0, 2, 1, 3)
SMALL_ROWS = 48
bf16, f32 = jnp.bfloat16, jnp.float32


def dot(left, right, left_dim=1, right_dim=0):
    return lax.dot_general(
        left, right, (((left_dim,), (right_dim,)), ((), ())), preferred_element_type=f32
    )


def position_rows(frames, width):
    offset = np.arange(2 * frames - 1, dtype=np.float32) - np.float32(frames - 1)
    rates = np.exp(
        np.arange(width // 2, dtype=np.float32) * np.float32(-2.0 * math.log(10000.0) / width)
    )
    angles = (offset[:, None] * rates[None, :]).astype(np.float32)
    table = np.stack([np.sin(angles), np.cos(angles)], -1).reshape(2 * frames - 1, width)
    blank = np.zeros((1, width), np.float32)
    return jnp.asarray(np.concatenate([table[::-1], blank, table, blank]), bf16)


def layer_kernel(dims, *refs):
    T, width, dp, groups = dims
    C = width // 4
    (lengths, inputs, cot, ng_in, nb_in, fin, fout, ain, aout, cin, cout, pos_in, bng_in, bns_in, dw_in, e2_in) = refs[:16]
    (LO, IG, PA, PB, n0_out, b0_out, act0_out, slope0_out, in1_out, out1_out, qkv_out, ao_out, ci_out, co_out) = refs[16:30]
    refs = refs[30:]
    (Win, Wout, Wqkv, Wr, Wo, Wci, Wco, R2, SM) = refs[:9]
    (H, XH, RS, X, G, ARR, HOP, QKV, PRB, GVG, CT, UP, DP) = refs[9:22]
    (SfSt, SbSt, PAst, PAb, PAin, PBst, PBin, STF, STB, RSst, RSin) = refs[22:33]
    (ng, nb, pos, bng, bns, dw, e2, lens, pairs, spread) = refs[33:43]
    (Nall, Ball, Sf, Sb, ACT, SLOPE, HG, gin1, gout1, gqkv, gao, gci, gco) = refs[43:56]
    dummy, ss, rs, ls, os = refs[56:61]

    s, t, d = lax.axis_index(SECTION), lax.axis_index(TENSOR), lax.axis_index(DATA)
    first, second = s == 0, s == 1
    taps = dw.shape[0]
    peers = [(s, t ^ k, d) for k in range(4)]
    sib, yp = peers[1], peers[2]
    around = {j: lax.rem(d + j + dp, dp) for j in range(1 - dp, dp)}
    zpeers = [(s, t, around[r]) for r in range(dp)]
    zpair = (s, t, d ^ 1)
    partner = (1 - s, t, d)
    half = lax.rem(d, 2)
    R4 = 4 * T
    reach = range(1 - groups, groups)
    base_of = {j: pl.multiple_of(around[j] * R4, R4) if groups > 1 else 0 for j in reach}
    second_of, high_of, last_of = (
        {j: pl.multiple_of(around[j] * R4 + n * T, T) if groups > 1 else n * T for j in reach} for n in (1, 2, 3)
    )
    there = {j: d + j >= 0 if j < 0 else d + j <= dp - 1 for j in reach}
    through = {
        (j, to): there[j] & there[to] for j in reach for to in (1, -1) if j * to < 0 and groups > 1
    }
    base = base_of[0]
    trow = pl.multiple_of(t * T, T)
    mine = d if groups > 1 else 0

    recv_index, send_index, sent = {}, {}, {}

    def size_of(view):
        return math.prod(view.shape) * view.dtype.itemsize

    def copy_of(key, src, dst, dev, group):
        i = recv_index.setdefault(key, len(recv_index))
        j = send_index.setdefault(id(group), len(send_index))
        return pltpu.make_async_remote_copy(
            src_ref=src, dst_ref=dst, send_sem=ss.at[j], recv_sem=rs.at[i], device_id=dev, device_id_type=MESH,
        )

    def start(key, src, dst, dev, cond=None, part=0):
        view = src()
        copy_of(key, view, dst(), dev, cond).start()
        sent.setdefault(id(cond), (cond, {}))[1][key, part] = size_of(view)

    def arrived(key, dst):
        copy_of(key, dst, dst, partner, None).wait_recv()

    def room(size):
        return dummy.at[pl.ds(0, size // (4 * dummy.shape[1]))]

    def all_arrived(key, size):
        if size:
            arrived(key, room(size))

    locals_ = {}

    def fetch(name, src, dst):
        locals_[name] = lambda: pltpu.make_async_copy(src(), dst(), ls.at[list(locals_).index(name)])
        locals_[name]().start()

    def fetched(*names):
        for name in names:
            locals_[name]().wait()

    @pl.when(first)
    def _():
        pltpu.make_async_copy(inputs.at[t], X.at[0], ls.at[20]).start()

    @pl.when(second)
    def _():
        pltpu.make_async_copy(cot.at[t], G, ls.at[20]).start()

    fetch("ng", lambda: ng_in, lambda: ng)
    fetch("nb", lambda: nb_in, lambda: nb)
    fetch("in0", lambda: fin.at[0], lambda: Win.at[0, 0])
    fetch("out0", lambda: fout.at[0], lambda: Wout.at[0, 0])
    fetch("wr", lambda: ain.at[3], lambda: Wr)
    fetch("e2", lambda: e2_in, lambda: e2)
    fetch("pos", lambda: pos_in, lambda: pos)
    fetch("bng", lambda: bng_in, lambda: bng)
    fetch("bns", lambda: bns_in, lambda: bns)
    fetch("dw", lambda: dw_in, lambda: dw)
    fetch("len", lambda: lengths, lambda: lens)
    fetch("qkv", lambda: ain.at[pl.ds(0, 3)], lambda: Wqkv.at[:, :, pl.ds(0, C)])
    fetch("o", lambda: aout, lambda: Wo.at[pl.ds(0, C)])
    fetch("ci", lambda: cin, lambda: pairs)
    fetch("co", lambda: cout, lambda: Wco.at[pl.ds(0, C)])
    fetch("in1", lambda: fin.at[1], lambda: Win.at[1, 0])
    fetch("out1", lambda: fout.at[1], lambda: Wout.at[1, 0])

    barrier = pltpu.get_barrier_semaphore()
    greet = peers[1:] + zpeers[1:] + [partner]
    for dev in greet:
        pl.semaphore_signal(barrier, inc=1, device_id=dev, device_id_type=MESH)
    pl.semaphore_wait(barrier, len(greet))

    starts = {}

    def lines(first_row, n, which):
        if which is None:
            return pl.ds(first_row, n)
        at = (first_row, n, which)
        if at not in starts:
            starts[at] = pl.multiple_of(first_row + n // 2 * (half if which == "own" else 1 - half), n // 2)
        return pl.ds(starts[at], n // 2)

    def cols(k):
        return pl.ds(C * k, C)

    def feed_chunks(j):
        Q = width // 2
        return [
            (
                lambda w, src=src, q=q: src.at[j, lines(Q * q, Q, w)],
                lambda k, w, dst=dst, q=q: dst.at[j, k, lines(Q * q, Q, w)],
            )
            for src, dst in ((fin, Win), (fout, Wout))
            for q in range(2)
        ]

    def row_chunk(src, dst):
        return [(lambda w: src.at[lines(0, C, w)], lambda k, w: dst.at[lines(C * k, C, w)])]

    def column_chunks(src, dst, n):
        return [
            (lambda w, i=i: src(i, lines(0, width, w)), lambda k, w, i=i: dst.at[i, lines(0, width, w), cols(k)])
            for i in range(n)
        ]

    chunks = (
        feed_chunks(0)
        + column_chunks(lambda i, rows: ain.at[i, rows], Wqkv, 3)
        + row_chunk(aout, Wo)
        + column_chunks(lambda i, rows: Wci.at[i, rows, cols(0)], Wci, 2)
        + row_chunk(cout, Wco)
        + feed_chunks(1)
    )
    for n, at in ((width // 2, 0), (width // 2, width // 2), (width, 0)) + tuple((C, C * k) for k in range(4)):
        for w in ("own", "other"):
            lines(at, n, w)
    only = {i: second for i in range(4)}

    def send_chunks(names):
        for i in names:
            src, dst = chunks[i]
            start(("sib", i), lambda src=src: src(None), lambda dst=dst: dst(1, None), sib, only.get(i))
            start(("y", i), lambda src=src: src("own"), lambda dst=dst: dst(2, "own"), yp, only.get(i))

    def step_a(i):
        dst = chunks[i][1]
        arrived(("y", i), dst(2, "own"))
        start(("z", i), lambda: dst(2, "own"), lambda: dst(2, "own"), zpair, only.get(i))
        start(("sib", i), lambda: dst(2, "own"), lambda: dst(3, "own"), sib, only.get(i), 1)

    def step_b(i):
        dst = chunks[i][1]
        arrived(("z", i), dst(2, "other"))
        start(("sib", i), lambda: dst(2, "other"), lambda: dst(3, "other"), sib, only.get(i), 2)

    def step_c(i):
        all_arrived(("sib", i), 2 * size_of(chunks[i][1](1, None)))

    def steps(cond, *plan):
        @pl.when(cond)
        def _():
            for step, i in plan:
                step(i)

    A, B, W = step_a, step_b, step_c

    def norm(i, x):
        centre = x - jnp.mean(x, -1, keepdims=True)
        rate = lax.rsqrt(jnp.mean(centre * centre, -1, keepdims=True) + EPSILON)
        hat = centre * rate
        XH[i] = hat
        RS[i] = jnp.broadcast_to(rate, RS.shape[1:])
        return hat * ng[i] + nb[i]

    def norm_back(i, grad):
        hat = XH[i]
        PBst[i : i + 1] = jnp.sum(grad * hat, 0, keepdims=True)
        PBst[8 + i : 9 + i] = jnp.sum(grad, 0, keepdims=True)
        g = grad * ng[i]
        return RS[i][:, 0:1] * (
            g - jnp.mean(g, -1, keepdims=True) - hat * jnp.mean(g * hat, -1, keepdims=True)
        )

    def silu(h):
        return h * jax.nn.sigmoid(h)

    def place(k):
        return pl.ds(base + T * PLACE[k], T)

    own, four = pl.ds(base, T), pl.ds(base, R4)

    def block(i, n=1):
        return pl.ds(i * width, n * width)

    def to_tensor(name, ref, c):
        for k in (1, 2, 3):
            start(name, lambda: ref.at[own, c], lambda k=k: ref.at[place(k), c], peers[k], None, k)

    def from_tensor(name, ref, c):
        all_arrived(name, 3 * size_of(ref.at[own, c]))

    def feed(j, i, before, after):
        x = X[before]
        a = norm(i, x).astype(bf16)
        Nall[own, i * width : (i + 1) * width] = a
        to_tensor(("n", i), Nall, block(i))
        active = []
        for k in range(4):
            h = dot(a, Win[j, k])
            H[j, k] = h
            active.append(silu(h).astype(bf16))
        total = dot(active[0], Wout[j, 0])
        for k in range(1, 4):
            total += dot(active[k], Wout[j, k])
        X[after] = x + 0.5 * total

    def sum_to_owner(name, slot, total):
        for k in (1, 2, 3):
            RSst[slot, k - 1] = total[T * PLACE[k] : T * (PLACE[k] + 1)].astype(bf16)
        for k in (1, 2, 3):
            start(name, lambda k=k: RSst.at[slot, k - 1], lambda k=k: RSin.at[slot, k - 1], peers[k], first, k)
        return total[0:T]

    def summed_here(name, slot, total):
        all_arrived(name, size_of(RSin.at[slot]))
        for k in (1, 2, 3):
            total += RSin[slot, k - 1].astype(f32)
        return total

    def shared_feed(j, i):
        from_tensor(("n", i), Nall, block(i))
        active = silu(dot(Nall[four, i * width : (i + 1) * width], Win[j, 0])).astype(bf16)
        return sum_to_owner(("s", j), j, dot(active, Wout[j, 0]))

    fetched("ng", "nb")

    @pl.when(first)
    def _():
        send_chunks((4,))
        pltpu.make_async_copy(inputs.at[t], X.at[0], ls.at[20]).wait()
        Nall[own, 0:width] = norm(0, X[0]).astype(bf16)
        to_tensor(("n", 0), Nall, block(0))
        send_chunks((5,))

    @pl.when(second)
    def _():
        send_chunks(range(4))
        pltpu.make_async_copy(cot.at[t], G, ls.at[20]).wait()

    fetched("in0", "out0")

    @pl.when(first)
    def _():
        X[1] = shared_feed(0, 0)
        send_chunks((6,))
        step_a(4)

    fetched("pos", "bng", "bns", "dw", "wr", "e2", "len", "ci")
    spread[...] = pairs[...].astype(f32)
    for i in range(2):
        Wci[i, :, 0:C] = spread[pl.ds(i, width, stride=2), :].astype(bf16)
    SM[:, 0:C] = jnp.zeros((SMALL_ROWS, C), f32)
    SM[0:2, 0:C] = pos[...]
    SM[2:3, 0:C] = bng[...]
    SM[3:4, 0:C] = bns[...]
    for k in range(taps):
        SM[4 + k : 5 + k, 0:C] = dw[k]
    R2[:, 0:C] = dot(e2[...], Wr[...]).astype(bf16)
    for k in (1, 2, 3):
        start("small", lambda: SM.at[:, cols(0)], lambda k=k: SM.at[:, cols(k)], peers[k], None, k)
        start("small", lambda: R2.at[:, cols(0)], lambda k=k: R2.at[:, cols(k)], peers[k], None, 3 + k)
    @pl.when(first)
    def _():
        send_chunks(range(7, 13))
        step_a(5)
        X[1] = X[0] + 0.5 * summed_here(("s", 0), 0, X[1])
        step_a(6)
        step_b(4)
        step_b(5)

    @pl.when(second)
    def _():
        send_chunks(range(4, 15))

    fetched("qkv", "o", "co", "in1", "out1")
    margin = 16
    UP[...] = jnp.zeros(UP.shape, f32)
    DP[...] = jnp.zeros(DP.shape, f32)
    PAst[...] = jnp.zeros(PAst.shape, f32)
    PBst[...] = jnp.zeros(PBst.shape, f32)

    length = lens[t]
    row_mask = (lax.broadcasted_iota(jnp.int32, (T, 1), 0) < length).astype(f32)
    key_mask = lax.broadcasted_iota(jnp.int32, (2 * T, T), 1) < length
    first_head = lax.broadcasted_iota(jnp.int32, (T, 2 * HEAD), 1) < HEAD
    flip = (
        lax.broadcasted_iota(jnp.int32, (T, 4 * T), 0) + lax.broadcasted_iota(jnp.int32, (T, 4 * T), 1)
        == T - 1
    ).astype(f32).astype(bf16)

    def pair_rows(v):
        return jnp.concatenate([jnp.where(first_head, v, 0.0), jnp.where(first_head, 0.0, v)], 0)

    def unpair(v):
        return jnp.where(first_head, v[:T], v[T:])

    @pl.when(second)
    def _():
        for i in range(14):
            step_a(i)
            if i > 1:
                step_b(i - 2)
        for i in range(7):
            step_c(i)
        arrived("hop", ARR)
        X[0] = ARR[...].astype(f32)
        feed(0, 0, 0, 1)

    def send_rows_second(i):
        @pl.when(second)
        def _():
            to_tensor(("n", i), Nall, block(i))

    x = X[1]
    a = norm(1, x).astype(bf16)
    Nall[own, width : 2 * width] = a
    send_rows_second(1)
    steps(second, (A, 14), (B, 12))
    steps(first, (W, 4), (W, 5))
    all_arrived("small", 3 * (size_of(SM.at[:, cols(0)]) + size_of(R2.at[:, cols(0)])))
    steps(first, (A, 7), (B, 6), (W, 6))
    q = dot(a, Wqkv[0])
    QKV[0] = q + SM[0:1]
    QKV[1] = q + SM[1:2]
    QKV[2] = dot(a, Wqkv[1])
    QKV[3] = dot(a, Wqkv[2])
    mixed = []
    for p in range(4):
        c = pl.ds(2 * HEAD * p, 2 * HEAD)
        qu = pair_rows(QKV[0, :, c]).astype(bf16)
        qv = pair_rows(QKV[1, :, c]).astype(bf16)
        content = dot(qu, QKV[2, :, c].astype(bf16), 1, 1)
        whole = dot(qv, R2[:, c], 1, 1)
        placed = jnp.concatenate(
            [
                pltpu.roll(whole[e * T : (e + 1) * T], 4 * T - (T - 1), 1, stride=1, stride_axis=0)[:, :T]
                for e in range(2)
            ],
            0,
        )
        scores = jnp.where(key_mask, (content + placed) * HEAD ** (-0.5), -1e30)
        e = jnp.exp(scores - jnp.max(scores, -1, keepdims=True))
        probs = e / jnp.sum(e, -1, keepdims=True)
        PRB[p] = probs
        mixed.append(unpair(dot(probs.astype(bf16), QKV[3, :, c].astype(bf16))).astype(bf16))
    for k in range(4):
        SfSt[k, :, 0:C] = mixed[k]
    steps(first, (A, 8), (B, 7), (A, 9))
    step_c(7)
    total = dot(mixed[0], Wo[0:C])
    for k in range(1, 4):
        total += dot(mixed[k], Wo[C * k : C * (k + 1)])
    x = x + total
    X[2] = x

    a = norm(2, x).astype(bf16)
    Nall[own, 2 * width : 3 * width] = a
    send_rows_second(2)
    steps(first, (B, 8), (A, 10), (B, 9))
    step_c(8)
    step_c(9)
    GVG[0] = dot(a, Wci[0])
    GVG[1] = dot(a, Wci[1])
    UP[margin : margin + T] = GVG[0] * jax.nn.sigmoid(GVG[1]) * row_mask
    for p in range(4):
        c = pl.ds(C * p, C)
        acc = SM[4:5, c] * UP[margin - taps // 2 : margin - taps // 2 + T, c]
        for k in range(1, taps):
            o = margin - taps // 2 + k
            acc += SM[4 + k : 5 + k, c] * UP[o : o + T, c]
        CT[:, c] = acc
    conv = CT[...]

    def dp_sums(name, ref, rows):
        n = len(rows)
        ref[d] = jnp.concatenate(rows + [jnp.zeros((8 - n, width), f32)], 0)
        for r in range(1, dp):
            start(name, lambda: ref.at[d], lambda: ref.at[d], zpeers[r], None, r)

    def summed(name, ref):
        all_arrived(name, (dp - 1) * size_of(ref.at[0]))
        total = ref[0]
        for r in range(1, dp):
            total += ref[r]
        return total

    def total_of(v):
        return jnp.sum(v, 0, keepdims=True)

    masked = conv * row_mask
    frames_row = jnp.broadcast_to(total_of(row_mask), (1, width))
    dp_sums("bnf", STF, [total_of(masked), total_of(masked * conv), frames_row])
    steps(first, (B, 10))
    step_c(10)
    sums = summed("bnf", STF)
    count = sums[2:3]
    bn_mean = sums[0:1] / count
    inv_std = lax.rsqrt(sums[1:2] / count - bn_mean * bn_mean + EPSILON)
    hat = (conv - bn_mean) * inv_std
    CT[...] = hat
    active = silu(hat * SM[2:3] + SM[3:4]).astype(bf16)
    for k in range(4):
        SfSt[k, :, C : 2 * C] = active[:, C * k : C * (k + 1)]
    X[3] = X[2] + dot(active, Wco[...])

    @pl.when(first)
    def _():
        Nall[own, 3 * width : 4 * width] = norm(3, X[3]).astype(bf16)
        to_tensor(("n", 3), Nall, block(3))
        total = shared_feed(1, 3)
        send_chunks((13, 14))
        step_a(11)
        step_a(12)
        X[4] = X[3] + 0.5 * summed_here(("s", 1), 1, total)

    @pl.when(second)
    def _():
        for i in (13, 14):
            step_b(i)
        for i in range(11, 15):
            step_c(i)
        feed(1, 3, 3, 4)
    out = (norm(4, X[4]) * row_mask).astype(bf16)
    HOP[...] = out

    @pl.when(first)
    def _():
        start("hop", lambda: HOP, lambda: ARR, partner, first)

    LO[pl.ds(trow, T)] = out
    out_rows = lambda: LO.at[pl.ds(trow, T)]
    for k in (1, 2, 3):
        start("out", out_rows, out_rows, peers[k], None, k)

    def line_start(name, region):
        for way, to, back in (("up", 1, -1), ("down", -1, 1)):
            if groups > 1:

                @pl.when(there[to])
                def _():
                    start(
                        (name, 0, back % dp), lambda: region(0), lambda: region(0), (s, t, around[to]), there[to], way
                    )

    def line_hop(name, region, n, after=None):
        for way, to, back in (("up", 1, -1), ("down", -1, 1)):
            if n < groups:

                @pl.when(there[back * n])
                def _():
                    j = back * n
                    arrived((name, 0, j % dp), region(j))
                    if n + 1 < groups:

                        @pl.when(there[to])
                        def _():
                            start(
                                (name, 0, (j + back) % dp), lambda: region(j), lambda: region(j),
                                (s, t, around[to]), through[j, to], way,
                            )

                    if after is not None:
                        after(name, j)

    def rows_region(ref, n, c):
        return lambda j: ref.at[pl.ds(base_of[j], n), c]

    def share(ref, c):
        def go(name, j):
            rows = lambda: ref.at[pl.ds(base_of[j], T), c]
            start((name, 1, j % dp), rows, lambda: ref.at[pl.ds(second_of[j], T), c], yp, there[j], j)
            start((name, 2, 0), rows, lambda: ref.at[pl.ds(high_of[j], T), c], sib, there[j], j)

        return go

    def share_on(name, ref, c, n):
        for j in (n, -n):
            if n < groups:

                @pl.when(there[j])
                def _():
                    rows = lambda: ref.at[pl.ds(second_of[j], T), c]
                    arrived((name, 1, j % dp), rows())
                    start((name, 2, 0), rows, lambda: ref.at[pl.ds(last_of[j], T), c], sib, there[j], dp + j)

    def shared(name, ref, c):
        all_arrived((name, 2, 0), 2 * (groups - 1) * size_of(ref.at[own, c]))

    every = block(0, 4)
    sf_cols = pl.ds(0, 2 * C)
    qkv_cols, gate_cols = pl.ds(0, 3 * C), pl.ds(3 * C, 2 * C)
    lines_of = {
        "n": (rows_region(Nall, T, every), share(Nall, every)),
        "sf": (rows_region(Sf, R4, sf_cols), None),
        "gates": (rows_region(Sb, R4, gate_cols), None),
        "qkv": (rows_region(Sb, R4, qkv_cols), None),
        "pa": (lambda j: PA.at[around[j] if groups > 1 else 0], None),
        "pb": (lambda j: PB.at[around[j] if groups > 1 else 0], None),
    }
    for i in range(4):
        lines_of["b", i] = (rows_region(Ball, T, block(i)), share(Ball, block(i)))

    def set_off(*names):
        for name in names:
            line_start(name, lines_of[name][0])

    def hop(n, *names):
        for name in names:
            line_hop(name, lines_of[name][0], n, lines_of[name][1])

    def hand_on(n, *names):
        for name in names:
            ref, c = (Nall, every) if name == "n" else (Ball, block(name[1]))
            share_on(name, ref, c, n)

    Sf[own] = SfSt[0]
    for k in (1, 2, 3):
        start("sf", lambda k=k: SfSt.at[k], lambda k=k: Sf.at[place(k)], peers[k], None, k)

    written = []

    def write(src, dst):
        copy = pltpu.make_async_copy(src, dst, os.at[len(written)])
        copy.start()
        written.append(copy)

    R = Nall.shape[0]
    row_blocks = [slice(r, r + R4) for r in range(0, R, R4)]

    def slope(h, sig):
        return sig * (1.0 + h * (1.0 - sig))

    def hidden_rows(j, i):
        for rows in row_blocks:
            h = dot(Nall[rows, i * width : (i + 1) * width], Win[j, 0])
            sig = jax.nn.sigmoid(h)
            ACT[j, rows] = (h * sig).astype(bf16)
            SLOPE[j, rows] = slope(h, sig)

    def second_feed_grads():
        c = slice(3 * width, 4 * width)
        for rows in row_blocks:
            HG[rows] = (dot(Ball[rows, c], Wout[1, 0], 1, 1) * SLOPE[1, rows]).astype(bf16)
        gin1[...] = dot(Nall[:, c], HG[...], 0, 0)
        write(gin1, in1_out)
        gout1[...] = dot(ACT[1], Ball[:, c], 0, 0)
        write(gout1, out1_out)

    def convolution_grads():
        gates = dot(Nall[:, 2 * width : 3 * width], Sb[:, 3 * C : 5 * C], 0, 0)
        for i in range(2):
            gci[pl.ds(i, width, stride=2), :] = gates[:, C * i : C * (i + 1)]
        write(gci, ci_out)
        gco[...] = dot(Sf[:, C : 2 * C], Ball[:, 2 * width : 3 * width], 0, 0)
        write(gco, co_out)

    def attention_grads():
        grads = dot(Nall[:, width : 2 * width], Sb[:, 0 : 3 * C], 0, 0)
        for i in range(3):
            gqkv[i] = grads[:, C * i : C * (i + 1)]
        write(gqkv, qkv_out)
        gao[...] = dot(Sf[:, 0:C], Ball[:, width : 2 * width], 0, 0)
        write(gao, ao_out)

    @pl.when(first)
    def _():
        set_off("n")
        for i in (1, 2):
            to_tensor(("n", i), Nall, block(i))
        step_b(11)
        step_b(12)
        from_tensor("sf", Sf, sf_cols)
        set_off("sf")
        step_a(13)
        hop(1, "n", "sf")
        step_a(14)
        step_b(13)
        hop(2, "n", "sf")
        step_b(14)
        for i in range(11, 15):
            step_c(i)
        for k in range(4):
            H[1, k] = dot(Nall[own, 3 * width : 4 * width], Win[1, k])
        hand_on(1, "n")
        hop(3, "n", "sf")
        for i in (1, 2):
            from_tensor(("n", i), Nall, block(i))
        hand_on(2, "n")
        hand_on(3, "n")

    @pl.when(first)
    def _():
        arrived("back", ARR)
        G[...] = ARR[...].astype(f32)

    back_rows = lambda: IG.at[pl.ds(trow, T)]

    def feed_back(j, i, g):
        b = (0.5 * g).astype(bf16)
        Ball[own, i * width : (i + 1) * width] = b
        to_tensor(("b", i), Ball, block(i))
        grad = None
        for k in range(4):
            h = H[j, k]
            sig = jax.nn.sigmoid(h)
            hg = (dot(b, Wout[j, k], 1, 1) * slope(h, sig)).astype(bf16)
            part = dot(hg, Win[j, k], 1, 1)
            grad = part if grad is None else grad + part
        return g + norm_back(i, grad)
    g = norm_back(4, G[...] * row_mask)
    g = feed_back(1, 3, g)
    b = g.astype(bf16)
    Ball[own, 2 * width : 3 * width] = b
    to_tensor(("b", 2), Ball, block(2))
    hat = CT[...]
    y = hat * SM[2:3] + SM[3:4]
    sig = jax.nn.sigmoid(y)
    dy = dot(b, Wco[...], 1, 1) * slope(y, sig)
    PAst[2:3] = total_of(dy * hat)
    PAst[3:4] = total_of(dy)
    dhat = dy * SM[2:3]
    masked = dhat * row_mask
    dp_sums("bnb", STB, [total_of(masked), total_of(masked * hat)])
    sums = summed("bnb", STB)

    @pl.when(second)
    def _():
        set_off("n")
        from_tensor("sf", Sf, sf_cols)
        set_off("sf")

    set_off(("b", 3), ("b", 2))
    dc = inv_std * (dhat - (sums[0:1] + hat * sums[1:2]) / count) * row_mask
    DP[margin : margin + T] = dc
    for p in range(4):
        c = pl.ds(C * p, C)
        here = DP[margin : margin + T, c]
        acc = None
        for k in range(taps):
            o = margin + taps // 2 - k
            term = SM[4 + k : 5 + k, c] * DP[o : o + T, c]
            acc = term if acc is None else acc + term
            o = margin - taps // 2 + k
            PAst[4 + k : 5 + k, c] = total_of(here * UP[o : o + T, c])
        CT[:, c] = acc
    du = CT[...] * row_mask
    sig = jax.nn.sigmoid(GVG[1])
    dvalue = (du * sig).astype(bf16)
    dgate = (du * GVG[0] * (sig * (1.0 - sig))).astype(bf16)
    for k in range(4):
        SbSt[k, :, 3 * C : 4 * C] = dvalue[:, C * k : C * (k + 1)]
        SbSt[k, :, 4 * C : 5 * C] = dgate[:, C * k : C * (k + 1)]
    Sb[own, 3 * C : 5 * C] = SbSt[0, :, 3 * C : 5 * C]

    def sb_to_tensor(name, c):
        for k in (1, 2, 3):
            start(name, lambda k=k: SbSt.at[k, :, c], lambda k=k: Sb.at[place(k), c], peers[k], None, k)

    sb_to_tensor("gates", gate_cols)
    g = g + norm_back(2, dot(dvalue, Wci[0], 1, 1) + dot(dgate, Wci[1], 1, 1))
    b = g.astype(bf16)
    Ball[own, width : 2 * width] = b
    to_tensor(("b", 1), Ball, block(1))
    dmix = dot(b, Wo[...], 1, 1).astype(bf16).astype(f32)
    scale = HEAD ** (-0.5)
    dq, dk, dv = [], [], []
    for p in range(4):
        c = pl.ds(2 * HEAD * p, 2 * HEAD)
        qu = pair_rows(QKV[0, :, c]).astype(bf16)
        qv = pair_rows(QKV[1, :, c]).astype(bf16)
        key = QKV[2, :, c].astype(bf16)
        val = QKV[3, :, c].astype(bf16)
        do = pair_rows(dmix[:, 2 * HEAD * p : 2 * HEAD * (p + 1)]).astype(bf16)
        probs = PRB[p]
        dprob = dot(do, val, 1, 1)
        ds = (probs * (dprob - jnp.sum(probs * dprob, -1, keepdims=True))).astype(bf16)
        du_rows = unpair(dot(ds, key)) * scale
        turned = dot(ds, flip)
        whole = jnp.concatenate(
            [
                pltpu.roll(turned[e * T : (e + 1) * T], 0, 1, stride=1, stride_axis=0)[:, : 2 * T]
                for e in range(2)
            ],
            0,
        ).astype(bf16)
        dv_rows = unpair(dot(whole, R2[2 * T : 4 * T, c])) * scale
        dk.append((dot(ds, qu, 0, 0) * scale).astype(bf16))
        dv.append(dot(probs.astype(bf16), do, 0, 0).astype(bf16))
        dq.append((du_rows + dv_rows).astype(bf16))
        PAst[0:1, c] = total_of(du_rows)
        PAst[1:2, c] = total_of(dv_rows)
        PAst[SMALL_ROWS : SMALL_ROWS + 2 * T, c] = dot(whole, qv, 0, 0) * scale
    for k in range(4):
        SbSt[k, :, 0:C] = dq[k]
        SbSt[k, :, C : 2 * C] = dk[k]
        SbSt[k, :, 2 * C : 3 * C] = dv[k]
    Sb[own, 0 : 3 * C] = SbSt[0, :, 0 : 3 * C]
    sb_to_tensor("qkv", qkv_cols)
    set_off(("b", 1))

    @pl.when(first)
    def _():
        from_tensor("gates", Sb, gate_cols)
        set_off("gates")
        hop(1, ("b", 3), ("b", 2))
    grad = dot(jnp.concatenate(dq, 1), Wqkv[0], 1, 1)
    grad += dot(jnp.concatenate(dk, 1), Wqkv[1], 1, 1)
    grad += dot(jnp.concatenate(dv, 1), Wqkv[2], 1, 1)
    g = g + norm_back(1, grad)

    @pl.when(second)
    def _():
        IG[pl.ds(trow, T)] = feed_back(0, 0, g).astype(bf16)
        start("back", back_rows, lambda: ARR, partner, second)

    @pl.when(first)
    def _():
        Ball[own, 0:width] = (0.5 * g).astype(bf16)
        to_tensor(("b", 0), Ball, block(0))
        G[...] = g

    set_off(("b", 0))
    PAb[...] = PAst[...].astype(bf16)
    for k in (1, 2, 3):
        start("pa", lambda k=k: PAb.at[:, cols(k)], lambda k=k: PAin.at[k], peers[k], None, k)


    @pl.when(second)
    def _():
        from_tensor("gates", Sb, gate_cols)
        set_off("gates")

    @pl.when(first)
    def _():
        shared("n", Nall, every)
        hidden_rows(1, 3)

    from_tensor("qkv", Sb, qkv_cols)
    set_off("qkv")

    @pl.when(first)
    def _():
        hidden_rows(0, 0)
        from_tensor(("b", 0), Ball, block(0))
        h = dot(Nall[four, 0:width], Win[0, 0])
        sig = jax.nn.sigmoid(h)
        hg = dot(Ball[four, 0:width], Wout[0, 0], 1, 1) * slope(h, sig)
        total = sum_to_owner("s2", 2, dot(hg.astype(bf16), Win[0, 0], 1, 1))
        hop(2, ("b", 3), ("b", 2))
        hop(1, "gates", ("b", 1))
        hand_on(1, ("b", 3), ("b", 2))
        g = G[...] + norm_back(0, summed_here("s2", 2, total))
        IG[pl.ds(trow, T)] = g.astype(bf16)

    PBin[t] = PBst[...].astype(bf16)
    for k in (1, 2, 3):
        start("pb", lambda: PBin.at[t], lambda: PBin.at[t], peers[k], None, k)
        start("grad", back_rows, back_rows, peers[k], None, k)
    PAin[0] = PAb[:, 0:C]
    all_arrived("pa", 3 * size_of(PAin.at[0]))
    PA[mine] = sum(PAin[k].astype(f32) for k in range(4)).astype(bf16)
    set_off("pa")

    @pl.when(second)
    def _():
        for n in (1, 2):
            hop(n, "n", "sf", ("b", 3), ("b", 2))
        hand_on(1, "n", ("b", 3), ("b", 2))
        hop(1, "gates", ("b", 1))
    hop(1, ("b", 0), "qkv")
    hop(3, ("b", 3), ("b", 2))
    hop(2, "gates", ("b", 1))
    all_arrived("pb", 3 * size_of(PBin.at[0]))
    PB[mine] = sum(PBin[k].astype(f32) for k in range(4)).astype(bf16)
    set_off("pb")
    hop(1, "pa")
    hand_on(1, ("b", 1), ("b", 0))
    hand_on(2, ("b", 3), ("b", 2))

    @pl.when(second)
    def _():
        hop(3, "n", "sf")
        hand_on(2, "n")
    hop(2, ("b", 0), "qkv")
    hop(3, "gates", ("b", 1))
    hop(1, "pb")
    hop(2, "pa")
    hand_on(2, ("b", 1), ("b", 0))
    hand_on(3, ("b", 3), ("b", 2))

    @pl.when(second)
    def _():
        hand_on(3, "n")
    hop(3, ("b", 0))

    @pl.when(second)
    def _():
        for i in range(4):
            from_tensor(("n", i), Nall, block(i))
        shared("n", Nall, every)
        hidden_rows(1, 3)
        hidden_rows(0, 0)

    write(Nall.at[:, block(0)], n0_out)
    write(ACT.at[0], act0_out)
    write(SLOPE.at[0], slope0_out)
    for i in (3, 2):
        from_tensor(("b", i), Ball, block(i))
        shared(("b", i), Ball, block(i))
    second_feed_grads()
    hand_on(3, ("b", 1), ("b", 0))
    hop(3, "qkv")
    hop(2, "pb")
    hop(3, "pa")
    convolution_grads()
    from_tensor(("b", 1), Ball, block(1))
    shared(("b", 1), Ball, block(1))
    attention_grads()
    hop(3, "pb")

    @pl.when(second)
    def _():
        from_tensor(("b", 0), Ball, block(0))

    shared(("b", 0), Ball, block(0))
    write(Ball.at[:, block(0)], b0_out)
    all_arrived("out", 3 * size_of(out_rows()))
    all_arrived("grad", 3 * size_of(back_rows()))
    for copy in written:
        copy.wait()
    for cond, sizes in sent.values():

        def all_sent():
            view = room(sum(sizes.values()))
            copy_of("out", view, view, partner, cond).wait_send()

        all_sent() if cond is None else pl.when(cond)(all_sent)
    assert len(recv_index) <= rs.shape[0] and len(send_index) <= ss.shape[0]


def last_kernel(*refs):
    given, outs, held, made, in_sems, out_sems = refs[:16], refs[16:30], refs[30:46], refs[46:57], refs[57], refs[58]
    lo, ig, pa, pb, n0, b0, act0, slope0, fout, table, in1, out1, qkv, ao, ci, co = held
    LO, IG, ng, nb, w_in, w_out, w_rel, pos, w_dw, bng, bns = made
    copies = []

    def send(src, dst):
        copy = pltpu.make_async_copy(src, dst, out_sems.at[len(copies)])
        copy.start()
        copies.append(copy)

    given = [m.at[0] if i == 8 else m for i, m in enumerate(given)]
    loads = [pltpu.make_async_copy(given[i], held[i], in_sems.at[i]) for i in range(len(held))]
    for i in (5, 8, 7, 4, 6, 10, 11, 12, 14, 13, 15, 2, 3, 0, 1, 9):
        loads[i].start()
    for i in (5, 8, 7, 4):
        loads[i].wait()
    hidden = (dot(b0[...], fout[...], 1, 1) * slope0[...]).astype(bf16)
    w_in[...] = dot(n0[...], hidden, 0, 0)
    send(w_in, outs[4].at[0])
    loads[6].wait()
    w_out[...] = dot(act0[...], b0[...], 0, 0)
    send(w_out, outs[5].at[0])
    for i, dst in (
        (10, outs[4].at[1]), (11, outs[5].at[1]), (12, outs[6].at[pl.ds(0, 3)]), (14, outs[9]), (13, outs[8]),
        (15, outs[13]),
    ):
        loads[i].wait()
        send(held[i], dst)
    for i in (2, 3, 0, 1, 9):
        loads[i].wait()
    sums, norms = pa[0].astype(f32), pb[0].astype(f32)
    for g in range(1, pa.shape[0]):
        sums += pa[g].astype(f32)
        norms += pb[g].astype(f32)
    w_rel[...] = dot(table[...], sums[SMALL_ROWS:].astype(bf16), 0, 0)
    send(w_rel, outs[6].at[3])
    LO[...] = lo[...].astype(f32)
    IG[...] = ig[...].astype(f32)
    for i in range(5):
        ng[i] = norms[i : i + 1]
        nb[i] = norms[8 + i : 9 + i]
    pos[...] = sums[0:2]
    bng[...] = sums[2:3]
    bns[...] = sums[3:4]
    for k in range(w_dw.shape[0]):
        w_dw[k] = sums[4 + k : 5 + k]
    for i, src in ((0, LO), (1, IG), (2, ng), (3, nb), (7, pos), (10, w_dw), (11, bng), (12, bns)):
        send(src, outs[i])
    for copy in copies:
        copy.wait()


def on_device(
    inputs, lengths, cotangent, norm_gain, norm_bias, ffn_in, ffn_out, attn_in, pos_bias, attn_out,
    conv_in, depthwise, bn_gain, bn_shift, conv_out,
):
    dp = lax.axis_size(DATA)
    group, frames, width = inputs.shape
    C = width // 4
    taps = depthwise.shape[1]
    groups = dp if dp <= 4 else 1
    R = groups * group * frames
    table = position_rows(frames, width)
    vm = pl.BlockSpec(memory_space=pltpu.VMEM)
    hbm = pl.BlockSpec(memory_space=pltpu.HBM)
    sums_rows = SMALL_ROWS + 2 * frames

    def shape(dims, dtype=bf16):
        return jax.ShapeDtypeStruct(dims, dtype)

    made_first = [
        shape((width, width), f32), shape((width, width), f32), shape((3, width, C), f32), shape((C, width), f32),
        shape((2 * width, C), f32), shape((C, width), f32),
    ]
    n_recv = 73 + 15 * (groups - 1)
    n_send = 3 + 2 * (groups - 1) + 2 * max(groups - 2, 0)
    operands = (
        lengths, inputs, cotangent, norm_gain.transpose(1, 0, 2), norm_bias.transpose(1, 0, 2), ffn_in[0],
        ffn_out[0], attn_in[0], attn_out[0], conv_in.reshape(2 * width, C), conv_out[0], pos_bias[0], bn_gain,
        bn_shift, depthwise.transpose(1, 0, 2), table,
    )
    lo, ig, pa, pb, n0, b0, act0, slope0, *ready = pl.pallas_call(
        lambda *refs: layer_kernel((frames, width, dp, groups), *refs),
        out_shape=[
            shape((group * frames, width)), shape((group * frames, width)),
            shape((groups, sums_rows, C)), shape((groups, 16, width)),
            shape((R, width)), shape((R, width)), shape((R, width)), shape((R, width), f32),
        ]
        + made_first,
        in_specs=[hbm] * 16,
        out_specs=[vm] * 4 + [hbm] * 10,
        scratch_shapes=[
            pltpu.VMEM((2, 4, width, width), bf16),
            pltpu.VMEM((2, 4, width, width), bf16),
            pltpu.VMEM((3, width, width), bf16),
            pltpu.VMEM((width, C), bf16),
            pltpu.VMEM((width, width), bf16),
            pltpu.VMEM((2, width, width), bf16),
            pltpu.VMEM((width, width), bf16),
            pltpu.VMEM((4 * frames, width), bf16),
            pltpu.VMEM((SMALL_ROWS, width), f32),
            pltpu.VMEM((2, 4, frames, width), f32),
            pltpu.VMEM((5, frames, width), f32),
            pltpu.VMEM((5, frames, 128), f32),
            pltpu.VMEM((5, frames, width), f32),
            pltpu.VMEM((frames, width), f32),
            pltpu.VMEM((frames, width), bf16),
            pltpu.VMEM((frames, width), bf16),
            pltpu.VMEM((4, frames, width), f32),
            pltpu.VMEM((4, 2 * frames, frames), f32),
            pltpu.VMEM((2, frames, width), f32),
            pltpu.VMEM((frames, width), f32),
            pltpu.VMEM((frames + 32, width), f32),
            pltpu.VMEM((frames + 32, width), f32),
            pltpu.VMEM((4, frames, 2 * C), bf16),
            pltpu.VMEM((4, frames, 5 * C), bf16),
            pltpu.VMEM((sums_rows, width), f32),
            pltpu.VMEM((sums_rows, width), bf16),
            pltpu.VMEM((4, sums_rows, C), bf16),
            pltpu.VMEM((16, width), f32),
            pltpu.VMEM((4, 16, width), bf16),
            pltpu.VMEM((dp, 8, width), f32),
            pltpu.VMEM((dp, 8, width), f32),
            pltpu.VMEM((3, 3, frames, width), bf16),
            pltpu.VMEM((3, 3, frames, width), bf16),
            pltpu.VMEM((5, 1, width), f32),
            pltpu.VMEM((5, 1, width), f32),
            pltpu.VMEM((2, C), f32),
            pltpu.VMEM((1, C), f32),
            pltpu.VMEM((1, C), f32),
            pltpu.VMEM((taps, 1, C), f32),
            pltpu.VMEM((4 * frames, width), bf16),
            pltpu.SMEM((group,), jnp.int32),
            pltpu.VMEM((2 * width, C), bf16),
            pltpu.VMEM((2 * width, C), f32),
            pltpu.VMEM((R, 4 * width), bf16),
            pltpu.VMEM((R, 4 * width), bf16),
            pltpu.VMEM((R, 2 * C), bf16),
            pltpu.VMEM((R, 5 * C), bf16),
            pltpu.VMEM((2, R, width), bf16),
            pltpu.VMEM((2, R, width), f32),
            pltpu.VMEM((R, width), bf16),
        ]
        + [pltpu.VMEM(m.shape, m.dtype) for m in made_first]
        + [
            pltpu.VMEM((2**23 // 512, 128), f32),
            pltpu.SemaphoreType.DMA((n_send,)),
            pltpu.SemaphoreType.DMA((n_recv,)),
            pltpu.SemaphoreType.DMA((21,)),
            pltpu.SemaphoreType.DMA((10,)),
        ],
        compiler_params=pltpu.CompilerParams(
            collective_id=0, has_side_effects=True, vmem_limit_bytes=62 * 2**20
        ),
    )(*operands)

    gradients = [
        shape((group * frames, width), f32), shape((group * frames, width), f32), shape((5, 1, width), f32),
        shape((5, 1, width), f32), shape((2, width, width), f32), shape((2, width, width), f32),
        shape((4, width, C), f32), shape((2, C), f32), shape((C, width), f32), shape((2 * width, C), f32),
        shape((taps, 1, C), f32), shape((1, C), f32), shape((1, C), f32), shape((C, width), f32),
    ]
    given = (lo, ig, pa, pb, n0, b0, act0, slope0, ffn_out[0], table[2 * frames :], *ready)
    held = list(given)
    held[8] = shape((width, width))
    made = [m for i, m in enumerate(gradients) if i not in (8, 9, 13)]
    made[4] = made[5] = shape((width, width), f32)
    made[6] = shape((width, C), f32)
    outs = pl.pallas_call(
        last_kernel,
        out_shape=gradients,
        in_specs=[hbm] * 16,
        out_specs=[hbm] * len(gradients),
        scratch_shapes=[pltpu.VMEM(m.shape, m.dtype) for m in held]
        + [pltpu.VMEM(m.shape, m.dtype) for m in made]
        + [pltpu.SemaphoreType.DMA((len(given),)), pltpu.SemaphoreType.DMA((len(gradients) + 4,))],
        compiler_params=pltpu.CompilerParams(vmem_limit_bytes=62 * 2**20),
    )(*given)
    if groups == 1:
        outs = list(outs[:2]) + [lax.psum(m.astype(bf16), DATA).astype(f32) for m in outs[2:]]
    (lo, ig, ng, nb, w_in, w_out, w_ain, pos, w_aout, w_cin, w_dw, bng, bns, w_cout) = outs
    rows = (1, group, frames, width)
    return (
        lo.reshape(rows), ig.reshape(rows), ng.transpose(1, 0, 2), nb.transpose(1, 0, 2), w_in[None], w_out[None],
        w_ain[None], pos[None], w_aout[None], w_cin.reshape(conv_in.shape), w_dw.transpose(1, 0, 2), bng, bns,
        w_cout[None],
    )


def solution(mesh):
    placed = (
        P(DATA, None, None),
        P(DATA),
        P(DATA, None, None),
        P(SECTION, None, None),
        P(SECTION, None, None),
        P(SECTION, None, None, TENSOR),
        P(SECTION, None, TENSOR, None),
        P(SECTION, None, None, TENSOR),
        P(SECTION, None, TENSOR),
        P(SECTION, TENSOR, None),
        P(SECTION, None, None, TENSOR),
        P(SECTION, None, TENSOR),
        P(SECTION, TENSOR),
        P(SECTION, TENSOR),
        P(SECTION, TENSOR, None),
    )
    return jax.shard_map(
        on_device,
        mesh=mesh,
        in_specs=placed,
        out_specs=(
            P(SECTION, DATA, None, None),
            P(SECTION, DATA, None, None),
            P(SECTION, None, None),
            P(SECTION, None, None),
            P(SECTION, None, None, TENSOR),
            P(SECTION, None, TENSOR, None),
            P(SECTION, None, None, TENSOR),
            P(SECTION, None, TENSOR),
            P(SECTION, TENSOR, None),
            P(SECTION, None, None, TENSOR),
            P(SECTION, None, TENSOR),
            P(SECTION, TENSOR),
            P(SECTION, TENSOR),
            P(SECTION, TENSOR, None),
        ),
        check_vma=False,
    )
```

```python
import math

import jax
import jax.numpy as jnp
import numpy as np
from jax import lax
from jax.experimental import pallas as pl
from jax.experimental.pallas import tpu as pltpu
from jax.sharding import PartitionSpec as P

HEAD = 64
EPSILON = 1e-05
MESH = pl.DeviceIdType.MESH
SECTION, TENSOR, DATA = "section", "tensor", "dp"
PLACE = (0, 2, 1, 3)
SMALL_ROWS = 48


def relative_at(groups):
    return 16 if groups > 1 else SMALL_ROWS


bf16, f32 = jnp.bfloat16, jnp.float32


def dot(left, right, left_dim=1, right_dim=0):
    return lax.dot_general(
        left, right, (((left_dim,), (right_dim,)), ((), ())), preferred_element_type=f32
    )


def position_rows(frames, width):
    offset = np.arange(2 * frames - 1, dtype=np.float32) - np.float32(frames - 1)
    rates = np.exp(
        np.arange(width // 2, dtype=np.float32) * np.float32(-2.0 * math.log(10000.0) / width)
    )
    angles = (offset[:, None] * rates[None, :]).astype(np.float32)
    table = np.stack([np.sin(angles), np.cos(angles)], -1).reshape(2 * frames - 1, width)
    blank = np.zeros((1, width), np.float32)
    return jnp.asarray(np.concatenate([table[::-1], blank, table, blank]), bf16)


def layer_kernel(dims, *refs):
    T, width, dp, groups = dims
    C = width // 4
    (lengths, inputs, cot, ng_in, nb_in, fin, fout, ain, aout, cin, cout, pos_in, bng_in, bns_in, dw_in, e2_in) = refs[:16]
    (LO, IG, PA, PB, CS, n0_out, b0_out, act0_out, slope0_out) = refs[16:25]
    (in1_out, out1_out, qkv_out, ao_out, ci_out, co_out) = refs[25:31]
    refs = refs[31:]
    (Win, Wout, Wqkv, Wr, Wo, Wci, Wco, R2, SM) = refs[:9]
    (H, XH, RS, X, G, ARR, HOP, QKV, PRB, GVG, CT, UP, DP) = refs[9:22]
    (SfSt, SbSt, PAst, PAb, PAin, PBst, PBin, STF, STB, RSst, RSin) = refs[22:33]
    (ng, nb, pos, bng, bns, dw, e2, lens, pairs, spread) = refs[33:43]
    (Nall, Ball, Sf, Sb, ACT, SLOPE, HG, gin1, gout1, gqkv, gao, gci, gco) = refs[43:56]
    GA, HATA, UA, DYA, DA, DWACC, INVA = refs[56:63]
    dummy, ss, rs, ls, os = refs[63:68]
    gathered = groups > 1

    s, t, d = lax.axis_index(SECTION), lax.axis_index(TENSOR), lax.axis_index(DATA)
    first, second = s == 0, s == 1
    taps = dw.shape[0]
    peers = [(s, t ^ k, d) for k in range(4)]
    sib, yp = peers[1], peers[2]
    around = {j: lax.rem(d + j + dp, dp) for j in range(1 - dp, dp)}
    zpeers = [(s, t, around[r]) for r in range(dp)]
    zpair = (s, t, d ^ 1)
    partner = (1 - s, t, d)
    half = lax.rem(d, 2)
    R4 = 4 * T
    reach = range(1 - groups, groups)
    base_of = {j: pl.multiple_of(around[j] * R4, R4) if groups > 1 else 0 for j in reach}
    second_of, high_of, last_of = (
        {j: pl.multiple_of(around[j] * R4 + n * T, T) if groups > 1 else n * T for j in reach} for n in (1, 2, 3)
    )
    there = {j: d + j >= 0 if j < 0 else d + j <= dp - 1 for j in reach}
    through = {
        (j, to): there[j] & there[to] for j in reach for to in (1, -1) if j * to < 0 and groups > 1
    }
    base = base_of[0]
    trow = pl.multiple_of(t * T, T)
    mine = d if groups > 1 else 0

    recv_index, send_index, sent = {}, {}, {}

    def size_of(view):
        return math.prod(view.shape) * view.dtype.itemsize

    def copy_of(key, src, dst, dev, group):
        i = recv_index.setdefault(key, len(recv_index))
        j = send_index.setdefault(id(group), len(send_index))
        return pltpu.make_async_remote_copy(
            src_ref=src, dst_ref=dst, send_sem=ss.at[j], recv_sem=rs.at[i], device_id=dev, device_id_type=MESH,
        )

    def start(key, src, dst, dev, cond=None, part=0):
        view = src()
        copy_of(key, view, dst(), dev, cond).start()
        sent.setdefault(id(cond), (cond, {}))[1][key, part] = size_of(view)

    def arrived(key, dst):
        copy_of(key, dst, dst, partner, None).wait_recv()

    def room(size):
        return dummy.at[pl.ds(0, size // (4 * dummy.shape[1]))]

    def all_arrived(key, size):
        if size:
            arrived(key, room(size))

    locals_ = {}

    def fetch(name, src, dst):
        locals_[name] = lambda: pltpu.make_async_copy(src(), dst(), ls.at[list(locals_).index(name)])
        locals_[name]().start()

    def fetched(*names):
        for name in names:
            locals_[name]().wait()

    @pl.when(first)
    def _():
        pltpu.make_async_copy(inputs.at[t], X.at[0], ls.at[20]).start()

    @pl.when(second)
    def _():
        pltpu.make_async_copy(cot.at[t], G, ls.at[20]).start()

    fetch("ng", lambda: ng_in, lambda: ng)
    fetch("nb", lambda: nb_in, lambda: nb)
    fetch("in0", lambda: fin.at[0], lambda: Win.at[0, 0])
    fetch("out0", lambda: fout.at[0], lambda: Wout.at[0, 0])
    fetch("wr", lambda: ain.at[3], lambda: Wr)
    fetch("e2", lambda: e2_in, lambda: e2)
    fetch("pos", lambda: pos_in, lambda: pos)
    fetch("bng", lambda: bng_in, lambda: bng)
    fetch("bns", lambda: bns_in, lambda: bns)
    fetch("dw", lambda: dw_in, lambda: dw)
    fetch("len", lambda: lengths, lambda: lens)
    fetch("qkv", lambda: ain.at[pl.ds(0, 3)], lambda: Wqkv.at[:, :, pl.ds(0, C)])
    fetch("o", lambda: aout, lambda: Wo.at[pl.ds(0, C)])
    fetch("ci", lambda: cin, lambda: pairs)
    fetch("co", lambda: cout, lambda: Wco.at[pl.ds(0, C)])
    fetch("in1", lambda: fin.at[1], lambda: Win.at[1, 0])
    fetch("out1", lambda: fout.at[1], lambda: Wout.at[1, 0])

    barrier = pltpu.get_barrier_semaphore()
    greet = peers[1:] + zpeers[1:] + [partner]
    for dev in greet:
        pl.semaphore_signal(barrier, inc=1, device_id=dev, device_id_type=MESH)
    pl.semaphore_wait(barrier, len(greet))

    starts = {}

    def lines(first_row, n, which):
        if which is None:
            return pl.ds(first_row, n)
        at = (first_row, n, which)
        if at not in starts:
            starts[at] = pl.multiple_of(first_row + n // 2 * (half if which == "own" else 1 - half), n // 2)
        return pl.ds(starts[at], n // 2)

    def cols(k):
        return pl.ds(C * k, C)

    def feed_chunks(j):
        Q = width // 2
        return [
            (
                lambda w, src=src, q=q: src.at[j, lines(Q * q, Q, w)],
                lambda k, w, dst=dst, q=q: dst.at[j, k, lines(Q * q, Q, w)],
            )
            for src, dst in ((fin, Win), (fout, Wout))
            for q in range(2)
        ]

    def row_chunk(src, dst):
        return [(lambda w: src.at[lines(0, C, w)], lambda k, w: dst.at[lines(C * k, C, w)])]

    def column_chunks(src, dst, n):
        return [
            (lambda w, i=i: src(i, lines(0, width, w)), lambda k, w, i=i: dst.at[i, lines(0, width, w), cols(k)])
            for i in range(n)
        ]

    chunks = (
        feed_chunks(0)
        + column_chunks(lambda i, rows: ain.at[i, rows], Wqkv, 3)
        + row_chunk(aout, Wo)
        + column_chunks(lambda i, rows: Wci.at[i, rows, cols(0)], Wci, 2)
        + row_chunk(cout, Wco)
        + feed_chunks(1)
    )
    for n, at in ((width // 2, 0), (width // 2, width // 2), (width, 0)) + tuple((C, C * k) for k in range(4)):
        for w in ("own", "other"):
            lines(at, n, w)
    only = {i: second for i in range(4)}
    over_y = {i: "own" for i in range(14)}

    def send_chunks(names):
        for i in names:
            src, dst = chunks[i]
            start(("sib", i), lambda src=src: src(None), lambda dst=dst: dst(1, None), sib, only.get(i))
            w = over_y.get(i)
            start(("y", i), lambda src=src, w=w: src(w), lambda dst=dst, w=w: dst(2, w), yp, only.get(i))

    def step_a(i):
        dst, w = chunks[i][1], over_y.get(i)
        arrived(("y", i), dst(2, w))
        if w:
            start(("z", i), lambda: dst(2, w), lambda: dst(2, w), zpair, only.get(i))
        start(("sib", i), lambda: dst(2, w), lambda: dst(3, w), sib, only.get(i), 1)

    def step_b(i):
        dst = chunks[i][1]
        arrived(("z", i), dst(2, "other"))
        start(("sib", i), lambda: dst(2, "other"), lambda: dst(3, "other"), sib, only.get(i), 2)

    def step_c(i):
        all_arrived(("sib", i), 2 * size_of(chunks[i][1](1, None)))

    def steps(cond, *plan):
        @pl.when(cond)
        def _():
            for step, i in plan:
                step(i)

    A, B, W = step_a, step_b, step_c

    def norm(i, x):
        centre = x - jnp.mean(x, -1, keepdims=True)
        rate = lax.rsqrt(jnp.mean(centre * centre, -1, keepdims=True) + EPSILON)
        hat = centre * rate
        XH[i] = hat
        RS[i] = jnp.broadcast_to(rate, RS.shape[1:])
        return hat * ng[i] + nb[i]

    def norm_back(i, grad):
        hat = XH[i]
        PBst[i : i + 1] = jnp.sum(grad * hat, 0, keepdims=True)
        PBst[8 + i : 9 + i] = jnp.sum(grad, 0, keepdims=True)
        g = grad * ng[i]
        return RS[i][:, 0:1] * (
            g - jnp.mean(g, -1, keepdims=True) - hat * jnp.mean(g * hat, -1, keepdims=True)
        )

    def silu(h):
        return h * jax.nn.sigmoid(h)

    def place(k):
        return pl.ds(base + T * PLACE[k], T)

    own, four = pl.ds(base, T), pl.ds(base, R4)

    def block(i, n=1):
        return pl.ds(i * width, n * width)

    def to_tensor(name, ref, c):
        for k in (1, 2, 3):
            start(name, lambda: ref.at[own, c], lambda k=k: ref.at[place(k), c], peers[k], None, k)

    def from_tensor(name, ref, c):
        all_arrived(name, 3 * size_of(ref.at[own, c]))

    def feed(j, i, before, after):
        x = X[before]
        a = norm(i, x).astype(bf16)
        Nall[own, i * width : (i + 1) * width] = a
        to_tensor(("n", i), Nall, block(i))
        active = []
        for k in range(4):
            h = dot(a, Win[j, k])
            H[j, k] = h
            active.append(silu(h).astype(bf16))
        total = dot(active[0], Wout[j, 0])
        for k in range(1, 4):
            total += dot(active[k], Wout[j, k])
        X[after] = x + 0.5 * total

    def sum_to_owner(name, slot, total):
        for k in (1, 2, 3):
            RSst[slot, k - 1] = total[T * PLACE[k] : T * (PLACE[k] + 1)].astype(bf16)
        for k in (1, 2, 3):
            start(name, lambda k=k: RSst.at[slot, k - 1], lambda k=k: RSin.at[slot, k - 1], peers[k], first, k)
        return total[0:T]

    def summed_here(name, slot, total):
        all_arrived(name, size_of(RSin.at[slot]))
        for k in (1, 2, 3):
            total += RSin[slot, k - 1].astype(f32)
        return total

    def shared_feed(j, i):
        from_tensor(("n", i), Nall, block(i))
        active = silu(dot(Nall[four, i * width : (i + 1) * width], Win[j, 0])).astype(bf16)
        return sum_to_owner(("s", j), j, dot(active, Wout[j, 0]))

    fetched("ng", "nb")

    @pl.when(first)
    def _():
        pltpu.make_async_copy(inputs.at[t], X.at[0], ls.at[20]).wait()
        Nall[own, 0:width] = norm(0, X[0]).astype(bf16)
        to_tensor(("n", 0), Nall, block(0))

    @pl.when(second)
    def _():
        send_chunks(range(4))
        pltpu.make_async_copy(cot.at[t], G, ls.at[20]).wait()

    fetched("pos", "bng", "bns", "dw", "wr", "e2", "len", "ci")
    spread[...] = pairs[...].astype(f32)
    for i in range(2):
        Wci[i, :, 0:C] = spread[pl.ds(i, width, stride=2), :].astype(bf16)
    SM[:, 0:C] = jnp.zeros((SMALL_ROWS, C), f32)
    SM[0:2, 0:C] = pos[...]
    SM[2:3, 0:C] = bng[...]
    SM[3:4, 0:C] = bns[...]
    for k in range(taps):
        SM[4 + k : 5 + k, 0:C] = dw[k]
    R2[:, 0:C] = dot(e2[...], Wr[...]).astype(bf16)
    fetched("in0", "out0")

    @pl.when(first)
    def _():
        send_chunks((8,))
        X[1] = shared_feed(0, 0)
        send_chunks((9, 10))

    for k in (1, 2, 3):
        start("small", lambda: SM.at[:, cols(0)], lambda k=k: SM.at[:, cols(k)], peers[k], None, k)

    def send_relative():
        for k in (1, 2, 3):
            start("rel", lambda: R2.at[:, cols(0)], lambda k=k: R2.at[:, cols(k)], peers[k], None, k)

    @pl.when(first)
    def _():
        step_a(8)
        X[1] = X[0] + 0.5 * summed_here(("s", 0), 0, X[1])

    @pl.when(second)
    def _():
        send_relative()
        send_chunks(range(4, 15))

    fetched("qkv", "o", "co", "in1", "out1")
    margin = 16
    UP[...] = jnp.zeros(UP.shape, f32)
    DP[...] = jnp.zeros(DP.shape, f32)
    PAst[...] = jnp.zeros(PAst.shape, f32)
    PBst[...] = jnp.zeros(PBst.shape, f32)
    CS[...] = jnp.zeros(CS.shape, f32)
    if gathered:
        DA[...] = jnp.zeros(DA.shape, f32)
        DWACC[...] = jnp.zeros(DWACC.shape, f32)

    def keys_of(length):
        return lax.broadcasted_iota(jnp.int32, (2 * T, T), 1) < length

    row_mask = (lax.broadcasted_iota(jnp.int32, (T, 1), 0) < lens[t]).astype(f32)
    first_head = lax.broadcasted_iota(jnp.int32, (T, 2 * HEAD), 1) < HEAD
    flip = (
        lax.broadcasted_iota(jnp.int32, (T, 4 * T), 0) + lax.broadcasted_iota(jnp.int32, (T, 4 * T), 1)
        == T - 1
    ).astype(f32).astype(bf16)

    def pair_rows(v):
        return jnp.concatenate([jnp.where(first_head, v, 0.0), jnp.where(first_head, 0.0, v)], 0)

    def unpair(v):
        return jnp.where(first_head, v[:T], v[T:])

    def attend(qu, qv, key, value, relative, keys):
        content = dot(pair_rows(qu).astype(bf16), key, 1, 1)
        whole = dot(pair_rows(qv).astype(bf16), relative, 1, 1)
        placed = jnp.concatenate(
            [
                pltpu.roll(whole[e * T : (e + 1) * T], 4 * T - (T - 1), 1, stride=1, stride_axis=0)[:, :T]
                for e in range(2)
            ],
            0,
        )
        scores = jnp.where(keys, (content + placed) * HEAD ** (-0.5), -1e30)
        e = jnp.exp(scores - jnp.max(scores, -1, keepdims=True))
        probs = e / jnp.sum(e, -1, keepdims=True)
        return probs, unpair(dot(probs.astype(bf16), value)).astype(bf16)

    def attention_here():
        a = Nall[own, width : 2 * width]
        q = dot(a, Wqkv[0])
        QKV[0] = q + SM[0:1]
        QKV[1] = q + SM[1:2]
        QKV[2] = dot(a, Wqkv[1])
        QKV[3] = dot(a, Wqkv[2])
        keys, mixed = keys_of(lens[t]), []
        for p in range(4):
            c = pl.ds(2 * HEAD * p, 2 * HEAD)
            probs, out = attend(
                QKV[0, :, c], QKV[1, :, c], QKV[2, :, c].astype(bf16), QKV[3, :, c].astype(bf16), R2[:, c], keys
            )
            PRB[p] = probs
            mixed.append(out)
        return mixed

    def shared_attention():
        a = Nall[four, width : 2 * width]
        q, key, value = (dot(a, Wqkv[i, :, 0:C]) for i in range(3))
        qu, qv, key, value = q + SM[0:1, 0:C], q + SM[1:2, 0:C], key.astype(bf16), value.astype(bf16)
        mixed = []
        for p in range(4):
            rows = slice(T * p, T * (p + 1))
            keys = keys_of(lens[t ^ PLACE[p]])
            mixed.append(attend(qu[rows], qv[rows], key[rows], value[rows], R2[:, 0:C], keys)[1])
        mixed = jnp.concatenate(mixed, 0)
        Sf[four, 0:C] = mixed
        return sum_to_owner(("s", 3), 3, dot(mixed, Wo[0:C]))

    def small_arrived():
        all_arrived("small", 3 * size_of(SM.at[:, cols(0)]))

    def relative_arrived():
        all_arrived("rel", 3 * size_of(R2.at[:, cols(0)]))


    @pl.when(first)
    def _():
        Nall[own, width : 2 * width] = norm(1, X[1]).astype(bf16)
        to_tensor(("n", 1), Nall, block(1))
        send_chunks((4, 5))
        step_a(9)
        step_a(10)
        step_b(8)
        step_b(9)
        from_tensor(("n", 1), Nall, block(1))
        total = shared_attention()
        send_chunks((6,))
        send_relative()
        send_chunks((7,))
        step_b(10)
        X[2] = X[1] + summed_here(("s", 3), 3, total)
        small_arrived()

    @pl.when(second)
    def _():
        for i in range(13):
            step_a(i)
            if i > 1:
                step_b(i - 2)
        for i in range(7):
            step_c(i)
        small_arrived()
        relative_arrived()
        arrived("hop", ARR)
        X[0] = ARR[...].astype(f32)
        feed(0, 0, 0, 1)
        Nall[own, width : 2 * width] = norm(1, X[1]).astype(bf16)
        to_tensor(("n", 1), Nall, block(1))
        step_b(11)
        mixed = attention_here()
        step_a(13)
        step_b(12)
        for k in range(4):
            SfSt[k, :, 0:C] = mixed[k]
        step_c(7)
        X[2] = X[1] + dot(jnp.concatenate(mixed, 1), Wo[...])

    def send_rows_second(i):
        @pl.when(second)
        def _():
            to_tensor(("n", i), Nall, block(i))

    a = norm(2, X[2]).astype(bf16)
    Nall[own, 2 * width : 3 * width] = a
    send_rows_second(2)

    @pl.when(first)
    def _():
        send_chunks((11,))

    step_c(8)
    step_c(9)
    GVG[0] = dot(a, Wci[0])
    GVG[1] = dot(a, Wci[1])
    UP[margin : margin + T] = GVG[0] * jax.nn.sigmoid(GVG[1]) * row_mask
    for p in range(4):
        c = pl.ds(C * p, C)
        acc = SM[4:5, c] * UP[margin - taps // 2 : margin - taps // 2 + T, c]
        for k in range(1, taps):
            o = margin - taps // 2 + k
            acc += SM[4 + k : 5 + k, c] * UP[o : o + T, c]
        CT[:, c] = acc
    conv = CT[...]

    def dp_sums(name, ref, rows):
        n = len(rows)
        ref[d] = jnp.concatenate(rows + [jnp.zeros((8 - n, width), f32)], 0)
        for r in range(1, dp):
            start(name, lambda: ref.at[d], lambda: ref.at[d], zpeers[r], None, r)

    def summed(name, ref):
        all_arrived(name, (dp - 1) * size_of(ref.at[0]))
        total = ref[0]
        for r in range(1, dp):
            total += ref[r]
        return total

    def total_of(v):
        return jnp.sum(v, 0, keepdims=True)

    masked = conv * row_mask
    frames_row = jnp.broadcast_to(total_of(row_mask), (1, width))
    lengths_row = jnp.concatenate(
        [jnp.broadcast_to(lens[t ^ PLACE[p]].astype(f32), (1, C)) for p in range(4)], 1
    )
    dp_sums("bnf", STF, [total_of(masked), total_of(masked * conv), frames_row, lengths_row])
    steps(second, (A, 14))
    step_c(10)
    sums = summed("bnf", STF)
    steps(first, (A, 4), (A, 5), (A, 6))
    steps(second, (B, 13))
    count = sums[2:3]
    bn_mean = sums[0:1] / count
    inv_std = lax.rsqrt(sums[1:2] / count - bn_mean * bn_mean + EPSILON)
    hat = (conv - bn_mean) * inv_std
    CT[...] = hat
    active = silu(hat * SM[2:3] + SM[3:4]).astype(bf16)
    if not gathered:
        for k in range(4):
            SfSt[k, :, C : 2 * C] = active[:, C * k : C * (k + 1)]
    X[3] = X[2] + dot(active, Wco[...])

    @pl.when(first)
    def _():
        Nall[own, 3 * width : 4 * width] = norm(3, X[3]).astype(bf16)
        to_tensor(("n", 3), Nall, block(3))
        total = shared_feed(1, 3)
        send_chunks((12, 13, 14))
        step_a(7)
        step_a(11)
        step_b(4)
        X[4] = X[3] + 0.5 * summed_here(("s", 1), 1, total)

    @pl.when(second)
    def _():
        for i in range(11, 15):
            step_c(i)
        feed(1, 3, 3, 4)
    out = (norm(4, X[4]) * row_mask).astype(bf16)
    HOP[...] = out

    @pl.when(first)
    def _():
        start("hop", lambda: HOP, lambda: ARR, partner, first)

    LO[pl.ds(trow, T)] = out
    out_rows = lambda: LO.at[pl.ds(trow, T)]
    for k in (1, 2, 3):
        start("out", out_rows, out_rows, peers[k], None, k)

    def line_start(name, region):
        for way, to, back in (("up", 1, -1), ("down", -1, 1)):
            if groups > 1:

                @pl.when(there[to])
                def _():
                    start(
                        (name, 0, back % dp), lambda: region(0), lambda: region(0), (s, t, around[to]), there[to], way
                    )

    def line_hop(name, region, n, after=None):
        for way, to, back in (("up", 1, -1), ("down", -1, 1)):
            if n < groups:

                @pl.when(there[back * n])
                def _():
                    j = back * n
                    arrived((name, 0, j % dp), region(j))
                    if n + 1 < groups:

                        @pl.when(there[to])
                        def _():
                            start(
                                (name, 0, (j + back) % dp), lambda: region(j), lambda: region(j),
                                (s, t, around[to]), through[j, to], way,
                            )

                    if after is not None:
                        after(name, j)

    def rows_region(ref, n, c):
        return lambda j: ref.at[pl.ds(base_of[j], n), c]

    def share(ref, c):
        def go(name, j):
            rows = lambda: ref.at[pl.ds(base_of[j], T), c]
            start((name, 1, j % dp), rows, lambda: ref.at[pl.ds(second_of[j], T), c], yp, there[j], j)
            start((name, 2, 0), rows, lambda: ref.at[pl.ds(high_of[j], T), c], sib, there[j], j)

        return go

    def share_on(name, ref, c, n):
        for j in (n, -n):
            if n < groups:

                @pl.when(there[j])
                def _():
                    rows = lambda: ref.at[pl.ds(second_of[j], T), c]
                    arrived((name, 1, j % dp), rows())
                    start((name, 2, 0), rows, lambda: ref.at[pl.ds(last_of[j], T), c], sib, there[j], dp + j)

    def shared(name, ref, c):
        all_arrived((name, 2, 0), 2 * (groups - 1) * size_of(ref.at[own, c]))

    every = block(0, 4)
    sf_cols = pl.ds(0, C if gathered else 2 * C)
    qkv_cols, gate_cols = pl.ds(0, 3 * C), pl.ds(3 * C, 2 * C)
    lines_of = {
        "n": (rows_region(Nall, T, every), share(Nall, every)),
        "sf": (rows_region(Sf, R4, sf_cols), None),
        "qkv": (rows_region(Sb, R4, qkv_cols), None),
    }
    for i in range(4):
        lines_of["b", i] = (rows_region(Ball, T, block(i)), share(Ball, block(i)))

    def set_off(*names):
        for name in names:
            line_start(name, lines_of[name][0])

    def hop(n, *names):
        for name in names:
            line_hop(name, lines_of[name][0], n, lines_of[name][1])

    def hand_on(n, *names):
        for name in names:
            ref, c = (Nall, every) if name == "n" else (Ball, block(name[1]))
            share_on(name, ref, c, n)

    for cond, c in ((first, pl.ds(C, C)), (second, sf_cols))[gathered:]:

        @pl.when(cond)
        def _():
            Sf[own, c] = SfSt[0, :, c]
            for k in (1, 2, 3):
                start("sf", lambda k=k: SfSt.at[k, :, c], lambda k=k: Sf.at[place(k), c], peers[k], cond, k)

    written = []

    def write(src, dst):
        copy = pltpu.make_async_copy(src, dst, os.at[len(written)])
        copy.start()
        written.append(copy)

    R = Nall.shape[0]
    row_blocks = [slice(r, r + R4) for r in range(0, R, R4)]

    def slope(h, sig):
        return sig * (1.0 + h * (1.0 - sig))

    def hidden_rows(j, i):
        for rows in row_blocks:
            h = dot(Nall[rows, i * width : (i + 1) * width], Win[j, 0])
            sig = jax.nn.sigmoid(h)
            ACT[j, rows] = (h * sig).astype(bf16)
            SLOPE[j, rows] = slope(h, sig)

    def second_feed_grads():
        c = slice(3 * width, 4 * width)
        for rows in row_blocks:
            HG[rows] = (dot(Ball[rows, c], Wout[1, 0], 1, 1) * SLOPE[1, rows]).astype(bf16)
        gin1[...] = dot(Nall[:, c], HG[...], 0, 0)
        write(gin1, in1_out)
        gout1[...] = dot(ACT[1], Ball[:, c], 0, 0)
        write(gout1, out1_out)

    def mask_of(g, p):
        return (lax.broadcasted_iota(jnp.int32, (T, C), 0).astype(f32) < STF[g, 3:4, C * p : C * (p + 1)]).astype(f32)

    places = [(p, [(g, slice(R4 * g + T * p, R4 * g + T * (p + 1))) for g in range(groups)]) for p in range(4)]

    def convolution_rows():
        for i in range(2):
            GA[i] = dot(Nall[:, 2 * width : 3 * width], Wci[i, :, 0:C])
        UA[...] = jnp.zeros(UA.shape, f32)
        for p, parts in places:
            for g, rows in parts:
                UA[4 * g + p, margin : margin + T] = GA[0, rows] * jax.nn.sigmoid(GA[1, rows]) * mask_of(g, p)

        def one(b, carry):
            acc = SM[4:5, 0:C] * UA[b, margin - taps // 2 : margin - taps // 2 + T]
            for k in range(1, taps):
                o = margin - taps // 2 + k
                acc += SM[4 + k : 5 + k, 0:C] * UA[b, o : o + T]
            HATA[pl.ds(b * T, T)] = acc
            return carry

        lax.fori_loop(0, 4 * groups, one, 0)
        for p, parts in places:
            n = sum(STF[g, 3:4, C * p : C * (p + 1)] for g, _ in parts)
            masked = [HATA[rows] * mask_of(g, p) for g, rows in parts]
            mean = sum(total_of(m) for m in masked) / n
            square = sum(total_of(m * HATA[rows]) for m, (_, rows) in zip(masked, parts)) / n
            inv = lax.rsqrt(square - mean * mean + EPSILON)
            INVA[p, 0:1] = inv
            INVA[p, 1:2] = n
            for g, rows in parts:
                h = (HATA[rows] - mean) * inv
                HATA[rows] = h
                Sf[rows, C : 2 * C] = silu(h * SM[2:3, 0:C] + SM[3:4, 0:C]).astype(bf16)

    def convolution_rows_back():
        DYA[...] = dot(Ball[:, 2 * width : 3 * width], Wco[0:C], 1, 1)
        gain_sum = shift_sum = jnp.zeros((1, C), f32)
        for p, parts in places:
            first_sum = second_sum = jnp.zeros((1, C), f32)
            for g, rows in parts:
                h = HATA[rows]
                y = h * SM[2:3, 0:C] + SM[3:4, 0:C]
                dy = DYA[rows] * slope(y, jax.nn.sigmoid(y))
                gain_sum += total_of(dy * h)
                shift_sum += total_of(dy)
                dh = dy * SM[2:3, 0:C]
                DYA[rows] = dh
                dh = dh * mask_of(g, p)
                first_sum += total_of(dh)
                second_sum += total_of(dh * h)
            inv, n = INVA[p, 0:1], INVA[p, 1:2]
            for g, rows in parts:
                dc = inv * (DYA[rows] - (first_sum + HATA[rows] * second_sum) / n) * mask_of(g, p)
                DA[4 * g + p, margin : margin + T] = dc
        CS[taps : taps + 1] = gain_sum
        CS[taps + 1 : taps + 2] = shift_sum

        def one(b, carry):
            here = DA[b, margin : margin + T]
            acc = jnp.zeros((T, C), f32)
            for k in range(taps):
                o = margin + taps // 2 - k
                acc += SM[4 + k : 5 + k, 0:C] * DA[b, o : o + T]
                o = margin - taps // 2 + k
                term = here * UA[b, o : o + T]
                DWACC[k] += sum(term[8 * i : 8 * (i + 1)] for i in range(T // 8))
            DYA[pl.ds(b * T, T)] = acc
            return carry

        lax.fori_loop(0, 4 * groups, one, 0)
        for k in range(taps):
            CS[k : k + 1] = total_of(DWACC[k])
        for p, parts in places:
            for g, rows in parts:
                sig = jax.nn.sigmoid(GA[1, rows])
                dua = DYA[rows] * mask_of(g, p)
                Sb[rows, 3 * C : 4 * C] = (dua * sig).astype(bf16)
                Sb[rows, 4 * C : 5 * C] = (dua * GA[0, rows] * (sig * (1.0 - sig))).astype(bf16)

    def convolution_grads():
        gates = dot(Nall[:, 2 * width : 3 * width], Sb[:, 3 * C : 5 * C], 0, 0)
        for i in range(2):
            gci[pl.ds(i, width, stride=2), :] = gates[:, C * i : C * (i + 1)]
        write(gci, ci_out)
        gco[...] = dot(Sf[:, C : 2 * C], Ball[:, 2 * width : 3 * width], 0, 0)
        write(gco, co_out)

    def attention_grads():
        grads = dot(Nall[:, width : 2 * width], Sb[:, 0 : 3 * C], 0, 0)
        for i in range(3):
            gqkv[i] = grads[:, C * i : C * (i + 1)]
        write(gqkv, qkv_out)
        gao[...] = dot(Sf[:, 0:C], Ball[:, width : 2 * width], 0, 0)
        write(gao, ao_out)

    @pl.when(first)
    def _():
        set_off("n", "sf")
        to_tensor(("n", 2), Nall, block(2))
        for i in (5, 6, 7):
            step_b(i)
        step_a(12)
        step_b(11)
        for i in (4, 5, 6, 7):
            step_c(i)
        relative_arrived()
        attention_here()
        step_a(13)
        step_b(12)
        if not gathered:
            from_tensor("sf", Sf, pl.ds(C, C))
        step_a(14)
        hop(1, "n", "sf")
        step_b(13)
        for i in range(11, 15):
            step_c(i)
        for k in range(4):
            H[1, k] = dot(Nall[own, 3 * width : 4 * width], Win[1, k])
        hop(2, "n", "sf")
        hand_on(1, "n")
        hop(3, "n", "sf")
        hand_on(2, "n")

    @pl.when(first)
    def _():
        arrived("back", ARR)
        G[...] = ARR[...].astype(f32)

    back_rows = lambda: IG.at[pl.ds(trow, T)]

    def feed_back(j, i, g):
        b = (0.5 * g).astype(bf16)
        Ball[own, i * width : (i + 1) * width] = b
        to_tensor(("b", i), Ball, block(i))
        if j:
            set_off(("b", i))
        grad = None
        for k in range(4):
            h = H[j, k]
            sig = jax.nn.sigmoid(h)
            hg = (dot(b, Wout[j, k], 1, 1) * slope(h, sig)).astype(bf16)
            part = dot(hg, Win[j, k], 1, 1)
            grad = part if grad is None else grad + part
        return g + norm_back(i, grad)
    g = norm_back(4, G[...] * row_mask)
    g = feed_back(1, 3, g)
    b = g.astype(bf16)
    Ball[own, 2 * width : 3 * width] = b
    to_tensor(("b", 2), Ball, block(2))
    hat = CT[...]
    y = hat * SM[2:3] + SM[3:4]
    sig = jax.nn.sigmoid(y)
    dy = dot(b, Wco[...], 1, 1) * slope(y, sig)
    if not gathered:
        PAst[2:3] = total_of(dy * hat)
        PAst[3:4] = total_of(dy)
    dhat = dy * SM[2:3]
    masked = dhat * row_mask
    dp_sums("bnb", STB, [total_of(masked), total_of(masked * hat)])
    sums = summed("bnb", STB)

    @pl.when(second)
    def _():
        set_off("n")
        from_tensor("sf", Sf, sf_cols)
        set_off("sf")

    @pl.when(first)
    def _():
        hop(1, ("b", 3))
        hand_on(3, "n")

    set_off(("b", 2))
    dc = inv_std * (dhat - (sums[0:1] + hat * sums[1:2]) / count) * row_mask
    DP[margin : margin + T] = dc
    for p in range(4):
        c = pl.ds(C * p, C)
        here = DP[margin : margin + T, c]
        acc = None
        for k in range(taps):
            o = margin + taps // 2 - k
            term = SM[4 + k : 5 + k, c] * DP[o : o + T, c]
            acc = term if acc is None else acc + term
            if not gathered:
                o = margin - taps // 2 + k
                PAst[4 + k : 5 + k, c] = total_of(here * UP[o : o + T, c])
        CT[:, c] = acc
    du = CT[...] * row_mask
    sig = jax.nn.sigmoid(GVG[1])
    dvalue = (du * sig).astype(bf16)
    dgate = (du * GVG[0] * (sig * (1.0 - sig))).astype(bf16)
    def sb_to_tensor(name, c):
        for k in (1, 2, 3):
            start(name, lambda k=k: SbSt.at[k, :, c], lambda k=k: Sb.at[place(k), c], peers[k], None, k)

    if not gathered:
        for k in range(4):
            SbSt[k, :, 3 * C : 4 * C] = dvalue[:, C * k : C * (k + 1)]
            SbSt[k, :, 4 * C : 5 * C] = dgate[:, C * k : C * (k + 1)]
        Sb[own, 3 * C : 5 * C] = SbSt[0, :, 3 * C : 5 * C]
        sb_to_tensor("gates", gate_cols)
    g = g + norm_back(2, dot(dvalue, Wci[0], 1, 1) + dot(dgate, Wci[1], 1, 1))
    b = g.astype(bf16)
    Ball[own, width : 2 * width] = b
    to_tensor(("b", 1), Ball, block(1))
    dmix = dot(b, Wo[...], 1, 1).astype(bf16).astype(f32)
    scale = HEAD ** (-0.5)
    dq, dk, dv = [], [], []
    for p in range(4):
        c = pl.ds(2 * HEAD * p, 2 * HEAD)
        qu = pair_rows(QKV[0, :, c]).astype(bf16)
        qv = pair_rows(QKV[1, :, c]).astype(bf16)
        key = QKV[2, :, c].astype(bf16)
        val = QKV[3, :, c].astype(bf16)
        do = pair_rows(dmix[:, 2 * HEAD * p : 2 * HEAD * (p + 1)]).astype(bf16)
        probs = PRB[p]
        dprob = dot(do, val, 1, 1)
        ds = (probs * (dprob - jnp.sum(probs * dprob, -1, keepdims=True))).astype(bf16)
        du_rows = unpair(dot(ds, key)) * scale
        turned = dot(ds, flip)
        whole = jnp.concatenate(
            [
                pltpu.roll(turned[e * T : (e + 1) * T], 0, 1, stride=1, stride_axis=0)[:, : 2 * T]
                for e in range(2)
            ],
            0,
        ).astype(bf16)
        dv_rows = unpair(dot(whole, R2[2 * T : 4 * T, c])) * scale
        dk.append((dot(ds, qu, 0, 0) * scale).astype(bf16))
        dv.append(dot(probs.astype(bf16), do, 0, 0).astype(bf16))
        dq.append((du_rows + dv_rows).astype(bf16))
        PAst[0:1, c] = total_of(du_rows)
        PAst[1:2, c] = total_of(dv_rows)
        PAst[relative_at(groups) : relative_at(groups) + 2 * T, c] = dot(whole, qv, 0, 0) * scale
    for k in range(4):
        SbSt[k, :, 0:C] = dq[k]
        SbSt[k, :, C : 2 * C] = dk[k]
        SbSt[k, :, 2 * C : 3 * C] = dv[k]
    Sb[own, 0 : 3 * C] = SbSt[0, :, 0 : 3 * C]
    sb_to_tensor("qkv", qkv_cols)
    set_off(("b", 1))

    @pl.when(first)
    def _():
        if not gathered:
            from_tensor("gates", Sb, gate_cols)
        hop(2, ("b", 3))
        hop(1, ("b", 2))
    grad = dot(jnp.concatenate(dq, 1), Wqkv[0], 1, 1)
    grad += dot(jnp.concatenate(dk, 1), Wqkv[1], 1, 1)
    grad += dot(jnp.concatenate(dv, 1), Wqkv[2], 1, 1)
    g = g + norm_back(1, grad)

    @pl.when(second)
    def _():
        IG[pl.ds(trow, T)] = feed_back(0, 0, g).astype(bf16)
        start("back", back_rows, lambda: ARR, partner, second)

    @pl.when(first)
    def _():
        Ball[own, 0:width] = (0.5 * g).astype(bf16)
        to_tensor(("b", 0), Ball, block(0))
        G[...] = g

    set_off(("b", 0))
    PAb[...] = PAst[...].astype(bf16)
    for k in (1, 2, 3):
        start("pa", lambda k=k: PAb.at[:, cols(k)], lambda k=k: PAin.at[k], peers[k], None, k)

    def sums_over_tensor(name, parts, ref):
        all_arrived(name, 3 * size_of(parts.at[0]))
        ref[mine] = sum(parts[k].astype(f32) for k in range(4)).astype(bf16)
        for r in range(1, groups):
            start((name, 3), lambda: ref.at[mine], lambda: ref.at[mine], zpeers[r], None, r)

    def send_ends():
        PBin[t] = PBst[...].astype(bf16)
        for k in (1, 2, 3):
            start("pb", lambda: PBin.at[t], lambda: PBin.at[t], peers[k], None, k)
            start("grad", back_rows, back_rows, peers[k], None, k)

    bs = [("b", i) for i in range(4)]
    if not gathered:

        @pl.when(second)
        def _():
            from_tensor("gates", Sb, gate_cols)

    @pl.when(first)
    def _():
        from_tensor(("n", 2), Nall, block(2))
        shared("n", Nall, every)

    @pl.when(second)
    def _():
        send_ends()
        from_tensor("qkv", Sb, qkv_cols)
        set_off("qkv")
        hop(1, "n", "sf", bs[3], bs[2], bs[1], bs[0], "qkv")
        hop(2, "n", "sf")
        hand_on(1, "n")
        hop(2, bs[3], bs[2], bs[1], bs[0], "qkv")
        hand_on(1, bs[3], bs[2])
        hop(3, "n", "sf")
        hand_on(2, "n")
        hand_on(1, bs[1], bs[0])
        hop(3, bs[3], bs[2])
        hand_on(3, "n")
        hand_on(2, bs[3], bs[2], bs[1], bs[0])
        hop(3, bs[1], bs[0])
        for i in range(4):
            from_tensor(("n", i), Nall, block(i))
        shared("n", Nall, every)
    hidden_rows(1, 3)

    @pl.when(first)
    def _():
        from_tensor("qkv", Sb, qkv_cols)
        set_off("qkv")
        hop(2, bs[2])
        hop(3, bs[3])
        hop(1, bs[1])
        from_tensor(bs[0], Ball, block(0))
        h = dot(Nall[four, 0:width], Win[0, 0])
        sig = jax.nn.sigmoid(h)
        hg = dot(Ball[four, 0:width], Wout[0, 0], 1, 1) * slope(h, sig)
        X[0] = sum_to_owner(("s", 2), 2, dot(hg.astype(bf16), Win[0, 0], 1, 1))
        hop(1, bs[0])
        hand_on(1, bs[3], bs[2])
    hidden_rows(0, 0)
    write(Nall.at[:, block(0)], n0_out)
    write(ACT.at[0], act0_out)
    write(SLOPE.at[0], slope0_out)
    if gathered:
        convolution_rows()

    @pl.when(first)
    def _():
        hop(1, "qkv")
        hop(3, bs[2])
        hop(2, bs[1])
        g = G[...] + norm_back(0, summed_here(("s", 2), 2, X[0]))
        IG[pl.ds(trow, T)] = g.astype(bf16)
        send_ends()
        hop(2, bs[0])
        hand_on(1, bs[1], bs[0])
        hand_on(2, bs[3], bs[2])

    PAin[0] = PAb[:, 0:C]
    sums_over_tensor("pa", PAin, PA)
    hand_on(3, bs[3], bs[2])
    for i in (3, 2):
        from_tensor(bs[i], Ball, block(i))
        shared(bs[i], Ball, block(i))
    second_feed_grads()
    sums_over_tensor("pb", PBin, PB)

    @pl.when(first)
    def _():
        hop(2, "qkv")
        hop(3, bs[1], bs[0])
        hand_on(2, bs[1], bs[0])
    if gathered:
        convolution_rows_back()
    hop(3, "qkv")
    hand_on(3, bs[1], bs[0])
    convolution_grads()
    from_tensor(bs[1], Ball, block(1))
    shared(bs[1], Ball, block(1))
    attention_grads()

    @pl.when(second)
    def _():
        from_tensor(bs[0], Ball, block(0))

    shared(bs[0], Ball, block(0))
    write(Ball.at[:, block(0)], b0_out)
    for name, ref in (("pa", PA), ("pb", PB)):
        all_arrived((name, 3), (groups - 1) * size_of(ref.at[0]))
    all_arrived("out", 3 * size_of(out_rows()))
    all_arrived("grad", 3 * size_of(back_rows()))
    for copy in written:
        copy.wait()
    for cond, sizes in sent.values():

        def all_sent():
            view = room(sum(sizes.values()))
            copy_of("out", view, view, partner, cond).wait_send()

        all_sent() if cond is None else pl.when(cond)(all_sent)
    assert len(recv_index) <= rs.shape[0] and len(send_index) <= ss.shape[0]


def last_kernel(*refs):
    given, outs, held, made, in_sems, out_sems = refs[:17], refs[17:31], refs[31:48], refs[48:59], refs[59], refs[60]
    lo, ig, pa, pb, n0, b0, act0, slope0, fout, table, in1, out1, qkv, ao, ci, co, cs = held
    LO, IG, ng, nb, w_in, w_out, w_rel, pos, w_dw, bng, bns = made
    copies = []

    def send(src, dst):
        copy = pltpu.make_async_copy(src, dst, out_sems.at[len(copies)])
        copy.start()
        copies.append(copy)

    given = [m.at[0] if i == 8 else m for i, m in enumerate(given)]
    loads = [pltpu.make_async_copy(given[i], held[i], in_sems.at[i]) for i in range(len(held))]
    for i in (5, 8, 7, 4, 6, 10, 11, 12, 14, 13, 15, 2, 3, 0, 1, 9, 16):
        loads[i].start()
    for i in (5, 8, 7, 4):
        loads[i].wait()
    hidden = (dot(b0[...], fout[...], 1, 1) * slope0[...]).astype(bf16)
    w_in[...] = dot(n0[...], hidden, 0, 0)
    send(w_in, outs[4].at[0])
    loads[6].wait()
    w_out[...] = dot(act0[...], b0[...], 0, 0)
    send(w_out, outs[5].at[0])
    for i, dst in (
        (10, outs[4].at[1]), (11, outs[5].at[1]), (12, outs[6].at[pl.ds(0, 3)]), (14, outs[9]), (13, outs[8]),
        (15, outs[13]),
    ):
        loads[i].wait()
        send(held[i], dst)
    for i in (2, 3, 0, 1, 9, 16):
        loads[i].wait()
    sums, norms = pa[0].astype(f32), pb[0].astype(f32)
    for g in range(1, pa.shape[0]):
        sums += pa[g].astype(f32)
        norms += pb[g].astype(f32)
    w_rel[...] = dot(table[...], sums[relative_at(pa.shape[0]) :].astype(bf16), 0, 0)
    send(w_rel, outs[6].at[3])
    LO[...] = lo[...].astype(f32)
    IG[...] = ig[...].astype(f32)
    for i in range(5):
        ng[i] = norms[i : i + 1]
        nb[i] = norms[8 + i : 9 + i]
    pos[...] = sums[0:2]
    taps = w_dw.shape[0]
    if pa.shape[0] > 1:
        sums = jnp.concatenate([sums[0:2], cs[taps : taps + 2], cs[0:taps]], 0)
    bng[...] = sums[2:3]
    bns[...] = sums[3:4]
    for k in range(taps):
        w_dw[k] = sums[4 + k : 5 + k]
    for i, src in ((0, LO), (1, IG), (2, ng), (3, nb), (7, pos), (10, w_dw), (11, bng), (12, bns)):
        send(src, outs[i])
    for copy in copies:
        copy.wait()


def on_device(
    inputs, lengths, cotangent, norm_gain, norm_bias, ffn_in, ffn_out, attn_in, pos_bias, attn_out,
    conv_in, depthwise, bn_gain, bn_shift, conv_out,
):
    dp = lax.axis_size(DATA)
    group, frames, width = inputs.shape
    C = width // 4
    taps = depthwise.shape[1]
    groups = dp if dp <= 4 else 1
    R = groups * group * frames
    table = position_rows(frames, width)
    vm = pl.BlockSpec(memory_space=pltpu.VMEM)
    hbm = pl.BlockSpec(memory_space=pltpu.HBM)
    sums_rows = relative_at(groups) + 2 * frames

    def shape(dims, dtype=bf16):
        return jax.ShapeDtypeStruct(dims, dtype)

    made_first = [
        shape((width, width), f32), shape((width, width), f32), shape((3, width, C), f32), shape((C, width), f32),
        shape((2 * width, C), f32), shape((C, width), f32),
    ]
    n_recv = 75 + 15 * (groups - 1)
    n_send = 3 + 2 * (groups - 1) + 2 * max(groups - 2, 0)
    operands = (
        lengths, inputs, cotangent, norm_gain.transpose(1, 0, 2), norm_bias.transpose(1, 0, 2), ffn_in[0],
        ffn_out[0], attn_in[0], attn_out[0], conv_in.reshape(2 * width, C), conv_out[0], pos_bias[0], bn_gain,
        bn_shift, depthwise.transpose(1, 0, 2), table,
    )
    lo, ig, pa, pb, cs, n0, b0, act0, slope0, *ready = pl.pallas_call(
        lambda *refs: layer_kernel((frames, width, dp, groups), *refs),
        out_shape=[
            shape((group * frames, width)), shape((group * frames, width)),
            shape((groups, sums_rows, C)), shape((groups, 16, width)), shape((40, C), f32),
            shape((R, width)), shape((R, width)), shape((R, width)), shape((R, width), f32),
        ]
        + made_first,
        in_specs=[hbm] * 16,
        out_specs=[vm] * 5 + [hbm] * 10,
        scratch_shapes=[
            pltpu.VMEM((2, 4, width, width), bf16),
            pltpu.VMEM((2, 4, width, width), bf16),
            pltpu.VMEM((3, width, width), bf16),
            pltpu.VMEM((width, C), bf16),
            pltpu.VMEM((width, width), bf16),
            pltpu.VMEM((2, width, width), bf16),
            pltpu.VMEM((width, width), bf16),
            pltpu.VMEM((4 * frames, width), bf16),
            pltpu.VMEM((SMALL_ROWS, width), f32),
            pltpu.VMEM((2, 4, frames, width), f32),
            pltpu.VMEM((5, frames, width), f32),
            pltpu.VMEM((5, frames, 128), f32),
            pltpu.VMEM((5, frames, width), f32),
            pltpu.VMEM((frames, width), f32),
            pltpu.VMEM((frames, width), bf16),
            pltpu.VMEM((frames, width), bf16),
            pltpu.VMEM((4, frames, width), f32),
            pltpu.VMEM((4, 2 * frames, frames), f32),
            pltpu.VMEM((2, frames, width), f32),
            pltpu.VMEM((frames, width), f32),
            pltpu.VMEM((frames + 32, width), f32),
            pltpu.VMEM((frames + 32, width), f32),
            pltpu.VMEM((4, frames, 2 * C), bf16),
            pltpu.VMEM((4, frames, 5 * C), bf16),
            pltpu.VMEM((sums_rows, width), f32),
            pltpu.VMEM((sums_rows, width), bf16),
            pltpu.VMEM((4, sums_rows, C), bf16),
            pltpu.VMEM((16, width), f32),
            pltpu.VMEM((4, 16, width), bf16),
            pltpu.VMEM((dp, 8, width), f32),
            pltpu.VMEM((dp, 8, width), f32),
            pltpu.VMEM((4, 3, frames, width), bf16),
            pltpu.VMEM((4, 3, frames, width), bf16),
            pltpu.VMEM((5, 1, width), f32),
            pltpu.VMEM((5, 1, width), f32),
            pltpu.VMEM((2, C), f32),
            pltpu.VMEM((1, C), f32),
            pltpu.VMEM((1, C), f32),
            pltpu.VMEM((taps, 1, C), f32),
            pltpu.VMEM((4 * frames, width), bf16),
            pltpu.SMEM((group,), jnp.int32),
            pltpu.VMEM((2 * width, C), bf16),
            pltpu.VMEM((2 * width, C), f32),
            pltpu.VMEM((R, 4 * width), bf16),
            pltpu.VMEM((R, 4 * width), bf16),
            pltpu.VMEM((R, 2 * C), bf16),
            pltpu.VMEM((R, 5 * C), bf16),
            pltpu.VMEM((2, R, width), bf16),
            pltpu.VMEM((2, R, width), f32),
            pltpu.VMEM((R, width), bf16),
        ]
        + [pltpu.VMEM(m.shape, m.dtype) for m in made_first]
        + [
            pltpu.VMEM((2, R, C), f32),
            pltpu.VMEM((R, C), f32),
            pltpu.VMEM((R // frames, frames + 32, C), f32),
            pltpu.VMEM((R, C), f32),
            pltpu.VMEM((R // frames, frames + 32, C), f32),
            pltpu.VMEM((taps, 8, C), f32),
            pltpu.VMEM((4, 8, C), f32),
            pltpu.VMEM((2**23 // 512, 128), f32),
            pltpu.SemaphoreType.DMA((n_send,)),
            pltpu.SemaphoreType.DMA((n_recv,)),
            pltpu.SemaphoreType.DMA((21,)),
            pltpu.SemaphoreType.DMA((10,)),
        ],
        compiler_params=pltpu.CompilerParams(
            collective_id=0, has_side_effects=True, vmem_limit_bytes=62 * 2**20
        ),
    )(*operands)

    gradients = [
        shape((group * frames, width), f32), shape((group * frames, width), f32), shape((5, 1, width), f32),
        shape((5, 1, width), f32), shape((2, width, width), f32), shape((2, width, width), f32),
        shape((4, width, C), f32), shape((2, C), f32), shape((C, width), f32), shape((2 * width, C), f32),
        shape((taps, 1, C), f32), shape((1, C), f32), shape((1, C), f32), shape((C, width), f32),
    ]
    given = (lo, ig, pa, pb, n0, b0, act0, slope0, ffn_out[0], table[2 * frames :], *ready, cs)
    held = list(given)
    held[8] = shape((width, width))
    made = [m for i, m in enumerate(gradients) if i not in (8, 9, 13)]
    made[4] = made[5] = shape((width, width), f32)
    made[6] = shape((width, C), f32)
    outs = pl.pallas_call(
        last_kernel,
        out_shape=gradients,
        in_specs=[hbm] * len(given),
        out_specs=[hbm] * len(gradients),
        scratch_shapes=[pltpu.VMEM(m.shape, m.dtype) for m in held]
        + [pltpu.VMEM(m.shape, m.dtype) for m in made]
        + [pltpu.SemaphoreType.DMA((len(given),)), pltpu.SemaphoreType.DMA((len(gradients) + 4,))],
        compiler_params=pltpu.CompilerParams(vmem_limit_bytes=62 * 2**20),
    )(*given)
    if groups == 1:
        outs = list(outs[:2]) + [lax.psum(m.astype(bf16), DATA).astype(f32) for m in outs[2:]]
    (lo, ig, ng, nb, w_in, w_out, w_ain, pos, w_aout, w_cin, w_dw, bng, bns, w_cout) = outs
    rows = (1, group, frames, width)
    return (
        lo.reshape(rows), ig.reshape(rows), ng.transpose(1, 0, 2), nb.transpose(1, 0, 2), w_in[None], w_out[None],
        w_ain[None], pos[None], w_aout[None], w_cin.reshape(conv_in.shape), w_dw.transpose(1, 0, 2), bng, bns,
        w_cout[None],
    )


def solution(mesh):
    placed = (
        P(DATA, None, None),
        P(DATA),
        P(DATA, None, None),
        P(SECTION, None, None),
        P(SECTION, None, None),
        P(SECTION, None, None, TENSOR),
        P(SECTION, None, TENSOR, None),
        P(SECTION, None, None, TENSOR),
        P(SECTION, None, TENSOR),
        P(SECTION, TENSOR, None),
        P(SECTION, None, None, TENSOR),
        P(SECTION, None, TENSOR),
        P(SECTION, TENSOR),
        P(SECTION, TENSOR),
        P(SECTION, TENSOR, None),
    )
    return jax.shard_map(
        on_device,
        mesh=mesh,
        in_specs=placed,
        out_specs=(
            P(SECTION, DATA, None, None),
            P(SECTION, DATA, None, None),
            P(SECTION, None, None),
            P(SECTION, None, None),
            P(SECTION, None, None, TENSOR),
            P(SECTION, None, TENSOR, None),
            P(SECTION, None, None, TENSOR),
            P(SECTION, None, TENSOR),
            P(SECTION, TENSOR, None),
            P(SECTION, None, None, TENSOR),
            P(SECTION, None, TENSOR),
            P(SECTION, TENSOR),
            P(SECTION, TENSOR),
            P(SECTION, TENSOR, None),
        ),
        check_vma=False,
    )
```

```python
import math

import jax
import jax.numpy as jnp
import numpy as np
from jax import lax
from jax.experimental import pallas as pl
from jax.experimental.pallas import tpu as pltpu
from jax.sharding import PartitionSpec as P

HEAD = 64
EPSILON = 1e-05
MESH = pl.DeviceIdType.MESH
SECTION, TENSOR, DATA = "section", "tensor", "dp"
PLACE = (0, 2, 1, 3)
SMALL_ROWS = 48


def relative_at(groups):
    return 16 if groups > 1 else SMALL_ROWS


bf16, f32 = jnp.bfloat16, jnp.float32


def dot(left, right, left_dim=1, right_dim=0):
    return lax.dot_general(
        left, right, (((left_dim,), (right_dim,)), ((), ())), preferred_element_type=f32
    )


def position_rows(frames, width):
    offset = np.arange(2 * frames - 1, dtype=np.float32) - np.float32(frames - 1)
    rates = np.exp(
        np.arange(width // 2, dtype=np.float32) * np.float32(-2.0 * math.log(10000.0) / width)
    )
    angles = (offset[:, None] * rates[None, :]).astype(np.float32)
    table = np.stack([np.sin(angles), np.cos(angles)], -1).reshape(2 * frames - 1, width)
    blank = np.zeros((1, width), np.float32)
    return [jnp.asarray(np.concatenate([rows, blank]), bf16) for rows in (table[::-1], table)]


def layer_kernel(dims, *refs):
    T, width, dp, groups = dims
    C = width // 4
    (lengths, inputs, cot, ng_in, nb_in, fin, fout, ain, aout, cin, cout, pos_in, bng_in, bns_in, dw_in, e2_in) = refs[:16]
    (lo_out, ig_out, pa_out, pb_out, cs_out) = refs[16:21]
    (in_out, out_out, qkv_out, ao_out, ci_out, co_out) = refs[21:27]
    refs = refs[27:]
    (Win, Wout, Wqkv, Wr, Wo, Wci, Wco, R2, SM) = refs[:9]
    (H, XH, RS, X, G, ARR, HOP, QKV, PRB, GVG, CT, UP, DP) = refs[9:22]
    (SfSt, SbSt, PAst, PAb, PAin, PBst, PBin, STF, STB, RSst, RSin) = refs[22:33]
    (ng, nb, pos, bng, bns, dw, e2, lens, pairs, spread) = refs[33:43]
    (Nall, Ball, Sf, Sb, ACT, SLOPE, HG, gin, gout, gqkv, gao, gci, gco) = refs[43:56]
    GA, HATA, UA, DYA, DA, DWACC, INVA = refs[56:63]
    LO, IG, PA, PB, CS, dummy, ss, rs, ls, os = refs[63:73]
    gathered = groups > 1

    s, t, d = lax.axis_index(SECTION), lax.axis_index(TENSOR), lax.axis_index(DATA)
    first, second = s == 0, s == 1
    taps = dw.shape[0]
    peers = [(s, t ^ k, d) for k in range(4)]
    sib, yp = peers[1], peers[2]
    around = {j: lax.rem(d + j + dp, dp) for j in range(1 - dp, dp)}
    zpeers = [(s, t, around[r]) for r in range(dp)]
    zpair = (s, t, d ^ 1)
    partner = (1 - s, t, d)
    half = lax.rem(d, 2)
    R4 = 4 * T
    reach = range(1 - groups, groups)
    base_of = {j: pl.multiple_of(around[j] * R4, R4) if groups > 1 else 0 for j in reach}
    second_of, high_of, last_of = (
        {j: pl.multiple_of(around[j] * R4 + n * T, T) if groups > 1 else n * T for j in reach} for n in (1, 2, 3)
    )
    there = {j: d + j >= 0 if j < 0 else d + j <= dp - 1 for j in reach}
    through = {
        (j, to): there[j] & there[to] for j in reach for to in (1, -1) if j * to < 0 and groups > 1
    }
    base = base_of[0]
    trow, yrow = pl.multiple_of(t * T, T), pl.multiple_of((t ^ 2) * T, T)
    mine = d if groups > 1 else 0

    recv_index, send_index, sent = {}, {}, {}

    def size_of(view):
        return math.prod(view.shape) * view.dtype.itemsize

    def copy_of(key, src, dst, dev, group):
        i = recv_index.setdefault(key, len(recv_index))
        j = send_index.setdefault(id(group), len(send_index))
        return pltpu.make_async_remote_copy(
            src_ref=src, dst_ref=dst, send_sem=ss.at[j], recv_sem=rs.at[i], device_id=dev, device_id_type=MESH,
        )

    def start(key, src, dst, dev, cond=None, part=0):
        view = src()
        copy_of(key, view, dst(), dev, cond).start()
        sent.setdefault(id(cond), (cond, {}))[1][key, part] = size_of(view)

    def arrived(key, dst):
        copy_of(key, dst, dst, partner, None).wait_recv()

    def room(size):
        return dummy.at[pl.ds(0, size // (4 * dummy.shape[1]))]

    def all_arrived(key, size):
        if size:
            arrived(key, room(size))

    locals_ = {}

    def fetch(name, src, dst):
        locals_[name] = lambda: pltpu.make_async_copy(src(), dst(), ls.at[list(locals_).index(name)])
        locals_[name]().start()

    def fetched(*names):
        for name in names:
            locals_[name]().wait()

    @pl.when(first)
    def _():
        pltpu.make_async_copy(inputs.at[t], X.at[0], ls.at[20]).start()

    @pl.when(second)
    def _():
        pltpu.make_async_copy(cot.at[t], G, ls.at[20]).start()

    fetch("ng", lambda: ng_in, lambda: ng)
    fetch("nb", lambda: nb_in, lambda: nb)
    fetch("in0", lambda: fin.at[0], lambda: Win.at[0, 0])
    fetch("out0", lambda: fout.at[0], lambda: Wout.at[0, 0])
    fetch("wr", lambda: ain.at[3], lambda: Wr)
    fetch("e2", lambda: e2_in, lambda: e2)
    fetch("pos", lambda: pos_in, lambda: pos)
    fetch("bng", lambda: bng_in, lambda: bng)
    fetch("bns", lambda: bns_in, lambda: bns)
    fetch("dw", lambda: dw_in, lambda: dw)
    fetch("len", lambda: lengths, lambda: lens)
    fetch("qkv", lambda: ain.at[pl.ds(0, 3)], lambda: Wqkv.at[:, :, pl.ds(0, C)])
    fetch("o", lambda: aout, lambda: Wo.at[pl.ds(0, C)])
    fetch("ci", lambda: cin, lambda: pairs)
    fetch("co", lambda: cout, lambda: Wco.at[pl.ds(0, C)])
    fetch("in1", lambda: fin.at[1], lambda: Win.at[1, 0])
    fetch("out1", lambda: fout.at[1], lambda: Wout.at[1, 0])

    barrier = pltpu.get_barrier_semaphore()
    greet = peers[1:] + zpeers[1:] + [partner]
    for dev in greet:
        pl.semaphore_signal(barrier, inc=1, device_id=dev, device_id_type=MESH)
    pl.semaphore_wait(barrier, len(greet))

    starts = {}

    def lines(first_row, n, which):
        if which is None:
            return pl.ds(first_row, n)
        at = (first_row, n, which)
        if at not in starts:
            starts[at] = pl.multiple_of(first_row + n // 2 * (half if which == "own" else 1 - half), n // 2)
        return pl.ds(starts[at], n // 2)

    def cols(k):
        return pl.ds(C * k, C)

    def feed_chunks(j):
        Q = width // 2
        return [
            (
                lambda w, src=src, q=q: src.at[j, lines(Q * q, Q, w)],
                lambda k, w, dst=dst, q=q: dst.at[j, k, lines(Q * q, Q, w)],
            )
            for src, dst in ((fin, Win), (fout, Wout))
            for q in range(2)
        ]

    def row_chunk(src, dst):
        return [(lambda w: src.at[lines(0, C, w)], lambda k, w: dst.at[lines(C * k, C, w)])]

    def column_chunks(src, dst, n):
        return [
            (lambda w, i=i: src(i, lines(0, width, w)), lambda k, w, i=i: dst.at[i, lines(0, width, w), cols(k)])
            for i in range(n)
        ]

    chunks = (
        feed_chunks(0)
        + column_chunks(lambda i, rows: ain.at[i, rows], Wqkv, 3)
        + row_chunk(aout, Wo)
        + column_chunks(lambda i, rows: Wci.at[i, rows, cols(0)], Wci, 2)
        + row_chunk(cout, Wco)
        + feed_chunks(1)
        + [
            (lambda w: SM.at[:, cols(0)], lambda k, w: SM.at[:, cols(k)]),
            (lambda w: R2.at[pl.ds(0, 2 * T), cols(0)], lambda k, w: R2.at[pl.ds(0, 2 * T), cols(k)]),
        ]
    )
    for n, at in ((width // 2, 0), (width // 2, width // 2), (width, 0)) + tuple((C, C * k) for k in range(4)):
        for w in ("own", "other"):
            lines(at, n, w)
    only = {i: second for i in range(4)}
    over_y = {i: "own" for i in range(14)}

    def send_chunks(names):
        for i in names:
            src, dst = chunks[i]
            start(("sib", i), lambda src=src: src(None), lambda dst=dst: dst(1, None), sib, only.get(i))
            w = over_y.get(i)
            start(("y", i), lambda src=src, w=w: src(w), lambda dst=dst, w=w: dst(2, w), yp, only.get(i))

    def step_a(i):
        dst, w = chunks[i][1], over_y.get(i)
        arrived(("y", i), dst(2, w))
        if w:
            start(("z", i), lambda: dst(2, w), lambda: dst(2, w), zpair, only.get(i))
        start(("sib", i), lambda: dst(2, w), lambda: dst(3, w), sib, only.get(i), 1)

    def step_b(i):
        if i not in over_y:
            return
        dst = chunks[i][1]
        arrived(("z", i), dst(2, "other"))
        start(("sib", i), lambda: dst(2, "other"), lambda: dst(3, "other"), sib, only.get(i), 2)

    def step_c(i):
        all_arrived(("sib", i), 2 * size_of(chunks[i][1](1, None)))

    def steps(cond, *plan):
        @pl.when(cond)
        def _():
            for step, i in plan:
                step(i)

    A, B, W = step_a, step_b, step_c

    def norm(i, x):
        centre = x - jnp.mean(x, -1, keepdims=True)
        rate = lax.rsqrt(jnp.mean(centre * centre, -1, keepdims=True) + EPSILON)
        hat = centre * rate
        XH[i] = hat
        RS[i] = jnp.broadcast_to(rate, RS.shape[1:])
        return hat * ng[i] + nb[i]

    def norm_back(i, grad):
        hat = XH[i]
        PBst[i : i + 1] = jnp.sum(grad * hat, 0, keepdims=True)
        PBst[8 + i : 9 + i] = jnp.sum(grad, 0, keepdims=True)
        g = grad * ng[i]
        return RS[i][:, 0:1] * (
            g - jnp.mean(g, -1, keepdims=True) - hat * jnp.mean(g * hat, -1, keepdims=True)
        )

    def total_of(v):
        return jnp.sum(v, 0, keepdims=True)

    def silu(h):
        return h * jax.nn.sigmoid(h)

    def place(k):
        return pl.ds(base + T * PLACE[k], T)

    own, four = pl.ds(base, T), pl.ds(base, R4)

    def block(i, n=1):
        return pl.ds(i * width, n * width)

    def to_tensor(name, ref, c, cond=None):
        for k in (1, 2, 3):
            start(name, lambda: ref.at[own, c], lambda k=k: ref.at[place(k), c], peers[k], cond, k)

    def from_tensor(name, ref, c):
        all_arrived(name, 3 * size_of(ref.at[own, c]))

    def to_pair(name, ref, c, cond=None):
        start(name, lambda: ref.at[own, c], lambda: ref.at[place(1), c], sib, cond, 4)
        start((name, 4), lambda: ref.at[own, c], lambda: ref.at[place(2), c], yp, cond)

    def relay(name, ref, c, cond=None):
        arrived((name, 4), ref.at[place(2), c])
        start(name, lambda: ref.at[place(2), c], lambda: ref.at[place(3), c], sib, cond, 5)

    def from_pair(name, ref, c):
        all_arrived(name, 2 * size_of(ref.at[own, c]))

    def feed(j, i, before, after):
        x = X[before]
        a = norm(i, x).astype(bf16)
        Nall[own, i * width : (i + 1) * width] = a
        to_pair(("n", i), Nall, block(i), second)
        active = []
        for k in range(4):
            h = dot(a, Win[j, k])
            H[j, k] = h
            active.append(silu(h).astype(bf16))
        total = dot(active[0], Wout[j, 0])
        for k in range(1, 4):
            total += dot(active[k], Wout[j, k])
        X[after] = x + 0.5 * total

    def sum_to_owner(name, slot, total):
        for k in (1, 2, 3):
            RSst[slot, k - 1] = total[T * PLACE[k] : T * (PLACE[k] + 1)].astype(bf16)
        for k in (1, 2, 3):
            start(name, lambda k=k: RSst.at[slot, k - 1], lambda k=k: RSin.at[slot, k - 1], peers[k], first, k)
        return total[0:T]

    def summed_here(name, slot, total):
        all_arrived(name, size_of(RSin.at[slot]))
        for k in (1, 2, 3):
            total += RSin[slot, k - 1].astype(f32)
        return total

    def shared_feed(j, i):
        from_tensor(("n", i), Nall, block(i))
        active = silu(dot(Nall[four, i * width : (i + 1) * width], Win[j, 0])).astype(bf16)
        return sum_to_owner(("s", j), j, dot(active, Wout[j, 0]))

    fetched("ng", "nb")

    @pl.when(first)
    def _():
        pltpu.make_async_copy(inputs.at[t], X.at[0], ls.at[20]).wait()
        Nall[own, 0:width] = norm(0, X[0]).astype(bf16)
        to_tensor(("n", 0), Nall, block(0), first)

    @pl.when(second)
    def _():
        send_chunks(range(4))
        pltpu.make_async_copy(cot.at[t], G, ls.at[20]).wait()

    fetched("pos", "bng", "bns", "dw", "wr", "e2", "len", "ci")
    spread[...] = pairs[...].astype(f32)
    for i in range(2):
        Wci[i, :, 0:C] = spread[pl.ds(i, width, stride=2), :].astype(bf16)
    SM[:, 0:C] = jnp.zeros((SMALL_ROWS, C), f32)
    SM[0:2, 0:C] = pos[...]
    SM[2:3, 0:C] = bng[...]
    SM[3:4, 0:C] = bns[...]
    for k in range(taps):
        SM[4 + k : 5 + k, 0:C] = dw[k]
    R2[0 : 2 * T, 0:C] = dot(e2[...], Wr[...]).astype(bf16)
    fetched("in0", "out0")

    @pl.when(first)
    def _():
        send_chunks((8,))
        X[1] = shared_feed(0, 0)
        send_chunks((9,))

    @pl.when(first)
    def _():
        step_a(8)
        X[1] = X[0] + 0.5 * summed_here(("s", 0), 0, X[1])

    @pl.when(second)
    def _():
        send_chunks((15, 16, *range(4, 15)))

    fetched("qkv", "o", "co", "in1", "out1")
    margin = 16
    UP[...] = jnp.zeros(UP.shape, f32)
    DP[...] = jnp.zeros(DP.shape, f32)
    PAst[...] = jnp.zeros(PAst.shape, f32)
    PBst[...] = jnp.zeros(PBst.shape, f32)
    CS[...] = jnp.zeros(CS.shape, f32)
    if gathered:
        DA[...] = jnp.zeros(DA.shape, f32)
        DWACC[...] = jnp.zeros(DWACC.shape, f32)

    def keys_of(length):
        return lax.broadcasted_iota(jnp.int32, (2 * T, T), 1) < length

    row_mask = (lax.broadcasted_iota(jnp.int32, (T, 1), 0) < lens[t]).astype(f32)
    first_head = lax.broadcasted_iota(jnp.int32, (T, 2 * HEAD), 1) < HEAD
    flip = (
        lax.broadcasted_iota(jnp.int32, (T, 4 * T), 0) + lax.broadcasted_iota(jnp.int32, (T, 4 * T), 1)
        == T - 1
    ).astype(f32).astype(bf16)

    def pair_rows(v):
        return jnp.concatenate([jnp.where(first_head, v, 0.0), jnp.where(first_head, 0.0, v)], 0)

    def unpair(v):
        return jnp.where(first_head, v[:T], v[T:])

    def attend(qu, qv, key, value, relative, keys):
        content = dot(pair_rows(qu).astype(bf16), key, 1, 1)
        whole = dot(pair_rows(qv).astype(bf16), jnp.concatenate([relative, jnp.zeros_like(relative)], 0), 1, 1)
        placed = jnp.concatenate(
            [
                pltpu.roll(whole[e * T : (e + 1) * T], 4 * T - (T - 1), 1, stride=1, stride_axis=0)[:, :T]
                for e in range(2)
            ],
            0,
        )
        scores = jnp.where(keys, (content + placed) * HEAD ** (-0.5), -1e30)
        e = jnp.exp(scores - jnp.max(scores, -1, keepdims=True))
        probs = e / jnp.sum(e, -1, keepdims=True)
        return probs, unpair(dot(probs.astype(bf16), value)).astype(bf16)

    def attention_here():
        a = Nall[own, width : 2 * width]
        q = dot(a, Wqkv[0])
        QKV[0] = q + SM[0:1]
        QKV[1] = q + SM[1:2]
        QKV[2] = dot(a, Wqkv[1])
        QKV[3] = dot(a, Wqkv[2])
        keys, mixed = keys_of(lens[t]), []
        for p in range(4):
            c = pl.ds(2 * HEAD * p, 2 * HEAD)
            probs, out = attend(
                QKV[0, :, c], QKV[1, :, c], QKV[2, :, c].astype(bf16), QKV[3, :, c].astype(bf16), R2[0 : 2 * T, c], keys
            )
            PRB[p] = probs
            mixed.append(out)
        return mixed

    def shared_attention():
        a = Nall[four, width : 2 * width]
        q, key, value = (dot(a, Wqkv[i, :, 0:C]) for i in range(3))
        qu, qv, key, value = q + SM[0:1, 0:C], q + SM[1:2, 0:C], key.astype(bf16), value.astype(bf16)
        mixed = []
        for p in range(4):
            rows = slice(T * p, T * (p + 1))
            keys = keys_of(lens[t ^ PLACE[p]])
            mixed.append(attend(qu[rows], qv[rows], key[rows], value[rows], R2[0 : 2 * T, 0:C], keys)[1])
        mixed = jnp.concatenate(mixed, 0)
        Sf[four, 0:C] = mixed
        return sum_to_owner(("s", 3), 3, dot(mixed, Wo[0:C]))

    def relative_arrived():
        step_c(16)
        turned_back = (
            lax.broadcasted_iota(jnp.int32, (2 * T, 2 * T), 0) + lax.broadcasted_iota(jnp.int32, (2 * T, 2 * T), 1)
            == 2 * T - 2
        ).astype(f32).astype(bf16)
        R2[2 * T : 4 * T] = dot(turned_back, R2[0 : 2 * T]).astype(bf16)


    @pl.when(first)
    def _():
        Nall[own, width : 2 * width] = norm(1, X[1]).astype(bf16)
        to_tensor(("n", 1), Nall, block(1), first)
        send_chunks((10, 15))
        step_a(9)
        step_b(8)
        from_tensor(("n", 1), Nall, block(1))
        total = shared_attention()
        send_chunks((4, 5, 6, 16, 7))
        step_a(10)
        step_a(15)
        step_b(9)
        X[2] = X[1] + summed_here(("s", 3), 3, total)
        step_b(10)
        step_c(15)

    @pl.when(second)
    def _():
        coming = (*range(4), 15, 16, *range(4, 13))
        for n, i in enumerate(coming):
            step_a(i)
            if n > 1:
                step_b(coming[n - 2])
        for i in range(7):
            step_c(i)
        step_c(15)
        relative_arrived()
        arrived("hop", ARR)
        X[0] = ARR[...].astype(f32)
        feed(0, 0, 0, 1)
        Nall[own, width : 2 * width] = norm(1, X[1]).astype(bf16)
        to_pair(("n", 1), Nall, block(1), second)
        step_b(11)
        mixed = attention_here()
        step_a(13)
        step_b(12)
        for k in range(4):
            SfSt[k, :, 0:C] = mixed[k]
        step_c(7)
        X[2] = X[1] + dot(jnp.concatenate(mixed, 1), Wo[...])

    def line_start(name, region):
        for way, to, back in (("up", 1, -1), ("down", -1, 1)):
            if groups > 1:

                @pl.when(there[to])
                def _():
                    start(
                        (name, 0, back % dp), lambda: region(0), lambda: region(0), (s, t, around[to]), there[to], way
                    )

    def line_hop(name, region, n, after=None):
        for way, to, back in (("up", 1, -1), ("down", -1, 1)):
            if n < groups:

                @pl.when(there[back * n])
                def _():
                    j = back * n
                    arrived((name, 0, j % dp), region(j))
                    if n + 1 < groups:

                        @pl.when(there[to])
                        def _():
                            start(
                                (name, 0, (j + back) % dp), lambda: region(j), lambda: region(j),
                                (s, t, around[to]), through[j, to], way,
                            )

                    if after is not None:
                        after(name, j)

    def rows_region(ref, n, c):
        return lambda j: ref.at[pl.ds(base_of[j], n), c]

    def share(ref, c):
        def go(name, j):
            rows = lambda: ref.at[pl.ds(base_of[j], T), c]
            start((name, 1, j % dp), rows, lambda: ref.at[pl.ds(second_of[j], T), c], yp, there[j], j)
            start((name, 2, 0), rows, lambda: ref.at[pl.ds(high_of[j], T), c], sib, there[j], j)

        return go

    def share_on(name, ref, c, n):
        for j in (n, -n):
            if n < groups:

                @pl.when(there[j])
                def _():
                    rows = lambda: ref.at[pl.ds(second_of[j], T), c]
                    arrived((name, 1, j % dp), rows())
                    start((name, 2, 0), rows, lambda: ref.at[pl.ds(last_of[j], T), c], sib, there[j], dp + j)

    def shared(name, ref, c):
        all_arrived((name, 2, 0), 2 * (groups - 1) * size_of(ref.at[own, c]))

    def set_off_to_all(name):
        ref, c = whole_rows(name)
        mine = lambda: ref.at[own, c]
        for r in range(1, groups):
            start((name, 0, (-r) % dp), mine, mine, zpeers[r], None, r)

    def from_all(name):
        ref, c = whole_rows(name)
        for r in range(1, groups):
            rows = lambda r=r: ref.at[pl.ds(base_of[r], T), c]
            arrived((name, 0, r), rows())
            start((name, 1, r), rows, lambda r=r: ref.at[pl.ds(second_of[r], T), c], yp, None, r)
            start((name, 2, 0), rows, lambda r=r: ref.at[pl.ds(high_of[r], T), c], sib, None, r)

    def hand_on_all(name):
        ref, c = whole_rows(name)
        for r in range(1, groups):
            rows = lambda r=r: ref.at[pl.ds(second_of[r], T), c]
            arrived((name, 1, r), rows())
            start((name, 2, 0), rows, lambda r=r: ref.at[pl.ds(last_of[r], T), c], sib, None, dp + r)

    def all_shared(*names):
        for name in names:
            shared(name, *whole_rows(name))

    sf_cols = pl.ds(0, C if gathered else 2 * C)
    qkv_cols, gate_cols = pl.ds(0, 3 * C), pl.ds(3 * C, 2 * C)
    lines_of = {
        "n": (rows_region(Nall, T, block(0, 3)), share(Nall, block(0, 3))),
        "m": (rows_region(Nall, T, block(3)), share(Nall, block(3))),
        "sf": (rows_region(Sf, R4, sf_cols), None),
        "qkv": (rows_region(Sb, R4, qkv_cols), None),
    }
    for i in range(4):
        lines_of["b", i] = (rows_region(Ball, T, block(i)), share(Ball, block(i)))

    def set_off(*names):
        for name in names:
            line_start(name, lines_of[name][0])

    def hop(n, *names):
        for name in names:
            line_hop(name, lines_of[name][0], n, lines_of[name][1])

    def whole_rows(name):
        if name in ("n", "m"):
            return Nall, block(0, 3) if name == "n" else block(3)
        return Ball, block(name[1])

    def hand_on(n, *names):
        for name in names:
            share_on(name, *whole_rows(name), n)

    written = []

    def write(src, dst):
        pltpu.make_async_copy(src, dst, os.at[0]).start()
        written.append(size_of(src))

    R = Nall.shape[0]
    row_blocks = [slice(r, r + R4) for r in range(0, R, R4)]

    def slope(h, sig):
        return sig * (1.0 + h * (1.0 - sig))

    def hidden_rows(j, i):
        for rows in row_blocks:
            h = dot(Nall[rows, i * width : (i + 1) * width], Win[j, 0])
            sig = jax.nn.sigmoid(h)
            ACT[j, rows] = (h * sig).astype(bf16)
            SLOPE[j, rows] = slope(h, sig)

    def feed_grads(j, i):
        c = slice(i * width, (i + 1) * width)
        for rows in row_blocks:
            HG[rows] = (dot(Ball[rows, c], Wout[j, 0], 1, 1) * SLOPE[j, rows]).astype(bf16)
        gin[j] = dot(Nall[:, c], HG[...], 0, 0).astype(bf16)
        write(gin.at[j], in_out.at[j])
        gout[j] = dot(ACT[j], Ball[:, c], 0, 0).astype(bf16)
        write(gout.at[j], out_out.at[j])

    def mask_of(g, p):
        return (lax.broadcasted_iota(jnp.int32, (T, C), 0).astype(f32) < STF[g, 3:4, C * p : C * (p + 1)]).astype(f32)

    places = [(p, [(g, slice(R4 * g + T * p, R4 * g + T * (p + 1))) for g in range(groups)]) for p in range(4)]

    def convolution_rows():
        for i in range(2):
            GA[i] = dot(Nall[:, 2 * width : 3 * width], Wci[i, :, 0:C])
        UA[...] = jnp.zeros(UA.shape, f32)
        for p, parts in places:
            for g, rows in parts:
                UA[4 * g + p, margin : margin + T] = GA[0, rows] * jax.nn.sigmoid(GA[1, rows]) * mask_of(g, p)

        def one(b, carry):
            acc = SM[4:5, 0:C] * UA[b, margin - taps // 2 : margin - taps // 2 + T]
            for k in range(1, taps):
                o = margin - taps // 2 + k
                acc += SM[4 + k : 5 + k, 0:C] * UA[b, o : o + T]
            HATA[pl.ds(b * T, T)] = acc
            return carry

        lax.fori_loop(0, 4 * groups, one, 0)
        for p, parts in places:
            n = sum(STF[g, 3:4, C * p : C * (p + 1)] for g, _ in parts)
            masked = [HATA[rows] * mask_of(g, p) for g, rows in parts]
            mean = sum(total_of(m) for m in masked) / n
            square = sum(total_of(m * HATA[rows]) for m, (_, rows) in zip(masked, parts)) / n
            inv = lax.rsqrt(square - mean * mean + EPSILON)
            INVA[p, 0:1] = inv
            INVA[p, 1:2] = n
            for g, rows in parts:
                h = (HATA[rows] - mean) * inv
                HATA[rows] = h
                Sf[rows, C : 2 * C] = silu(h * SM[2:3, 0:C] + SM[3:4, 0:C]).astype(bf16)

    def convolution_rows_back():
        DYA[...] = dot(Ball[:, 2 * width : 3 * width], Wco[0:C], 1, 1)
        gain_sum = shift_sum = jnp.zeros((1, C), f32)
        for p, parts in places:
            first_sum = second_sum = jnp.zeros((1, C), f32)
            for g, rows in parts:
                h = HATA[rows]
                y = h * SM[2:3, 0:C] + SM[3:4, 0:C]
                dy = DYA[rows] * slope(y, jax.nn.sigmoid(y))
                gain_sum += total_of(dy * h)
                shift_sum += total_of(dy)
                dh = dy * SM[2:3, 0:C]
                DYA[rows] = dh
                dh = dh * mask_of(g, p)
                first_sum += total_of(dh)
                second_sum += total_of(dh * h)
            inv, n = INVA[p, 0:1], INVA[p, 1:2]
            for g, rows in parts:
                dc = inv * (DYA[rows] - (first_sum + HATA[rows] * second_sum) / n) * mask_of(g, p)
                DA[4 * g + p, margin : margin + T] = dc
        CS[taps : taps + 1] = gain_sum
        CS[taps + 1 : taps + 2] = shift_sum

        def one(b, carry):
            here = DA[b, margin : margin + T]
            acc = jnp.zeros((T, C), f32)
            for k in range(taps):
                o = margin + taps // 2 - k
                acc += SM[4 + k : 5 + k, 0:C] * DA[b, o : o + T]
                o = margin - taps // 2 + k
                term = here * UA[b, o : o + T]
                DWACC[k] += sum(term[8 * i : 8 * (i + 1)] for i in range(T // 8))
            DYA[pl.ds(b * T, T)] = acc
            return carry

        lax.fori_loop(0, 4 * groups, one, 0)
        for k in range(taps):
            CS[k : k + 1] = total_of(DWACC[k])
        for p, parts in places:
            for g, rows in parts:
                sig = jax.nn.sigmoid(GA[1, rows])
                dua = DYA[rows] * mask_of(g, p)
                Sb[rows, 3 * C : 4 * C] = (dua * sig).astype(bf16)
                Sb[rows, 4 * C : 5 * C] = (dua * GA[0, rows] * (sig * (1.0 - sig))).astype(bf16)

    def convolution_grads():
        gci[...] = dot(Nall[:, 2 * width : 3 * width], Sb[:, 3 * C : 5 * C], 0, 0).astype(bf16)
        write(gci, ci_out)
        gco[...] = dot(Sf[:, C : 2 * C], Ball[:, 2 * width : 3 * width], 0, 0).astype(bf16)
        write(gco, co_out)

    def attention_grads():
        grads = dot(Nall[:, width : 2 * width], Sb[:, 0 : 3 * C], 0, 0)
        for i in range(3):
            gqkv[i] = grads[:, C * i : C * (i + 1)].astype(bf16)
        write(gqkv, qkv_out)
        gao[...] = dot(Sf[:, 0:C], Ball[:, width : 2 * width], 0, 0).astype(bf16)
        write(gao, ao_out)

    def forward_values():
        hidden_rows(1, 3)
        hidden_rows(0, 0)
        if gathered:
            convolution_rows()

    a = norm(2, X[2]).astype(bf16)
    Nall[own, 2 * width : 3 * width] = a
    to_pair(("n", 2), Nall, block(2))

    step_c(8)
    step_c(9)
    GVG[0] = dot(a, Wci[0])
    GVG[1] = dot(a, Wci[1])
    UP[margin : margin + T] = GVG[0] * jax.nn.sigmoid(GVG[1]) * row_mask
    for p in range(4):
        c = pl.ds(C * p, C)
        acc = SM[4:5, c] * UP[margin - taps // 2 : margin - taps // 2 + T, c]
        for k in range(1, taps):
            o = margin - taps // 2 + k
            acc += SM[4 + k : 5 + k, c] * UP[o : o + T, c]
        CT[:, c] = acc
    conv = CT[...]

    def dp_sums(name, ref, rows):
        n = len(rows)
        ref[d] = jnp.concatenate(rows + [jnp.zeros((8 - n, width), f32)], 0)
        for r in range(1, dp):
            start(name, lambda: ref.at[d], lambda: ref.at[d], zpeers[r], None, r)

    def summed(name, ref):
        all_arrived(name, (dp - 1) * size_of(ref.at[0]))
        total = ref[0]
        for r in range(1, dp):
            total += ref[r]
        return total

    masked = conv * row_mask
    frames_row = jnp.broadcast_to(total_of(row_mask), (1, width))
    lengths_row = jnp.concatenate(
        [jnp.broadcast_to(lens[t ^ PLACE[p]].astype(f32), (1, C)) for p in range(4)], 1
    )
    dp_sums("bnf", STF, [total_of(masked), total_of(masked * conv), frames_row, lengths_row])
    steps(second, (A, 14), (B, 13))
    step_c(10)
    sums = summed("bnf", STF)
    steps(first, (A, 4), (A, 5), (A, 6), (A, 16))

    @pl.when(second)
    def _():
        set_off("n")
    count = sums[2:3]
    bn_mean = sums[0:1] / count
    inv_std = lax.rsqrt(sums[1:2] / count - bn_mean * bn_mean + EPSILON)
    hat = (conv - bn_mean) * inv_std
    CT[...] = hat
    active = silu(hat * SM[2:3] + SM[3:4]).astype(bf16)
    if not gathered:
        for k in range(4):
            SfSt[k, :, C : 2 * C] = active[:, C * k : C * (k + 1)]
    X[3] = X[2] + dot(active, Wco[...])

    @pl.when(first)
    def _():
        Nall[own, 3 * width : 4 * width] = norm(3, X[3]).astype(bf16)
        to_tensor(("n", 3), Nall, block(3), first)
        send_chunks((11,))
        total = shared_feed(1, 3)
        send_chunks((12, 13, 14))
        step_a(7)
        step_b(4)
        step_b(5)
        X[4] = X[3] + 0.5 * summed_here(("s", 1), 1, total)

    @pl.when(second)
    def _():
        for i in range(11, 15):
            step_c(i)
        feed(1, 3, 3, 4)
    out = (norm(4, X[4]) * row_mask).astype(bf16)
    HOP[...] = out

    @pl.when(first)
    def _():
        start("hop", lambda: HOP, lambda: ARR, partner, first)

    LO[pl.ds(trow, T)] = out
    def output_to_pair(name, ref):
        rows = lambda: ref.at[pl.ds(trow, T)]
        start(name, rows, rows, sib)
        start((name, 4), rows, rows, yp)

    def relay_output(name, ref):
        rows = lambda: ref.at[pl.ds(yrow, T)]
        arrived((name, 4), rows())
        start(name, rows, rows, sib, None, 1)

    output_to_pair("out", LO)

    for cond, c in ((first, pl.ds(C, C)), (second, sf_cols))[gathered:]:

        @pl.when(cond)
        def _():
            Sf[own, c] = SfSt[0, :, c]
            for k in (1, 2, 3):
                start("sf", lambda k=k: SfSt.at[k, :, c], lambda k=k: Sf.at[place(k), c], peers[k], cond, k)

    @pl.when(first)
    def _():
        set_off("n", "m", "sf")
        relay(("n", 2), Nall, block(2))
        step_a(11)
        for i in (6, 7):
            step_b(i)
        step_a(12)
        step_b(11)
        for i in (4, 5, 6, 7):
            step_c(i)
        relative_arrived()
        attention_here()
        step_a(13)
        step_b(12)
        if not gathered:
            from_tensor("sf", Sf, pl.ds(C, C))
        step_a(14)
        hop(1, "n", "m", "sf")
        step_b(13)
        for i in range(11, 15):
            step_c(i)
        for k in range(4):
            H[1, k] = dot(Nall[own, 3 * width : 4 * width], Win[1, k])
        hop(2, "n", "m", "sf")
        hand_on(1, "n", "m")
        hop(3, "n", "m", "sf")
        hand_on(2, "n", "m")

    @pl.when(first)
    def _():
        arrived("back", ARR)
        G[...] = ARR[...].astype(f32)

    back_rows = lambda: IG.at[pl.ds(trow, T)]

    def feed_back(j, i, g):
        b = (0.5 * g).astype(bf16)
        Ball[own, i * width : (i + 1) * width] = b
        if j:
            to_pair(("b", i), Ball, block(i))
            set_off(("b", i))
        else:
            to_tensor(("b", i), Ball, block(i))
        grad = None
        for k in range(4):
            h = H[j, k]
            sig = jax.nn.sigmoid(h)
            hg = (dot(b, Wout[j, k], 1, 1) * slope(h, sig)).astype(bf16)
            part = dot(hg, Win[j, k], 1, 1)
            grad = part if grad is None else grad + part
        return g + norm_back(i, grad)
    g = norm_back(4, G[...] * row_mask)
    g = feed_back(1, 3, g)
    b = g.astype(bf16)
    Ball[own, 2 * width : 3 * width] = b
    to_pair(("b", 2), Ball, block(2))
    hat = CT[...]
    y = hat * SM[2:3] + SM[3:4]
    sig = jax.nn.sigmoid(y)
    dy = dot(b, Wco[...], 1, 1) * slope(y, sig)
    if not gathered:
        PAst[2:3] = total_of(dy * hat)
        PAst[3:4] = total_of(dy)
    dhat = dy * SM[2:3]
    masked = dhat * row_mask
    dp_sums("bnb", STB, [total_of(masked), total_of(masked * hat)])

    @pl.when(first)
    def _():
        hand_on(3, "n", "m")
        from_pair(("n", 2), Nall, block(2))
        all_shared("n", "m")
        forward_values()
        hop(1, ("b", 3))

    relay(("b", 3), Ball, block(3))
    sums = summed("bnb", STB)

    @pl.when(second)
    def _():
        for i in range(4):
            relay(("n", i), Nall, block(i), None if i == 2 else second)
        hop(1, "n")
        set_off("m")
        from_tensor("sf", Sf, sf_cols)
        set_off("sf")

    relay_output("out", LO)
    relay(("b", 2), Ball, block(2))
    set_off_to_all(("b", 2))
    dc = inv_std * (dhat - (sums[0:1] + hat * sums[1:2]) / count) * row_mask
    DP[margin : margin + T] = dc
    for p in range(4):
        c = pl.ds(C * p, C)
        here = DP[margin : margin + T, c]
        acc = None
        for k in range(taps):
            o = margin + taps // 2 - k
            term = SM[4 + k : 5 + k, c] * DP[o : o + T, c]
            acc = term if acc is None else acc + term
            if not gathered:
                o = margin - taps // 2 + k
                PAst[4 + k : 5 + k, c] = total_of(here * UP[o : o + T, c])
        CT[:, c] = acc
    du = CT[...] * row_mask
    sig = jax.nn.sigmoid(GVG[1])
    dvalue = (du * sig).astype(bf16)
    dgate = (du * GVG[0] * (sig * (1.0 - sig))).astype(bf16)
    def sb_to_tensor(name, c, k):
        start(name, lambda: SbSt.at[k, :, c], lambda: Sb.at[place(k), c], peers[k], None, k)

    if not gathered:
        for k in range(4):
            SbSt[k, :, 3 * C : 4 * C] = dvalue[:, C * k : C * (k + 1)]
            SbSt[k, :, 4 * C : 5 * C] = dgate[:, C * k : C * (k + 1)]
        Sb[own, 3 * C : 5 * C] = SbSt[0, :, 3 * C : 5 * C]
        for k in (1, 2, 3):
            sb_to_tensor("gates", gate_cols, k)
    g = g + norm_back(2, dot(dvalue, Wci[0], 1, 1) + dot(dgate, Wci[1], 1, 1))
    b = g.astype(bf16)
    Ball[own, width : 2 * width] = b
    to_pair(("b", 1), Ball, block(1))
    set_off(("b", 1))
    dmix = dot(b, Wo[...], 1, 1).astype(bf16).astype(f32)
    scale = HEAD ** (-0.5)
    dq, dk, dv = [None] * 4, [None] * 4, [None] * 4
    for p in (2, 3, 1, 0):
        c = pl.ds(2 * HEAD * p, 2 * HEAD)
        qu = pair_rows(QKV[0, :, c]).astype(bf16)
        qv = pair_rows(QKV[1, :, c]).astype(bf16)
        key = QKV[2, :, c].astype(bf16)
        val = QKV[3, :, c].astype(bf16)
        do = pair_rows(dmix[:, 2 * HEAD * p : 2 * HEAD * (p + 1)]).astype(bf16)
        probs = PRB[p]
        dprob = dot(do, val, 1, 1)
        ds = (probs * (dprob - jnp.sum(probs * dprob, -1, keepdims=True))).astype(bf16)
        du_rows = unpair(dot(ds, key)) * scale
        turned = dot(ds, flip)
        whole = jnp.concatenate(
            [
                pltpu.roll(turned[e * T : (e + 1) * T], 0, 1, stride=1, stride_axis=0)[:, : 2 * T]
                for e in range(2)
            ],
            0,
        ).astype(bf16)
        dv_rows = unpair(dot(whole, R2[2 * T : 4 * T, c])) * scale
        dk[p] = (dot(ds, qu, 0, 0) * scale).astype(bf16)
        dv[p] = dot(probs.astype(bf16), do, 0, 0).astype(bf16)
        dq[p] = (du_rows + dv_rows).astype(bf16)
        SbSt[p, :, 0:C] = dq[p]
        SbSt[p, :, C : 2 * C] = dk[p]
        SbSt[p, :, 2 * C : 3 * C] = dv[p]
        if p:
            sb_to_tensor("qkv", qkv_cols, p)
        PAst[0:1, c] = total_of(du_rows)
        PAst[1:2, c] = total_of(dv_rows)
        PAst[relative_at(groups) : relative_at(groups) + 2 * T, c] = dot(whole, qv, 0, 0) * scale
    Sb[own, 0 : 3 * C] = SbSt[0, :, 0 : 3 * C]
    @pl.when(first)
    def _():
        if not gathered:
            from_tensor("gates", Sb, gate_cols)
        hop(2, ("b", 3))
        relay(("b", 1), Ball, block(1))
    grad = dot(jnp.concatenate(dq, 1), Wqkv[0], 1, 1)
    grad += dot(jnp.concatenate(dk, 1), Wqkv[1], 1, 1)
    grad += dot(jnp.concatenate(dv, 1), Wqkv[2], 1, 1)
    g = g + norm_back(1, grad)

    @pl.when(second)
    def _():
        IG[pl.ds(trow, T)] = feed_back(0, 0, g).astype(bf16)
        start("back", back_rows, lambda: ARR, partner, second)

    @pl.when(first)
    def _():
        Ball[own, 0:width] = (0.5 * g).astype(bf16)
        to_tensor(("b", 0), Ball, block(0))
        G[...] = g

    set_off_to_all(("b", 0))
    from_all(("b", 2))
    def sums_over_tensor(name, parts, ref):
        all_arrived(name, 3 * size_of(parts.at[0]))
        ref[mine] = sum(parts[k].astype(f32) for k in range(4)).astype(bf16)
        for r in range(1, groups):
            start((name, 3), lambda: ref.at[mine], lambda: ref.at[mine], zpeers[r], None, r)

    def send_sums():
        PAb[...] = PAst[...].astype(bf16)
        for k in (1, 2, 3):
            start("pa", lambda k=k: PAb.at[:, cols(k)], lambda k=k: PAin.at[k], peers[k], None, k)

    def send_ends():
        output_to_pair("grad", IG)
        PBin[t] = PBst[...].astype(bf16)
        for k in (1, 2, 3):
            start("pb", lambda: PBin.at[t], lambda: PBin.at[t], peers[k], None, k)

    bs = [("b", i) for i in range(4)]
    if not gathered:

        @pl.when(second)
        def _():
            from_tensor("gates", Sb, gate_cols)

    @pl.when(second)
    def _():
        send_ends()
        send_sums()
        hop(2, "n")
        hop(1, "m", "sf", bs[3])
        relay(bs[1], Ball, block(1))
        from_tensor("qkv", Sb, qkv_cols)
        set_off("qkv")
        hop(1, bs[1])
        hand_on(1, "n")
        from_all(bs[0])
        hand_on_all(bs[2])
        hop(3, "n")
        hop(2, "m", "sf", bs[3], bs[1])
        hand_on(2, "n")
        hop(1, "qkv")
        hand_on(1, "m", bs[3], bs[1])
        hop(3, "m", "sf", bs[3])
        hand_on(3, "n")
        hand_on_all(bs[0])
        hop(3, bs[1])
        hand_on(2, "m", bs[3], bs[1])
        hop(2, "qkv")
        hand_on(3, "m")
        for i in range(4):
            from_pair(("n", i), Nall, block(i))
        all_shared("n", "m")
        forward_values()

    @pl.when(first)
    def _():
        from_tensor("qkv", Sb, qkv_cols)
        set_off("qkv")
        hop(3, bs[3])
        hop(1, bs[1])
        hand_on(1, bs[3])
        hand_on(2, bs[3])
        from_tensor(bs[0], Ball, block(0))
        h = dot(Nall[four, 0:width], Win[0, 0])
        sig = jax.nn.sigmoid(h)
        hg = dot(Ball[four, 0:width], Wout[0, 0], 1, 1) * slope(h, sig)
        X[0] = sum_to_owner(("s", 2), 2, dot(hg.astype(bf16), Win[0, 0], 1, 1))
        send_sums()
        hand_on_all(bs[2])
        from_all(bs[0])
        hop(1, "qkv")
        hop(2, bs[1])
    hand_on(3, bs[3])
    from_pair(bs[3], Ball, block(3))
    shared(bs[3], *whole_rows(bs[3]))
    feed_grads(1, 3)

    @pl.when(first)
    def _():
        g = G[...] + norm_back(0, summed_here(("s", 2), 2, X[0]))
        IG[pl.ds(trow, T)] = g.astype(bf16)
        send_ends()
        hand_on_all(bs[0])
        hop(2, "qkv")

    PAin[0] = PAb[:, 0:C]
    sums_over_tensor("pa", PAin, PA)
    from_pair(bs[2], Ball, block(2))
    shared(bs[2], *whole_rows(bs[2]))
    if gathered:
        convolution_rows_back()
    sums_over_tensor("pb", PBin, PB)

    @pl.when(first)
    def _():
        hop(3, bs[1])
        hand_on(1, bs[1])
        hand_on(2, bs[1])

    convolution_grads()
    relay_output("grad", IG)

    @pl.when(second)
    def _():
        from_tensor(bs[0], Ball, block(0))

    shared(bs[0], *whole_rows(bs[0]))
    feed_grads(0, 0)
    hand_on(3, bs[1])
    hop(3, "qkv")
    from_pair(bs[1], Ball, block(1))
    shared(bs[1], *whole_rows(bs[1]))
    attention_grads()
    for name, ref in (("pa", PA), ("pb", PB)):
        all_arrived((name, 3), (groups - 1) * size_of(ref.at[0]))
    all_arrived("out", 2 * size_of(back_rows()))
    all_arrived("grad", 2 * size_of(back_rows()))
    for src, dst in ((LO, lo_out), (IG, ig_out), (PA, pa_out), (PB, pb_out), (CS, cs_out)):
        write(src, dst)
    pltpu.make_async_copy(room(sum(written)), room(sum(written)), os.at[0]).wait()
    for cond, sizes in sent.values():

        def all_sent():
            view = room(sum(sizes.values()))
            copy_of("out", view, view, partner, cond).wait_send()

        all_sent() if cond is None else pl.when(cond)(all_sent)
    assert len(recv_index) <= rs.shape[0] and len(send_index) <= ss.shape[0]


def last_kernel(*refs):
    given, outs, held, made, in_sems, out_sems = refs[:12], refs[12:26], refs[26:38], refs[38:52], refs[52], refs[53]
    in_grad, out_grad, qkv, ao, ci, co, pa, pb, cs, lo, ig, table = held
    (LO, IG, ng, nb, w_in, w_out, w_ain, pos, w_aout, w_cin, w_dw, bng, bns, w_cout) = made
    C, width = ao.shape
    copies = []

    def send(src, dst):
        copy = pltpu.make_async_copy(src, dst, out_sems.at[len(copies)])
        copy.start()
        copies.append(copy)

    loads = [pltpu.make_async_copy(given[i], held[i], in_sems.at[i]) for i in range(len(held))]
    for load in loads:
        load.start()
    for i, src, dst, out in ((0, in_grad, w_in, outs[4]), (1, out_grad, w_out, outs[5])):
        loads[i].wait()
        for j in range(2):
            dst[j] = src[j].astype(f32)
            send(dst.at[j], out.at[j])
    loads[2].wait()
    w_ain[0:3] = qkv[...].astype(f32)
    send(w_ain.at[pl.ds(0, 3)], outs[6].at[pl.ds(0, 3)])
    loads[3].wait()
    w_aout[...] = ao[...].astype(f32)
    send(w_aout, outs[8])
    loads[4].wait()
    for i in range(2):
        w_cin[pl.ds(i, width, stride=2), :] = ci[:, C * i : C * (i + 1)].astype(f32)
    send(w_cin, outs[9])
    loads[5].wait()
    w_cout[...] = co[...].astype(f32)
    send(w_cout, outs[13])
    for load in loads[6:]:
        load.wait()
    sums, norms = pa[0].astype(f32), pb[0].astype(f32)
    for g in range(1, pa.shape[0]):
        sums += pa[g].astype(f32)
        norms += pb[g].astype(f32)
    w_ain[3] = dot(table[...], sums[relative_at(pa.shape[0]) :].astype(bf16), 0, 0)
    send(w_ain.at[3], outs[6].at[3])
    LO[...] = lo[...].astype(f32)
    IG[...] = ig[...].astype(f32)
    for i in range(5):
        ng[i] = norms[i : i + 1]
        nb[i] = norms[8 + i : 9 + i]
    pos[...] = sums[0:2]
    taps = w_dw.shape[0]
    if pa.shape[0] > 1:
        sums = jnp.concatenate([sums[0:2], cs[taps : taps + 2], cs[0:taps]], 0)
    bng[...] = sums[2:3]
    bns[...] = sums[3:4]
    for k in range(taps):
        w_dw[k] = sums[4 + k : 5 + k]
    for i in (0, 1, 2, 3, 7, 10, 11, 12):
        send(made[i], outs[i])
    for copy in copies:
        copy.wait()


def on_device(
    inputs, lengths, cotangent, norm_gain, norm_bias, ffn_in, ffn_out, attn_in, pos_bias, attn_out,
    conv_in, depthwise, bn_gain, bn_shift, conv_out,
):
    dp = lax.axis_size(DATA)
    group, frames, width = inputs.shape
    C = width // 4
    taps = depthwise.shape[1]
    groups = dp if dp <= 4 else 1
    R = groups * group * frames
    table = position_rows(frames, width)
    hbm = pl.BlockSpec(memory_space=pltpu.HBM)
    sums_rows = relative_at(groups) + 2 * frames

    def shape(dims, dtype=bf16):
        return jax.ShapeDtypeStruct(dims, dtype)

    small_first = [
        shape((group * frames, width)), shape((group * frames, width)), shape((groups, sums_rows, C)),
        shape((groups, 16, width)), shape((40, C), f32),
    ]
    made_first = [
        shape((2, width, width)), shape((2, width, width)), shape((3, width, C)), shape((C, width)),
        shape((width, 2 * C)), shape((C, width)),
    ]
    n_recv = 84 + 15 * (groups - 1)
    n_send = 3 + 2 * (groups - 1) + 2 * max(groups - 2, 0)
    operands = (
        lengths, inputs, cotangent, norm_gain.transpose(1, 0, 2), norm_bias.transpose(1, 0, 2), ffn_in[0],
        ffn_out[0], attn_in[0], attn_out[0], conv_in.reshape(2 * width, C), conv_out[0], pos_bias[0], bn_gain,
        bn_shift, depthwise.transpose(1, 0, 2), table[0],
    )
    lo, ig, pa, pb, cs, *ready = pl.pallas_call(
        lambda *refs: layer_kernel((frames, width, dp, groups), *refs),
        out_shape=small_first + made_first,
        in_specs=[hbm] * 16,
        out_specs=[hbm] * 11,
        scratch_shapes=[
            pltpu.VMEM((2, 4, width, width), bf16),
            pltpu.VMEM((2, 4, width, width), bf16),
            pltpu.VMEM((3, width, width), bf16),
            pltpu.VMEM((width, C), bf16),
            pltpu.VMEM((width, width), bf16),
            pltpu.VMEM((2, width, width), bf16),
            pltpu.VMEM((width, width), bf16),
            pltpu.VMEM((4 * frames, width), bf16),
            pltpu.VMEM((SMALL_ROWS, width), f32),
            pltpu.VMEM((2, 4, frames, width), f32),
            pltpu.VMEM((5, frames, width), f32),
            pltpu.VMEM((5, frames, 128), f32),
            pltpu.VMEM((5, frames, width), f32),
            pltpu.VMEM((frames, width), f32),
            pltpu.VMEM((frames, width), bf16),
            pltpu.VMEM((frames, width), bf16),
            pltpu.VMEM((4, frames, width), f32),
            pltpu.VMEM((4, 2 * frames, frames), f32),
            pltpu.VMEM((2, frames, width), f32),
            pltpu.VMEM((frames, width), f32),
            pltpu.VMEM((frames + 32, width), f32),
            pltpu.VMEM((frames + 32, width), f32),
            pltpu.VMEM((4, frames, 2 * C), bf16),
            pltpu.VMEM((4, frames, 5 * C), bf16),
            pltpu.VMEM((sums_rows, width), f32),
            pltpu.VMEM((sums_rows, width), bf16),
            pltpu.VMEM((4, sums_rows, C), bf16),
            pltpu.VMEM((16, width), f32),
            pltpu.VMEM((4, 16, width), bf16),
            pltpu.VMEM((dp, 8, width), f32),
            pltpu.VMEM((dp, 8, width), f32),
            pltpu.VMEM((4, 3, frames, width), bf16),
            pltpu.VMEM((4, 3, frames, width), bf16),
            pltpu.VMEM((5, 1, width), f32),
            pltpu.VMEM((5, 1, width), f32),
            pltpu.VMEM((2, C), f32),
            pltpu.VMEM((1, C), f32),
            pltpu.VMEM((1, C), f32),
            pltpu.VMEM((taps, 1, C), f32),
            pltpu.VMEM((2 * frames, width), bf16),
            pltpu.SMEM((group,), jnp.int32),
            pltpu.VMEM((2 * width, C), bf16),
            pltpu.VMEM((2 * width, C), f32),
            pltpu.VMEM((R, 4 * width), bf16),
            pltpu.VMEM((R, 4 * width), bf16),
            pltpu.VMEM((R, 2 * C), bf16),
            pltpu.VMEM((R, 5 * C), bf16),
            pltpu.VMEM((2, R, width), bf16),
            pltpu.VMEM((2, R, width), f32),
            pltpu.VMEM((R, width), bf16),
        ]
        + [pltpu.VMEM(m.shape, m.dtype) for m in made_first]
        + [
            pltpu.VMEM((2, R, C), f32),
            pltpu.VMEM((R, C), f32),
            pltpu.VMEM((R // frames, frames + 32, C), f32),
            pltpu.VMEM((R, C), f32),
            pltpu.VMEM((R // frames, frames + 32, C), f32),
            pltpu.VMEM((taps, 8, C), f32),
            pltpu.VMEM((4, 8, C), f32),
        ]
        + [pltpu.VMEM(m.shape, m.dtype) for m in small_first]
        + [
            pltpu.VMEM((2**23 // 512, 128), f32),
            pltpu.SemaphoreType.DMA((n_send,)),
            pltpu.SemaphoreType.DMA((n_recv,)),
            pltpu.SemaphoreType.DMA((21,)),
            pltpu.SemaphoreType.DMA((1,)),
        ],
        compiler_params=pltpu.CompilerParams(
            collective_id=0, has_side_effects=True, vmem_limit_bytes=62 * 2**20
        ),
    )(*operands)

    gradients = [
        shape((group * frames, width), f32), shape((group * frames, width), f32), shape((5, 1, width), f32),
        shape((5, 1, width), f32), shape((2, width, width), f32), shape((2, width, width), f32),
        shape((4, width, C), f32), shape((2, C), f32), shape((C, width), f32), shape((2 * width, C), f32),
        shape((taps, 1, C), f32), shape((1, C), f32), shape((1, C), f32), shape((C, width), f32),
    ]
    given = (*ready, pa, pb, cs, lo, ig, table[1])
    outs = pl.pallas_call(
        last_kernel,
        out_shape=gradients,
        in_specs=[hbm] * len(given),
        out_specs=[hbm] * len(gradients),
        scratch_shapes=[pltpu.VMEM(m.shape, m.dtype) for m in given]
        + [pltpu.VMEM(m.shape, m.dtype) for m in gradients]
        + [pltpu.SemaphoreType.DMA((len(given),)), pltpu.SemaphoreType.DMA((len(gradients) + 4,))],
        compiler_params=pltpu.CompilerParams(vmem_limit_bytes=62 * 2**20),
    )(*given)
    if groups == 1:
        outs = list(outs[:2]) + [lax.psum(m.astype(bf16), DATA).astype(f32) for m in outs[2:]]
    (lo, ig, ng, nb, w_in, w_out, w_ain, pos, w_aout, w_cin, w_dw, bng, bns, w_cout) = outs
    rows = (1, group, frames, width)
    return (
        lo.reshape(rows), ig.reshape(rows), ng.transpose(1, 0, 2), nb.transpose(1, 0, 2), w_in[None], w_out[None],
        w_ain[None], pos[None], w_aout[None], w_cin.reshape(conv_in.shape), w_dw.transpose(1, 0, 2), bng, bns,
        w_cout[None],
    )


def solution(mesh):
    placed = (
        P(DATA, None, None),
        P(DATA),
        P(DATA, None, None),
        P(SECTION, None, None),
        P(SECTION, None, None),
        P(SECTION, None, None, TENSOR),
        P(SECTION, None, TENSOR, None),
        P(SECTION, None, None, TENSOR),
        P(SECTION, None, TENSOR),
        P(SECTION, TENSOR, None),
        P(SECTION, None, None, TENSOR),
        P(SECTION, None, TENSOR),
        P(SECTION, TENSOR),
        P(SECTION, TENSOR),
        P(SECTION, TENSOR, None),
    )
    return jax.shard_map(
        on_device,
        mesh=mesh,
        in_specs=placed,
        out_specs=(
            P(SECTION, DATA, None, None),
            P(SECTION, DATA, None, None),
            P(SECTION, None, None),
            P(SECTION, None, None),
            P(SECTION, None, None, TENSOR),
            P(SECTION, None, TENSOR, None),
            P(SECTION, None, None, TENSOR),
            P(SECTION, None, TENSOR),
            P(SECTION, TENSOR, None),
            P(SECTION, None, None, TENSOR),
            P(SECTION, None, TENSOR),
            P(SECTION, TENSOR),
            P(SECTION, TENSOR),
            P(SECTION, TENSOR, None),
        ),
        check_vma=False,
    )
```

```python
import math

import jax
import jax.numpy as jnp
import numpy as np
from jax import lax
from jax.experimental import pallas as pl
from jax.experimental.pallas import tpu as pltpu
from jax.sharding import PartitionSpec as P

HEAD = 64
EPSILON = 1e-05
MESH = pl.DeviceIdType.MESH
SECTION, TENSOR, DATA = "section", "tensor", "dp"
PLACE = (0, 2, 1, 3)
SMALL_ROWS = 48


def relative_at(groups):
    return 16 if groups > 1 else SMALL_ROWS


bf16, f32 = jnp.bfloat16, jnp.float32


def dot(left, right, left_dim=1, right_dim=0):
    return lax.dot_general(
        left, right, (((left_dim,), (right_dim,)), ((), ())), preferred_element_type=f32
    )


def position_rows(frames, width):
    offset = np.arange(2 * frames - 1, dtype=np.float32) - np.float32(frames - 1)
    rates = np.exp(
        np.arange(width // 2, dtype=np.float32) * np.float32(-2.0 * math.log(10000.0) / width)
    )
    angles = (offset[:, None] * rates[None, :]).astype(np.float32)
    table = np.stack([np.sin(angles), np.cos(angles)], -1).reshape(2 * frames - 1, width)
    blank = np.zeros((1, width), np.float32)
    return [jnp.asarray(np.concatenate([rows, blank]), bf16) for rows in (table[::-1], table)]


def layer_kernel(dims, *refs):
    T, width, dp, groups = dims
    C = width // 4
    (lengths, inputs, cot, ng_in, nb_in, fin, fout, ain, aout, cin, cout, pos_in, bng_in, bns_in, dw_in, e2_in) = refs[:16]
    (lo_out, ig_out, pa_out, pb_out, cs_out) = refs[16:21]
    (in_out, out_out, qkv_out, ao_out, ci_out, co_out) = refs[21:27]
    refs = refs[27:]
    (Win, Wout, Wqkv, Wr, Wo, Wci, Wco, R2, SM) = refs[:9]
    (H, XH, RS, X, G, ARR, HOP, QKV, PRB, GVG, CT, UP, DP) = refs[9:22]
    (SfSt, SbSt, PAst, PAb, PAin, PBst, PBin, STF, STB, RSst, RSin) = refs[22:33]
    (ng, nb, pos, bng, bns, dw, e2, lens, pairs, spread) = refs[33:43]
    (Nall, Ball, Sf, Sb, ACT, SLOPE, HG, gin, gout, gqkv, gao, gci, gco) = refs[43:56]
    GA, HATA, UA, DYA, DA, DWACC, INVA, OST, STL, VIA = refs[56:66]
    LO, IG, PA, PB, CS, dummy, ss, rs, ls, os = refs[66:76]
    gathered = groups > 1

    s, t, d = lax.axis_index(SECTION), lax.axis_index(TENSOR), lax.axis_index(DATA)
    first, second = s == 0, s == 1
    taps = dw.shape[0]
    peers = [(s, t ^ k, d) for k in range(4)]
    sib, yp = peers[1], peers[2]
    around = {j: lax.rem(d + j + dp, dp) for j in range(1 - dp, dp)}
    zpeers = [(s, t, around[r]) for r in range(dp)]
    zpair = (s, t, d ^ 1)
    partner = (1 - s, t, d)
    half = lax.rem(d, 2)
    R4 = 4 * T
    reach = range(1 - groups, groups)
    base_of = {j: pl.multiple_of(around[j] * R4, R4) if groups > 1 else 0 for j in reach}
    second_of, high_of, last_of = (
        {j: pl.multiple_of(around[j] * R4 + n * T, T) if groups > 1 else n * T for j in reach} for n in (1, 2, 3)
    )
    there = {j: d + j >= 0 if j < 0 else d + j <= dp - 1 for j in reach}
    through = {
        (j, to): there[j] & there[to] for j in reach for to in (1, -1) if j * to < 0 and groups > 1
    }
    base = base_of[0]
    trow, yrow = pl.multiple_of(t * T, T), pl.multiple_of((t ^ 2) * T, T)
    mine = d if groups > 1 else 0

    recv_index, send_index, sent = {}, {}, {}

    def size_of(view):
        return math.prod(view.shape) * view.dtype.itemsize

    def copy_of(key, src, dst, dev, group):
        i = recv_index.setdefault(key, len(recv_index))
        j = send_index.setdefault(id(group), len(send_index))
        return pltpu.make_async_remote_copy(
            src_ref=src, dst_ref=dst, send_sem=ss.at[j], recv_sem=rs.at[i], device_id=dev, device_id_type=MESH,
        )

    def start(key, src, dst, dev, cond=None, part=0):
        view = src()
        copy_of(key, view, dst(), dev, cond).start()
        sent.setdefault(id(cond), (cond, {}))[1][key, part] = size_of(view)

    def arrived(key, dst):
        copy_of(key, dst, dst, partner, None).wait_recv()

    def room(size):
        return dummy.at[pl.ds(0, size // (4 * dummy.shape[1]))]

    def all_arrived(key, size):
        if size:
            arrived(key, room(size))

    locals_ = {}

    def fetch(name, src, dst):
        locals_[name] = lambda: pltpu.make_async_copy(src(), dst(), ls.at[list(locals_).index(name)])
        locals_[name]().start()

    def fetched(*names):
        for name in names:
            locals_[name]().wait()

    @pl.when(first)
    def _():
        pltpu.make_async_copy(inputs.at[t], X.at[0], ls.at[20]).start()

    @pl.when(second)
    def _():
        pltpu.make_async_copy(cot.at[t], G, ls.at[20]).start()

    fetch("ng", lambda: ng_in, lambda: ng)
    fetch("nb", lambda: nb_in, lambda: nb)
    fetch("in0", lambda: fin.at[0], lambda: Win.at[0, 0])
    fetch("out0", lambda: fout.at[0], lambda: Wout.at[0, 0])
    fetch("wr", lambda: ain.at[3], lambda: Wr)
    fetch("e2", lambda: e2_in, lambda: e2)
    fetch("pos", lambda: pos_in, lambda: pos)
    fetch("bng", lambda: bng_in, lambda: bng)
    fetch("bns", lambda: bns_in, lambda: bns)
    fetch("dw", lambda: dw_in, lambda: dw)
    fetch("len", lambda: lengths, lambda: lens)
    fetch("qkv", lambda: ain.at[pl.ds(0, 3)], lambda: Wqkv.at[:, :, pl.ds(0, C)])
    fetch("o", lambda: aout, lambda: Wo.at[pl.ds(0, C)])
    fetch("ci", lambda: cin, lambda: pairs)
    fetch("co", lambda: cout, lambda: Wco.at[pl.ds(0, C)])
    fetch("in1", lambda: fin.at[1], lambda: Win.at[1, 0])
    fetch("out1", lambda: fout.at[1], lambda: Wout.at[1, 0])

    barrier = pltpu.get_barrier_semaphore()
    greet = peers[1:] + zpeers[1:] + [partner]
    for dev in greet:
        pl.semaphore_signal(barrier, inc=1, device_id=dev, device_id_type=MESH)
    pl.semaphore_wait(barrier, len(greet))

    starts = {}

    def lines(first_row, n, which):
        if which is None:
            return pl.ds(first_row, n)
        at = (first_row, n, which)
        if at not in starts:
            starts[at] = pl.multiple_of(first_row + n // 2 * (half if which == "own" else 1 - half), n // 2)
        return pl.ds(starts[at], n // 2)

    def cols(k):
        return pl.ds(C * k, C)

    def feed_chunks(j):
        Q = width // 2
        return [
            (
                lambda w, src=src, q=q: src.at[j, lines(Q * q, Q, w)],
                lambda k, w, dst=dst, q=q: dst.at[j, k, lines(Q * q, Q, w)],
            )
            for src, dst in ((fin, Win), (fout, Wout))
            for q in range(2)
        ]

    def row_chunk(src, dst):
        return [(lambda w: src.at[lines(0, C, w)], lambda k, w: dst.at[lines(C * k, C, w)])]

    def column_chunks(src, dst, n):
        return [
            (lambda w, i=i: src(i, lines(0, width, w)), lambda k, w, i=i: dst.at[i, lines(0, width, w), cols(k)])
            for i in range(n)
        ]

    chunks = (
        feed_chunks(0)
        + column_chunks(lambda i, rows: ain.at[i, rows], Wqkv, 3)
        + row_chunk(aout, Wo)
        + column_chunks(lambda i, rows: Wci.at[i, rows, cols(0)], Wci, 2)
        + row_chunk(cout, Wco)
        + feed_chunks(1)
        + [
            (lambda w: SM.at[:, cols(0)], lambda k, w: SM.at[:, cols(k)]),
            (lambda w: R2.at[pl.ds(0, 2 * T), cols(0)], lambda k, w: R2.at[pl.ds(0, 2 * T), cols(k)]),
        ]
    )
    for n, at in ((width // 2, 0), (width // 2, width // 2), (width, 0)) + tuple((C, C * k) for k in range(4)):
        for w in ("own", "other"):
            lines(at, n, w)
    only = {i: second for i in range(4)}
    over_y = {i: "own" for i in range(14)}

    def send_core(names):
        for i in names:
            src, dst = chunks[i]
            start(("sib", i), lambda src=src: src(None), lambda dst=dst: dst(1, None), sib)

    def send_y(names):
        for i in names:
            (src, dst), w = chunks[i], over_y.get(i)
            cond = first if i == 13 else only.get(i)
            start(("y", i), lambda src=src, w=w: src(w), lambda dst=dst, w=w: dst(2, w), yp, cond)

    def send_round():
        start(("r", 0), lambda: chunks[13][0]("own"), lambda: VIA.at[0], partner, second)

    def pass_round(n):
        arrived(("r", n - 1), VIA.at[n - 1])
        if n == 1:
            start(("r", 1), lambda: VIA.at[0], lambda: VIA.at[1], yp, first)
        else:
            start(("r", 2), lambda: VIA.at[1], lambda: chunks[13][1](2, "own"), partner, first)

    def step_a(i, by="y"):
        dst, w = chunks[i][1], over_y.get(i)
        arrived(("r", 2) if by == "r" else ("y", i), dst(2, w))
        if w:
            start(("z", i), lambda: dst(2, w), lambda: dst(2, w), zpair, only.get(i))
        start(("on", i), lambda: dst(2, w), lambda: dst(3, w), sib, only.get(i), 1)

    def step_b(i):
        if i not in over_y:
            return
        dst = chunks[i][1]
        arrived(("z", i), dst(2, "other"))
        start(("on", i), lambda: dst(2, "other"), lambda: dst(3, "other"), sib, only.get(i), 2)

    def core_part(i):
        arrived(("sib", i), chunks[i][1](1, None))

    def passed_part(i):
        all_arrived(("on", i), size_of(chunks[i][1](1, None)))

    def step_c(i):
        core_part(i)
        passed_part(i)

    def steps(cond, *plan):
        @pl.when(cond)
        def _():
            for step, i in plan:
                step(i)

    A, B, W = step_a, step_b, step_c

    def norm(i, x):
        centre = x - jnp.mean(x, -1, keepdims=True)
        rate = lax.rsqrt(jnp.mean(centre * centre, -1, keepdims=True) + EPSILON)
        hat = centre * rate
        XH[i] = hat
        RS[i] = jnp.broadcast_to(rate, RS.shape[1:])
        return hat * ng[i] + nb[i]

    def norm_back(i, grad):
        hat = XH[i]
        PBst[i : i + 1] = jnp.sum(grad * hat, 0, keepdims=True)
        PBst[8 + i : 9 + i] = jnp.sum(grad, 0, keepdims=True)
        g = grad * ng[i]
        return RS[i][:, 0:1] * (
            g - jnp.mean(g, -1, keepdims=True) - hat * jnp.mean(g * hat, -1, keepdims=True)
        )

    def total_of(v):
        return jnp.sum(v, 0, keepdims=True)

    def silu(h):
        return h * jax.nn.sigmoid(h)

    def place(k):
        return pl.ds(base + T * PLACE[k], T)

    own, two = pl.ds(base, T), pl.ds(base, 2 * T)

    def block(i, n=1):
        return pl.ds(i * width, n * width)

    def from_tensor(name, ref, c):
        all_arrived(name, 3 * size_of(ref.at[own, c]))

    def to_pair(name, ref, c, cond=None):
        start(name, lambda: ref.at[own, c], lambda: ref.at[place(1), c], sib, cond, 4)
        start((name, 4), lambda: ref.at[own, c], lambda: ref.at[place(2), c], yp, cond)

    def relay(name, ref, c, cond=None):
        arrived((name, 4), ref.at[place(2), c])
        start(name, lambda: ref.at[place(2), c], lambda: ref.at[place(3), c], sib, cond, 5)

    def from_pair(name, ref, c):
        all_arrived(name, 2 * size_of(ref.at[own, c]))

    def feed(j, i, before, after):
        x = X[before]
        a = norm(i, x).astype(bf16)
        Nall[own, i * width : (i + 1) * width] = a
        to_pair(("n", i), Nall, block(i))
        if j:
            step_c(11)
            step_c(12)
        active = []
        for k in range(4):
            h = dot(a, Win[j, k])
            H[j, k] = h
            active.append(silu(h).astype(bf16))
        Q, total = width // 2, 0.0
        for q in range(2):
            if j:
                step_c(13 + q)
            for k in range(4):
                total += dot(active[k][:, Q * q : Q * (q + 1)], Wout[j, k, Q * q : Q * (q + 1)])
        X[after] = x + 0.5 * total

    def sum_to_owner(name, slot, total):
        RSst[slot] = total[T : 2 * T].astype(bf16)
        start(name, lambda: RSst.at[slot], lambda: RSin.at[slot], yp, first)
        return total[0:T]

    def summed_here(name, slot, total):
        arrived(name, RSin.at[slot])
        return total + RSin[slot].astype(f32)

    def shared_feed(j, i):
        relay(("n", i), Nall, block(i))
        a = Nall[two, i * width : (i + 1) * width]
        total = dot(silu(dot(a, Win[j, 0])).astype(bf16), Wout[j, 0])
        for k in range(11 * j, 11 * j + 4):
            core_part(k)
        total += dot(silu(dot(a, Win[j, 1])).astype(bf16), Wout[j, 1])
        return sum_to_owner(("s", j), j, total)

    fetched("ng", "nb")

    @pl.when(first)
    def _():
        pltpu.make_async_copy(inputs.at[t], X.at[0], ls.at[20]).wait()
        Nall[own, 0:width] = norm(0, X[0]).astype(bf16)
        to_pair(("n", 0), Nall, block(0))

    send_core(range(4))

    @pl.when(second)
    def _():
        send_round()
        send_y(range(4))
        pltpu.make_async_copy(cot.at[t], G, ls.at[20]).wait()

    fetched("pos", "bng", "bns", "dw", "wr", "e2", "len", "ci")
    spread[...] = pairs[...].astype(f32)
    for i in range(2):
        Wci[i, :, 0:C] = spread[pl.ds(i, width, stride=2), :].astype(bf16)
    SM[:, 0:C] = jnp.zeros((SMALL_ROWS, C), f32)
    SM[0:2, 0:C] = pos[...]
    SM[2:3, 0:C] = bng[...]
    SM[3:4, 0:C] = bns[...]
    for k in range(taps):
        SM[4 + k : 5 + k, 0:C] = dw[k]
    R2[0 : 2 * T, 0:C] = dot(e2[...], Wr[...]).astype(bf16)
    lengths_here = [jnp.broadcast_to(lens[t ^ PLACE[p]].astype(f32), (1, C)) for p in range(4)]
    STL[d] = jnp.concatenate(lengths_here + [jnp.zeros((4, C), f32)], 0)
    for r in range(1, dp):
        start("len", lambda: STL.at[d], lambda: STL.at[d], zpeers[r], None, r)
    fetched("in0", "out0")

    @pl.when(first)
    def _():
        send_core((15, 16, 4, 5, 6, 7, 8, 9, 10))
        send_y((8,))
        X[1] = shared_feed(0, 0)
        send_y((9,))

    @pl.when(first)
    def _():
        step_a(8)
        X[1] = X[0] + 0.5 * summed_here(("s", 0), 0, X[1])

    @pl.when(second)
    def _():
        for i in (15, 16, *range(4, 15)):
            send_core((i,))
            if i != 13:
                send_y((i,))

    fetched("qkv", "o", "co", "in1", "out1")
    margin = 16
    UP[...] = jnp.zeros(UP.shape, f32)
    DP[...] = jnp.zeros(DP.shape, f32)
    PAst[...] = jnp.zeros(PAst.shape, f32)
    PBst[...] = jnp.zeros(PBst.shape, f32)
    CS[...] = jnp.zeros(CS.shape, f32)
    if gathered:
        DA[...] = jnp.zeros(DA.shape, f32)
        DWACC[...] = jnp.zeros(DWACC.shape, f32)

    def keys_of(length):
        return lax.broadcasted_iota(jnp.int32, (2 * T, T), 1) < length

    row_mask = (lax.broadcasted_iota(jnp.int32, (T, 1), 0) < lens[t]).astype(f32)
    first_head = lax.broadcasted_iota(jnp.int32, (T, 2 * HEAD), 1) < HEAD
    flip = (
        lax.broadcasted_iota(jnp.int32, (T, 4 * T), 0) + lax.broadcasted_iota(jnp.int32, (T, 4 * T), 1)
        == T - 1
    ).astype(f32).astype(bf16)

    def pair_rows(v):
        return jnp.concatenate([jnp.where(first_head, v, 0.0), jnp.where(first_head, 0.0, v)], 0)

    def unpair(v):
        return jnp.where(first_head, v[:T], v[T:])

    def attend(qu, qv, key, value, relative, keys):
        content = dot(pair_rows(qu).astype(bf16), key, 1, 1)
        whole = dot(pair_rows(qv).astype(bf16), jnp.concatenate([relative, jnp.zeros_like(relative)], 0), 1, 1)
        placed = jnp.concatenate(
            [
                pltpu.roll(whole[e * T : (e + 1) * T], 4 * T - (T - 1), 1, stride=1, stride_axis=0)[:, :T]
                for e in range(2)
            ],
            0,
        )
        scores = jnp.where(keys, (content + placed) * HEAD ** (-0.5), -1e30)
        e = jnp.exp(scores - jnp.max(scores, -1, keepdims=True))
        probs = e / jnp.sum(e, -1, keepdims=True)
        return probs, unpair(dot(probs.astype(bf16), value)).astype(bf16)

    def attention_here():
        a = Nall[own, width : 2 * width]
        q = dot(a, Wqkv[0])
        QKV[0] = q + SM[0:1]
        QKV[1] = q + SM[1:2]
        QKV[2] = dot(a, Wqkv[1])
        QKV[3] = dot(a, Wqkv[2])
        keys, mixed = keys_of(lens[t]), []
        for p in range(4):
            c = pl.ds(2 * HEAD * p, 2 * HEAD)
            probs, out = attend(
                QKV[0, :, c], QKV[1, :, c], QKV[2, :, c].astype(bf16), QKV[3, :, c].astype(bf16), R2[0 : 2 * T, c], keys
            )
            PRB[p] = probs
            mixed.append(out)
        return mixed

    def shared_attention():
        for i in (4, 5, 6, 15, 16):
            core_part(i)
        a = Nall[two, width : 2 * width]
        q, key, value = (dot(a, Wqkv[i, :, 0 : 2 * C]) for i in range(3))
        qu, qv, key, value = q + SM[0:1, 0 : 2 * C], q + SM[1:2, 0 : 2 * C], key.astype(bf16), value.astype(bf16)
        mixed = [[], []]
        for p in range(2):
            rows, keys = slice(T * p, T * (p + 1)), keys_of(lens[t ^ PLACE[p]])
            for k in range(2):
                c = slice(C * k, C * (k + 1))
                mixed[k].append(
                    attend(qu[rows, c], qv[rows, c], key[rows, c], value[rows, c], R2[0 : 2 * T, c], keys)[1]
                )
        mixed = [jnp.concatenate(m, 0) for m in mixed]
        Sf[two, 0:C] = mixed[0]
        OST[...] = mixed[1]
        start("sf", lambda: OST, lambda: Sf.at[pl.ds(high_of[0], 2 * T), pl.ds(0, C)], sib, first, 4)
        core_part(7)
        return sum_to_owner(("s", 3), 3, dot(mixed[0], Wo[0:C]) + dot(mixed[1], Wo[C : 2 * C]))

    def relative_arrived():
        passed_part(16)
        turned_back = (
            lax.broadcasted_iota(jnp.int32, (2 * T, 2 * T), 0) + lax.broadcasted_iota(jnp.int32, (2 * T, 2 * T), 1)
            == 2 * T - 2
        ).astype(f32).astype(bf16)
        R2[2 * T : 4 * T] = dot(turned_back, R2[0 : 2 * T]).astype(bf16)


    @pl.when(first)
    def _():
        Nall[own, width : 2 * width] = norm(1, X[1]).astype(bf16)
        to_pair(("n", 1), Nall, block(1))
        send_y((15,))
        pass_round(1)
        send_y((10,))
        step_a(9)
        step_b(8)
        relay(("n", 1), Nall, block(1))
        total = shared_attention()
        send_y((4, 5, 6, 16, 7))
        step_a(15)
        step_b(9)
        X[2] = X[1] + summed_here(("s", 3), 3, total)
        pass_round(2)
        step_a(10)
        passed_part(15)

    @pl.when(second)
    def _():
        coming = (*range(4), 15, 16, *range(4, 14))
        for n, i in enumerate(coming):
            step_a(i, "r" if i == 13 else "y")
            if n > 1 and i != 13:
                step_b(coming[n - 2])
        for i in range(7):
            step_c(i)
        step_c(15)
        core_part(16)
        relative_arrived()
        arrived("hop", ARR)
        X[0] = ARR[...].astype(f32)
        feed(0, 0, 0, 1)
        Nall[own, width : 2 * width] = norm(1, X[1]).astype(bf16)
        to_pair(("n", 1), Nall, block(1))
        step_b(11)
        mixed = attention_here()
        step_b(12)
        for k in range(4):
            SfSt[k, :, 0:C] = mixed[k]
        step_c(7)
        X[2] = X[1] + dot(jnp.concatenate(mixed, 1), Wo[...])

    def line_start(name, region):
        for way, to, back in (("up", 1, -1), ("down", -1, 1)):
            if groups > 1:

                @pl.when(there[to])
                def _():
                    start(
                        (name, 0, back % dp), lambda: region(0), lambda: region(0), (s, t, around[to]), there[to], way
                    )

    def line_hop(name, region, n, after=None):
        for way, to, back in (("up", 1, -1), ("down", -1, 1)):
            if n < groups:

                @pl.when(there[back * n])
                def _():
                    j = back * n
                    arrived((name, 0, j % dp), region(j))
                    if n + 1 < groups:

                        @pl.when(there[to])
                        def _():
                            start(
                                (name, 0, (j + back) % dp), lambda: region(j), lambda: region(j),
                                (s, t, around[to]), through[j, to], way,
                            )

                    if after is not None:
                        after(name, j)

    def rows_region(ref, n, c):
        return lambda j: ref.at[pl.ds(base_of[j], n), c]

    def share(ref, c):
        def go(name, j):
            rows = lambda: ref.at[pl.ds(base_of[j], T), c]
            start((name, 1, j % dp), rows, lambda: ref.at[pl.ds(second_of[j], T), c], yp, there[j], j)
            start((name, 2, 0), rows, lambda: ref.at[pl.ds(high_of[j], T), c], sib, there[j], j)

        return go

    def share_on(name, ref, c, n):
        for j in (n, -n):
            if n < groups:

                @pl.when(there[j])
                def _():
                    rows = lambda: ref.at[pl.ds(second_of[j], T), c]
                    arrived((name, 1, j % dp), rows())
                    start((name, 2, 0), rows, lambda: ref.at[pl.ds(last_of[j], T), c], sib, there[j], dp + j)

    def shared(name, ref, c):
        all_arrived((name, 2, 0), 2 * (groups - 1) * size_of(ref.at[own, c]))

    def set_off_to_all(name):
        ref, c = whole_rows(name)
        mine = lambda: ref.at[own, c]
        for r in range(1, groups):
            start((name, 0, (-r) % dp), mine, mine, zpeers[r], None, r)

    def from_all(name):
        ref, c = whole_rows(name)
        for r in range(1, groups):
            rows = lambda r=r: ref.at[pl.ds(base_of[r], T), c]
            arrived((name, 0, r), rows())
            start((name, 1, r), rows, lambda r=r: ref.at[pl.ds(second_of[r], T), c], yp, None, r)
            start((name, 2, 0), rows, lambda r=r: ref.at[pl.ds(high_of[r], T), c], sib, None, r)

    def hand_on_all(name):
        ref, c = whole_rows(name)
        for r in range(1, groups):
            rows = lambda r=r: ref.at[pl.ds(second_of[r], T), c]
            arrived((name, 1, r), rows())
            start((name, 2, 0), rows, lambda r=r: ref.at[pl.ds(last_of[r], T), c], sib, None, dp + r)

    def all_shared(*names):
        for name in names:
            shared(name, *whole_rows(name))

    sf_cols = pl.ds(0, C if gathered else 2 * C)
    qkv_cols, gate_cols = pl.ds(0, 3 * C), pl.ds(3 * C, 2 * C)
    lines_of = {
        "n": (rows_region(Nall, T, block(0, 3)), share(Nall, block(0, 3))),
        "m": (rows_region(Nall, T, block(3)), share(Nall, block(3))),
        "sf": (rows_region(Sf, R4, sf_cols), None),
        "qkv": (rows_region(Sb, R4, qkv_cols), None),
    }
    for i in range(4):
        lines_of["b", i] = (rows_region(Ball, T, block(i)), share(Ball, block(i)))

    def set_off(*names):
        for name in names:
            line_start(name, lines_of[name][0])

    def hop(n, *names):
        for name in names:
            line_hop(name, lines_of[name][0], n, lines_of[name][1])

    def whole_rows(name):
        if name in ("n", "m"):
            return Nall, block(0, 3) if name == "n" else block(3)
        return Ball, block(name[1])

    def hand_on(n, *names):
        for name in names:
            share_on(name, *whole_rows(name), n)

    written = []

    def write(src, dst):
        pltpu.make_async_copy(src, dst, os.at[0]).start()
        written.append(size_of(src))

    R = Nall.shape[0]
    row_blocks = [slice(r, r + R4) for r in range(0, R, R4)]

    def slope(h, sig):
        return sig * (1.0 + h * (1.0 - sig))

    def hidden_rows(j, i):
        for rows in row_blocks:
            h = dot(Nall[rows, i * width : (i + 1) * width], Win[j, 0])
            sig = jax.nn.sigmoid(h)
            ACT[j, rows] = (h * sig).astype(bf16)
            SLOPE[j, rows] = slope(h, sig)

    def feed_grads(j, i):
        c = slice(i * width, (i + 1) * width)
        for rows in row_blocks:
            HG[rows] = (dot(Ball[rows, c], Wout[j, 0], 1, 1) * SLOPE[j, rows]).astype(bf16)
        gin[j] = dot(Nall[:, c], HG[...], 0, 0).astype(bf16)
        write(gin.at[j], in_out.at[j])
        gout[j] = dot(ACT[j], Ball[:, c], 0, 0).astype(bf16)
        write(gout.at[j], out_out.at[j])

    def mask_of(g, p):
        return (lax.broadcasted_iota(jnp.int32, (T, C), 0).astype(f32) < STL[g, p : p + 1]).astype(f32)

    places = [(p, [(g, slice(R4 * g + T * p, R4 * g + T * (p + 1))) for g in range(groups)]) for p in range(4)]

    def convolution_rows():
        for i in range(2):
            GA[i] = dot(Nall[:, 2 * width : 3 * width], Wci[i, :, 0:C])
        UA[...] = jnp.zeros(UA.shape, f32)
        for p, parts in places:
            for g, rows in parts:
                UA[4 * g + p, margin : margin + T] = GA[0, rows] * jax.nn.sigmoid(GA[1, rows]) * mask_of(g, p)

        def one(b, carry):
            acc = SM[4:5, 0:C] * UA[b, margin - taps // 2 : margin - taps // 2 + T]
            for k in range(1, taps):
                o = margin - taps // 2 + k
                acc += SM[4 + k : 5 + k, 0:C] * UA[b, o : o + T]
            HATA[pl.ds(b * T, T)] = acc
            return carry

        lax.fori_loop(0, 4 * groups, one, 0)
        for p, parts in places:
            n = sum(STL[g, p : p + 1] for g, _ in parts)
            masked = [HATA[rows] * mask_of(g, p) for g, rows in parts]
            mean = sum(total_of(m) for m in masked) / n
            square = sum(total_of(m * HATA[rows]) for m, (_, rows) in zip(masked, parts)) / n
            inv = lax.rsqrt(square - mean * mean + EPSILON)
            INVA[p, 0:1] = inv
            INVA[p, 1:2] = n
            for g, rows in parts:
                h = (HATA[rows] - mean) * inv
                HATA[rows] = h
                Sf[rows, C : 2 * C] = silu(h * SM[2:3, 0:C] + SM[3:4, 0:C]).astype(bf16)

    def convolution_rows_back():
        DYA[...] = dot(Ball[:, 2 * width : 3 * width], Wco[0:C], 1, 1)
        gain_sum = shift_sum = jnp.zeros((1, C), f32)
        for p, parts in places:
            first_sum = second_sum = jnp.zeros((1, C), f32)
            for g, rows in parts:
                h = HATA[rows]
                y = h * SM[2:3, 0:C] + SM[3:4, 0:C]
                dy = DYA[rows] * slope(y, jax.nn.sigmoid(y))
                gain_sum += total_of(dy * h)
                shift_sum += total_of(dy)
                dh = dy * SM[2:3, 0:C]
                DYA[rows] = dh
                dh = dh * mask_of(g, p)
                first_sum += total_of(dh)
                second_sum += total_of(dh * h)
            inv, n = INVA[p, 0:1], INVA[p, 1:2]
            for g, rows in parts:
                dc = inv * (DYA[rows] - (first_sum + HATA[rows] * second_sum) / n) * mask_of(g, p)
                DA[4 * g + p, margin : margin + T] = dc
        CS[taps : taps + 1] = gain_sum
        CS[taps + 1 : taps + 2] = shift_sum

        def one(b, carry):
            here = DA[b, margin : margin + T]
            acc = jnp.zeros((T, C), f32)
            for k in range(taps):
                o = margin + taps // 2 - k
                acc += SM[4 + k : 5 + k, 0:C] * DA[b, o : o + T]
                o = margin - taps // 2 + k
                term = here * UA[b, o : o + T]
                DWACC[k] += sum(term[8 * i : 8 * (i + 1)] for i in range(T // 8))
            DYA[pl.ds(b * T, T)] = acc
            return carry

        lax.fori_loop(0, 4 * groups, one, 0)
        for k in range(taps):
            CS[k : k + 1] = total_of(DWACC[k])
        for p, parts in places:
            for g, rows in parts:
                sig = jax.nn.sigmoid(GA[1, rows])
                dua = DYA[rows] * mask_of(g, p)
                Sb[rows, 3 * C : 4 * C] = (dua * sig).astype(bf16)
                Sb[rows, 4 * C : 5 * C] = (dua * GA[0, rows] * (sig * (1.0 - sig))).astype(bf16)

    def convolution_grads():
        gci[...] = dot(Nall[:, 2 * width : 3 * width], Sb[:, 3 * C : 5 * C], 0, 0).astype(bf16)
        write(gci, ci_out)
        gco[...] = dot(Sf[:, C : 2 * C], Ball[:, 2 * width : 3 * width], 0, 0).astype(bf16)
        write(gco, co_out)

    def attention_grads():
        grads = dot(Nall[:, width : 2 * width], Sb[:, 0 : 3 * C], 0, 0)
        for i in range(3):
            gqkv[i] = grads[:, C * i : C * (i + 1)].astype(bf16)
        write(gqkv, qkv_out)
        gao[...] = dot(Sf[:, 0:C], Ball[:, width : 2 * width], 0, 0).astype(bf16)
        write(gao, ao_out)

    def forward_values():
        hidden_rows(1, 3)
        hidden_rows(0, 0)
        if gathered:
            convolution_rows()

    a = norm(2, X[2]).astype(bf16)
    Nall[own, 2 * width : 3 * width] = a
    to_pair(("n", 2), Nall, block(2))

    step_c(8)
    step_c(9)
    GVG[0] = dot(a, Wci[0])
    GVG[1] = dot(a, Wci[1])
    UP[margin : margin + T] = GVG[0] * jax.nn.sigmoid(GVG[1]) * row_mask
    for p in range(4):
        c = pl.ds(C * p, C)
        acc = SM[4:5, c] * UP[margin - taps // 2 : margin - taps // 2 + T, c]
        for k in range(1, taps):
            o = margin - taps // 2 + k
            acc += SM[4 + k : 5 + k, c] * UP[o : o + T, c]
        CT[:, c] = acc
    conv = CT[...]

    def dp_sums(name, ref, rows):
        ref[d] = jnp.concatenate([row[:, C * k : C * (k + 1)] for row in rows for k in range(4)], 0)
        for r in range(1, dp):
            start(name, lambda: ref.at[d], lambda: ref.at[d], zpeers[r], None, r)

    def summed(name, ref):
        all_arrived(name, (dp - 1) * size_of(ref.at[0]))
        total = ref[0]
        for r in range(1, dp):
            total += ref[r]
        return [jnp.concatenate([total[4 * i + k : 4 * i + k + 1] for k in range(4)], 1) for i in range(2)]

    masked = conv * row_mask
    dp_sums("bnf", STF, [total_of(masked), total_of(masked * conv)])
    steps(second, (A, 14))
    steps(first, (B, 10))
    step_c(10)
    sums = summed("bnf", STF)
    steps(second, (B, 13))
    steps(first, (A, 4), (A, 5), (A, 6), (A, 16))

    @pl.when(second)
    def _():
        set_off("n")
    all_arrived("len", (dp - 1) * size_of(STL.at[0]))
    count = sum(STL[r, 0:1, 0:1] for r in range(dp))
    bn_mean = sums[0] / count
    inv_std = lax.rsqrt(sums[1] / count - bn_mean * bn_mean + EPSILON)
    hat = (conv - bn_mean) * inv_std
    CT[...] = hat
    active = silu(hat * SM[2:3] + SM[3:4]).astype(bf16)
    if not gathered:
        for k in range(4):
            SfSt[k, :, C : 2 * C] = active[:, C * k : C * (k + 1)]
    X[3] = X[2] + dot(active, Wco[...])

    @pl.when(first)
    def _():
        Nall[own, 3 * width : 4 * width] = norm(3, X[3]).astype(bf16)
        to_pair(("n", 3), Nall, block(3))
        send_core((11, 12, 13, 14))
        total = shared_feed(1, 3)
        send_y((11, 12, 13, 14))
        step_a(7)
        step_b(4)
        step_b(5)
        X[4] = X[3] + 0.5 * summed_here(("s", 1), 1, total)

    @pl.when(second)
    def _():
        feed(1, 3, 3, 4)
    out = (norm(4, X[4]) * row_mask).astype(bf16)
    HOP[...] = out

    @pl.when(first)
    def _():
        start("hop", lambda: HOP, lambda: ARR, partner, first)

    LO[pl.ds(trow, T)] = out
    def output_to_pair(name, ref):
        rows = lambda: ref.at[pl.ds(trow, T)]
        start(name, rows, rows, sib)
        start((name, 4), rows, rows, yp)

    def relay_output(name, ref):
        rows = lambda: ref.at[pl.ds(yrow, T)]
        arrived((name, 4), rows())
        start(name, rows, rows, sib, None, 1)

    output_to_pair("out", LO)

    for cond, c in ((first, pl.ds(C, C)), (second, sf_cols))[gathered:]:

        @pl.when(cond)
        def _():
            Sf[own, c] = SfSt[0, :, c]
            for k in (1, 2, 3):
                start("sf", lambda k=k: SfSt.at[k, :, c], lambda k=k: Sf.at[place(k), c], peers[k], cond, k)

    @pl.when(first)
    def _():
        set_off("n", "m")
        if gathered:
            all_arrived("sf", size_of(OST))
            set_off("sf")
        relay(("n", 2), Nall, block(2))
        step_a(11)
        for i in (6, 7):
            step_b(i)
        step_a(12)
        step_b(11)
        for i in (4, 5, 6, 7):
            passed_part(i)
        relative_arrived()
        attention_here()
        step_a(13)
        step_b(12)
        if not gathered:
            all_arrived("sf", size_of(OST) + 3 * size_of(Sf.at[own, pl.ds(C, C)]))
        step_a(14)
        hop(1, "n", "m", "sf")
        step_b(13)
        for i in range(11, 15):
            passed_part(i)
        for k in range(4):
            H[1, k] = dot(Nall[own, 3 * width : 4 * width], Win[1, k])
        hop(2, "n", "m", "sf")
        hand_on(1, "n", "m")
        hop(3, "n", "m", "sf")
        hand_on(2, "n", "m")

    @pl.when(first)
    def _():
        arrived("back", ARR)
        G[...] = ARR[...].astype(f32)

    back_rows = lambda: IG.at[pl.ds(trow, T)]

    def feed_back(j, i, g):
        b = (0.5 * g).astype(bf16)
        Ball[own, i * width : (i + 1) * width] = b
        to_pair(("b", i), Ball, block(i))
        if j:
            set_off(("b", i))
        grad = None
        for k in range(4):
            h = H[j, k]
            sig = jax.nn.sigmoid(h)
            hg = (dot(b, Wout[j, k], 1, 1) * slope(h, sig)).astype(bf16)
            part = dot(hg, Win[j, k], 1, 1)
            grad = part if grad is None else grad + part
        return g + norm_back(i, grad)
    g = norm_back(4, G[...] * row_mask)
    g = feed_back(1, 3, g)
    b = g.astype(bf16)
    Ball[own, 2 * width : 3 * width] = b
    to_pair(("b", 2), Ball, block(2))
    hat = CT[...]
    y = hat * SM[2:3] + SM[3:4]
    sig = jax.nn.sigmoid(y)
    dy = dot(b, Wco[...], 1, 1) * slope(y, sig)
    if not gathered:
        PAst[2:3] = total_of(dy * hat)
        PAst[3:4] = total_of(dy)
    dhat = dy * SM[2:3]
    masked = dhat * row_mask
    dp_sums("bnb", STB, [total_of(masked), total_of(masked * hat)])

    @pl.when(first)
    def _():
        hand_on(3, "n", "m")
        for i in range(4):
            from_pair(("n", i), Nall, block(i))
        all_shared("n", "m")
        forward_values()
        hop(1, ("b", 3))

    relay(("b", 3), Ball, block(3))
    sums = summed("bnb", STB)

    @pl.when(second)
    def _():
        for i in range(4):
            relay(("n", i), Nall, block(i))
        hop(1, "n")
        set_off("m")
        from_tensor("sf", Sf, sf_cols)
        set_off("sf")

    relay_output("out", LO)
    relay(("b", 2), Ball, block(2))
    set_off_to_all(("b", 2))
    dc = inv_std * (dhat - (sums[0] + hat * sums[1]) / count) * row_mask
    DP[margin : margin + T] = dc
    for p in range(4):
        c = pl.ds(C * p, C)
        here = DP[margin : margin + T, c]
        acc = None
        for k in range(taps):
            o = margin + taps // 2 - k
            term = SM[4 + k : 5 + k, c] * DP[o : o + T, c]
            acc = term if acc is None else acc + term
            if not gathered:
                o = margin - taps // 2 + k
                PAst[4 + k : 5 + k, c] = total_of(here * UP[o : o + T, c])
        CT[:, c] = acc
    du = CT[...] * row_mask
    sig = jax.nn.sigmoid(GVG[1])
    dvalue = (du * sig).astype(bf16)
    dgate = (du * GVG[0] * (sig * (1.0 - sig))).astype(bf16)
    def sb_to_tensor(name, c, k):
        start(name, lambda: SbSt.at[k, :, c], lambda: Sb.at[place(k), c], peers[k], None, k)

    if not gathered:
        for k in range(4):
            SbSt[k, :, 3 * C : 4 * C] = dvalue[:, C * k : C * (k + 1)]
            SbSt[k, :, 4 * C : 5 * C] = dgate[:, C * k : C * (k + 1)]
        Sb[own, 3 * C : 5 * C] = SbSt[0, :, 3 * C : 5 * C]
        for k in (1, 2, 3):
            sb_to_tensor("gates", gate_cols, k)
    g = g + norm_back(2, dot(dvalue, Wci[0], 1, 1) + dot(dgate, Wci[1], 1, 1))
    b = g.astype(bf16)
    Ball[own, width : 2 * width] = b
    to_pair(("b", 1), Ball, block(1))
    set_off(("b", 1))
    dmix = dot(b, Wo[...], 1, 1).astype(bf16).astype(f32)
    scale = HEAD ** (-0.5)
    dq, dk, dv = [None] * 4, [None] * 4, [None] * 4
    for p in (2, 3, 1, 0):
        c = pl.ds(2 * HEAD * p, 2 * HEAD)
        qu = pair_rows(QKV[0, :, c]).astype(bf16)
        qv = pair_rows(QKV[1, :, c]).astype(bf16)
        key = QKV[2, :, c].astype(bf16)
        val = QKV[3, :, c].astype(bf16)
        do = pair_rows(dmix[:, 2 * HEAD * p : 2 * HEAD * (p + 1)]).astype(bf16)
        probs = PRB[p]
        dprob = dot(do, val, 1, 1)
        ds = (probs * (dprob - jnp.sum(probs * dprob, -1, keepdims=True))).astype(bf16)
        du_rows = unpair(dot(ds, key)) * scale
        turned = dot(ds, flip)
        whole = jnp.concatenate(
            [
                pltpu.roll(turned[e * T : (e + 1) * T], 0, 1, stride=1, stride_axis=0)[:, : 2 * T]
                for e in range(2)
            ],
            0,
        ).astype(bf16)
        dv_rows = unpair(dot(whole, R2[2 * T : 4 * T, c])) * scale
        dk[p] = (dot(ds, qu, 0, 0) * scale).astype(bf16)
        dv[p] = dot(probs.astype(bf16), do, 0, 0).astype(bf16)
        dq[p] = (du_rows + dv_rows).astype(bf16)
        SbSt[p, :, 0:C] = dq[p]
        SbSt[p, :, C : 2 * C] = dk[p]
        SbSt[p, :, 2 * C : 3 * C] = dv[p]
        if p:
            sb_to_tensor("qkv", qkv_cols, p)
        PAst[0:1, c] = total_of(du_rows)
        PAst[1:2, c] = total_of(dv_rows)
        PAst[relative_at(groups) : relative_at(groups) + 2 * T, c] = dot(whole, qv, 0, 0) * scale
    Sb[own, 0 : 3 * C] = SbSt[0, :, 0 : 3 * C]
    @pl.when(first)
    def _():
        if not gathered:
            from_tensor("gates", Sb, gate_cols)
        hop(2, ("b", 3))
        relay(("b", 1), Ball, block(1))
    grad = dot(jnp.concatenate(dq, 1), Wqkv[0], 1, 1)
    grad += dot(jnp.concatenate(dk, 1), Wqkv[1], 1, 1)
    grad += dot(jnp.concatenate(dv, 1), Wqkv[2], 1, 1)
    g = g + norm_back(1, grad)

    @pl.when(second)
    def _():
        IG[pl.ds(trow, T)] = feed_back(0, 0, g).astype(bf16)
        start("back", back_rows, lambda: ARR, partner, second)

    @pl.when(first)
    def _():
        Ball[own, 0:width] = (0.5 * g).astype(bf16)
        to_pair(("b", 0), Ball, block(0))
        G[...] = g

    set_off_to_all(("b", 0))
    from_all(("b", 2))
    def sums_over_tensor(name, parts, ref):
        all_arrived(name, 3 * size_of(parts.at[0]))
        ref[mine] = sum(parts[k].astype(f32) for k in range(4)).astype(bf16)
        for r in range(1, groups):
            start((name, 3), lambda: ref.at[mine], lambda: ref.at[mine], zpeers[r], None, r)

    def send_sums():
        PAb[...] = PAst[...].astype(bf16)
        for k in (1, 2, 3):
            start("pa", lambda k=k: PAb.at[:, cols(k)], lambda k=k: PAin.at[k], peers[k], None, k)

    def send_ends():
        output_to_pair("grad", IG)
        PBin[t] = PBst[...].astype(bf16)
        for k in (1, 2, 3):
            start("pb", lambda: PBin.at[t], lambda: PBin.at[t], peers[k], None, k)

    bs = [("b", i) for i in range(4)]
    if not gathered:

        @pl.when(second)
        def _():
            from_tensor("gates", Sb, gate_cols)

    @pl.when(second)
    def _():
        send_ends()
        send_sums()
        hop(2, "n")
        hop(1, "m", "sf", bs[3])
        relay(bs[1], Ball, block(1))
        relay(bs[0], Ball, block(0))
        from_tensor("qkv", Sb, qkv_cols)
        set_off("qkv")
        hop(1, bs[1])
        hand_on(1, "n")
        from_all(bs[0])
        hand_on_all(bs[2])
        hop(3, "n")
        hop(2, "m", "sf", bs[3], bs[1])
        hand_on(2, "n")
        hop(1, "qkv")
        hand_on(1, "m", bs[3], bs[1])
        hop(3, "m", "sf", bs[3])
        hand_on(3, "n")
        hand_on_all(bs[0])
        hop(3, bs[1])
        hand_on(2, "m", bs[3], bs[1])
        hop(2, "qkv")
        hand_on(3, "m")
        for i in range(4):
            from_pair(("n", i), Nall, block(i))
        all_shared("n", "m")
        forward_values()

    @pl.when(first)
    def _():
        from_tensor("qkv", Sb, qkv_cols)
        set_off("qkv")
        hop(3, bs[3])
        hop(1, bs[1])
        hand_on(1, bs[3])
        hand_on(2, bs[3])
        relay(bs[0], Ball, block(0))
        total = 0.0
        for k in range(2):
            h = dot(Nall[two, 0:width], Win[0, k])
            hg = dot(Ball[two, 0:width], Wout[0, k], 1, 1) * slope(h, jax.nn.sigmoid(h))
            total += dot(hg.astype(bf16), Win[0, k], 1, 1)
        X[0] = sum_to_owner(("s", 2), 2, total)
        send_sums()
        hand_on_all(bs[2])
        from_all(bs[0])
        hop(1, "qkv")
        hop(2, bs[1])
    hand_on(3, bs[3])
    from_pair(bs[3], Ball, block(3))
    shared(bs[3], *whole_rows(bs[3]))
    feed_grads(1, 3)

    @pl.when(first)
    def _():
        g = G[...] + norm_back(0, summed_here(("s", 2), 2, X[0]))
        IG[pl.ds(trow, T)] = g.astype(bf16)
        send_ends()
        hand_on_all(bs[0])
        hop(2, "qkv")
        hop(3, bs[1])

    PAin[0] = PAb[:, 0:C]
    sums_over_tensor("pa", PAin, PA)
    from_pair(bs[2], Ball, block(2))
    shared(bs[2], *whole_rows(bs[2]))
    if gathered:
        convolution_rows_back()
    sums_over_tensor("pb", PBin, PB)

    @pl.when(first)
    def _():
        hand_on(1, bs[1])
        hand_on(2, bs[1])

    convolution_grads()
    relay_output("grad", IG)
    hand_on(3, bs[1])

    from_pair(bs[0], Ball, block(0))
    shared(bs[0], *whole_rows(bs[0]))
    feed_grads(0, 0)
    hop(3, "qkv")
    from_pair(bs[1], Ball, block(1))
    shared(bs[1], *whole_rows(bs[1]))
    attention_grads()
    for name, ref in (("pa", PA), ("pb", PB)):
        all_arrived((name, 3), (groups - 1) * size_of(ref.at[0]))
    all_arrived("out", 2 * size_of(back_rows()))
    all_arrived("grad", 2 * size_of(back_rows()))
    for src, dst in ((LO, lo_out), (IG, ig_out), (PA, pa_out), (PB, pb_out), (CS, cs_out)):
        write(src, dst)
    pltpu.make_async_copy(room(sum(written)), room(sum(written)), os.at[0]).wait()
    for cond, sizes in sent.values():

        def all_sent():
            view = room(sum(sizes.values()))
            copy_of("out", view, view, partner, cond).wait_send()

        all_sent() if cond is None else pl.when(cond)(all_sent)
    assert len(recv_index) <= rs.shape[0] and len(send_index) <= ss.shape[0]


def last_kernel(*refs):
    given, outs, held, made, in_sems, out_sems = refs[:12], refs[12:26], refs[26:38], refs[38:52], refs[52], refs[53]
    in_grad, out_grad, qkv, ao, ci, co, pa, pb, cs, lo, ig, table = held
    (LO, IG, ng, nb, w_in, w_out, w_ain, pos, w_aout, w_cin, w_dw, bng, bns, w_cout) = made
    C, width = ao.shape
    copies = []

    def send(src, dst):
        copy = pltpu.make_async_copy(src, dst, out_sems.at[len(copies)])
        copy.start()
        copies.append(copy)

    loads = [pltpu.make_async_copy(given[i], held[i], in_sems.at[i]) for i in range(len(held))]
    for load in loads:
        load.start()
    for i, src, dst, out in ((0, in_grad, w_in, outs[4]), (1, out_grad, w_out, outs[5])):
        loads[i].wait()
        for j in range(2):
            dst[j] = src[j].astype(f32)
            send(dst.at[j], out.at[j])
    loads[2].wait()
    w_ain[0:3] = qkv[...].astype(f32)
    send(w_ain.at[pl.ds(0, 3)], outs[6].at[pl.ds(0, 3)])
    loads[3].wait()
    w_aout[...] = ao[...].astype(f32)
    send(w_aout, outs[8])
    loads[4].wait()
    for i in range(2):
        w_cin[pl.ds(i, width, stride=2), :] = ci[:, C * i : C * (i + 1)].astype(f32)
    send(w_cin, outs[9])
    loads[5].wait()
    w_cout[...] = co[...].astype(f32)
    send(w_cout, outs[13])
    for load in loads[6:]:
        load.wait()
    sums, norms = pa[0].astype(f32), pb[0].astype(f32)
    for g in range(1, pa.shape[0]):
        sums += pa[g].astype(f32)
        norms += pb[g].astype(f32)
    w_ain[3] = dot(table[...], sums[relative_at(pa.shape[0]) :].astype(bf16), 0, 0)
    send(w_ain.at[3], outs[6].at[3])
    LO[...] = lo[...].astype(f32)
    IG[...] = ig[...].astype(f32)
    for i in range(5):
        ng[i] = norms[i : i + 1]
        nb[i] = norms[8 + i : 9 + i]
    pos[...] = sums[0:2]
    taps = w_dw.shape[0]
    if pa.shape[0] > 1:
        sums = jnp.concatenate([sums[0:2], cs[taps : taps + 2], cs[0:taps]], 0)
    bng[...] = sums[2:3]
    bns[...] = sums[3:4]
    for k in range(taps):
        w_dw[k] = sums[4 + k : 5 + k]
    for i in (0, 1, 2, 3, 7, 10, 11, 12):
        send(made[i], outs[i])
    for copy in copies:
        copy.wait()


def on_device(
    inputs, lengths, cotangent, norm_gain, norm_bias, ffn_in, ffn_out, attn_in, pos_bias, attn_out,
    conv_in, depthwise, bn_gain, bn_shift, conv_out,
):
    dp = lax.axis_size(DATA)
    group, frames, width = inputs.shape
    C = width // 4
    taps = depthwise.shape[1]
    groups = dp if dp <= 4 else 1
    R = groups * group * frames
    table = position_rows(frames, width)
    hbm = pl.BlockSpec(memory_space=pltpu.HBM)
    sums_rows = relative_at(groups) + 2 * frames

    def shape(dims, dtype=bf16):
        return jax.ShapeDtypeStruct(dims, dtype)

    small_first = [
        shape((group * frames, width)), shape((group * frames, width)), shape((groups, sums_rows, C)),
        shape((groups, 16, width)), shape((40, C), f32),
    ]
    made_first = [
        shape((2, width, width)), shape((2, width, width)), shape((3, width, C)), shape((C, width)),
        shape((width, 2 * C)), shape((C, width)),
    ]
    n_recv = 109 + 15 * (groups - 1)
    n_send = 3 + 2 * (groups - 1) + 2 * max(groups - 2, 0)
    operands = (
        lengths, inputs, cotangent, norm_gain.transpose(1, 0, 2), norm_bias.transpose(1, 0, 2), ffn_in[0],
        ffn_out[0], attn_in[0], attn_out[0], conv_in.reshape(2 * width, C), conv_out[0], pos_bias[0], bn_gain,
        bn_shift, depthwise.transpose(1, 0, 2), table[0],
    )
    lo, ig, pa, pb, cs, *ready = pl.pallas_call(
        lambda *refs: layer_kernel((frames, width, dp, groups), *refs),
        out_shape=small_first + made_first,
        in_specs=[hbm] * 16,
        out_specs=[hbm] * 11,
        scratch_shapes=[
            pltpu.VMEM((2, 4, width, width), bf16),
            pltpu.VMEM((2, 4, width, width), bf16),
            pltpu.VMEM((3, width, width), bf16),
            pltpu.VMEM((width, C), bf16),
            pltpu.VMEM((width, width), bf16),
            pltpu.VMEM((2, width, width), bf16),
            pltpu.VMEM((width, width), bf16),
            pltpu.VMEM((4 * frames, width), bf16),
            pltpu.VMEM((SMALL_ROWS, width), f32),
            pltpu.VMEM((2, 4, frames, width), f32),
            pltpu.VMEM((5, frames, width), f32),
            pltpu.VMEM((5, frames, 128), f32),
            pltpu.VMEM((5, frames, width), f32),
            pltpu.VMEM((frames, width), f32),
            pltpu.VMEM((frames, width), bf16),
            pltpu.VMEM((frames, width), bf16),
            pltpu.VMEM((4, frames, width), f32),
            pltpu.VMEM((4, 2 * frames, frames), f32),
            pltpu.VMEM((2, frames, width), f32),
            pltpu.VMEM((frames, width), f32),
            pltpu.VMEM((frames + 32, width), f32),
            pltpu.VMEM((frames + 32, width), f32),
            pltpu.VMEM((4, frames, 2 * C), bf16),
            pltpu.VMEM((4, frames, 5 * C), bf16),
            pltpu.VMEM((sums_rows, width), f32),
            pltpu.VMEM((sums_rows, width), bf16),
            pltpu.VMEM((4, sums_rows, C), bf16),
            pltpu.VMEM((16, width), f32),
            pltpu.VMEM((4, 16, width), bf16),
            pltpu.VMEM((dp, 8, C), f32),
            pltpu.VMEM((dp, 8, C), f32),
            pltpu.VMEM((4, frames, width), bf16),
            pltpu.VMEM((4, frames, width), bf16),
            pltpu.VMEM((5, 1, width), f32),
            pltpu.VMEM((5, 1, width), f32),
            pltpu.VMEM((2, C), f32),
            pltpu.VMEM((1, C), f32),
            pltpu.VMEM((1, C), f32),
            pltpu.VMEM((taps, 1, C), f32),
            pltpu.VMEM((2 * frames, width), bf16),
            pltpu.SMEM((group,), jnp.int32),
            pltpu.VMEM((2 * width, C), bf16),
            pltpu.VMEM((2 * width, C), f32),
            pltpu.VMEM((R, 4 * width), bf16),
            pltpu.VMEM((R, 4 * width), bf16),
            pltpu.VMEM((R, 2 * C), bf16),
            pltpu.VMEM((R, 5 * C), bf16),
            pltpu.VMEM((2, R, width), bf16),
            pltpu.VMEM((2, R, width), f32),
            pltpu.VMEM((R, width), bf16),
        ]
        + [pltpu.VMEM(m.shape, m.dtype) for m in made_first]
        + [
            pltpu.VMEM((2, R, C), f32),
            pltpu.VMEM((R, C), f32),
            pltpu.VMEM((R // frames, frames + 32, C), f32),
            pltpu.VMEM((R, C), f32),
            pltpu.VMEM((R // frames, frames + 32, C), f32),
            pltpu.VMEM((taps, 8, C), f32),
            pltpu.VMEM((4, 8, C), f32),
            pltpu.VMEM((2 * frames, C), bf16),
            pltpu.VMEM((dp, 8, C), f32),
            pltpu.VMEM((2, width // 4, width), bf16),
        ]
        + [pltpu.VMEM(m.shape, m.dtype) for m in small_first]
        + [
            pltpu.VMEM((10 * 2**20 // 512, 128), f32),
            pltpu.SemaphoreType.DMA((n_send,)),
            pltpu.SemaphoreType.DMA((n_recv,)),
            pltpu.SemaphoreType.DMA((21,)),
            pltpu.SemaphoreType.DMA((1,)),
        ],
        compiler_params=pltpu.CompilerParams(
            collective_id=0, has_side_effects=True, vmem_limit_bytes=62 * 2**20
        ),
    )(*operands)

    gradients = [
        shape((group * frames, width), f32), shape((group * frames, width), f32), shape((5, 1, width), f32),
        shape((5, 1, width), f32), shape((2, width, width), f32), shape((2, width, width), f32),
        shape((4, width, C), f32), shape((2, C), f32), shape((C, width), f32), shape((2 * width, C), f32),
        shape((taps, 1, C), f32), shape((1, C), f32), shape((1, C), f32), shape((C, width), f32),
    ]
    given = (*ready, pa, pb, cs, lo, ig, table[1])
    outs = pl.pallas_call(
        last_kernel,
        out_shape=gradients,
        in_specs=[hbm] * len(given),
        out_specs=[hbm] * len(gradients),
        scratch_shapes=[pltpu.VMEM(m.shape, m.dtype) for m in given]
        + [pltpu.VMEM(m.shape, m.dtype) for m in gradients]
        + [pltpu.SemaphoreType.DMA((len(given),)), pltpu.SemaphoreType.DMA((len(gradients) + 4,))],
        compiler_params=pltpu.CompilerParams(vmem_limit_bytes=62 * 2**20),
    )(*given)
    if groups == 1:
        outs = list(outs[:2]) + [lax.psum(m.astype(bf16), DATA).astype(f32) for m in outs[2:]]
    (lo, ig, ng, nb, w_in, w_out, w_ain, pos, w_aout, w_cin, w_dw, bng, bns, w_cout) = outs
    rows = (1, group, frames, width)
    return (
        lo.reshape(rows), ig.reshape(rows), ng.transpose(1, 0, 2), nb.transpose(1, 0, 2), w_in[None], w_out[None],
        w_ain[None], pos[None], w_aout[None], w_cin.reshape(conv_in.shape), w_dw.transpose(1, 0, 2), bng, bns,
        w_cout[None],
    )


def solution(mesh):
    placed = (
        P(DATA, None, None),
        P(DATA),
        P(DATA, None, None),
        P(SECTION, None, None),
        P(SECTION, None, None),
        P(SECTION, None, None, TENSOR),
        P(SECTION, None, TENSOR, None),
        P(SECTION, None, None, TENSOR),
        P(SECTION, None, TENSOR),
        P(SECTION, TENSOR, None),
        P(SECTION, None, None, TENSOR),
        P(SECTION, None, TENSOR),
        P(SECTION, TENSOR),
        P(SECTION, TENSOR),
        P(SECTION, TENSOR, None),
    )
    return jax.shard_map(
        on_device,
        mesh=mesh,
        in_specs=placed,
        out_specs=(
            P(SECTION, DATA, None, None),
            P(SECTION, DATA, None, None),
            P(SECTION, None, None),
            P(SECTION, None, None),
            P(SECTION, None, None, TENSOR),
            P(SECTION, None, TENSOR, None),
            P(SECTION, None, None, TENSOR),
            P(SECTION, None, TENSOR),
            P(SECTION, TENSOR, None),
            P(SECTION, None, None, TENSOR),
            P(SECTION, None, TENSOR),
            P(SECTION, TENSOR),
            P(SECTION, TENSOR),
            P(SECTION, TENSOR, None),
        ),
        check_vma=False,
    )
```

```python
import math

import jax
import jax.numpy as jnp
import numpy as np
from jax import lax
from jax.experimental import pallas as pl
from jax.experimental.pallas import tpu as pltpu
from jax.sharding import PartitionSpec as P

HEAD = 64
EPSILON = 1e-05
MESH = pl.DeviceIdType.MESH
SECTION, TENSOR, DATA = "section", "tensor", "dp"
PLACE = (0, 2, 1, 3)
SMALL_ROWS = 48


def relative_at(groups):
    return 16 if groups > 1 else SMALL_ROWS


bf16, f32 = jnp.bfloat16, jnp.float32


def dot(left, right, left_dim=1, right_dim=0):
    return lax.dot_general(
        left, right, (((left_dim,), (right_dim,)), ((), ())), preferred_element_type=f32
    )


def position_rows(frames, width):
    offset = np.arange(2 * frames - 1, dtype=np.float32) - np.float32(frames - 1)
    rates = np.exp(
        np.arange(width // 2, dtype=np.float32) * np.float32(-2.0 * math.log(10000.0) / width)
    )
    angles = (offset[:, None] * rates[None, :]).astype(np.float32)
    table = np.stack([np.sin(angles), np.cos(angles)], -1).reshape(2 * frames - 1, width)
    blank = np.zeros((1, width), np.float32)
    return [jnp.asarray(np.concatenate([rows, blank]), bf16) for rows in (table[::-1], table)]


def layer_kernel(dims, *refs):
    T, width, dp, groups = dims
    C = width // 4
    (lengths, inputs, cot, ng_in, nb_in, fin, fout, ain, aout, cin, cout, pos_in, bng_in, bns_in, dw_in, e2_in) = refs[:16]
    (lo_out, ig_out, pa_out, pb_out, cs_out) = refs[16:21]
    (in_out, out_out, qkv_out, ao_out, ci_out, co_out) = refs[21:27]
    refs = refs[27:]
    (Win, Wout, Wqkv, Wr, Wo, Wci, Wco, R2, SM) = refs[:9]
    (H, XH, RS, X, G, ARR, HOP, QKV, PRB, GVG, CT, UP, DP) = refs[9:22]
    (SfSt, SbSt, PAst, PAb, PAin, PBst, PBin, STF, STB, RSst, RSin) = refs[22:33]
    (ng, nb, pos, bng, bns, dw, e2, lens, pairs, spread) = refs[33:43]
    (Nall, Ball, Sf, Sb, ACT, SLOPE, HG, gin, gout, gqkv, gao, gci, gco) = refs[43:56]
    GA, HATA, UA, DYA, DA, DWACC, INVA, OST, STL, VIA = refs[56:66]
    LO, IG, PA, PB, CS, dummy, ss, rs, ls, os = refs[66:76]
    gathered = groups > 1

    s, t, d = lax.axis_index(SECTION), lax.axis_index(TENSOR), lax.axis_index(DATA)
    first, second = s == 0, s == 1
    taps = dw.shape[0]
    peers = [(s, t ^ k, d) for k in range(4)]
    sib, yp = peers[1], peers[2]
    around = {j: lax.rem(d + j + dp, dp) for j in range(1 - dp, dp)}
    zpeers = [(s, t, around[r]) for r in range(dp)]
    zpair = (s, t, d ^ 1)
    partner = (1 - s, t, d)
    half = lax.rem(d, 2)
    R4 = 4 * T
    reach = range(1 - groups, groups)
    base_of = {j: pl.multiple_of(around[j] * R4, R4) if groups > 1 else 0 for j in reach}
    second_of, high_of, last_of = (
        {j: pl.multiple_of(around[j] * R4 + n * T, T) if groups > 1 else n * T for j in reach} for n in (1, 2, 3)
    )
    there = {j: d + j >= 0 if j < 0 else d + j <= dp - 1 for j in reach}
    through = {
        (j, to): there[j] & there[to] for j in reach for to in (1, -1) if j * to < 0 and groups > 1
    }
    base = base_of[0]
    trow, yrow = pl.multiple_of(t * T, T), pl.multiple_of((t ^ 2) * T, T)
    mine = d if groups > 1 else 0

    recv_index, send_index, sent = {}, {}, {}

    def size_of(view):
        return math.prod(view.shape) * view.dtype.itemsize

    def copy_of(key, src, dst, dev, group):
        i = recv_index.setdefault(key, len(recv_index))
        j = send_index.setdefault(id(group), len(send_index))
        return pltpu.make_async_remote_copy(
            src_ref=src, dst_ref=dst, send_sem=ss.at[j], recv_sem=rs.at[i], device_id=dev, device_id_type=MESH,
        )

    def start(key, src, dst, dev, cond=None, part=0):
        view = src()
        copy_of(key, view, dst(), dev, cond).start()
        sent.setdefault(id(cond), (cond, {}))[1][key, part] = size_of(view)

    def arrived(key, dst):
        copy_of(key, dst, dst, partner, None).wait_recv()

    def room(size):
        return dummy.at[pl.ds(0, size // (4 * dummy.shape[1]))]

    def all_arrived(key, size):
        if size:
            arrived(key, room(size))

    locals_ = {}

    def fetch(name, src, dst):
        locals_[name] = lambda: pltpu.make_async_copy(src(), dst(), ls.at[list(locals_).index(name)])
        locals_[name]().start()

    def fetched(*names):
        for name in names:
            locals_[name]().wait()

    @pl.when(first)
    def _():
        pltpu.make_async_copy(inputs.at[t], X.at[0], ls.at[20]).start()

    @pl.when(second)
    def _():
        pltpu.make_async_copy(cot.at[t], G, ls.at[20]).start()

    fetch("ng", lambda: ng_in, lambda: ng)
    fetch("nb", lambda: nb_in, lambda: nb)
    fetch("in0", lambda: fin.at[0], lambda: Win.at[0, 0])
    fetch("out0", lambda: fout.at[0], lambda: Wout.at[0, 0])
    fetch("wr", lambda: ain.at[3], lambda: Wr)
    fetch("e2", lambda: e2_in, lambda: e2)
    fetch("pos", lambda: pos_in, lambda: pos)
    fetch("bng", lambda: bng_in, lambda: bng)
    fetch("bns", lambda: bns_in, lambda: bns)
    fetch("dw", lambda: dw_in, lambda: dw)
    fetch("len", lambda: lengths, lambda: lens)
    fetch("qkv", lambda: ain.at[pl.ds(0, 3)], lambda: Wqkv.at[:, :, pl.ds(0, C)])
    fetch("o", lambda: aout, lambda: Wo.at[pl.ds(0, C)])
    fetch("ci", lambda: cin, lambda: pairs)
    fetch("co", lambda: cout, lambda: Wco.at[pl.ds(0, C)])
    fetch("in1", lambda: fin.at[1], lambda: Win.at[1, 0])
    fetch("out1", lambda: fout.at[1], lambda: Wout.at[1, 0])

    barrier = pltpu.get_barrier_semaphore()
    greet = peers[1:] + zpeers[1:] + [partner]
    for dev in greet:
        pl.semaphore_signal(barrier, inc=1, device_id=dev, device_id_type=MESH)
    pl.semaphore_wait(barrier, len(greet))

    starts = {}

    def lines(first_row, n, which):
        if which is None:
            return pl.ds(first_row, n)
        at = (first_row, n, which)
        if at not in starts:
            starts[at] = pl.multiple_of(first_row + n // 2 * (half if which == "own" else 1 - half), n // 2)
        return pl.ds(starts[at], n // 2)

    def cols(k):
        return pl.ds(C * k, C)

    def feed_chunks(j):
        Q = width // 2
        return [
            (
                lambda w, src=src, q=q: src.at[j, lines(Q * q, Q, w)],
                lambda k, w, dst=dst, q=q: dst.at[j, k, lines(Q * q, Q, w)],
            )
            for src, dst in ((fin, Win), (fout, Wout))
            for q in range(2)
        ]

    def row_chunk(src, dst):
        return [(lambda w: src.at[lines(0, C, w)], lambda k, w: dst.at[lines(C * k, C, w)])]

    def column_chunks(src, dst, n):
        return [
            (lambda w, i=i: src(i, lines(0, width, w)), lambda k, w, i=i: dst.at[i, lines(0, width, w), cols(k)])
            for i in range(n)
        ]

    chunks = (
        feed_chunks(0)
        + column_chunks(lambda i, rows: ain.at[i, rows], Wqkv, 3)
        + row_chunk(aout, Wo)
        + column_chunks(lambda i, rows: Wci.at[i, rows, cols(0)], Wci, 2)
        + row_chunk(cout, Wco)
        + feed_chunks(1)
        + [
            (lambda w: SM.at[:, cols(0)], lambda k, w: SM.at[:, cols(k)]),
            (lambda w: R2.at[pl.ds(0, 2 * T), cols(0)], lambda k, w: R2.at[pl.ds(0, 2 * T), cols(k)]),
        ]
    )
    for n, at in ((width // 2, 0), (width // 2, width // 2), (width, 0)) + tuple((C, C * k) for k in range(4)):
        for w in ("own", "other"):
            lines(at, n, w)
    only = {i: second for i in range(4)}
    over_y = {i: "own" for i in range(14)}

    def send_core(names):
        for i in names:
            src, dst = chunks[i]
            start(("sib", i), lambda src=src: src(None), lambda dst=dst: dst(1, None), sib)

    def send_y(names):
        for i in names:
            (src, dst), w = chunks[i], over_y.get(i)
            cond = first if i == 13 else only.get(i)
            start(("y", i), lambda src=src, w=w: src(w), lambda dst=dst, w=w: dst(2, w), yp, cond)

    def send_round():
        start(("r", 0), lambda: chunks[13][0]("own"), lambda: VIA.at[0], partner, second)

    def pass_round(n):
        arrived(("r", n - 1), VIA.at[n - 1])
        if n == 1:
            start(("r", 1), lambda: VIA.at[0], lambda: VIA.at[1], yp, first)
        else:
            start(("r", 2), lambda: VIA.at[1], lambda: chunks[13][1](2, "own"), partner, first)

    def step_a(i, by="y"):
        dst, w = chunks[i][1], over_y.get(i)
        arrived(("r", 2) if by == "r" else ("y", i), dst(2, w))
        if w:
            start(("z", i), lambda: dst(2, w), lambda: dst(2, w), zpair, only.get(i))
        start(("on", i), lambda: dst(2, w), lambda: dst(3, w), sib, only.get(i), 1)

    def step_b(i):
        if i not in over_y:
            return
        dst = chunks[i][1]
        arrived(("z", i), dst(2, "other"))
        start(("on", i), lambda: dst(2, "other"), lambda: dst(3, "other"), sib, only.get(i), 2)

    def core_part(i):
        arrived(("sib", i), chunks[i][1](1, None))

    def passed_part(i):
        all_arrived(("on", i), size_of(chunks[i][1](1, None)))

    def step_c(i):
        core_part(i)
        passed_part(i)

    def steps(cond, *plan):
        @pl.when(cond)
        def _():
            for step, i in plan:
                step(i)

    A, B, W = step_a, step_b, step_c

    def norm(i, x):
        centre = x - jnp.mean(x, -1, keepdims=True)
        rate = lax.rsqrt(jnp.mean(centre * centre, -1, keepdims=True) + EPSILON)
        hat = centre * rate
        XH[i] = hat
        RS[i] = jnp.broadcast_to(rate, RS.shape[1:])
        return hat * ng[i] + nb[i]

    def norm_back(i, grad):
        hat = XH[i]
        PBst[i : i + 1] = jnp.sum(grad * hat, 0, keepdims=True)
        PBst[8 + i : 9 + i] = jnp.sum(grad, 0, keepdims=True)
        g = grad * ng[i]
        return RS[i][:, 0:1] * (
            g - jnp.mean(g, -1, keepdims=True) - hat * jnp.mean(g * hat, -1, keepdims=True)
        )

    def total_of(v):
        return jnp.sum(v, 0, keepdims=True)

    def silu(h):
        return h * jax.nn.sigmoid(h)

    def place(k):
        return pl.ds(base + T * PLACE[k], T)

    own, two = pl.ds(base, T), pl.ds(base, 2 * T)

    def block(i, n=1):
        return pl.ds(i * width, n * width)

    def from_tensor(name, ref, c):
        all_arrived(name, 3 * size_of(ref.at[own, c]))

    def to_pair(name, ref, c, cond=None):
        start(name, lambda: ref.at[own, c], lambda: ref.at[place(1), c], sib, cond, 4)
        start((name, 4), lambda: ref.at[own, c], lambda: ref.at[place(2), c], yp, cond)

    def relay(name, ref, c, cond=None):
        arrived((name, 4), ref.at[place(2), c])
        start(name, lambda: ref.at[place(2), c], lambda: ref.at[place(3), c], sib, cond, 5)

    def from_pair(name, ref, c):
        all_arrived(name, 2 * size_of(ref.at[own, c]))

    def feed(j, i, before, after):
        x = X[before]
        a = norm(i, x).astype(bf16)
        Nall[own, i * width : (i + 1) * width] = a
        to_pair(("n", i), Nall, block(i))
        if j:
            step_c(11)
            step_c(12)
        active = []
        for k in range(4):
            h = dot(a, Win[j, k])
            H[j, k] = h
            active.append(silu(h).astype(bf16))
        Q, total = width // 2, 0.0
        for q in range(2):
            if j:
                step_c(13 + q)
            for k in range(4):
                total += dot(active[k][:, Q * q : Q * (q + 1)], Wout[j, k, Q * q : Q * (q + 1)])
        X[after] = x + 0.5 * total

    def sum_to_owner(name, slot, total):
        RSst[slot] = total[T : 2 * T].astype(bf16)
        start(name, lambda: RSst.at[slot], lambda: RSin.at[slot], yp, first)
        return total[0:T]

    def summed_here(name, slot, total):
        arrived(name, RSin.at[slot])
        return total + RSin[slot].astype(f32)

    def shared_feed(j, i):
        relay(("n", i), Nall, block(i))
        a = Nall[two, i * width : (i + 1) * width]
        total = dot(silu(dot(a, Win[j, 0])).astype(bf16), Wout[j, 0])
        for k in range(11 * j, 11 * j + 4):
            core_part(k)
        total += dot(silu(dot(a, Win[j, 1])).astype(bf16), Wout[j, 1])
        return sum_to_owner(("s", j), j, total)

    fetched("ng", "nb")

    @pl.when(first)
    def _():
        pltpu.make_async_copy(inputs.at[t], X.at[0], ls.at[20]).wait()
        Nall[own, 0:width] = norm(0, X[0]).astype(bf16)
        to_pair(("n", 0), Nall, block(0))

    send_core(range(4))

    @pl.when(second)
    def _():
        send_round()
        send_y(range(4))
        pltpu.make_async_copy(cot.at[t], G, ls.at[20]).wait()

    fetched("pos", "bng", "bns", "dw", "wr", "e2", "len", "ci")
    spread[...] = pairs[...].astype(f32)
    for i in range(2):
        Wci[i, :, 0:C] = spread[pl.ds(i, width, stride=2), :].astype(bf16)
    SM[:, 0:C] = jnp.zeros((SMALL_ROWS, C), f32)
    SM[0:2, 0:C] = pos[...]
    SM[2:3, 0:C] = bng[...]
    SM[3:4, 0:C] = bns[...]
    for k in range(taps):
        SM[4 + k : 5 + k, 0:C] = dw[k]
    R2[0 : 2 * T, 0:C] = dot(e2[...], Wr[...]).astype(bf16)
    lengths_here = [jnp.broadcast_to(lens[t ^ PLACE[p]].astype(f32), (1, C)) for p in range(4)]
    STL[d] = jnp.concatenate(lengths_here + [jnp.zeros((4, C), f32)], 0)
    for r in range(1, dp):
        start("len", lambda: STL.at[d], lambda: STL.at[d], zpeers[r], None, r)
    fetched("in0", "out0")

    @pl.when(first)
    def _():
        send_core((15, 16, 4, 5, 6, 7, 8, 9, 10))
        send_y((8,))
        X[1] = shared_feed(0, 0)
        send_y((9,))

    @pl.when(first)
    def _():
        step_a(8)
        X[1] = X[0] + 0.5 * summed_here(("s", 0), 0, X[1])

    @pl.when(second)
    def _():
        for i in (15, 16, *range(4, 15)):
            send_core((i,))
            if i != 13:
                send_y((i,))

    fetched("qkv", "o", "co", "in1", "out1")
    margin = 16
    UP[...] = jnp.zeros(UP.shape, f32)
    DP[...] = jnp.zeros(DP.shape, f32)
    PAst[...] = jnp.zeros(PAst.shape, f32)
    PBst[...] = jnp.zeros(PBst.shape, f32)
    CS[...] = jnp.zeros(CS.shape, f32)
    if gathered:
        DA[...] = jnp.zeros(DA.shape, f32)
        DWACC[...] = jnp.zeros(DWACC.shape, f32)

    def keys_of(length):
        return lax.broadcasted_iota(jnp.int32, (2 * T, T), 1) < length

    row_mask = (lax.broadcasted_iota(jnp.int32, (T, 1), 0) < lens[t]).astype(f32)
    first_head = lax.broadcasted_iota(jnp.int32, (T, 2 * HEAD), 1) < HEAD
    flip = (
        lax.broadcasted_iota(jnp.int32, (T, 4 * T), 0) + lax.broadcasted_iota(jnp.int32, (T, 4 * T), 1)
        == T - 1
    ).astype(f32).astype(bf16)

    def pair_rows(v):
        return jnp.concatenate([jnp.where(first_head, v, 0.0), jnp.where(first_head, 0.0, v)], 0)

    def unpair(v):
        return jnp.where(first_head, v[:T], v[T:])

    def attend(qu, qv, key, value, relative, keys):
        content = dot(pair_rows(qu).astype(bf16), key, 1, 1)
        whole = dot(pair_rows(qv).astype(bf16), jnp.concatenate([relative, jnp.zeros_like(relative)], 0), 1, 1)
        placed = jnp.concatenate(
            [
                pltpu.roll(whole[e * T : (e + 1) * T], 4 * T - (T - 1), 1, stride=1, stride_axis=0)[:, :T]
                for e in range(2)
            ],
            0,
        )
        scores = jnp.where(keys, (content + placed) * HEAD ** (-0.5), -1e30)
        e = jnp.exp(scores - jnp.max(scores, -1, keepdims=True))
        probs = e / jnp.sum(e, -1, keepdims=True)
        return probs, unpair(dot(probs.astype(bf16), value)).astype(bf16)

    def attention_here():
        a = Nall[own, width : 2 * width]
        q = dot(a, Wqkv[0])
        QKV[0] = q + SM[0:1]
        QKV[1] = q + SM[1:2]
        QKV[2] = dot(a, Wqkv[1])
        QKV[3] = dot(a, Wqkv[2])
        keys, mixed = keys_of(lens[t]), []
        for p in range(4):
            c = pl.ds(2 * HEAD * p, 2 * HEAD)
            probs, out = attend(
                QKV[0, :, c], QKV[1, :, c], QKV[2, :, c].astype(bf16), QKV[3, :, c].astype(bf16), R2[0 : 2 * T, c], keys
            )
            PRB[p] = probs
            mixed.append(out)
        return mixed

    def shared_attention():
        for i in (4, 5, 6, 15, 16):
            core_part(i)
        a = Nall[two, width : 2 * width]
        q, key, value = (dot(a, Wqkv[i, :, 0 : 2 * C]) for i in range(3))
        qu, qv, key, value = q + SM[0:1, 0 : 2 * C], q + SM[1:2, 0 : 2 * C], key.astype(bf16), value.astype(bf16)
        mixed = [[], []]
        for p in range(2):
            rows, keys = slice(T * p, T * (p + 1)), keys_of(lens[t ^ PLACE[p]])
            for k in range(2):
                c = slice(C * k, C * (k + 1))
                mixed[k].append(
                    attend(qu[rows, c], qv[rows, c], key[rows, c], value[rows, c], R2[0 : 2 * T, c], keys)[1]
                )
        mixed = [jnp.concatenate(m, 0) for m in mixed]
        Sf[two, 0:C] = mixed[0]
        OST[...] = mixed[1]
        start("sf", lambda: OST, lambda: Sf.at[pl.ds(high_of[0], 2 * T), pl.ds(0, C)], sib, first, 4)
        core_part(7)
        return sum_to_owner(("s", 3), 3, dot(mixed[0], Wo[0:C]) + dot(mixed[1], Wo[C : 2 * C]))

    def relative_arrived():
        passed_part(16)
        turned_back = (
            lax.broadcasted_iota(jnp.int32, (2 * T, 2 * T), 0) + lax.broadcasted_iota(jnp.int32, (2 * T, 2 * T), 1)
            == 2 * T - 2
        ).astype(f32).astype(bf16)
        R2[2 * T : 4 * T] = dot(turned_back, R2[0 : 2 * T]).astype(bf16)


    @pl.when(first)
    def _():
        Nall[own, width : 2 * width] = norm(1, X[1]).astype(bf16)
        to_pair(("n", 1), Nall, block(1))
        send_y((15,))
        pass_round(1)
        send_y((10,))
        step_a(9)
        step_b(8)
        relay(("n", 1), Nall, block(1))
        total = shared_attention()
        send_y((4, 5, 6, 16, 7))
        step_a(15)
        step_b(9)
        X[2] = X[1] + summed_here(("s", 3), 3, total)
        pass_round(2)
        step_a(10)
        passed_part(15)

    @pl.when(second)
    def _():
        coming = (*range(4), 15, 16, *range(4, 14))
        for n, i in enumerate(coming):
            step_a(i, "r" if i == 13 else "y")
            if n > 1 and i != 13:
                step_b(coming[n - 2])
        for i in range(7):
            step_c(i)
        step_c(15)
        core_part(16)
        relative_arrived()
        arrived("hop", ARR)
        X[0] = ARR[...].astype(f32)
        feed(0, 0, 0, 1)
        Nall[own, width : 2 * width] = norm(1, X[1]).astype(bf16)
        to_pair(("n", 1), Nall, block(1))
        mixed = attention_here()
        step_b(11)
        for k in range(4):
            SfSt[k, :, 0:C] = mixed[k]
        step_c(7)
        X[2] = X[1] + dot(jnp.concatenate(mixed, 1), Wo[...])

    def line_start(name, region):
        for way, to, back in (("up", 1, -1), ("down", -1, 1)):
            if groups > 1:

                @pl.when(there[to])
                def _():
                    start(
                        (name, 0, back % dp), lambda: region(0), lambda: region(0), (s, t, around[to]), there[to], way
                    )

    def line_hop(name, region, n, after=None):
        for way, to, back in (("up", 1, -1), ("down", -1, 1)):
            if n < groups:

                @pl.when(there[back * n])
                def _():
                    j = back * n
                    arrived((name, 0, j % dp), region(j))
                    if n + 1 < groups:

                        @pl.when(there[to])
                        def _():
                            start(
                                (name, 0, (j + back) % dp), lambda: region(j), lambda: region(j),
                                (s, t, around[to]), through[j, to], way,
                            )

                    if after is not None:
                        after(name, j)

    def rows_region(ref, n, c):
        return lambda j: ref.at[pl.ds(base_of[j], n), c]

    def share(ref, c):
        def go(name, j):
            rows = lambda: ref.at[pl.ds(base_of[j], T), c]
            start((name, 1, j % dp), rows, lambda: ref.at[pl.ds(second_of[j], T), c], yp, there[j], j)
            start((name, 2, 0), rows, lambda: ref.at[pl.ds(high_of[j], T), c], sib, there[j], j)

        return go

    def share_on(name, ref, c, n):
        for j in (n, -n):
            if n < groups:

                @pl.when(there[j])
                def _():
                    rows = lambda: ref.at[pl.ds(second_of[j], T), c]
                    arrived((name, 1, j % dp), rows())
                    start((name, 2, 0), rows, lambda: ref.at[pl.ds(last_of[j], T), c], sib, there[j], dp + j)

    def shared(name, ref, c):
        all_arrived((name, 2, 0), 2 * (groups - 1) * size_of(ref.at[own, c]))

    def set_off_to_all(name):
        ref, c = whole_rows(name)
        mine = lambda: ref.at[own, c]
        for r in range(1, groups):
            start((name, 0, (-r) % dp), mine, mine, zpeers[r], None, r)

    def from_all(name):
        ref, c = whole_rows(name)
        for r in range(1, groups):
            rows = lambda r=r: ref.at[pl.ds(base_of[r], T), c]
            arrived((name, 0, r), rows())
            start((name, 1, r), rows, lambda r=r: ref.at[pl.ds(second_of[r], T), c], yp, None, r)
            start((name, 2, 0), rows, lambda r=r: ref.at[pl.ds(high_of[r], T), c], sib, None, r)

    def hand_on_all(name):
        ref, c = whole_rows(name)
        for r in range(1, groups):
            rows = lambda r=r: ref.at[pl.ds(second_of[r], T), c]
            arrived((name, 1, r), rows())
            start((name, 2, 0), rows, lambda r=r: ref.at[pl.ds(last_of[r], T), c], sib, None, dp + r)

    def all_shared(*names):
        for name in names:
            shared(name, *whole_rows(name))

    sf_cols = pl.ds(0, C if gathered else 2 * C)
    qkv_cols, gate_cols = pl.ds(0, 3 * C), pl.ds(3 * C, 2 * C)
    lines_of = {
        "n": (rows_region(Nall, T, block(0, 3)), share(Nall, block(0, 3))),
        "m": (rows_region(Nall, T, block(3)), share(Nall, block(3))),
        "sf": (rows_region(Sf, R4, sf_cols), None),
        "qkv": (rows_region(Sb, R4, qkv_cols), None),
    }
    for i in range(4):
        lines_of["b", i] = (rows_region(Ball, T, block(i)), share(Ball, block(i)))

    def set_off(*names):
        for name in names:
            line_start(name, lines_of[name][0])

    def hop(n, *names):
        for name in names:
            line_hop(name, lines_of[name][0], n, lines_of[name][1])

    def whole_rows(name):
        if name in ("n", "m"):
            return Nall, block(0, 3) if name == "n" else block(3)
        return Ball, block(name[1])

    def hand_on(n, *names):
        for name in names:
            share_on(name, *whole_rows(name), n)

    written = []

    def write(src, dst):
        pltpu.make_async_copy(src, dst, os.at[0]).start()
        written.append(size_of(src))

    R = Nall.shape[0]
    row_blocks = [slice(r, r + R4) for r in range(0, R, R4)]

    def slope(h, sig):
        return sig * (1.0 + h * (1.0 - sig))

    def hidden_rows(j, i):
        for rows in row_blocks:
            h = dot(Nall[rows, i * width : (i + 1) * width], Win[j, 0])
            sig = jax.nn.sigmoid(h)
            ACT[j, rows] = (h * sig).astype(bf16)
            SLOPE[j, rows] = slope(h, sig)

    def feed_grads(j, i):
        c = slice(i * width, (i + 1) * width)
        for rows in row_blocks:
            HG[rows] = (dot(Ball[rows, c], Wout[j, 0], 1, 1) * SLOPE[j, rows]).astype(bf16)
        gin[j] = dot(Nall[:, c], HG[...], 0, 0).astype(bf16)
        write(gin.at[j], in_out.at[j])
        gout[j] = dot(ACT[j], Ball[:, c], 0, 0).astype(bf16)
        write(gout.at[j], out_out.at[j])

    def mask_of(g, p):
        return (lax.broadcasted_iota(jnp.int32, (T, C), 0).astype(f32) < STL[g, p : p + 1]).astype(f32)

    places = [(p, [(g, slice(R4 * g + T * p, R4 * g + T * (p + 1))) for g in range(groups)]) for p in range(4)]

    def convolution_rows():
        for i in range(2):
            GA[i] = dot(Nall[:, 2 * width : 3 * width], Wci[i, :, 0:C])
        UA[...] = jnp.zeros(UA.shape, f32)
        for p, parts in places:
            for g, rows in parts:
                UA[4 * g + p, margin : margin + T] = GA[0, rows] * jax.nn.sigmoid(GA[1, rows]) * mask_of(g, p)

        def one(b, carry):
            acc = SM[4:5, 0:C] * UA[b, margin - taps // 2 : margin - taps // 2 + T]
            for k in range(1, taps):
                o = margin - taps // 2 + k
                acc += SM[4 + k : 5 + k, 0:C] * UA[b, o : o + T]
            HATA[pl.ds(b * T, T)] = acc
            return carry

        lax.fori_loop(0, 4 * groups, one, 0)
        for p, parts in places:
            n = sum(STL[g, p : p + 1] for g, _ in parts)
            masked = [HATA[rows] * mask_of(g, p) for g, rows in parts]
            mean = sum(total_of(m) for m in masked) / n
            square = sum(total_of(m * HATA[rows]) for m, (_, rows) in zip(masked, parts)) / n
            inv = lax.rsqrt(square - mean * mean + EPSILON)
            INVA[p, 0:1] = inv
            INVA[p, 1:2] = n
            for g, rows in parts:
                h = (HATA[rows] - mean) * inv
                HATA[rows] = h
                Sf[rows, C : 2 * C] = silu(h * SM[2:3, 0:C] + SM[3:4, 0:C]).astype(bf16)

    def convolution_rows_back():
        DYA[...] = dot(Ball[:, 2 * width : 3 * width], Wco[0:C], 1, 1)
        gain_sum = shift_sum = jnp.zeros((1, C), f32)
        for p, parts in places:
            first_sum = second_sum = jnp.zeros((1, C), f32)
            for g, rows in parts:
                h = HATA[rows]
                y = h * SM[2:3, 0:C] + SM[3:4, 0:C]
                dy = DYA[rows] * slope(y, jax.nn.sigmoid(y))
                gain_sum += total_of(dy * h)
                shift_sum += total_of(dy)
                dh = dy * SM[2:3, 0:C]
                DYA[rows] = dh
                dh = dh * mask_of(g, p)
                first_sum += total_of(dh)
                second_sum += total_of(dh * h)
            inv, n = INVA[p, 0:1], INVA[p, 1:2]
            for g, rows in parts:
                dc = inv * (DYA[rows] - (first_sum + HATA[rows] * second_sum) / n) * mask_of(g, p)
                DA[4 * g + p, margin : margin + T] = dc
        CS[taps : taps + 1] = gain_sum
        CS[taps + 1 : taps + 2] = shift_sum

        def one(b, carry):
            here = DA[b, margin : margin + T]
            acc = jnp.zeros((T, C), f32)
            for k in range(taps):
                o = margin + taps // 2 - k
                acc += SM[4 + k : 5 + k, 0:C] * DA[b, o : o + T]
                o = margin - taps // 2 + k
                term = here * UA[b, o : o + T]
                DWACC[k] += sum(term[8 * i : 8 * (i + 1)] for i in range(T // 8))
            DYA[pl.ds(b * T, T)] = acc
            return carry

        lax.fori_loop(0, 4 * groups, one, 0)
        for k in range(taps):
            CS[k : k + 1] = total_of(DWACC[k])
        for p, parts in places:
            for g, rows in parts:
                sig = jax.nn.sigmoid(GA[1, rows])
                dua = DYA[rows] * mask_of(g, p)
                Sb[rows, 3 * C : 4 * C] = (dua * sig).astype(bf16)
                Sb[rows, 4 * C : 5 * C] = (dua * GA[0, rows] * (sig * (1.0 - sig))).astype(bf16)

    def convolution_grads():
        gci[...] = dot(Nall[:, 2 * width : 3 * width], Sb[:, 3 * C : 5 * C], 0, 0).astype(bf16)
        write(gci, ci_out)
        gco[...] = dot(Sf[:, C : 2 * C], Ball[:, 2 * width : 3 * width], 0, 0).astype(bf16)
        write(gco, co_out)

    def attention_grads():
        grads = dot(Nall[:, width : 2 * width], Sb[:, 0 : 3 * C], 0, 0)
        for i in range(3):
            gqkv[i] = grads[:, C * i : C * (i + 1)].astype(bf16)
        write(gqkv, qkv_out)
        gao[...] = dot(Sf[:, 0:C], Ball[:, width : 2 * width], 0, 0).astype(bf16)
        write(gao, ao_out)

    def forward_values():
        hidden_rows(1, 3)
        hidden_rows(0, 0)
        if gathered:
            convolution_rows()

    a = norm(2, X[2]).astype(bf16)
    Nall[own, 2 * width : 3 * width] = a
    to_pair(("n", 2), Nall, block(2))

    step_c(8)
    step_c(9)
    GVG[0] = dot(a, Wci[0])
    GVG[1] = dot(a, Wci[1])
    UP[margin : margin + T] = GVG[0] * jax.nn.sigmoid(GVG[1]) * row_mask
    for p in range(4):
        c = pl.ds(C * p, C)
        acc = SM[4:5, c] * UP[margin - taps // 2 : margin - taps // 2 + T, c]
        for k in range(1, taps):
            o = margin - taps // 2 + k
            acc += SM[4 + k : 5 + k, c] * UP[o : o + T, c]
        CT[:, c] = acc
    conv = CT[...]

    def dp_sums(name, ref, rows):
        ref[d] = jnp.concatenate([row[:, C * k : C * (k + 1)] for row in rows for k in range(4)], 0)
        for r in range(1, dp):
            start(name, lambda: ref.at[d], lambda: ref.at[d], zpeers[r], None, r)

    def summed(name, ref):
        all_arrived(name, (dp - 1) * size_of(ref.at[0]))
        total = ref[0]
        for r in range(1, dp):
            total += ref[r]
        return [jnp.concatenate([total[4 * i + k : 4 * i + k + 1] for k in range(4)], 1) for i in range(2)]

    masked = conv * row_mask
    dp_sums("bnf", STF, [total_of(masked), total_of(masked * conv)])
    steps(second, (B, 12), (A, 14))
    steps(first, (B, 10))
    step_c(10)
    sums = summed("bnf", STF)
    steps(second, (B, 13))
    steps(first, (A, 4), (A, 5), (A, 6), (A, 16))

    @pl.when(second)
    def _():
        set_off("n")
    all_arrived("len", (dp - 1) * size_of(STL.at[0]))
    count = sum(STL[r, 0:1, 0:1] for r in range(dp))
    bn_mean = sums[0] / count
    inv_std = lax.rsqrt(sums[1] / count - bn_mean * bn_mean + EPSILON)
    hat = (conv - bn_mean) * inv_std
    CT[...] = hat
    active = silu(hat * SM[2:3] + SM[3:4]).astype(bf16)
    if not gathered:
        for k in range(4):
            SfSt[k, :, C : 2 * C] = active[:, C * k : C * (k + 1)]
    X[3] = X[2] + dot(active, Wco[...])

    @pl.when(first)
    def _():
        Nall[own, 3 * width : 4 * width] = norm(3, X[3]).astype(bf16)
        to_pair(("n", 3), Nall, block(3))
        send_core((11, 12, 13, 14))
        total = shared_feed(1, 3)
        send_y((11, 12, 13, 14))
        step_a(7)
        step_b(4)
        step_b(5)
        X[4] = X[3] + 0.5 * summed_here(("s", 1), 1, total)

    @pl.when(second)
    def _():
        feed(1, 3, 3, 4)
    out = (norm(4, X[4]) * row_mask).astype(bf16)
    HOP[...] = out

    @pl.when(first)
    def _():
        start("hop", lambda: HOP, lambda: ARR, partner, first)

    LO[pl.ds(trow, T)] = out
    def output_to_pair(name, ref):
        rows = lambda: ref.at[pl.ds(trow, T)]
        start(name, rows, rows, sib)
        start((name, 4), rows, rows, yp)

    def relay_output(name, ref):
        rows = lambda: ref.at[pl.ds(yrow, T)]
        arrived((name, 4), rows())
        start(name, rows, rows, sib, None, 1)

    output_to_pair("out", LO)

    for cond, c in ((first, pl.ds(C, C)), (second, sf_cols))[gathered:]:

        @pl.when(cond)
        def _():
            Sf[own, c] = SfSt[0, :, c]
            for k in (1, 2, 3):
                start("sf", lambda k=k: SfSt.at[k, :, c], lambda k=k: Sf.at[place(k), c], peers[k], cond, k)

    @pl.when(first)
    def _():
        set_off("n", "m")
        if gathered:
            all_arrived("sf", size_of(OST))
            set_off("sf")
        relay(("n", 2), Nall, block(2))
        step_a(11)
        for i in (6, 7):
            step_b(i)
        step_a(12)
        step_b(11)
        for i in (4, 5, 6, 7):
            passed_part(i)
        relative_arrived()
        attention_here()
        step_a(13)
        step_b(12)
        if not gathered:
            all_arrived("sf", size_of(OST) + 3 * size_of(Sf.at[own, pl.ds(C, C)]))
        step_a(14)
        hop(1, "n", "m", "sf")
        step_b(13)
        for i in range(11, 15):
            passed_part(i)
        for k in range(4):
            H[1, k] = dot(Nall[own, 3 * width : 4 * width], Win[1, k])
        hop(2, "n", "m", "sf")
        hand_on(1, "n", "m")
        hop(3, "n", "m", "sf")
        hand_on(2, "n", "m")

    @pl.when(first)
    def _():
        arrived("back", ARR)
        G[...] = ARR[...].astype(f32)

    back_rows = lambda: IG.at[pl.ds(trow, T)]

    def feed_back(j, i, g):
        b = (0.5 * g).astype(bf16)
        Ball[own, i * width : (i + 1) * width] = b
        to_pair(("b", i), Ball, block(i))
        if j:
            set_off(("b", i))
        grad = None
        for k in range(4):
            h = H[j, k]
            sig = jax.nn.sigmoid(h)
            hg = (dot(b, Wout[j, k], 1, 1) * slope(h, sig)).astype(bf16)
            part = dot(hg, Win[j, k], 1, 1)
            grad = part if grad is None else grad + part
        return g + norm_back(i, grad)
    g = norm_back(4, G[...] * row_mask)
    g = feed_back(1, 3, g)
    b = g.astype(bf16)
    Ball[own, 2 * width : 3 * width] = b
    to_pair(("b", 2), Ball, block(2))
    hat = CT[...]
    y = hat * SM[2:3] + SM[3:4]
    sig = jax.nn.sigmoid(y)
    dy = dot(b, Wco[...], 1, 1) * slope(y, sig)
    if not gathered:
        PAst[2:3] = total_of(dy * hat)
        PAst[3:4] = total_of(dy)
    dhat = dy * SM[2:3]
    masked = dhat * row_mask
    dp_sums("bnb", STB, [total_of(masked), total_of(masked * hat)])

    @pl.when(first)
    def _():
        hand_on(3, "n", "m")
        for i in range(4):
            from_pair(("n", i), Nall, block(i))
        all_shared("n", "m")
        forward_values()
        hop(1, ("b", 3))

    relay(("b", 3), Ball, block(3))
    sums = summed("bnb", STB)

    @pl.when(second)
    def _():
        for i in range(4):
            relay(("n", i), Nall, block(i))
        hop(1, "n")
        set_off("m")
        from_tensor("sf", Sf, sf_cols)
        set_off("sf")

    relay_output("out", LO)
    relay(("b", 2), Ball, block(2))
    set_off_to_all(("b", 2))
    dc = inv_std * (dhat - (sums[0] + hat * sums[1]) / count) * row_mask
    DP[margin : margin + T] = dc
    for p in range(4):
        c = pl.ds(C * p, C)
        here = DP[margin : margin + T, c]
        acc = None
        for k in range(taps):
            o = margin + taps // 2 - k
            term = SM[4 + k : 5 + k, c] * DP[o : o + T, c]
            acc = term if acc is None else acc + term
            if not gathered:
                o = margin - taps // 2 + k
                PAst[4 + k : 5 + k, c] = total_of(here * UP[o : o + T, c])
        CT[:, c] = acc
    du = CT[...] * row_mask
    sig = jax.nn.sigmoid(GVG[1])
    dvalue = (du * sig).astype(bf16)
    dgate = (du * GVG[0] * (sig * (1.0 - sig))).astype(bf16)
    def sb_to_tensor(name, c, k):
        start(name, lambda: SbSt.at[k, :, c], lambda: Sb.at[place(k), c], peers[k], None, k)

    if not gathered:
        for k in range(4):
            SbSt[k, :, 3 * C : 4 * C] = dvalue[:, C * k : C * (k + 1)]
            SbSt[k, :, 4 * C : 5 * C] = dgate[:, C * k : C * (k + 1)]
        Sb[own, 3 * C : 5 * C] = SbSt[0, :, 3 * C : 5 * C]
        for k in (1, 2, 3):
            sb_to_tensor("gates", gate_cols, k)
    g = g + norm_back(2, dot(dvalue, Wci[0], 1, 1) + dot(dgate, Wci[1], 1, 1))
    b = g.astype(bf16)
    Ball[own, width : 2 * width] = b
    to_pair(("b", 1), Ball, block(1))
    set_off(("b", 1))
    dmix = dot(b, Wo[...], 1, 1).astype(bf16).astype(f32)
    scale = HEAD ** (-0.5)
    dq, dk, dv = [None] * 4, [None] * 4, [None] * 4
    for p in (2, 3, 1, 0):
        c = pl.ds(2 * HEAD * p, 2 * HEAD)
        qu = pair_rows(QKV[0, :, c]).astype(bf16)
        qv = pair_rows(QKV[1, :, c]).astype(bf16)
        key = QKV[2, :, c].astype(bf16)
        val = QKV[3, :, c].astype(bf16)
        do = pair_rows(dmix[:, 2 * HEAD * p : 2 * HEAD * (p + 1)]).astype(bf16)
        probs = PRB[p]
        dprob = dot(do, val, 1, 1)
        ds = (probs * (dprob - jnp.sum(probs * dprob, -1, keepdims=True))).astype(bf16)
        du_rows = unpair(dot(ds, key)) * scale
        turned = dot(ds, flip)
        whole = jnp.concatenate(
            [
                pltpu.roll(turned[e * T : (e + 1) * T], 0, 1, stride=1, stride_axis=0)[:, : 2 * T]
                for e in range(2)
            ],
            0,
        ).astype(bf16)
        dv_rows = unpair(dot(whole, R2[2 * T : 4 * T, c])) * scale
        dk[p] = (dot(ds, qu, 0, 0) * scale).astype(bf16)
        dv[p] = dot(probs.astype(bf16), do, 0, 0).astype(bf16)
        dq[p] = (du_rows + dv_rows).astype(bf16)
        SbSt[p, :, 0:C] = dq[p]
        SbSt[p, :, C : 2 * C] = dk[p]
        SbSt[p, :, 2 * C : 3 * C] = dv[p]
        if p:
            sb_to_tensor("qkv", qkv_cols, p)
        PAst[0:1, c] = total_of(du_rows)
        PAst[1:2, c] = total_of(dv_rows)
        PAst[relative_at(groups) : relative_at(groups) + 2 * T, c] = dot(whole, qv, 0, 0) * scale
    Sb[own, 0 : 3 * C] = SbSt[0, :, 0 : 3 * C]
    @pl.when(first)
    def _():
        if not gathered:
            from_tensor("gates", Sb, gate_cols)
        hop(2, ("b", 3))
        relay(("b", 1), Ball, block(1))
    grad = dot(jnp.concatenate(dq, 1), Wqkv[0], 1, 1)
    grad += dot(jnp.concatenate(dk, 1), Wqkv[1], 1, 1)
    grad += dot(jnp.concatenate(dv, 1), Wqkv[2], 1, 1)
    g = g + norm_back(1, grad)

    @pl.when(second)
    def _():
        IG[pl.ds(trow, T)] = feed_back(0, 0, g).astype(bf16)
        start("back", back_rows, lambda: ARR, partner, second)

    @pl.when(first)
    def _():
        Ball[own, 0:width] = (0.5 * g).astype(bf16)
        to_pair(("b", 0), Ball, block(0))
        G[...] = g

    set_off_to_all(("b", 0))
    from_all(("b", 2))
    def sums_over_tensor(name, parts, ref):
        all_arrived(name, 3 * size_of(parts.at[0]))
        ref[mine] = sum(parts[k].astype(f32) for k in range(4)).astype(bf16)
        for r in range(1, groups):
            start((name, 3), lambda: ref.at[mine], lambda: ref.at[mine], zpeers[r], None, r)

    def send_sums():
        PAb[...] = PAst[...].astype(bf16)
        for k in (1, 2, 3):
            start("pa", lambda k=k: PAb.at[:, cols(k)], lambda k=k: PAin.at[k], peers[k], None, k)

    def send_ends():
        output_to_pair("grad", IG)
        PBin[t] = PBst[...].astype(bf16)
        for k in (1, 2, 3):
            start("pb", lambda: PBin.at[t], lambda: PBin.at[t], peers[k], None, k)

    bs = [("b", i) for i in range(4)]
    if not gathered:

        @pl.when(second)
        def _():
            from_tensor("gates", Sb, gate_cols)

    @pl.when(second)
    def _():
        send_ends()
        send_sums()
        hop(2, "n")
        hop(1, "m", "sf", bs[3])
        relay(bs[1], Ball, block(1))
        relay(bs[0], Ball, block(0))
        from_tensor("qkv", Sb, qkv_cols)
        set_off("qkv")
        hop(1, bs[1])
        hand_on(1, "n")
        from_all(bs[0])
        hand_on_all(bs[2])
        hop(3, "n")
        hop(2, "m", "sf", bs[3], bs[1])
        hand_on(2, "n")
        hop(1, "qkv")
        hand_on(1, "m", bs[3], bs[1])
        hop(3, "m", "sf", bs[3])
        hand_on(3, "n")
        hand_on_all(bs[0])
        hop(3, bs[1])
        hand_on(2, "m", bs[3], bs[1])
        hop(2, "qkv")
        hand_on(3, "m")
        for i in range(4):
            from_pair(("n", i), Nall, block(i))
        all_shared("n", "m")
        forward_values()

    @pl.when(first)
    def _():
        from_tensor("qkv", Sb, qkv_cols)
        set_off("qkv")
        hop(3, bs[3])
        hop(1, bs[1])
        hand_on(1, bs[3])
        hand_on(2, bs[3])
        relay(bs[0], Ball, block(0))
        total = 0.0
        for k in range(2):
            h = dot(Nall[two, 0:width], Win[0, k])
            hg = dot(Ball[two, 0:width], Wout[0, k], 1, 1) * slope(h, jax.nn.sigmoid(h))
            total += dot(hg.astype(bf16), Win[0, k], 1, 1)
        X[0] = sum_to_owner(("s", 2), 2, total)
        send_sums()
        hand_on_all(bs[2])
        from_all(bs[0])
        hop(1, "qkv")
        hop(2, bs[1])
    hand_on(3, bs[3])
    from_pair(bs[3], Ball, block(3))
    shared(bs[3], *whole_rows(bs[3]))
    feed_grads(1, 3)

    @pl.when(first)
    def _():
        g = G[...] + norm_back(0, summed_here(("s", 2), 2, X[0]))
        IG[pl.ds(trow, T)] = g.astype(bf16)
        send_ends()
        hand_on_all(bs[0])
        hop(2, "qkv")
        hop(3, bs[1])

    PAin[0] = PAb[:, 0:C]
    sums_over_tensor("pa", PAin, PA)
    from_pair(bs[2], Ball, block(2))
    shared(bs[2], *whole_rows(bs[2]))
    if gathered:
        convolution_rows_back()
    sums_over_tensor("pb", PBin, PB)

    @pl.when(first)
    def _():
        hand_on(1, bs[1])
        hand_on(2, bs[1])

    convolution_grads()
    relay_output("grad", IG)
    hand_on(3, bs[1])

    from_pair(bs[0], Ball, block(0))
    shared(bs[0], *whole_rows(bs[0]))
    feed_grads(0, 0)
    hop(3, "qkv")
    from_pair(bs[1], Ball, block(1))
    shared(bs[1], *whole_rows(bs[1]))
    attention_grads()
    for name, ref in (("pa", PA), ("pb", PB)):
        all_arrived((name, 3), (groups - 1) * size_of(ref.at[0]))
    all_arrived("out", 2 * size_of(back_rows()))
    all_arrived("grad", 2 * size_of(back_rows()))
    for src, dst in ((LO, lo_out), (IG, ig_out), (PA, pa_out), (PB, pb_out), (CS, cs_out)):
        write(src, dst)
    pltpu.make_async_copy(room(sum(written)), room(sum(written)), os.at[0]).wait()
    for cond, sizes in sent.values():

        def all_sent():
            view = room(sum(sizes.values()))
            copy_of("out", view, view, partner, cond).wait_send()

        all_sent() if cond is None else pl.when(cond)(all_sent)
    assert len(recv_index) <= rs.shape[0] and len(send_index) <= ss.shape[0]


def last_kernel(*refs):
    given, outs, held, made, in_sems, out_sems = refs[:12], refs[12:26], refs[26:38], refs[38:52], refs[52], refs[53]
    in_grad, out_grad, qkv, ao, ci, co, pa, pb, cs, lo, ig, table = held
    (LO, IG, ng, nb, w_in, w_out, w_ain, pos, w_aout, w_cin, w_dw, bng, bns, w_cout) = made
    C, width = ao.shape
    copies = []

    def send(src, dst):
        copy = pltpu.make_async_copy(src, dst, out_sems.at[len(copies)])
        copy.start()
        copies.append(copy)

    whole = [5, 3, 4, 2, 6, 7, 8, 9, 10, 11]
    halves = [(i, j) for i in range(2) for j in range(2)]
    pieces = [(given[i], held[i]) for i in whole[:4]]
    pieces += [(given[i].at[j], held[i].at[j]) for i, j in halves]
    pieces += [(given[i], held[i]) for i in whole[4:]]
    loads = [pltpu.make_async_copy(src, dst, in_sems.at[n]) for n, (src, dst) in enumerate(pieces)]
    for load in loads:
        load.start()
    loads[0].wait()
    w_cout[...] = co[...].astype(f32)
    send(w_cout, outs[13])
    loads[1].wait()
    w_aout[...] = ao[...].astype(f32)
    send(w_aout, outs[8])
    loads[2].wait()
    for i in range(2):
        w_cin[pl.ds(i, width, stride=2), :] = ci[:, C * i : C * (i + 1)].astype(f32)
    send(w_cin, outs[9])
    loads[3].wait()
    w_ain[0:3] = qkv[...].astype(f32)
    send(w_ain.at[pl.ds(0, 3)], outs[6].at[pl.ds(0, 3)])
    for n, (i, j) in enumerate(halves):
        loads[4 + n].wait()
        src, dst, out = ((in_grad, w_in, outs[4]), (out_grad, w_out, outs[5]))[i]
        dst[j] = src[j].astype(f32)
        send(dst.at[j], out.at[j])
    for load in loads[8:]:
        load.wait()
    sums, norms = pa[0].astype(f32), pb[0].astype(f32)
    for g in range(1, pa.shape[0]):
        sums += pa[g].astype(f32)
        norms += pb[g].astype(f32)
    w_ain[3] = dot(table[...], sums[relative_at(pa.shape[0]) :].astype(bf16), 0, 0)
    send(w_ain.at[3], outs[6].at[3])
    LO[...] = lo[...].astype(f32)
    IG[...] = ig[...].astype(f32)
    for i in range(5):
        ng[i] = norms[i : i + 1]
        nb[i] = norms[8 + i : 9 + i]
    pos[...] = sums[0:2]
    taps = w_dw.shape[0]
    if pa.shape[0] > 1:
        sums = jnp.concatenate([sums[0:2], cs[taps : taps + 2], cs[0:taps]], 0)
    bng[...] = sums[2:3]
    bns[...] = sums[3:4]
    for k in range(taps):
        w_dw[k] = sums[4 + k : 5 + k]
    for i in (0, 1, 2, 3, 7, 10, 11, 12):
        send(made[i], outs[i])
    for copy in copies:
        copy.wait()


def on_device(
    inputs, lengths, cotangent, norm_gain, norm_bias, ffn_in, ffn_out, attn_in, pos_bias, attn_out,
    conv_in, depthwise, bn_gain, bn_shift, conv_out,
):
    dp = lax.axis_size(DATA)
    group, frames, width = inputs.shape
    C = width // 4
    taps = depthwise.shape[1]
    groups = dp if dp <= 4 else 1
    R = groups * group * frames
    table = position_rows(frames, width)
    hbm = pl.BlockSpec(memory_space=pltpu.HBM)
    sums_rows = relative_at(groups) + 2 * frames

    def shape(dims, dtype=bf16):
        return jax.ShapeDtypeStruct(dims, dtype)

    small_first = [
        shape((group * frames, width)), shape((group * frames, width)), shape((groups, sums_rows, C)),
        shape((groups, 16, width)), shape((40, C), f32),
    ]
    made_first = [
        shape((2, width, width)), shape((2, width, width)), shape((3, width, C)), shape((C, width)),
        shape((width, 2 * C)), shape((C, width)),
    ]
    n_recv = 109 + 15 * (groups - 1)
    n_send = 3 + 2 * (groups - 1) + 2 * max(groups - 2, 0)
    operands = (
        lengths, inputs, cotangent, norm_gain.transpose(1, 0, 2), norm_bias.transpose(1, 0, 2), ffn_in[0],
        ffn_out[0], attn_in[0], attn_out[0], conv_in.reshape(2 * width, C), conv_out[0], pos_bias[0], bn_gain,
        bn_shift, depthwise.transpose(1, 0, 2), table[0],
    )
    lo, ig, pa, pb, cs, *ready = pl.pallas_call(
        lambda *refs: layer_kernel((frames, width, dp, groups), *refs),
        out_shape=small_first + made_first,
        in_specs=[hbm] * 16,
        out_specs=[hbm] * 11,
        scratch_shapes=[
            pltpu.VMEM((2, 4, width, width), bf16),
            pltpu.VMEM((2, 4, width, width), bf16),
            pltpu.VMEM((3, width, width), bf16),
            pltpu.VMEM((width, C), bf16),
            pltpu.VMEM((width, width), bf16),
            pltpu.VMEM((2, width, width), bf16),
            pltpu.VMEM((width, width), bf16),
            pltpu.VMEM((4 * frames, width), bf16),
            pltpu.VMEM((SMALL_ROWS, width), f32),
            pltpu.VMEM((2, 4, frames, width), f32),
            pltpu.VMEM((5, frames, width), f32),
            pltpu.VMEM((5, frames, 128), f32),
            pltpu.VMEM((5, frames, width), f32),
            pltpu.VMEM((frames, width), f32),
            pltpu.VMEM((frames, width), bf16),
            pltpu.VMEM((frames, width), bf16),
            pltpu.VMEM((4, frames, width), f32),
            pltpu.VMEM((4, 2 * frames, frames), f32),
            pltpu.VMEM((2, frames, width), f32),
            pltpu.VMEM((frames, width), f32),
            pltpu.VMEM((frames + 32, width), f32),
            pltpu.VMEM((frames + 32, width), f32),
            pltpu.VMEM((4, frames, 2 * C), bf16),
            pltpu.VMEM((4, frames, 5 * C), bf16),
            pltpu.VMEM((sums_rows, width), f32),
            pltpu.VMEM((sums_rows, width), bf16),
            pltpu.VMEM((4, sums_rows, C), bf16),
            pltpu.VMEM((16, width), f32),
            pltpu.VMEM((4, 16, width), bf16),
            pltpu.VMEM((dp, 8, C), f32),
            pltpu.VMEM((dp, 8, C), f32),
            pltpu.VMEM((4, frames, width), bf16),
            pltpu.VMEM((4, frames, width), bf16),
            pltpu.VMEM((5, 1, width), f32),
            pltpu.VMEM((5, 1, width), f32),
            pltpu.VMEM((2, C), f32),
            pltpu.VMEM((1, C), f32),
            pltpu.VMEM((1, C), f32),
            pltpu.VMEM((taps, 1, C), f32),
            pltpu.VMEM((2 * frames, width), bf16),
            pltpu.SMEM((group,), jnp.int32),
            pltpu.VMEM((2 * width, C), bf16),
            pltpu.VMEM((2 * width, C), f32),
            pltpu.VMEM((R, 4 * width), bf16),
            pltpu.VMEM((R, 4 * width), bf16),
            pltpu.VMEM((R, 2 * C), bf16),
            pltpu.VMEM((R, 5 * C), bf16),
            pltpu.VMEM((2, R, width), bf16),
            pltpu.VMEM((2, R, width), f32),
            pltpu.VMEM((R, width), bf16),
        ]
        + [pltpu.VMEM(m.shape, m.dtype) for m in made_first]
        + [
            pltpu.VMEM((2, R, C), f32),
            pltpu.VMEM((R, C), f32),
            pltpu.VMEM((R // frames, frames + 32, C), f32),
            pltpu.VMEM((R, C), f32),
            pltpu.VMEM((R // frames, frames + 32, C), f32),
            pltpu.VMEM((taps, 8, C), f32),
            pltpu.VMEM((4, 8, C), f32),
            pltpu.VMEM((2 * frames, C), bf16),
            pltpu.VMEM((dp, 8, C), f32),
            pltpu.VMEM((2, width // 4, width), bf16),
        ]
        + [pltpu.VMEM(m.shape, m.dtype) for m in small_first]
        + [
            pltpu.VMEM((10 * 2**20 // 512, 128), f32),
            pltpu.SemaphoreType.DMA((n_send,)),
            pltpu.SemaphoreType.DMA((n_recv,)),
            pltpu.SemaphoreType.DMA((21,)),
            pltpu.SemaphoreType.DMA((1,)),
        ],
        compiler_params=pltpu.CompilerParams(
            collective_id=0, has_side_effects=True, vmem_limit_bytes=62 * 2**20
        ),
    )(*operands)

    gradients = [
        shape((group * frames, width), f32), shape((group * frames, width), f32), shape((5, 1, width), f32),
        shape((5, 1, width), f32), shape((2, width, width), f32), shape((2, width, width), f32),
        shape((4, width, C), f32), shape((2, C), f32), shape((C, width), f32), shape((2 * width, C), f32),
        shape((taps, 1, C), f32), shape((1, C), f32), shape((1, C), f32), shape((C, width), f32),
    ]
    given = (*ready, pa, pb, cs, lo, ig, table[1])
    outs = pl.pallas_call(
        last_kernel,
        out_shape=gradients,
        in_specs=[hbm] * len(given),
        out_specs=[hbm] * len(gradients),
        scratch_shapes=[pltpu.VMEM(m.shape, m.dtype) for m in given]
        + [pltpu.VMEM(m.shape, m.dtype) for m in gradients]
        + [pltpu.SemaphoreType.DMA((len(given) + 2,)), pltpu.SemaphoreType.DMA((len(gradients) + 4,))],
        compiler_params=pltpu.CompilerParams(vmem_limit_bytes=62 * 2**20),
    )(*given)
    if groups == 1:
        outs = list(outs[:2]) + [lax.psum(m.astype(bf16), DATA).astype(f32) for m in outs[2:]]
    (lo, ig, ng, nb, w_in, w_out, w_ain, pos, w_aout, w_cin, w_dw, bng, bns, w_cout) = outs
    rows = (1, group, frames, width)
    return (
        lo.reshape(rows), ig.reshape(rows), ng.transpose(1, 0, 2), nb.transpose(1, 0, 2), w_in[None], w_out[None],
        w_ain[None], pos[None], w_aout[None], w_cin.reshape(conv_in.shape), w_dw.transpose(1, 0, 2), bng, bns,
        w_cout[None],
    )


def solution(mesh):
    placed = (
        P(DATA, None, None),
        P(DATA),
        P(DATA, None, None),
        P(SECTION, None, None),
        P(SECTION, None, None),
        P(SECTION, None, None, TENSOR),
        P(SECTION, None, TENSOR, None),
        P(SECTION, None, None, TENSOR),
        P(SECTION, None, TENSOR),
        P(SECTION, TENSOR, None),
        P(SECTION, None, None, TENSOR),
        P(SECTION, None, TENSOR),
        P(SECTION, TENSOR),
        P(SECTION, TENSOR),
        P(SECTION, TENSOR, None),
    )
    return jax.shard_map(
        on_device,
        mesh=mesh,
        in_specs=placed,
        out_specs=(
            P(SECTION, DATA, None, None),
            P(SECTION, DATA, None, None),
            P(SECTION, None, None),
            P(SECTION, None, None),
            P(SECTION, None, None, TENSOR),
            P(SECTION, None, TENSOR, None),
            P(SECTION, None, None, TENSOR),
            P(SECTION, None, TENSOR),
            P(SECTION, TENSOR, None),
            P(SECTION, None, None, TENSOR),
            P(SECTION, None, TENSOR),
            P(SECTION, TENSOR),
            P(SECTION, TENSOR),
            P(SECTION, TENSOR, None),
        ),
        check_vma=False,
    )
```

```python
import math

import jax
import jax.numpy as jnp
import numpy as np
from jax import lax
from jax.experimental import pallas as pl
from jax.experimental.pallas import tpu as pltpu
from jax.sharding import PartitionSpec as P

HEAD = 64
EPSILON = 1e-05
MESH = pl.DeviceIdType.MESH
SECTION, TENSOR, DATA = "section", "tensor", "dp"
PLACE = (0, 2, 1, 3)
SMALL_ROWS = 48


def relative_at(groups):
    return 16 if groups > 1 else SMALL_ROWS


bf16, f32 = jnp.bfloat16, jnp.float32


def dot(left, right, left_dim=1, right_dim=0):
    return lax.dot_general(
        left, right, (((left_dim,), (right_dim,)), ((), ())), preferred_element_type=f32
    )


def position_rows(frames, width):
    offset = np.arange(2 * frames - 1, dtype=np.float32) - np.float32(frames - 1)
    rates = np.exp(
        np.arange(width // 2, dtype=np.float32) * np.float32(-2.0 * math.log(10000.0) / width)
    )
    angles = (offset[:, None] * rates[None, :]).astype(np.float32)
    table = np.stack([np.sin(angles), np.cos(angles)], -1).reshape(2 * frames - 1, width)
    blank = np.zeros((1, width), np.float32)
    return [jnp.asarray(np.concatenate([rows, blank]), bf16) for rows in (table[::-1], table)]


def layer_kernel(dims, *refs):
    T, width, dp, groups = dims
    C = width // 4
    (lengths, inputs, cot, ng_in, nb_in, fin, fout, ain, aout, cin, cout, pos_in, bng_in, bns_in, dw_in, e2_in) = refs[:16]
    (lo_out, ig_out, pa_out, pb_out, cs_out) = refs[16:21]
    (in_out, out_out, qkv_out, ao_out, ci_out, co_out) = refs[21:27]
    refs = refs[27:]
    (Win, Wout, Wqkv, Wr, Wo, Wci, Wco, R2, SM) = refs[:9]
    (H, XH, RS, X, G, ARR, HOP, QKV, PRB, GVG, CT, UP, DP) = refs[9:22]
    (SfSt, SbSt, PAst, PAb, PAin, PBst, PBin, STF, STB, RSst, RSin) = refs[22:33]
    (ng, nb, pos, bng, bns, dw, e2, lens, pairs, spread) = refs[33:43]
    (Nall, Ball, Sf, Sb, ACT, SLOPE, HG, gin, gout, gqkv, gao, gci, gco) = refs[43:56]
    GA, HATA, UA, DYA, DA, DWACC, INVA, OST, STL, VIA = refs[56:66]
    LO, IG, PA, PB, CS, dummy, ss, rs, ls, os = refs[66:76]
    gathered = groups > 1

    s, t, d = lax.axis_index(SECTION), lax.axis_index(TENSOR), lax.axis_index(DATA)
    first, second = s == 0, s == 1
    taps = dw.shape[0]
    peers = [(s, t ^ k, d) for k in range(4)]
    sib, yp = peers[1], peers[2]
    around = {j: lax.rem(d + j + dp, dp) for j in range(1 - dp, dp)}
    zpeers = [(s, t, around[r]) for r in range(dp)]
    zpair = (s, t, d ^ 1)
    partner = (1 - s, t, d)
    half = lax.rem(d, 2)
    R4 = 4 * T
    reach = range(1 - groups, groups)
    base_of = {j: pl.multiple_of(around[j] * R4, R4) if groups > 1 else 0 for j in reach}
    second_of, high_of, last_of = (
        {j: pl.multiple_of(around[j] * R4 + n * T, T) if groups > 1 else n * T for j in reach} for n in (1, 2, 3)
    )
    there = {j: d + j >= 0 if j < 0 else d + j <= dp - 1 for j in reach}
    through = {
        (j, to): there[j] & there[to] for j in reach for to in (1, -1) if j * to < 0 and groups > 1
    }
    base = base_of[0]
    trow, yrow = pl.multiple_of(t * T, T), pl.multiple_of((t ^ 2) * T, T)
    mine = d if groups > 1 else 0

    recv_index, send_index, sent = {}, {}, {}

    def size_of(view):
        return math.prod(view.shape) * view.dtype.itemsize

    def copy_of(key, src, dst, dev, group):
        i = recv_index.setdefault(key, len(recv_index))
        j = send_index.setdefault(id(group), len(send_index))
        return pltpu.make_async_remote_copy(
            src_ref=src, dst_ref=dst, send_sem=ss.at[j], recv_sem=rs.at[i], device_id=dev, device_id_type=MESH,
        )

    def start(key, src, dst, dev, cond=None, part=0):
        view = src()
        copy_of(key, view, dst(), dev, cond).start()
        sent.setdefault(id(cond), (cond, {}))[1][key, part] = size_of(view)

    def arrived(key, dst):
        copy_of(key, dst, dst, partner, None).wait_recv()

    def room(size):
        return dummy.at[pl.ds(0, size // (4 * dummy.shape[1]))]

    def all_arrived(key, size):
        if size:
            arrived(key, room(size))

    locals_ = {}

    def fetch(name, src, dst):
        locals_[name] = lambda: pltpu.make_async_copy(src(), dst(), ls.at[list(locals_).index(name)])
        locals_[name]().start()

    def fetched(*names):
        for name in names:
            locals_[name]().wait()

    @pl.when(first)
    def _():
        pltpu.make_async_copy(inputs.at[t], X.at[0], ls.at[20]).start()

    @pl.when(second)
    def _():
        pltpu.make_async_copy(cot.at[t], G, ls.at[20]).start()

    fetch("ng", lambda: ng_in, lambda: ng)
    fetch("nb", lambda: nb_in, lambda: nb)
    fetch("in0", lambda: fin.at[0], lambda: Win.at[0, 0])
    fetch("out0", lambda: fout.at[0], lambda: Wout.at[0, 0])
    fetch("wr", lambda: ain.at[3], lambda: Wr)
    fetch("e2", lambda: e2_in, lambda: e2)
    fetch("pos", lambda: pos_in, lambda: pos)
    fetch("bng", lambda: bng_in, lambda: bng)
    fetch("bns", lambda: bns_in, lambda: bns)
    fetch("dw", lambda: dw_in, lambda: dw)
    fetch("len", lambda: lengths, lambda: lens)
    fetch("qkv", lambda: ain.at[pl.ds(0, 3)], lambda: Wqkv.at[:, :, pl.ds(0, C)])
    fetch("o", lambda: aout, lambda: Wo.at[pl.ds(0, C)])
    fetch("ci", lambda: cin, lambda: pairs)
    fetch("co", lambda: cout, lambda: Wco.at[pl.ds(0, C)])
    fetch("in1", lambda: fin.at[1], lambda: Win.at[1, 0])
    fetch("out1", lambda: fout.at[1], lambda: Wout.at[1, 0])

    barrier = pltpu.get_barrier_semaphore()
    greet = peers[1:] + zpeers[1:] + [partner]
    for dev in greet:
        pl.semaphore_signal(barrier, inc=1, device_id=dev, device_id_type=MESH)
    pl.semaphore_wait(barrier, len(greet))

    starts = {}

    def lines(first_row, n, which):
        if which is None:
            return pl.ds(first_row, n)
        at = (first_row, n, which)
        if at not in starts:
            starts[at] = pl.multiple_of(first_row + n // 2 * (half if which == "own" else 1 - half), n // 2)
        return pl.ds(starts[at], n // 2)

    def cols(k):
        return pl.ds(C * k, C)

    def feed_chunks(j):
        Q = width // 2
        return [
            (
                lambda w, src=src, q=q: src.at[j, lines(Q * q, Q, w)],
                lambda k, w, dst=dst, q=q: dst.at[j, k, lines(Q * q, Q, w)],
            )
            for src, dst in ((fin, Win), (fout, Wout))
            for q in range(2)
        ]

    def row_chunk(src, dst):
        return [(lambda w: src.at[lines(0, C, w)], lambda k, w: dst.at[lines(C * k, C, w)])]

    def column_chunks(src, dst, n):
        return [
            (lambda w, i=i: src(i, lines(0, width, w)), lambda k, w, i=i: dst.at[i, lines(0, width, w), cols(k)])
            for i in range(n)
        ]

    chunks = (
        feed_chunks(0)
        + column_chunks(lambda i, rows: ain.at[i, rows], Wqkv, 3)
        + row_chunk(aout, Wo)
        + column_chunks(lambda i, rows: Wci.at[i, rows, cols(0)], Wci, 2)
        + row_chunk(cout, Wco)
        + feed_chunks(1)
        + [
            (lambda w: SM.at[:, cols(0)], lambda k, w: SM.at[:, cols(k)]),
            (lambda w: R2.at[pl.ds(0, 2 * T), cols(0)], lambda k, w: R2.at[pl.ds(0, 2 * T), cols(k)]),
        ]
    )
    for n, at in ((width // 2, 0), (width // 2, width // 2), (width, 0)) + tuple((C, C * k) for k in range(4)):
        for w in ("own", "other"):
            lines(at, n, w)
    only = {i: second for i in range(4)}
    over_y = {i: "own" for i in range(14)}

    def send_core(names):
        for i in names:
            src, dst = chunks[i]
            start(("sib", i), lambda src=src: src(None), lambda dst=dst: dst(1, None), sib)

    def send_y(names):
        for i in names:
            (src, dst), w = chunks[i], over_y.get(i)
            cond = first if i == 13 else only.get(i)
            start(("y", i), lambda src=src, w=w: src(w), lambda dst=dst, w=w: dst(2, w), yp, cond)

    def send_round():
        start(("r", 0), lambda: chunks[13][0]("own"), lambda: VIA.at[0], partner, second)

    def pass_round(n):
        arrived(("r", n - 1), VIA.at[n - 1])
        if n == 1:
            start(("r", 1), lambda: VIA.at[0], lambda: VIA.at[1], yp, first)
        else:
            start(("r", 2), lambda: VIA.at[1], lambda: chunks[13][1](2, "own"), partner, first)

    def step_a(i, by="y"):
        dst, w = chunks[i][1], over_y.get(i)
        arrived(("r", 2) if by == "r" else ("y", i), dst(2, w))
        if w:
            start(("z", i), lambda: dst(2, w), lambda: dst(2, w), zpair, only.get(i))
        start(("on", i), lambda: dst(2, w), lambda: dst(3, w), sib, only.get(i), 1)

    def step_b(i):
        if i not in over_y:
            return
        dst = chunks[i][1]
        arrived(("z", i), dst(2, "other"))
        start(("on", i), lambda: dst(2, "other"), lambda: dst(3, "other"), sib, only.get(i), 2)

    def core_part(i):
        arrived(("sib", i), chunks[i][1](1, None))

    def passed_part(i):
        all_arrived(("on", i), size_of(chunks[i][1](1, None)))

    def step_c(i):
        core_part(i)
        passed_part(i)

    def steps(cond, *plan):
        @pl.when(cond)
        def _():
            for step, i in plan:
                step(i)

    A, B, W = step_a, step_b, step_c

    def norm(i, x):
        centre = x - jnp.mean(x, -1, keepdims=True)
        rate = lax.rsqrt(jnp.mean(centre * centre, -1, keepdims=True) + EPSILON)
        hat = centre * rate
        XH[i] = hat
        RS[i] = jnp.broadcast_to(rate, RS.shape[1:])
        return hat * ng[i] + nb[i]

    def norm_back(i, grad):
        hat = XH[i]
        PBst[i : i + 1] = jnp.sum(grad * hat, 0, keepdims=True)
        PBst[8 + i : 9 + i] = jnp.sum(grad, 0, keepdims=True)
        g = grad * ng[i]
        return RS[i][:, 0:1] * (
            g - jnp.mean(g, -1, keepdims=True) - hat * jnp.mean(g * hat, -1, keepdims=True)
        )

    def total_of(v):
        return jnp.sum(v, 0, keepdims=True)

    def silu(h):
        return h * jax.nn.sigmoid(h)

    def place(k):
        return pl.ds(base + T * PLACE[k], T)

    own, two = pl.ds(base, T), pl.ds(base, 2 * T)

    def block(i, n=1):
        return pl.ds(i * width, n * width)

    def from_tensor(name, ref, c):
        all_arrived(name, 3 * size_of(ref.at[own, c]))

    def to_pair(name, ref, c, cond=None):
        start(name, lambda: ref.at[own, c], lambda: ref.at[place(1), c], sib, cond, 4)
        start((name, 4), lambda: ref.at[own, c], lambda: ref.at[place(2), c], yp, cond)

    def relay(name, ref, c, cond=None):
        arrived((name, 4), ref.at[place(2), c])
        start(name, lambda: ref.at[place(2), c], lambda: ref.at[place(3), c], sib, cond, 5)

    def from_pair(name, ref, c):
        all_arrived(name, 2 * size_of(ref.at[own, c]))

    def feed(j, i, before, after):
        x = X[before]
        a = norm(i, x).astype(bf16)
        Nall[own, i * width : (i + 1) * width] = a
        to_pair(("n", i), Nall, block(i))
        if j:
            step_c(11)
            step_c(12)
        active = []
        for k in range(4):
            h = dot(a, Win[j, k])
            H[j, k] = h
            active.append(silu(h).astype(bf16))
        Q, total = width // 2, 0.0
        for q in range(2):
            if j:
                step_c(13 + q)
            for k in range(4):
                total += dot(active[k][:, Q * q : Q * (q + 1)], Wout[j, k, Q * q : Q * (q + 1)])
        X[after] = x + 0.5 * total

    def sum_to_owner(name, slot, total):
        RSst[slot] = total[T : 2 * T].astype(bf16)
        start(name, lambda: RSst.at[slot], lambda: RSin.at[slot], yp, first)
        return total[0:T]

    def summed_here(name, slot, total):
        arrived(name, RSin.at[slot])
        return total + RSin[slot].astype(f32)

    def shared_feed(j, i):
        relay(("n", i), Nall, block(i))
        a = Nall[two, i * width : (i + 1) * width]
        total = dot(silu(dot(a, Win[j, 0])).astype(bf16), Wout[j, 0])
        for k in range(11 * j, 11 * j + 4):
            core_part(k)
        total += dot(silu(dot(a, Win[j, 1])).astype(bf16), Wout[j, 1])
        return sum_to_owner(("s", j), j, total)

    fetched("ng", "nb")

    @pl.when(first)
    def _():
        pltpu.make_async_copy(inputs.at[t], X.at[0], ls.at[20]).wait()
        Nall[own, 0:width] = norm(0, X[0]).astype(bf16)
        to_pair(("n", 0), Nall, block(0))

    send_core(range(4))

    @pl.when(second)
    def _():
        send_round()
        send_y(range(4))
        pltpu.make_async_copy(cot.at[t], G, ls.at[20]).wait()

    fetched("pos", "bng", "bns", "dw", "wr", "e2", "len", "ci")
    spread[...] = pairs[...].astype(f32)
    for i in range(2):
        Wci[i, :, 0:C] = spread[pl.ds(i, width, stride=2), :].astype(bf16)
    SM[:, 0:C] = jnp.zeros((SMALL_ROWS, C), f32)
    SM[0:2, 0:C] = pos[...]
    SM[2:3, 0:C] = bng[...]
    SM[3:4, 0:C] = bns[...]
    for k in range(taps):
        SM[4 + k : 5 + k, 0:C] = dw[k]
    R2[0 : 2 * T, 0:C] = dot(e2[...], Wr[...]).astype(bf16)
    lengths_here = [jnp.broadcast_to(lens[t ^ PLACE[p]].astype(f32), (1, C)) for p in range(4)]
    STL[d] = jnp.concatenate(lengths_here + [jnp.zeros((4, C), f32)], 0)
    for r in range(1, dp):
        start("len", lambda: STL.at[d], lambda: STL.at[d], zpeers[r], None, r)
    fetched("in0", "out0")

    @pl.when(first)
    def _():
        send_core((15, 16, 4, 5, 6, 7, 8, 9, 10))
        send_y((8,))
        X[1] = shared_feed(0, 0)
        send_y((9,))

    @pl.when(first)
    def _():
        step_a(8)
        X[1] = X[0] + 0.5 * summed_here(("s", 0), 0, X[1])

    @pl.when(second)
    def _():
        for i in (15, 16, *range(4, 15)):
            send_core((i,))
            if i != 13:
                send_y((i,))

    fetched("qkv", "o", "co", "in1", "out1")
    margin = 16
    UP[...] = jnp.zeros(UP.shape, f32)
    DP[...] = jnp.zeros(DP.shape, f32)
    PAst[...] = jnp.zeros(PAst.shape, f32)
    PBst[...] = jnp.zeros(PBst.shape, f32)
    CS[...] = jnp.zeros(CS.shape, f32)
    if gathered:
        DA[...] = jnp.zeros(DA.shape, f32)
        DWACC[...] = jnp.zeros(DWACC.shape, f32)

    def keys_of(length):
        return lax.broadcasted_iota(jnp.int32, (2 * T, T), 1) < length

    row_mask = (lax.broadcasted_iota(jnp.int32, (T, 1), 0) < lens[t]).astype(f32)
    first_head = lax.broadcasted_iota(jnp.int32, (T, 2 * HEAD), 1) < HEAD
    flip = (
        lax.broadcasted_iota(jnp.int32, (T, 4 * T), 0) + lax.broadcasted_iota(jnp.int32, (T, 4 * T), 1)
        == T - 1
    ).astype(f32).astype(bf16)

    def pair_rows(v):
        return jnp.concatenate([jnp.where(first_head, v, 0.0), jnp.where(first_head, 0.0, v)], 0)

    def unpair(v):
        return jnp.where(first_head, v[:T], v[T:])

    def attend(qu, qv, key, value, relative, keys):
        content = dot(pair_rows(qu).astype(bf16), key, 1, 1)
        whole = dot(pair_rows(qv).astype(bf16), jnp.concatenate([relative, jnp.zeros_like(relative)], 0), 1, 1)
        placed = jnp.concatenate(
            [
                pltpu.roll(whole[e * T : (e + 1) * T], 4 * T - (T - 1), 1, stride=1, stride_axis=0)[:, :T]
                for e in range(2)
            ],
            0,
        )
        scores = jnp.where(keys, (content + placed) * HEAD ** (-0.5), -1e30)
        e = jnp.exp(scores - jnp.max(scores, -1, keepdims=True))
        probs = e / jnp.sum(e, -1, keepdims=True)
        return probs, unpair(dot(probs.astype(bf16), value)).astype(bf16)

    def attention_here():
        a = Nall[own, width : 2 * width]
        q = dot(a, Wqkv[0])
        QKV[0] = q + SM[0:1]
        QKV[1] = q + SM[1:2]
        QKV[2] = dot(a, Wqkv[1])
        QKV[3] = dot(a, Wqkv[2])
        keys, mixed = keys_of(lens[t]), []
        for p in range(4):
            c = pl.ds(2 * HEAD * p, 2 * HEAD)
            probs, out = attend(
                QKV[0, :, c], QKV[1, :, c], QKV[2, :, c].astype(bf16), QKV[3, :, c].astype(bf16), R2[0 : 2 * T, c], keys
            )
            PRB[p] = probs
            mixed.append(out)
        return mixed

    def shared_attention():
        for i in (4, 5, 6, 15, 16):
            core_part(i)
        a = Nall[two, width : 2 * width]
        q, key, value = (dot(a, Wqkv[i, :, 0 : 2 * C]) for i in range(3))
        qu, qv, key, value = q + SM[0:1, 0 : 2 * C], q + SM[1:2, 0 : 2 * C], key.astype(bf16), value.astype(bf16)
        mixed = [[], []]
        for p in range(2):
            rows, keys = slice(T * p, T * (p + 1)), keys_of(lens[t ^ PLACE[p]])
            for k in range(2):
                c = slice(C * k, C * (k + 1))
                mixed[k].append(
                    attend(qu[rows, c], qv[rows, c], key[rows, c], value[rows, c], R2[0 : 2 * T, c], keys)[1]
                )
        mixed = [jnp.concatenate(m, 0) for m in mixed]
        Sf[two, 0:C] = mixed[0]
        OST[...] = mixed[1]
        start("sf", lambda: OST, lambda: Sf.at[pl.ds(high_of[0], 2 * T), pl.ds(0, C)], sib, first, 4)
        core_part(7)
        return sum_to_owner(("s", 3), 3, dot(mixed[0], Wo[0:C]) + dot(mixed[1], Wo[C : 2 * C]))

    def relative_arrived():
        passed_part(16)
        turned_back = (
            lax.broadcasted_iota(jnp.int32, (2 * T, 2 * T), 0) + lax.broadcasted_iota(jnp.int32, (2 * T, 2 * T), 1)
            == 2 * T - 2
        ).astype(f32).astype(bf16)
        R2[2 * T : 4 * T] = dot(turned_back, R2[0 : 2 * T]).astype(bf16)


    @pl.when(first)
    def _():
        Nall[own, width : 2 * width] = norm(1, X[1]).astype(bf16)
        to_pair(("n", 1), Nall, block(1))
        send_y((15,))
        pass_round(1)
        send_y((10,))
        step_a(9)
        step_b(8)
        relay(("n", 1), Nall, block(1))
        total = shared_attention()
        send_y((4, 5, 6, 16, 7))
        step_a(15)
        step_b(9)
        X[2] = X[1] + summed_here(("s", 3), 3, total)
        pass_round(2)
        step_a(10)
        passed_part(15)

    @pl.when(second)
    def _():
        coming = (*range(4), 15, 16, *range(4, 14))
        for n, i in enumerate(coming):
            step_a(i, "r" if i == 13 else "y")
            if n > 1 and i != 13:
                step_b(coming[n - 2])
        for i in range(7):
            step_c(i)
        step_c(15)
        core_part(16)
        relative_arrived()
        arrived("hop", ARR)
        X[0] = ARR[...].astype(f32)
        feed(0, 0, 0, 1)
        Nall[own, width : 2 * width] = norm(1, X[1]).astype(bf16)
        to_pair(("n", 1), Nall, block(1))
        mixed = attention_here()
        step_b(11)
        for k in range(4):
            SfSt[k, :, 0:C] = mixed[k]
        step_c(7)
        X[2] = X[1] + dot(jnp.concatenate(mixed, 1), Wo[...])

    def line_start(name, region):
        for way, to, back in (("up", 1, -1), ("down", -1, 1)):
            if groups > 1:

                @pl.when(there[to])
                def _():
                    start(
                        (name, 0, back % dp), lambda: region(0), lambda: region(0), (s, t, around[to]), there[to], way
                    )

    def line_hop(name, region, n, after=None):
        for way, to, back in (("up", 1, -1), ("down", -1, 1)):
            if n < groups:

                @pl.when(there[back * n])
                def _():
                    j = back * n
                    arrived((name, 0, j % dp), region(j))
                    if n + 1 < groups:

                        @pl.when(there[to])
                        def _():
                            start(
                                (name, 0, (j + back) % dp), lambda: region(j), lambda: region(j),
                                (s, t, around[to]), through[j, to], way,
                            )

                    if after is not None:
                        after(name, j)

    def rows_region(ref, n, c):
        return lambda j: ref.at[pl.ds(base_of[j], n), c]

    def share(ref, c):
        def go(name, j):
            rows = lambda: ref.at[pl.ds(base_of[j], T), c]
            start((name, 1, j % dp), rows, lambda: ref.at[pl.ds(second_of[j], T), c], yp, there[j], j)
            start((name, 2, 0), rows, lambda: ref.at[pl.ds(high_of[j], T), c], sib, there[j], j)

        return go

    def share_on(name, ref, c, n):
        for j in (n, -n):
            if n < groups:

                @pl.when(there[j])
                def _():
                    rows = lambda: ref.at[pl.ds(second_of[j], T), c]
                    arrived((name, 1, j % dp), rows())
                    start((name, 2, 0), rows, lambda: ref.at[pl.ds(last_of[j], T), c], sib, there[j], dp + j)

    def shared(name, ref, c):
        all_arrived((name, 2, 0), 2 * (groups - 1) * size_of(ref.at[own, c]))

    def set_off_to_all(name):
        ref, c = whole_rows(name)
        mine = lambda: ref.at[own, c]
        for r in range(1, groups):
            start((name, 0, (-r) % dp), mine, mine, zpeers[r], None, r)

    def from_all(name):
        ref, c = whole_rows(name)
        for r in range(1, groups):
            rows = lambda r=r: ref.at[pl.ds(base_of[r], T), c]
            arrived((name, 0, r), rows())
            start((name, 1, r), rows, lambda r=r: ref.at[pl.ds(second_of[r], T), c], yp, None, r)
            start((name, 2, 0), rows, lambda r=r: ref.at[pl.ds(high_of[r], T), c], sib, None, r)

    def hand_on_all(name):
        ref, c = whole_rows(name)
        for r in range(1, groups):
            rows = lambda r=r: ref.at[pl.ds(second_of[r], T), c]
            arrived((name, 1, r), rows())
            start((name, 2, 0), rows, lambda r=r: ref.at[pl.ds(last_of[r], T), c], sib, None, dp + r)

    def all_shared(*names):
        for name in names:
            shared(name, *whole_rows(name))

    sf_cols = pl.ds(0, C if gathered else 2 * C)
    qkv_cols, gate_cols = pl.ds(0, 3 * C), pl.ds(3 * C, 2 * C)
    lines_of = {
        "n": (rows_region(Nall, T, block(0, 3)), share(Nall, block(0, 3))),
        "m": (rows_region(Nall, T, block(3)), share(Nall, block(3))),
        "sf": (rows_region(Sf, R4, sf_cols), None),
        "qkv": (rows_region(Sb, R4, qkv_cols), None),
    }
    for i in range(4):
        lines_of["b", i] = (rows_region(Ball, T, block(i)), share(Ball, block(i)))

    def set_off(*names):
        for name in names:
            line_start(name, lines_of[name][0])

    def hop(n, *names):
        for name in names:
            line_hop(name, lines_of[name][0], n, lines_of[name][1])

    def whole_rows(name):
        if name in ("n", "m"):
            return Nall, block(0, 3) if name == "n" else block(3)
        return Ball, block(name[1])

    def hand_on(n, *names):
        for name in names:
            share_on(name, *whole_rows(name), n)

    written = []

    def write(src, dst):
        pltpu.make_async_copy(src, dst, os.at[0]).start()
        written.append(size_of(src))

    R = Nall.shape[0]
    row_blocks = [slice(r, r + R4) for r in range(0, R, R4)]

    def slope(h, sig):
        return sig * (1.0 + h * (1.0 - sig))

    def hidden_rows(j, i):
        for rows in row_blocks:
            h = dot(Nall[rows, i * width : (i + 1) * width], Win[j, 0])
            sig = jax.nn.sigmoid(h)
            ACT[j, rows] = (h * sig).astype(bf16)
            SLOPE[j, rows] = slope(h, sig)

    def feed_grads(j, i):
        c = slice(i * width, (i + 1) * width)
        for rows in row_blocks:
            HG[rows] = (dot(Ball[rows, c], Wout[j, 0], 1, 1) * SLOPE[j, rows]).astype(bf16)
        gin[j] = dot(Nall[:, c], HG[...], 0, 0).astype(bf16)
        write(gin.at[j], in_out.at[j])
        gout[j] = dot(ACT[j], Ball[:, c], 0, 0).astype(bf16)
        write(gout.at[j], out_out.at[j])

    def mask_of(g, p):
        return (lax.broadcasted_iota(jnp.int32, (T, C), 0).astype(f32) < STL[g, p : p + 1]).astype(f32)

    places = [(p, [(g, slice(R4 * g + T * p, R4 * g + T * (p + 1))) for g in range(groups)]) for p in range(4)]

    def convolution_rows():
        for i in range(2):
            GA[i] = dot(Nall[:, 2 * width : 3 * width], Wci[i, :, 0:C])
        UA[...] = jnp.zeros(UA.shape, f32)
        for p, parts in places:
            for g, rows in parts:
                UA[4 * g + p, margin : margin + T] = GA[0, rows] * jax.nn.sigmoid(GA[1, rows]) * mask_of(g, p)

        def one(b, carry):
            acc = SM[4:5, 0:C] * UA[b, margin - taps // 2 : margin - taps // 2 + T]
            for k in range(1, taps):
                o = margin - taps // 2 + k
                acc += SM[4 + k : 5 + k, 0:C] * UA[b, o : o + T]
            HATA[pl.ds(b * T, T)] = acc
            return carry

        lax.fori_loop(0, 4 * groups, one, 0)
        for p, parts in places:
            n = sum(STL[g, p : p + 1] for g, _ in parts)
            masked = [HATA[rows] * mask_of(g, p) for g, rows in parts]
            mean = sum(total_of(m) for m in masked) / n
            square = sum(total_of(m * HATA[rows]) for m, (_, rows) in zip(masked, parts)) / n
            inv = lax.rsqrt(square - mean * mean + EPSILON)
            INVA[p, 0:1] = inv
            INVA[p, 1:2] = n
            for g, rows in parts:
                h = (HATA[rows] - mean) * inv
                HATA[rows] = h
                Sf[rows, C : 2 * C] = silu(h * SM[2:3, 0:C] + SM[3:4, 0:C]).astype(bf16)

    def convolution_rows_back():
        DYA[...] = dot(Ball[:, 2 * width : 3 * width], Wco[0:C], 1, 1)
        gain_sum = shift_sum = jnp.zeros((1, C), f32)
        for p, parts in places:
            first_sum = second_sum = jnp.zeros((1, C), f32)
            for g, rows in parts:
                h = HATA[rows]
                y = h * SM[2:3, 0:C] + SM[3:4, 0:C]
                dy = DYA[rows] * slope(y, jax.nn.sigmoid(y))
                gain_sum += total_of(dy * h)
                shift_sum += total_of(dy)
                dh = dy * SM[2:3, 0:C]
                DYA[rows] = dh
                dh = dh * mask_of(g, p)
                first_sum += total_of(dh)
                second_sum += total_of(dh * h)
            inv, n = INVA[p, 0:1], INVA[p, 1:2]
            for g, rows in parts:
                dc = inv * (DYA[rows] - (first_sum + HATA[rows] * second_sum) / n) * mask_of(g, p)
                DA[4 * g + p, margin : margin + T] = dc
        CS[taps : taps + 1] = gain_sum
        CS[taps + 1 : taps + 2] = shift_sum

        def one(b, carry):
            here = DA[b, margin : margin + T]
            acc = jnp.zeros((T, C), f32)
            for k in range(taps):
                o = margin + taps // 2 - k
                acc += SM[4 + k : 5 + k, 0:C] * DA[b, o : o + T]
                o = margin - taps // 2 + k
                term = here * UA[b, o : o + T]
                DWACC[k] += sum(term[8 * i : 8 * (i + 1)] for i in range(T // 8))
            DYA[pl.ds(b * T, T)] = acc
            return carry

        lax.fori_loop(0, 4 * groups, one, 0)
        for k in range(taps):
            CS[k : k + 1] = total_of(DWACC[k])
        for p, parts in places:
            for g, rows in parts:
                sig = jax.nn.sigmoid(GA[1, rows])
                dua = DYA[rows] * mask_of(g, p)
                Sb[rows, 3 * C : 4 * C] = (dua * sig).astype(bf16)
                Sb[rows, 4 * C : 5 * C] = (dua * GA[0, rows] * (sig * (1.0 - sig))).astype(bf16)

    def convolution_grads():
        gci[...] = dot(Nall[:, 2 * width : 3 * width], Sb[:, 3 * C : 5 * C], 0, 0).astype(bf16)
        write(gci, ci_out)
        gco[...] = dot(Sf[:, C : 2 * C], Ball[:, 2 * width : 3 * width], 0, 0).astype(bf16)
        write(gco, co_out)

    def attention_grads():
        grads = dot(Nall[:, width : 2 * width], Sb[:, 0 : 3 * C], 0, 0)
        for i in range(3):
            gqkv[i] = grads[:, C * i : C * (i + 1)].astype(bf16)
        write(gqkv, qkv_out)
        gao[...] = dot(Sf[:, 0:C], Ball[:, width : 2 * width], 0, 0).astype(bf16)
        write(gao, ao_out)

    def forward_values():
        hidden_rows(1, 3)
        hidden_rows(0, 0)
        if gathered:
            convolution_rows()

    a = norm(2, X[2]).astype(bf16)
    Nall[own, 2 * width : 3 * width] = a
    to_pair(("n", 2), Nall, block(2))

    step_c(8)
    step_c(9)
    GVG[0] = dot(a, Wci[0])
    GVG[1] = dot(a, Wci[1])
    UP[margin : margin + T] = GVG[0] * jax.nn.sigmoid(GVG[1]) * row_mask
    for p in range(4):
        c = pl.ds(C * p, C)
        acc = SM[4:5, c] * UP[margin - taps // 2 : margin - taps // 2 + T, c]
        for k in range(1, taps):
            o = margin - taps // 2 + k
            acc += SM[4 + k : 5 + k, c] * UP[o : o + T, c]
        CT[:, c] = acc
    conv = CT[...]

    def dp_sums(name, ref, rows):
        ref[d] = jnp.concatenate([row[:, C * k : C * (k + 1)] for row in rows for k in range(4)], 0)
        for r in range(1, dp):
            start(name, lambda: ref.at[d], lambda: ref.at[d], zpeers[r], None, r)

    def summed(name, ref):
        all_arrived(name, (dp - 1) * size_of(ref.at[0]))
        total = ref[0]
        for r in range(1, dp):
            total += ref[r]
        return [jnp.concatenate([total[4 * i + k : 4 * i + k + 1] for k in range(4)], 1) for i in range(2)]

    masked = conv * row_mask
    dp_sums("bnf", STF, [total_of(masked), total_of(masked * conv)])
    steps(second, (B, 12), (A, 14))
    steps(first, (B, 10))
    step_c(10)
    sums = summed("bnf", STF)
    steps(second, (B, 13))
    steps(first, (A, 4), (A, 5), (A, 6), (A, 16))

    @pl.when(second)
    def _():
        set_off("n")
    all_arrived("len", (dp - 1) * size_of(STL.at[0]))
    count = sum(STL[r, 0:1, 0:1] for r in range(dp))
    bn_mean = sums[0] / count
    inv_std = lax.rsqrt(sums[1] / count - bn_mean * bn_mean + EPSILON)
    hat = (conv - bn_mean) * inv_std
    CT[...] = hat
    active = silu(hat * SM[2:3] + SM[3:4]).astype(bf16)
    if not gathered:
        for k in range(4):
            SfSt[k, :, C : 2 * C] = active[:, C * k : C * (k + 1)]
    X[3] = X[2] + dot(active, Wco[...])

    @pl.when(first)
    def _():
        Nall[own, 3 * width : 4 * width] = norm(3, X[3]).astype(bf16)
        to_pair(("n", 3), Nall, block(3))
        send_core((11, 12, 13, 14))
        total = shared_feed(1, 3)
        send_y((11, 12, 13, 14))
        step_a(7)
        step_b(4)
        step_b(5)
        X[4] = X[3] + 0.5 * summed_here(("s", 1), 1, total)

    @pl.when(second)
    def _():
        feed(1, 3, 3, 4)
    out = (norm(4, X[4]) * row_mask).astype(bf16)
    HOP[...] = out

    @pl.when(first)
    def _():
        start("hop", lambda: HOP, lambda: ARR, partner, first)

    LO[pl.ds(trow, T)] = out
    def output_to_pair(name, ref):
        rows = lambda: ref.at[pl.ds(trow, T)]
        start(name, rows, rows, sib)
        start((name, 4), rows, rows, yp)

    def relay_output(name, ref):
        rows = lambda: ref.at[pl.ds(yrow, T)]
        arrived((name, 4), rows())
        start(name, rows, rows, sib, None, 1)

    output_to_pair("out", LO)

    for cond, c in ((first, pl.ds(C, C)), (second, sf_cols))[gathered:]:

        @pl.when(cond)
        def _():
            Sf[own, c] = SfSt[0, :, c]
            for k in (1, 2, 3):
                start("sf", lambda k=k: SfSt.at[k, :, c], lambda k=k: Sf.at[place(k), c], peers[k], cond, k)

    @pl.when(first)
    def _():
        set_off("n", "m")
        if gathered:
            all_arrived("sf", size_of(OST))
            set_off("sf")
        relay(("n", 2), Nall, block(2))
        step_a(11)
        for i in (6, 7):
            step_b(i)
        step_a(12)
        step_b(11)
        for i in (4, 5, 6, 7):
            passed_part(i)
        relative_arrived()
        attention_here()
        step_a(13)
        step_b(12)
        if not gathered:
            all_arrived("sf", size_of(OST) + 3 * size_of(Sf.at[own, pl.ds(C, C)]))
        step_a(14)
        hop(1, "n", "m", "sf")
        step_b(13)
        for i in range(11, 15):
            passed_part(i)
        for k in range(4):
            H[1, k] = dot(Nall[own, 3 * width : 4 * width], Win[1, k])
        hop(2, "n", "m", "sf")
        hand_on(1, "n", "m")
        hop(3, "n", "m", "sf")
        hand_on(2, "n", "m")

    @pl.when(first)
    def _():
        arrived("back", ARR)
        G[...] = ARR[...].astype(f32)

    back_rows = lambda: IG.at[pl.ds(trow, T)]

    def feed_back(j, i, g):
        b = (0.5 * g).astype(bf16)
        Ball[own, i * width : (i + 1) * width] = b
        to_pair(("b", i), Ball, block(i))
        if j:
            set_off(("b", i))
        grad = None
        for k in range(4):
            h = H[j, k]
            sig = jax.nn.sigmoid(h)
            hg = (dot(b, Wout[j, k], 1, 1) * slope(h, sig)).astype(bf16)
            part = dot(hg, Win[j, k], 1, 1)
            grad = part if grad is None else grad + part
        return g + norm_back(i, grad)
    g = norm_back(4, G[...] * row_mask)
    g = feed_back(1, 3, g)
    b = g.astype(bf16)
    Ball[own, 2 * width : 3 * width] = b
    to_pair(("b", 2), Ball, block(2))
    hat = CT[...]
    y = hat * SM[2:3] + SM[3:4]
    sig = jax.nn.sigmoid(y)
    dy = dot(b, Wco[...], 1, 1) * slope(y, sig)
    if not gathered:
        PAst[2:3] = total_of(dy * hat)
        PAst[3:4] = total_of(dy)
    dhat = dy * SM[2:3]
    masked = dhat * row_mask
    dp_sums("bnb", STB, [total_of(masked), total_of(masked * hat)])

    @pl.when(first)
    def _():
        hand_on(3, "n", "m")
        for i in range(4):
            from_pair(("n", i), Nall, block(i))
        all_shared("n", "m")
        forward_values()
        hop(1, ("b", 3))

    relay(("b", 3), Ball, block(3))
    sums = summed("bnb", STB)

    @pl.when(second)
    def _():
        for i in range(4):
            relay(("n", i), Nall, block(i))
        hop(1, "n")
        set_off("m")
        from_tensor("sf", Sf, sf_cols)
        set_off("sf")

    relay_output("out", LO)
    relay(("b", 2), Ball, block(2))
    set_off_to_all(("b", 2))
    dc = inv_std * (dhat - (sums[0] + hat * sums[1]) / count) * row_mask
    DP[margin : margin + T] = dc
    for p in range(4):
        c = pl.ds(C * p, C)
        here = DP[margin : margin + T, c]
        acc = None
        for k in range(taps):
            o = margin + taps // 2 - k
            term = SM[4 + k : 5 + k, c] * DP[o : o + T, c]
            acc = term if acc is None else acc + term
            if not gathered:
                o = margin - taps // 2 + k
                PAst[4 + k : 5 + k, c] = total_of(here * UP[o : o + T, c])
        CT[:, c] = acc
    du = CT[...] * row_mask
    sig = jax.nn.sigmoid(GVG[1])
    dvalue = (du * sig).astype(bf16)
    dgate = (du * GVG[0] * (sig * (1.0 - sig))).astype(bf16)
    def sb_to_tensor(name, c, k):
        start(name, lambda: SbSt.at[k, :, c], lambda: Sb.at[place(k), c], peers[k], None, k)

    if not gathered:
        for k in range(4):
            SbSt[k, :, 3 * C : 4 * C] = dvalue[:, C * k : C * (k + 1)]
            SbSt[k, :, 4 * C : 5 * C] = dgate[:, C * k : C * (k + 1)]
        Sb[own, 3 * C : 5 * C] = SbSt[0, :, 3 * C : 5 * C]
        for k in (1, 2, 3):
            sb_to_tensor("gates", gate_cols, k)
    g = g + norm_back(2, dot(dvalue, Wci[0], 1, 1) + dot(dgate, Wci[1], 1, 1))
    b = g.astype(bf16)
    Ball[own, width : 2 * width] = b
    to_pair(("b", 1), Ball, block(1))
    set_off(("b", 1))
    dmix = dot(b, Wo[...], 1, 1).astype(bf16).astype(f32)
    scale = HEAD ** (-0.5)
    dq, dk, dv = [None] * 4, [None] * 4, [None] * 4
    for p in (2, 3, 1, 0):
        c = pl.ds(2 * HEAD * p, 2 * HEAD)
        qu = pair_rows(QKV[0, :, c]).astype(bf16)
        qv = pair_rows(QKV[1, :, c]).astype(bf16)
        key = QKV[2, :, c].astype(bf16)
        val = QKV[3, :, c].astype(bf16)
        do = pair_rows(dmix[:, 2 * HEAD * p : 2 * HEAD * (p + 1)]).astype(bf16)
        probs = PRB[p]
        dprob = dot(do, val, 1, 1)
        ds = (probs * (dprob - jnp.sum(probs * dprob, -1, keepdims=True))).astype(bf16)
        du_rows = unpair(dot(ds, key)) * scale
        turned = dot(ds, flip)
        whole = jnp.concatenate(
            [
                pltpu.roll(turned[e * T : (e + 1) * T], 0, 1, stride=1, stride_axis=0)[:, : 2 * T]
                for e in range(2)
            ],
            0,
        ).astype(bf16)
        dv_rows = unpair(dot(whole, R2[2 * T : 4 * T, c])) * scale
        dk[p] = (dot(ds, qu, 0, 0) * scale).astype(bf16)
        dv[p] = dot(probs.astype(bf16), do, 0, 0).astype(bf16)
        dq[p] = (du_rows + dv_rows).astype(bf16)
        SbSt[p, :, 0:C] = dq[p]
        SbSt[p, :, C : 2 * C] = dk[p]
        SbSt[p, :, 2 * C : 3 * C] = dv[p]
        if p:
            sb_to_tensor("qkv", qkv_cols, p)
        PAst[0:1, c] = total_of(du_rows)
        PAst[1:2, c] = total_of(dv_rows)
        PAst[relative_at(groups) : relative_at(groups) + 2 * T, c] = dot(whole, qv, 0, 0) * scale
    Sb[own, 0 : 3 * C] = SbSt[0, :, 0 : 3 * C]
    @pl.when(first)
    def _():
        if not gathered:
            from_tensor("gates", Sb, gate_cols)
        hop(2, ("b", 3))
        relay(("b", 1), Ball, block(1))
    grad = dot(jnp.concatenate(dq, 1), Wqkv[0], 1, 1)
    grad += dot(jnp.concatenate(dk, 1), Wqkv[1], 1, 1)
    grad += dot(jnp.concatenate(dv, 1), Wqkv[2], 1, 1)
    g = g + norm_back(1, grad)

    @pl.when(second)
    def _():
        IG[pl.ds(trow, T)] = feed_back(0, 0, g).astype(bf16)
        start("back", back_rows, lambda: ARR, partner, second)

    @pl.when(first)
    def _():
        Ball[own, 0:width] = (0.5 * g).astype(bf16)
        to_pair(("b", 0), Ball, block(0))
        G[...] = g

    set_off_to_all(("b", 0))
    from_all(("b", 2))
    def sums_over_tensor(name, parts, ref):
        all_arrived(name, 3 * size_of(parts.at[0]))
        ref[mine] = sum(parts[k].astype(f32) for k in range(4)).astype(bf16)
        for r in range(1, groups):
            start((name, 3), lambda: ref.at[mine], lambda: ref.at[mine], zpeers[r], None, r)

    def send_sums():
        PAb[...] = PAst[...].astype(bf16)
        for k in (1, 2, 3):
            start("pa", lambda k=k: PAb.at[:, cols(k)], lambda k=k: PAin.at[k], peers[k], None, k)

    def send_ends():
        output_to_pair("grad", IG)
        PBin[t] = PBst[...].astype(bf16)
        for k in (1, 2, 3):
            start("pb", lambda: PBin.at[t], lambda: PBin.at[t], peers[k], None, k)

    bs = [("b", i) for i in range(4)]
    if not gathered:

        @pl.when(second)
        def _():
            from_tensor("gates", Sb, gate_cols)

    @pl.when(second)
    def _():
        send_ends()
        send_sums()
        hop(2, "n")
        hop(1, "m", "sf", bs[3])
        relay(bs[1], Ball, block(1))
        relay(bs[0], Ball, block(0))
        from_tensor("qkv", Sb, qkv_cols)
        set_off("qkv")
        hop(1, bs[1])
        hand_on(1, "n")
        from_all(bs[0])
        hand_on_all(bs[2])
        hop(3, "n")
        hop(2, "m", "sf", bs[3], bs[1])
        hand_on(2, "n")
        hop(1, "qkv")
        hand_on(1, "m", bs[3], bs[1])
        hop(3, "m", "sf", bs[3])
        hand_on(3, "n")
        hand_on_all(bs[0])
        hop(3, bs[1])
        hand_on(2, "m", bs[3], bs[1])
        hop(2, "qkv")
        hand_on(3, "m")
        for i in range(4):
            from_pair(("n", i), Nall, block(i))
        all_shared("n", "m")
        forward_values()

    @pl.when(first)
    def _():
        from_tensor("qkv", Sb, qkv_cols)
        set_off("qkv")
        hop(3, bs[3])
        hop(1, bs[1])
        hand_on(1, bs[3])
        hand_on(2, bs[3])
        relay(bs[0], Ball, block(0))
        total = 0.0
        for k in range(2):
            h = dot(Nall[two, 0:width], Win[0, k])
            hg = dot(Ball[two, 0:width], Wout[0, k], 1, 1) * slope(h, jax.nn.sigmoid(h))
            total += dot(hg.astype(bf16), Win[0, k], 1, 1)
        X[0] = sum_to_owner(("s", 2), 2, total)
        send_sums()
        hand_on_all(bs[2])
        from_all(bs[0])
        hop(1, "qkv")
        hop(2, bs[1])
        g = G[...] + norm_back(0, summed_here(("s", 2), 2, X[0]))
        IG[pl.ds(trow, T)] = g.astype(bf16)
        send_ends()
    hand_on(3, bs[3])
    from_pair(bs[3], Ball, block(3))
    shared(bs[3], *whole_rows(bs[3]))
    feed_grads(1, 3)

    @pl.when(first)
    def _():
        hand_on_all(bs[0])
        hop(2, "qkv")
        hop(3, bs[1])

    PAin[0] = PAb[:, 0:C]
    sums_over_tensor("pa", PAin, PA)
    sums_over_tensor("pb", PBin, PB)
    from_pair(bs[2], Ball, block(2))
    shared(bs[2], *whole_rows(bs[2]))
    if gathered:
        convolution_rows_back()

    @pl.when(first)
    def _():
        hand_on(1, bs[1])
        hand_on(2, bs[1])

    convolution_grads()
    relay_output("grad", IG)
    hand_on(3, bs[1])

    from_pair(bs[0], Ball, block(0))
    shared(bs[0], *whole_rows(bs[0]))
    feed_grads(0, 0)
    hop(3, "qkv")
    from_pair(bs[1], Ball, block(1))
    shared(bs[1], *whole_rows(bs[1]))
    attention_grads()
    for name, ref in (("pa", PA), ("pb", PB)):
        all_arrived((name, 3), (groups - 1) * size_of(ref.at[0]))
    all_arrived("out", 2 * size_of(back_rows()))
    all_arrived("grad", 2 * size_of(back_rows()))
    for src, dst in ((LO, lo_out), (IG, ig_out), (PA, pa_out), (PB, pb_out), (CS, cs_out)):
        write(src, dst)
    pltpu.make_async_copy(room(sum(written)), room(sum(written)), os.at[0]).wait()
    for cond, sizes in sent.values():

        def all_sent():
            view = room(sum(sizes.values()))
            copy_of("out", view, view, partner, cond).wait_send()

        all_sent() if cond is None else pl.when(cond)(all_sent)
    assert len(recv_index) <= rs.shape[0] and len(send_index) <= ss.shape[0]


def last_kernel(*refs):
    given, outs, held, made, in_sems, out_sems = refs[:12], refs[12:26], refs[26:38], refs[38:52], refs[52], refs[53]
    in_grad, out_grad, qkv, ao, ci, co, pa, pb, cs, lo, ig, table = held
    (LO, IG, ng, nb, w_in, w_out, w_ain, pos, w_aout, w_cin, w_dw, bng, bns, w_cout) = made
    C, width = ao.shape
    copies = []

    def send(src, dst):
        copy = pltpu.make_async_copy(src, dst, out_sems.at[len(copies)])
        copy.start()
        copies.append(copy)

    whole = [5, 3, 4, 2, 6, 7, 8, 9, 10, 11]
    halves = [(i, j) for i in range(2) for j in range(2)]
    pieces = [(given[i], held[i]) for i in whole[:4]]
    pieces += [(given[i].at[j], held[i].at[j]) for i, j in halves]
    pieces += [(given[i], held[i]) for i in whole[4:]]
    loads = [pltpu.make_async_copy(src, dst, in_sems.at[n]) for n, (src, dst) in enumerate(pieces)]
    for load in loads:
        load.start()
    loads[0].wait()
    w_cout[...] = co[...].astype(f32)
    send(w_cout, outs[13])
    loads[1].wait()
    w_aout[...] = ao[...].astype(f32)
    send(w_aout, outs[8])
    loads[2].wait()
    for i in range(2):
        w_cin[pl.ds(i, width, stride=2), :] = ci[:, C * i : C * (i + 1)].astype(f32)
    send(w_cin, outs[9])
    loads[3].wait()
    w_ain[0:3] = qkv[...].astype(f32)
    send(w_ain.at[pl.ds(0, 3)], outs[6].at[pl.ds(0, 3)])
    for n, (i, j) in enumerate(halves):
        loads[4 + n].wait()
        src, dst, out = ((in_grad, w_in, outs[4]), (out_grad, w_out, outs[5]))[i]
        dst[j] = src[j].astype(f32)
        send(dst.at[j], out.at[j])
    for load in loads[8:]:
        load.wait()
    sums, norms = pa[0].astype(f32), pb[0].astype(f32)
    for g in range(1, pa.shape[0]):
        sums += pa[g].astype(f32)
        norms += pb[g].astype(f32)
    w_ain[3] = dot(table[...], sums[relative_at(pa.shape[0]) :].astype(bf16), 0, 0)
    send(w_ain.at[3], outs[6].at[3])
    LO[...] = lo[...].astype(f32)
    IG[...] = ig[...].astype(f32)
    for i in range(5):
        ng[i] = norms[i : i + 1]
        nb[i] = norms[8 + i : 9 + i]
    pos[...] = sums[0:2]
    taps = w_dw.shape[0]
    if pa.shape[0] > 1:
        sums = jnp.concatenate([sums[0:2], cs[taps : taps + 2], cs[0:taps]], 0)
    bng[...] = sums[2:3]
    bns[...] = sums[3:4]
    for k in range(taps):
        w_dw[k] = sums[4 + k : 5 + k]
    for i in (0, 1, 2, 3, 7, 10, 11, 12):
        send(made[i], outs[i])
    for copy in copies:
        copy.wait()


def on_device(
    inputs, lengths, cotangent, norm_gain, norm_bias, ffn_in, ffn_out, attn_in, pos_bias, attn_out,
    conv_in, depthwise, bn_gain, bn_shift, conv_out,
):
    dp = lax.axis_size(DATA)
    group, frames, width = inputs.shape
    C = width // 4
    taps = depthwise.shape[1]
    groups = dp if dp <= 4 else 1
    R = groups * group * frames
    table = position_rows(frames, width)
    hbm = pl.BlockSpec(memory_space=pltpu.HBM)
    sums_rows = relative_at(groups) + 2 * frames

    def shape(dims, dtype=bf16):
        return jax.ShapeDtypeStruct(dims, dtype)

    small_first = [
        shape((group * frames, width)), shape((group * frames, width)), shape((groups, sums_rows, C)),
        shape((groups, 16, width)), shape((40, C), f32),
    ]
    made_first = [
        shape((2, width, width)), shape((2, width, width)), shape((3, width, C)), shape((C, width)),
        shape((width, 2 * C)), shape((C, width)),
    ]
    n_recv = 109 + 15 * (groups - 1)
    n_send = 3 + 2 * (groups - 1) + 2 * max(groups - 2, 0)
    operands = (
        lengths, inputs, cotangent, norm_gain.transpose(1, 0, 2), norm_bias.transpose(1, 0, 2), ffn_in[0],
        ffn_out[0], attn_in[0], attn_out[0], conv_in.reshape(2 * width, C), conv_out[0], pos_bias[0], bn_gain,
        bn_shift, depthwise.transpose(1, 0, 2), table[0],
    )
    lo, ig, pa, pb, cs, *ready = pl.pallas_call(
        lambda *refs: layer_kernel((frames, width, dp, groups), *refs),
        out_shape=small_first + made_first,
        in_specs=[hbm] * 16,
        out_specs=[hbm] * 11,
        scratch_shapes=[
            pltpu.VMEM((2, 4, width, width), bf16),
            pltpu.VMEM((2, 4, width, width), bf16),
            pltpu.VMEM((3, width, width), bf16),
            pltpu.VMEM((width, C), bf16),
            pltpu.VMEM((width, width), bf16),
            pltpu.VMEM((2, width, width), bf16),
            pltpu.VMEM((width, width), bf16),
            pltpu.VMEM((4 * frames, width), bf16),
            pltpu.VMEM((SMALL_ROWS, width), f32),
            pltpu.VMEM((2, 4, frames, width), f32),
            pltpu.VMEM((5, frames, width), f32),
            pltpu.VMEM((5, frames, 128), f32),
            pltpu.VMEM((5, frames, width), f32),
            pltpu.VMEM((frames, width), f32),
            pltpu.VMEM((frames, width), bf16),
            pltpu.VMEM((frames, width), bf16),
            pltpu.VMEM((4, frames, width), f32),
            pltpu.VMEM((4, 2 * frames, frames), f32),
            pltpu.VMEM((2, frames, width), f32),
            pltpu.VMEM((frames, width), f32),
            pltpu.VMEM((frames + 32, width), f32),
            pltpu.VMEM((frames + 32, width), f32),
            pltpu.VMEM((4, frames, 2 * C), bf16),
            pltpu.VMEM((4, frames, 5 * C), bf16),
            pltpu.VMEM((sums_rows, width), f32),
            pltpu.VMEM((sums_rows, width), bf16),
            pltpu.VMEM((4, sums_rows, C), bf16),
            pltpu.VMEM((16, width), f32),
            pltpu.VMEM((4, 16, width), bf16),
            pltpu.VMEM((dp, 8, C), f32),
            pltpu.VMEM((dp, 8, C), f32),
            pltpu.VMEM((4, frames, width), bf16),
            pltpu.VMEM((4, frames, width), bf16),
            pltpu.VMEM((5, 1, width), f32),
            pltpu.VMEM((5, 1, width), f32),
            pltpu.VMEM((2, C), f32),
            pltpu.VMEM((1, C), f32),
            pltpu.VMEM((1, C), f32),
            pltpu.VMEM((taps, 1, C), f32),
            pltpu.VMEM((2 * frames, width), bf16),
            pltpu.SMEM((group,), jnp.int32),
            pltpu.VMEM((2 * width, C), bf16),
            pltpu.VMEM((2 * width, C), f32),
            pltpu.VMEM((R, 4 * width), bf16),
            pltpu.VMEM((R, 4 * width), bf16),
            pltpu.VMEM((R, 2 * C), bf16),
            pltpu.VMEM((R, 5 * C), bf16),
            pltpu.VMEM((2, R, width), bf16),
            pltpu.VMEM((2, R, width), f32),
            pltpu.VMEM((R, width), bf16),
        ]
        + [pltpu.VMEM(m.shape, m.dtype) for m in made_first]
        + [
            pltpu.VMEM((2, R, C), f32),
            pltpu.VMEM((R, C), f32),
            pltpu.VMEM((R // frames, frames + 32, C), f32),
            pltpu.VMEM((R, C), f32),
            pltpu.VMEM((R // frames, frames + 32, C), f32),
            pltpu.VMEM((taps, 8, C), f32),
            pltpu.VMEM((4, 8, C), f32),
            pltpu.VMEM((2 * frames, C), bf16),
            pltpu.VMEM((dp, 8, C), f32),
            pltpu.VMEM((2, width // 4, width), bf16),
        ]
        + [pltpu.VMEM(m.shape, m.dtype) for m in small_first]
        + [
            pltpu.VMEM((10 * 2**20 // 512, 128), f32),
            pltpu.SemaphoreType.DMA((n_send,)),
            pltpu.SemaphoreType.DMA((n_recv,)),
            pltpu.SemaphoreType.DMA((21,)),
            pltpu.SemaphoreType.DMA((1,)),
        ],
        compiler_params=pltpu.CompilerParams(
            collective_id=0, has_side_effects=True, vmem_limit_bytes=62 * 2**20
        ),
    )(*operands)

    gradients = [
        shape((group * frames, width), f32), shape((group * frames, width), f32), shape((5, 1, width), f32),
        shape((5, 1, width), f32), shape((2, width, width), f32), shape((2, width, width), f32),
        shape((4, width, C), f32), shape((2, C), f32), shape((C, width), f32), shape((2 * width, C), f32),
        shape((taps, 1, C), f32), shape((1, C), f32), shape((1, C), f32), shape((C, width), f32),
    ]
    given = (*ready, pa, pb, cs, lo, ig, table[1])
    outs = pl.pallas_call(
        last_kernel,
        out_shape=gradients,
        in_specs=[hbm] * len(given),
        out_specs=[hbm] * len(gradients),
        scratch_shapes=[pltpu.VMEM(m.shape, m.dtype) for m in given]
        + [pltpu.VMEM(m.shape, m.dtype) for m in gradients]
        + [pltpu.SemaphoreType.DMA((len(given) + 2,)), pltpu.SemaphoreType.DMA((len(gradients) + 4,))],
        compiler_params=pltpu.CompilerParams(vmem_limit_bytes=62 * 2**20),
    )(*given)
    if groups == 1:
        outs = list(outs[:2]) + [lax.psum(m.astype(bf16), DATA).astype(f32) for m in outs[2:]]
    (lo, ig, ng, nb, w_in, w_out, w_ain, pos, w_aout, w_cin, w_dw, bng, bns, w_cout) = outs
    rows = (1, group, frames, width)
    return (
        lo.reshape(rows), ig.reshape(rows), ng.transpose(1, 0, 2), nb.transpose(1, 0, 2), w_in[None], w_out[None],
        w_ain[None], pos[None], w_aout[None], w_cin.reshape(conv_in.shape), w_dw.transpose(1, 0, 2), bng, bns,
        w_cout[None],
    )


def solution(mesh):
    placed = (
        P(DATA, None, None),
        P(DATA),
        P(DATA, None, None),
        P(SECTION, None, None),
        P(SECTION, None, None),
        P(SECTION, None, None, TENSOR),
        P(SECTION, None, TENSOR, None),
        P(SECTION, None, None, TENSOR),
        P(SECTION, None, TENSOR),
        P(SECTION, TENSOR, None),
        P(SECTION, None, None, TENSOR),
        P(SECTION, None, TENSOR),
        P(SECTION, TENSOR),
        P(SECTION, TENSOR),
        P(SECTION, TENSOR, None),
    )
    return jax.shard_map(
        on_device,
        mesh=mesh,
        in_specs=placed,
        out_specs=(
            P(SECTION, DATA, None, None),
            P(SECTION, DATA, None, None),
            P(SECTION, None, None),
            P(SECTION, None, None),
            P(SECTION, None, None, TENSOR),
            P(SECTION, None, TENSOR, None),
            P(SECTION, None, None, TENSOR),
            P(SECTION, None, TENSOR),
            P(SECTION, TENSOR, None),
            P(SECTION, None, None, TENSOR),
            P(SECTION, None, TENSOR),
            P(SECTION, TENSOR),
            P(SECTION, TENSOR),
            P(SECTION, TENSOR, None),
        ),
        check_vma=False,
    )
```
